32 devices in a mesh: wide: 8 (over y, x, core), narrow: 4 (over z).
Axes of the slice: x: 2, y: 2, z: 4, core: 2. Of those that a mesh axis runs over, the one named last changes fastest.
Arguments:
- tokens: bfloat16 [4, 2048, 2048], P('narrow', 'wide'), may hold values from -6 to 6
- doc_starts: int32 [4, 4], replicated, may hold values from 1 to 2047, as said below
- query_weight: bfloat16 [2048, 2048], P(('wide', 'narrow')), may hold values from -0.125 to 0.125
- key_weight: bfloat16 [2048, 2048], P(('wide', 'narrow')), may hold values from -0.125 to 0.125
- value_weight: bfloat16 [2048, 2048], P(('wide', 'narrow')), may hold values from -0.125 to 0.125
- gate_weight: bfloat16 [2048, 2048], P(('wide', 'narrow')), may hold values from -0.125 to 0.125
- out_weight: bfloat16 [2048, 2048], P(('wide', 'narrow')), may hold values from -0.125 to 0.125
- ffn_value_weight: bfloat16 [2048, 5632], P(('wide', 'narrow')), may hold values from -0.125 to 0.125
- ffn_gate_weight: bfloat16 [2048, 5632], P(('wide', 'narrow')), may hold values from -0.125 to 0.125
- ffn_out_weight: bfloat16 [5632, 2048], P(('wide', 'narrow')), may hold values from -0.078125 to 0.078125
- cotangent: bfloat16 [4, 2048, 2048], P('narrow', 'wide'), may hold values from -6 to 6
Outputs:
- output: bfloat16 [4, 2048, 2048], P('narrow', 'wide')
- input_grad: float32 [4, 2048, 2048], P('narrow', 'wide')
- query_grad: float32 [2048, 2048], P(('wide', 'narrow'))
- key_grad: float32 [2048, 2048], P(('wide', 'narrow'))
- value_grad: float32 [2048, 2048], P(('wide', 'narrow'))
- gate_grad: float32 [2048, 2048], P(('wide', 'narrow'))
- out_grad: float32 [2048, 2048], P(('wide', 'narrow'))
- ffn_value_grad: float32 [2048, 5632], P(('wide', 'narrow'))
- ffn_gate_grad: float32 [2048, 5632], P(('wide', 'narrow'))
- ffn_out_grad: float32 [5632, 2048], P(('wide', 'narrow'))
The draws below stay inside these ranges and needn't reach their ends.
Inputs may be any that keep to these rules, and one draw needn't show every extreme that they name: Each row of doc_starts is ascending and may repeat entries; position 0 also starts a document; in one sequence, chosen by the seed, the entries lie in the first 256 or the last 256 positions, with 1 and 2047 among them.
All inputs are finite; a program needn't handle non-finite values.
Results may differ from the reference program's by a relative error of at most 0.014.
Values may be sent and summed in bfloat16 or wider, within the bound.
A program may use at most 448 MiB of HBM per device.

```python
import jax
import jax.numpy as jnp
from jax import lax

D = 2048
HEADS = 16
HEAD = 128
FF = 5632
BLOCK = 256
LAYERS = 16
LAYER = 12
DOCS = 4
TOK_DEV = 256
SEQS = 4
LENGTH = 2048


def draw_doc_starts(key, part):
    key = jax.random.fold_in(key, 11)
    key_all, key_pick, key_side, key_offset = jax.random.split(key, 4)
    general_rows = jax.random.randint(key_all, (SEQS, DOCS), 1, LENGTH)
    chosen_row = jax.random.randint(key_pick, (), 0, SEQS)
    pick_side = jax.random.randint(key_side, (DOCS,), 0, 2)
    offsets_in = jax.random.randint(key_offset, (DOCS,), 1, TOK_DEV)
    special = jnp.where(pick_side == 0, offsets_in, LENGTH - offsets_in)
    special = special.at[0].set(1).at[DOCS - 1].set(LENGTH - 1)
    all_rows = jnp.where(jnp.arange(SEQS)[:, None] == chosen_row, special[None, :], general_rows)
    return jnp.sort(all_rows, axis=1).astype(jnp.int32)


def levels(stream_key, extent, cuts, least, largest):
    gain = 1.0
    for axis_at, parts in cuts:
        heights = jax.random.uniform(jax.random.fold_in(jax.random.fold_in(stream_key, 6), axis_at), (parts,), jnp.float32, least / len(cuts), largest / len(cuts))
        gain = gain * jnp.repeat(jnp.exp(heights), extent[axis_at] // parts).reshape((-1,) + (1,) * (len(extent) - 1 - axis_at))
    return gain


def normal_values(rng, extent, deviation, most, cuts=(), held_as=jnp.bfloat16):
    drawn = jax.random.normal(rng, extent, jnp.float32) * deviation
    if len(cuts) > 0:
        drawn = levels(rng, extent, cuts, -0.22, 0.18) * drawn
    return jnp.clip(drawn, min=-most, max=most).astype(held_as)


def setup_inputs(seed: int = 0) -> dict:
    key_list = jax.random.split(jax.random.key(seed), 12)
    tokens = normal_values(key_list[0], (SEQS, LENGTH, D), 1.0, 6.0, ((0, 4), (1, 8)))
    doc_starts = draw_doc_starts(jax.random.fold_in(key_list[11], 71), 0)
    query_weight = normal_values(key_list[2], (D, D), D ** -0.5, 0.125, ((0, 32),))
    key_weight = normal_values(key_list[3], (D, D), D ** -0.5, 0.125, ((0, 32),))
    value_weight = normal_values(key_list[4], (D, D), D ** -0.5, 0.125, ((0, 32),))
    gate_weight = normal_values(key_list[5], (D, D), D ** -0.5, 0.125, ((0, 32),))
    out_weight = normal_values(key_list[6], (D, D), D ** -0.5, 0.125, ((0, 32),))
    ffn_value_weight = normal_values(key_list[7], (D, FF), D ** -0.5, 0.125, ((0, 32),))
    ffn_gate_weight = normal_values(key_list[8], (D, FF), D ** -0.5, 0.125, ((0, 32),))
    ffn_out_weight = normal_values(key_list[9], (FF, D), FF ** -0.5, 0.078125, ((0, 32),))
    cotangent = normal_values(key_list[10], (SEQS, LENGTH, D), 1.0, 6.0, ((0, 4), (1, 8)))
    return dict(tokens=tokens, doc_starts=doc_starts, query_weight=query_weight, key_weight=key_weight, value_weight=value_weight, gate_weight=gate_weight, out_weight=out_weight, ffn_value_weight=ffn_value_weight, ffn_gate_weight=ffn_gate_weight, ffn_out_weight=ffn_out_weight, cotangent=cotangent)


EPS = 1e-06
HIGH = lax.Precision.HIGHEST

@jax.custom_vjp
def low(v):
    return lax.optimization_barrier(v.astype(jnp.bfloat16)).astype(jnp.float32)

@jax.custom_vjp
def low_back(v):
    return v

def low_keep(v):
    return (low(v), None)

def low_pass(kept, grad):
    return (grad,)

def back_keep(v):
    return (v, None)

def back_low(kept, grad):
    return (low(grad),)
low.defvjp(low_keep, low_pass)
low_back.defvjp(back_keep, back_low)

def srms(values):
    return values * lax.rsqrt(lax.optimization_barrier(jnp.mean(values * values, axis=-1, keepdims=True)) + EPS)

def head_slopes():
    order = jnp.arange(HEADS, dtype=jnp.float32)
    return jnp.exp2(-8.0 * (order + 1.0) / HEADS) * (1.0 - LAYER / (LAYERS - 1) + 1e-05)

def project(left, right):
    return jnp.einsum('std,df->stf', left, right, precision=HIGH)

def lightning(queries, keys, values, doc_ids, prev_ids):
    seq_count = queries.shape[0]
    nblocks = LENGTH // BLOCK
    slope = head_slopes()
    offsets = jnp.arange(BLOCK, dtype=jnp.float32)
    lag = offsets[:, None] - offsets[None, :]
    decay = jnp.exp(-slope[:, None, None] * jnp.maximum(lag, 0.0)[None])
    entry_decay = jnp.exp(-slope[None, :] * (offsets[:, None] + 1.0))
    tail_decay = jnp.exp(-slope[None, :] * (BLOCK - 1.0 - offsets)[:, None])
    pass_decay = jnp.exp(-slope * BLOCK)

    def to_blocks(arr):
        return arr.reshape(seq_count, nblocks, BLOCK, HEADS, HEAD).transpose(1, 0, 2, 3, 4)

    def advance(state, item):
        q_blk, k_blk, v_blk, docs, prev = item
        within = (docs[:, :, None] == docs[:, None, :]) & (lag >= 0.0)[None]
        mask = jnp.where(within[:, None], decay[None], 0.0)
        scores = jnp.einsum('sihe,sjhe->shij', q_blk, k_blk, precision=HIGH)
        probs = low(low_back(scores) * mask)
        result = jnp.einsum('shij,sjhe->sihe', probs, v_blk, precision=HIGH)
        cont = (docs == prev[:, None]).astype(jnp.float32)
        entry = cont[:, :, None] * entry_decay[None]
        result = result + entry[..., None] * jnp.einsum('sihe,shef->sihf', q_blk, state, precision=HIGH)
        tail = (docs == docs[:, -1:]).astype(jnp.float32)[:, :, None] * tail_decay[None]
        passing = cont[:, -1:] * pass_decay[None]
        fresh = jnp.einsum('sjhe,sjhf->shef', k_blk * tail[..., None], v_blk, precision=HIGH)
        return (passing[:, :, None, None] * state + fresh, result)
    start_state = jnp.zeros((seq_count, HEADS, HEAD, HEAD), jnp.float32)
    docs_blocks = doc_ids.reshape(seq_count, nblocks, BLOCK).transpose(1, 0, 2)
    prev_blocks = prev_ids.transpose(1, 0)
    items = (to_blocks(queries), to_blocks(keys), to_blocks(values), docs_blocks, prev_blocks)
    final_state, outs = lax.scan(jax.checkpoint(advance), start_state, items)
    return outs.transpose(1, 0, 2, 3, 4).reshape(seq_count, LENGTH, HEADS * HEAD)

def reference(tokens, doc_starts, query_weight, key_weight, value_weight, gate_weight, out_weight, ffn_value_weight, ffn_gate_weight, ffn_out_weight, cotangent):
    nblocks = LENGTH // BLOCK
    positions = jnp.arange(LENGTH, dtype=jnp.int32)
    doc_ids = lax.optimization_barrier(jnp.sum((doc_starts[:, None, :] <= positions[None, :, None]).astype(jnp.int32), axis=2))
    firsts = jnp.arange(nblocks, dtype=jnp.int32) * BLOCK - 1
    prev_ids = lax.optimization_barrier(jnp.sum((doc_starts[:, None, :] <= firsts[None, :, None]).astype(jnp.int32), axis=2))

    def layer(inputs, w_query, w_key, w_value, w_gate, w_out, w_fval, w_fgate, w_fout):
        normed = low(srms(inputs))
        queries = low(jax.nn.silu(low_back(project(normed, w_query))))
        keys = low(jax.nn.silu(low_back(project(normed, w_key))))
        values = low(low_back(project(normed, w_value)))
        gate = low_back(project(normed, w_gate))
        attn = low_back(lightning(queries, keys, values, doc_ids, prev_ids))
        mixed = low(srms(attn) * gate)
        middle = inputs + low_back(project(mixed, w_out))
        middle_n = low(srms(middle))
        ffn_mix = low(low_back(project(middle_n, w_fval)) * low_back(project(middle_n, w_fgate)))
        return middle + low_back(project(ffn_mix, w_fout))
    primals = [a.astype(jnp.float32) for a in (tokens, query_weight, key_weight, value_weight, gate_weight, out_weight, ffn_value_weight, ffn_gate_weight, ffn_out_weight)]
    result, pullback = jax.vjp(layer, *primals)
    grads = pullback(cotangent.astype(jnp.float32))
    return (result.astype(jnp.bfloat16), grads[0], grads[1], grads[2], grads[3], grads[4], grads[5], grads[6], grads[7], grads[8])
```

```python
import jax
import jax.numpy as jnp
from jax import lax
from jax.sharding import PartitionSpec as P

HEADS = 16
HEAD = 128
BLOCK = 256
LAYERS = 16
LAYER = 12

EPS = 1e-06
BOTH = ("wide", "narrow")
BF = jnp.bfloat16
F32 = jnp.float32


def normalize(values):
    scale = lax.rsqrt(jnp.mean(values * values, axis=-1, keepdims=True) + EPS)
    return (values * scale, scale)


def normalize_back(normed, scale, grad):
    return scale * (grad - normed * jnp.mean(grad * normed, axis=-1, keepdims=True))


def silu_slope(values):
    sigma = jax.nn.sigmoid(values)
    return sigma * (1.0 + values * (1.0 - sigma))


def matmul(left, right):
    return jnp.dot(left, right, preferred_element_type=F32)


def matmul_right_t(left, right):
    return lax.dot_general(left, right, (((1,), (1,)), ((), ())), preferred_element_type=F32)


def weight_grad(left, right):
    return lax.dot_general(left, right, (((0,), (0,)), ((), ())), preferred_element_type=F32)


def ein(spec, left, right):
    return jnp.einsum(spec, left, right, preferred_element_type=F32)


def head_slopes():
    order = jnp.arange(HEADS, dtype=F32)
    return jnp.exp2(-8.0 * (order + 1.0) / HEADS) * (1.0 - LAYER / (LAYERS - 1) + 1e-05)


def local(
    tokens,
    doc_starts,
    query_weight,
    key_weight,
    value_weight,
    gate_weight,
    out_weight,
    ffn_value_weight,
    ffn_gate_weight,
    ffn_out_weight,
    cotangent,
):
    wide, narrow = lax.axis_size("wide"), lax.axis_size("narrow")
    rows_here, width = tokens.shape[1:]
    length = rows_here * wide
    blocks = length // BLOCK
    heads_here = HEADS // wide
    shard = query_weight.shape[0]

    def reorder(values):
        return values.reshape(-1, wide, narrow, shard).swapaxes(1, 2).reshape(-1, width)

    def restore(values):
        return values.reshape(-1, narrow, wide, shard).swapaxes(1, 2).reshape(-1, width)

    def columns(weight):
        part = lax.all_to_all(weight, "wide", split_axis=1, concat_axis=0, tiled=True)
        return lax.all_gather(part, "narrow", axis=0, tiled=True)

    def gather_rows(values):
        return lax.all_gather(values, "wide", axis=0, tiled=True)

    def scatter_rows(values):
        return lax.psum_scatter(
            values.astype(BF), "wide", scatter_dimension=0, tiled=True
        ).astype(F32)

    def to_tokens(values):
        return lax.all_to_all(values, "wide", split_axis=0, concat_axis=1, tiled=True)

    def to_heads(values):
        return lax.all_to_all(values, "wide", split_axis=1, concat_axis=0, tiled=True)

    def column_sums(grad):
        part = lax.psum_scatter(grad.astype(BF), "narrow", scatter_dimension=0, tiled=True)
        return lax.all_to_all(part, "wide", split_axis=0, concat_axis=1, tiled=True).astype(F32)

    w_query, w_key, w_value, w_gate = map(
        columns, (query_weight, key_weight, value_weight, gate_weight)
    )
    w_out = lax.all_gather(out_weight, BOTH, axis=0, tiled=True)
    w_fval, w_fgate = map(columns, (ffn_value_weight, ffn_gate_weight))
    w_fout = lax.all_gather(ffn_out_weight, "narrow", axis=0, tiled=True)

    starts = lax.dynamic_slice_in_dim(doc_starts, lax.axis_index("narrow"), 1, 0)[0]
    positions = jnp.arange(length, dtype=jnp.int32)
    doc_ids = jnp.sum((starts[None, :] <= positions[:, None]).astype(jnp.int32), axis=1)
    doc_ids = doc_ids.reshape(blocks, BLOCK)
    firsts = jnp.arange(blocks, dtype=jnp.int32) * BLOCK - 1
    prev_ids = jnp.sum((starts[None, :] <= firsts[:, None]).astype(jnp.int32), axis=1)
    slopes = lax.dynamic_slice_in_dim(
        head_slopes(), lax.axis_index("wide") * heads_here, heads_here, 0
    )
    offsets = jnp.arange(BLOCK, dtype=F32)
    lags = offsets[:, None] - offsets[None, :]
    decays = jnp.exp(-slopes[:, None, None] * jnp.maximum(lags, 0.0)[None])
    within = (doc_ids[:, :, None] == doc_ids[:, None, :]) & (lags >= 0.0)
    block_mask = jnp.where(within[:, None], decays[None], 0.0)
    continues = (doc_ids == prev_ids[:, None]).astype(F32)
    entry_scale = continues[..., None] * jnp.exp(-slopes[None, :] * (offsets[:, None] + 1.0))
    tail_scale = (doc_ids == doc_ids[:, -1:]).astype(F32)[..., None] * jnp.exp(
        -slopes[None, :] * (BLOCK - 1.0 - offsets)[:, None]
    )
    passing = continues[:, -1:] * jnp.exp(-slopes * BLOCK)

    def split_heads(values):
        return values.reshape(blocks, BLOCK, heads_here, HEAD)

    inputs = tokens[0].astype(F32)
    normed, in_scale = normalize(inputs)
    normed_bf = gather_rows(reorder(normed.astype(BF)))
    query_pre = matmul(normed_bf, w_query)
    key_pre = matmul(normed_bf, w_key)
    queries = split_heads(jax.nn.silu(query_pre).astype(BF))
    keys = split_heads(jax.nn.silu(key_pre).astype(BF))
    values = split_heads(matmul(normed_bf, w_value).astype(BF))
    gate = matmul(normed_bf, w_gate)
    scores = ein("bihe,bjhe->bhij", queries, keys)
    probs = (scores * block_mask).astype(BF)
    inner = ein("bhij,bjhe->bihe", probs, values)
    tail_keys = (keys.astype(F32) * tail_scale[..., None]).astype(BF)
    fresh = ein("bjhe,bjhf->bhef", tail_keys, values)
    state = jnp.zeros((heads_here, HEAD, HEAD), F32)
    entering = []
    for b in range(blocks):
        entering.append(state)
        state = passing[b][:, None, None] * state + fresh[b]
    block_in = jnp.stack(entering).astype(BF)
    across = entry_scale[..., None] * ein("bihe,bhef->bihf", queries, block_in)
    attention = (inner + across).reshape(query_pre.shape)

    attn_tok = to_tokens(attention)
    gate_tok = to_tokens(gate)
    attn_n, attn_scale = normalize(attn_tok)
    mixed = (attn_n * gate_tok).astype(BF)
    middle = inputs + matmul(mixed, w_out)
    middle_n, middle_scale = normalize(middle)
    middle_bf = gather_rows(reorder(middle_n.astype(BF)))
    ffn_val = matmul(middle_bf, w_fval)
    ffn_gat = matmul(middle_bf, w_fgate)
    ffn_mix = (ffn_val * ffn_gat).astype(BF)
    result = middle + scatter_rows(matmul(ffn_mix, w_fout))

    upstream = cotangent[0]
    up_all = gather_rows(upstream)
    grad_fout = weight_grad(ffn_mix, up_all)
    d_mix = matmul_right_t(up_all, w_fout)
    d_val = (d_mix * ffn_gat).astype(BF)
    d_gat = (d_mix * ffn_val).astype(BF)
    grad_fval = weight_grad(middle_bf, d_val)
    grad_fgate = weight_grad(middle_bf, d_gat)
    d_middle_n = restore(
        scatter_rows(matmul_right_t(d_val, w_fval) + matmul_right_t(d_gat, w_fgate))
    )
    d_middle = upstream.astype(F32) + normalize_back(middle_n, middle_scale, d_middle_n)
    d_branch = d_middle.astype(BF)
    grad_out = weight_grad(mixed, d_branch)
    d_mixed = matmul_right_t(d_branch, w_out)
    d_gate = to_heads((d_mixed * attn_n).astype(BF))
    d_attn = to_heads(normalize_back(attn_n, attn_scale, d_mixed * gate_tok).astype(BF))

    d_heads = split_heads(d_attn)
    d_probs = ein("bihe,bjhe->bhij", d_heads, values)
    d_scores = (d_probs * block_mask).astype(BF)
    d_query = ein("bhij,bjhe->bihe", d_scores, keys)
    d_key = ein("bhij,bihe->bjhe", d_scores, queries)
    d_value = ein("bhij,bihe->bjhe", probs, d_heads)
    d_query = d_query + entry_scale[..., None] * ein("bihf,bhef->bihe", d_heads, block_in)
    entry_queries = (queries.astype(F32) * entry_scale[..., None]).astype(BF)
    grad_in = ein("bihe,bihf->bhef", entry_queries, d_heads)
    state = jnp.zeros((heads_here, HEAD, HEAD), F32)
    leaving = [None] * blocks
    for b in reversed(range(blocks)):
        leaving[b] = state
        state = passing[b][:, None, None] * state + grad_in[b]
    block_out = jnp.stack(leaving).astype(BF)
    d_key = d_key + tail_scale[..., None] * ein("bjhf,bhef->bjhe", values, block_out)
    d_value = d_value + ein("bjhe,bhef->bjhf", tail_keys, block_out)
    dq_pre = (d_query.reshape(query_pre.shape) * silu_slope(query_pre)).astype(BF)
    dk_pre = (d_key.reshape(key_pre.shape) * silu_slope(key_pre)).astype(BF)
    dv_pre = d_value.reshape(query_pre.shape).astype(BF)
    grad_query = weight_grad(normed_bf, dq_pre)
    grad_key = weight_grad(normed_bf, dk_pre)
    grad_value = weight_grad(normed_bf, dv_pre)
    grad_gate = weight_grad(normed_bf, d_gate)
    d_normed = restore(
        scatter_rows(
            matmul_right_t(dq_pre, w_query)
            + matmul_right_t(dk_pre, w_key)
            + matmul_right_t(dv_pre, w_value)
            + matmul_right_t(d_gate, w_gate)
        )
    )
    d_inputs = d_middle + normalize_back(normed, in_scale, d_normed)
    return (
        result.astype(BF)[None],
        d_inputs[None],
        column_sums(grad_query),
        column_sums(grad_key),
        column_sums(grad_value),
        column_sums(grad_gate),
        lax.psum_scatter(grad_out.astype(BF), BOTH, scatter_dimension=0, tiled=True).astype(F32),
        column_sums(grad_fval),
        column_sums(grad_fgate),
        lax.psum_scatter(grad_fout.astype(BF), "narrow", scatter_dimension=0, tiled=True).astype(
            F32
        ),
    )


def solution(mesh):
    tok = P("narrow", "wide", None)
    row = P(BOTH, None)
    return jax.shard_map(
        local,
        mesh=mesh,
        in_specs=(tok, P()) + (row,) * 8 + (tok,),
        out_specs=(tok, tok) + (row,) * 8,
        check_vma=False,
    )
```

```python
import jax
import jax.numpy as jnp
from jax import lax
from jax.experimental import pallas as pl
from jax.experimental.pallas import tpu as pltpu
from jax.sharding import PartitionSpec as P

HEADS = 16
HEAD = 128
BLOCK = 256
LAYERS = 16
LAYER = 12

EPS = 1e-06
BOTH = ("wide", "narrow")
BF = jnp.bfloat16
F32 = jnp.float32


def normalize(values):
    scale = lax.rsqrt(jnp.mean(values * values, axis=-1, keepdims=True) + EPS)
    return (values * scale, scale)


def normalize_back(normed, scale, grad):
    return scale * (grad - normed * jnp.mean(grad * normed, axis=-1, keepdims=True))


def silu_slope(values):
    sigma = jax.nn.sigmoid(values)
    return sigma * (1.0 + values * (1.0 - sigma))


def matmul(left, right):
    return jnp.dot(left, right, preferred_element_type=F32)


def matmul_right_t(left, right):
    return lax.dot_general(left, right, (((1,), (1,)), ((), ())), preferred_element_type=F32)


def weight_grad(left, right):
    return lax.dot_general(left, right, (((0,), (0,)), ((), ())), preferred_element_type=F32)


def ein(spec, left, right):
    return jnp.einsum(spec, left, right, preferred_element_type=F32)


def head_slopes():
    order = jnp.arange(HEADS, dtype=F32)
    return jnp.exp2(-8.0 * (order + 1.0) / HEADS) * (1.0 - LAYER / (LAYERS - 1) + 1e-05)


def local(
    tokens,
    doc_starts,
    query_weight,
    key_weight,
    value_weight,
    gate_weight,
    out_weight,
    ffn_value_weight,
    ffn_gate_weight,
    ffn_out_weight,
    cotangent,
):
    wide, narrow = lax.axis_size("wide"), lax.axis_size("narrow")
    rows_here, width = tokens.shape[1:]
    length = rows_here * wide
    blocks = length // BLOCK
    heads_here = HEADS // wide
    shard = query_weight.shape[0]

    def reorder(values):
        return values.reshape(-1, wide, narrow, shard).swapaxes(1, 2).reshape(-1, width)

    def restore(values):
        return values.reshape(-1, narrow, wide, shard).swapaxes(1, 2).reshape(-1, width)

    def columns(weight):
        part = lax.all_to_all(weight, "wide", split_axis=1, concat_axis=0, tiled=True)
        return lax.all_gather(part, "narrow", axis=0, tiled=True)

    def gather_rows(values):
        return lax.all_gather(values, "wide", axis=0, tiled=True)

    def scatter_rows(values):
        return lax.psum_scatter(
            values.astype(BF), "wide", scatter_dimension=0, tiled=True
        ).astype(F32)

    def to_tokens(values):
        return lax.all_to_all(values, "wide", split_axis=0, concat_axis=1, tiled=True)

    def to_heads(values):
        return lax.all_to_all(values, "wide", split_axis=1, concat_axis=0, tiled=True)

    def column_sums(grad):
        part = lax.psum_scatter(grad.astype(BF), "narrow", scatter_dimension=0, tiled=True)
        return lax.all_to_all(part, "wide", split_axis=0, concat_axis=1, tiled=True).astype(F32)

    w_query, w_key, w_value, w_gate = map(
        columns, (query_weight, key_weight, value_weight, gate_weight)
    )
    w_out = lax.all_gather(out_weight, BOTH, axis=0, tiled=True)
    w_fval, w_fgate = map(columns, (ffn_value_weight, ffn_gate_weight))
    w_fout = lax.all_gather(ffn_out_weight, "narrow", axis=0, tiled=True)

    starts = lax.dynamic_slice_in_dim(doc_starts, lax.axis_index("narrow"), 1, 0)[0]
    positions = jnp.arange(length, dtype=jnp.int32)
    doc_ids = jnp.sum((starts[None, :] <= positions[:, None]).astype(jnp.int32), axis=1)
    doc_ids = doc_ids.reshape(blocks, BLOCK)
    firsts = jnp.arange(blocks, dtype=jnp.int32) * BLOCK - 1
    prev_ids = jnp.sum((starts[None, :] <= firsts[:, None]).astype(jnp.int32), axis=1)
    slopes = lax.dynamic_slice_in_dim(
        head_slopes(), lax.axis_index("wide") * heads_here, heads_here, 0
    )
    offsets = jnp.arange(BLOCK, dtype=F32)
    lags = offsets[:, None] - offsets[None, :]
    decays = jnp.exp(-slopes[:, None, None] * jnp.maximum(lags, 0.0)[None])
    within = (doc_ids[:, :, None] == doc_ids[:, None, :]) & (lags >= 0.0)
    block_mask = jnp.where(within[:, None], decays[None], 0.0)
    continues = (doc_ids == prev_ids[:, None]).astype(F32)
    entry_scale = continues[..., None] * jnp.exp(-slopes[None, :] * (offsets[:, None] + 1.0))
    tail_scale = (doc_ids == doc_ids[:, -1:]).astype(F32)[..., None] * jnp.exp(
        -slopes[None, :] * (BLOCK - 1.0 - offsets)[:, None]
    )
    passing = continues[:, -1:] * jnp.exp(-slopes * BLOCK)

    def split_heads(values):
        return values.reshape(blocks, BLOCK, heads_here, HEAD)

    inputs = tokens[0].astype(F32)
    normed, in_scale = normalize(inputs)
    normed_bf = gather_rows(reorder(normed.astype(BF)))
    query_pre = matmul(normed_bf, w_query)
    key_pre = matmul(normed_bf, w_key)
    queries = split_heads(jax.nn.silu(query_pre).astype(BF))
    keys = split_heads(jax.nn.silu(key_pre).astype(BF))
    values = split_heads(matmul(normed_bf, w_value).astype(BF))
    gate = matmul(normed_bf, w_gate)
    scores = ein("bihe,bjhe->bhij", queries, keys)
    probs = (scores * block_mask).astype(BF)
    inner = ein("bhij,bjhe->bihe", probs, values)
    tail_keys = (keys.astype(F32) * tail_scale[..., None]).astype(BF)
    fresh = ein("bjhe,bjhf->bhef", tail_keys, values)
    state = jnp.zeros((heads_here, HEAD, HEAD), F32)
    entering = []
    for b in range(blocks):
        entering.append(state)
        state = passing[b][:, None, None] * state + fresh[b]
    block_in = jnp.stack(entering).astype(BF)
    across = entry_scale[..., None] * ein("bihe,bhef->bihf", queries, block_in)
    attention = (inner + across).reshape(query_pre.shape)

    attn_tok = to_tokens(attention)
    gate_tok = to_tokens(gate)
    attn_n, attn_scale = normalize(attn_tok)
    mixed = (attn_n * gate_tok).astype(BF)
    middle = inputs + matmul(mixed, w_out)
    middle_n, middle_scale = normalize(middle)
    middle_bf = gather_rows(reorder(middle_n.astype(BF)))
    ffn_val = matmul(middle_bf, w_fval)
    ffn_gat = matmul(middle_bf, w_fgate)
    ffn_mix = (ffn_val * ffn_gat).astype(BF)
    result = middle + scatter_rows(matmul(ffn_mix, w_fout))

    upstream = cotangent[0]
    up_all = gather_rows(upstream)
    grad_fout = weight_grad(ffn_mix, up_all)
    d_mix = matmul_right_t(up_all, w_fout)
    d_val = (d_mix * ffn_gat).astype(BF)
    d_gat = (d_mix * ffn_val).astype(BF)
    grad_fval = weight_grad(middle_bf, d_val)
    grad_fgate = weight_grad(middle_bf, d_gat)
    d_middle_n = restore(
        scatter_rows(matmul_right_t(d_val, w_fval) + matmul_right_t(d_gat, w_fgate))
    )
    d_middle = upstream.astype(F32) + normalize_back(middle_n, middle_scale, d_middle_n)
    d_branch = d_middle.astype(BF)
    grad_out = weight_grad(mixed, d_branch)
    d_mixed = matmul_right_t(d_branch, w_out)
    d_gate = to_heads((d_mixed * attn_n).astype(BF))
    d_attn = to_heads(normalize_back(attn_n, attn_scale, d_mixed * gate_tok).astype(BF))

    d_heads = split_heads(d_attn)
    d_probs = ein("bihe,bjhe->bhij", d_heads, values)
    d_scores = (d_probs * block_mask).astype(BF)
    d_query = ein("bhij,bjhe->bihe", d_scores, keys)
    d_key = ein("bhij,bihe->bjhe", d_scores, queries)
    d_value = ein("bhij,bihe->bjhe", probs, d_heads)
    d_query = d_query + entry_scale[..., None] * ein("bihf,bhef->bihe", d_heads, block_in)
    entry_queries = (queries.astype(F32) * entry_scale[..., None]).astype(BF)
    grad_in = ein("bihe,bihf->bhef", entry_queries, d_heads)
    state = jnp.zeros((heads_here, HEAD, HEAD), F32)
    leaving = [None] * blocks
    for b in reversed(range(blocks)):
        leaving[b] = state
        state = passing[b][:, None, None] * state + grad_in[b]
    block_out = jnp.stack(leaving).astype(BF)
    d_key = d_key + tail_scale[..., None] * ein("bjhf,bhef->bjhe", values, block_out)
    d_value = d_value + ein("bjhe,bhef->bjhf", tail_keys, block_out)
    dq_pre = (d_query.reshape(query_pre.shape) * silu_slope(query_pre)).astype(BF)
    dk_pre = (d_key.reshape(key_pre.shape) * silu_slope(key_pre)).astype(BF)
    dv_pre = d_value.reshape(query_pre.shape).astype(BF)
    grad_query = weight_grad(normed_bf, dq_pre)
    grad_key = weight_grad(normed_bf, dk_pre)
    grad_value = weight_grad(normed_bf, dv_pre)
    grad_gate = weight_grad(normed_bf, d_gate)
    d_normed = restore(
        scatter_rows(
            matmul_right_t(dq_pre, w_query)
            + matmul_right_t(dk_pre, w_key)
            + matmul_right_t(dv_pre, w_value)
            + matmul_right_t(d_gate, w_gate)
        )
    )
    d_inputs = d_middle + normalize_back(normed, in_scale, d_normed)
    return (
        result.astype(BF)[None],
        d_inputs[None],
        column_sums(grad_query),
        column_sums(grad_key),
        column_sums(grad_value),
        column_sums(grad_gate),
        lax.psum_scatter(grad_out.astype(BF), BOTH, scatter_dimension=0, tiled=True).astype(F32),
        column_sums(grad_fval),
        column_sums(grad_fgate),
        lax.psum_scatter(grad_fout.astype(BF), "narrow", scatter_dimension=0, tiled=True).astype(
            F32
        ),
    )


MESH = pl.DeviceIdType.MESH
ANY = pl.BlockSpec(memory_space=pl.ANY)
VMEM = pl.BlockSpec(memory_space=pltpu.VMEM)
WIDE, NARROW = 8, 4
CHIPS = WIDE // 2


def dot(left, right):
    return jnp.dot(left, right, preferred_element_type=F32)


def dot_rt(left, right):
    return lax.dot_general(left, right, (((1,), (1,)), ((), ())), preferred_element_type=F32)


def dot_lt(left, right):
    return lax.dot_general(left, right, (((0,), (0,)), ((), ())), preferred_element_type=F32)


def at(start, size):
    return pl.ds(pl.multiple_of(start, size), size)


class Links:
    def __init__(self, send, recv, here):
        self.send, self.recv, self.here = send, recv, here
        self.count = 0
        self.sent, self.kept = [], []
        w = lax.axis_index("wide")
        n = lax.axis_index("narrow")
        self.w, self.n = w, n
        self.core = lax.rem(w, 2)
        self.chip = lax.div(w, 2)
        x, y = lax.rem(self.chip, 2), lax.div(self.chip, 2)
        self.wx = w + 2 - 4 * x
        self.wy = w + 4 - 8 * y
        self.wd = w + 6 - 4 * x - 8 * y
        self.ws = w + 1 - 2 * self.core
        self.px = self.chip + 1 - 2 * x
        self.py = self.chip + 2 - 4 * y
        self.pd = 3 - self.chip
        self.mid = lax.rem(lax.div(n + 1, 2), 2)
        self.pair = n + 1 - 2 * lax.rem(n, 2)
        self.cross = 2 - lax.div(n, 2)
        self.far = 3 - 3 * lax.div(n, 2)
        self.end_to = 3 * lax.rem(n + 1, 2)
        self.end_part = lax.rem(2 * n, 3) + 3 * lax.div(n, 3)

    def greet(self):
        barrier = pltpu.get_barrier_semaphore()
        for d in range(1, WIDE):
            pl.semaphore_signal(
                barrier, inc=1, device_id=(lax.rem(self.w + d, WIDE), self.n), device_id_type=MESH
            )
        for d in range(1, NARROW):
            pl.semaphore_signal(
                barrier, inc=1, device_id=(self.w, lax.rem(self.n + d, NARROW)), device_id_type=MESH
            )

    def met(self):
        pl.semaphore_wait(pltpu.get_barrier_semaphore(), WIDE + NARROW - 2)

    def take(self, number):
        base = self.count
        self.count += number
        return base

    def remote(self, src, dst, send, recv, wide=None, narrow=None):
        return pltpu.make_async_remote_copy(
            src_ref=src,
            dst_ref=dst,
            send_sem=self.send.at[send],
            recv_sem=self.recv.at[recv],
            device_id=(self.w if wide is None else wide, self.n if narrow is None else narrow),
            device_id_type=MESH,
        )

    def go(self, src, dst, send, recv, wide=None, narrow=None):
        copy = self.remote(src, dst, send, recv, wide, narrow)
        copy.start()
        self.sent.append(copy)

    def arrived(self, ref, recv):
        self.remote(ref, ref, recv, recv, wide=self.ws).wait_recv()

    def keep(self, src, dst):
        copy = pltpu.make_async_copy(src, dst, self.here.at[len(self.kept)])
        copy.start()
        self.kept.append(copy)
        return copy

    def drain(self):
        for copy in self.sent:
            copy.wait_send()


class Line:
    def __init__(self, links, part):
        self.links, self.part = links, part
        self.base = links.take(4)

    def start(self):
        k, b, mine = self.links, self.base, self.part(self.links.n)
        k.go(mine, mine, b, b + k.n, narrow=k.pair)
        k.go(mine, mine, b + 1, b + k.n, narrow=k.cross)
        last = self.part(k.end_part)
        self.last = k.remote(last, last, b + 2, b + k.end_part, narrow=k.end_to)

        @pl.when(k.mid == 0)
        def _():
            self.last.start()

    def wait(self, index):
        self.links.arrived(self.part(index), self.base + index)

    def forward(self):
        @pl.when(self.links.mid == 1)
        def _():
            self.wait(self.links.cross)
            self.last.start()

    def finish(self):
        k = self.links
        self.wait(k.pair)
        self.wait(k.far)

        @pl.when(k.mid == 0)
        def _():
            self.wait(k.cross)

        k.sent.append(self.last)


class Plane:
    def __init__(self, links, slot):
        self.links, self.slot = links, slot
        self.base = links.take(6)

    def start(self):
        k, b, slot = self.links, self.base, self.slot
        k.go(slot(k.w, 0), slot(k.w, 0), b, b, wide=k.wx)
        k.go(slot(k.w, 1), slot(k.w, 1), b + 3, b + 3, wide=k.wy)
        k.go(slot(k.w, 1), slot(k.w, 1), b + 1, b + 1, wide=k.wx)
        k.go(slot(k.w, 0), slot(k.w, 0), b + 2, b + 2, wide=k.wy)

    def forward(self):
        k, b, slot = self.links, self.base, self.slot
        k.arrived(slot(k.wx, 0), b)
        k.go(slot(k.wx, 0), slot(k.wx, 0), b + 4, b + 4, wide=k.wy)
        k.arrived(slot(k.wy, 1), b + 3)
        k.go(slot(k.wy, 1), slot(k.wy, 1), b + 5, b + 5, wide=k.wx)

    def finish_near(self):
        k, b, slot = self.links, self.base, self.slot
        k.arrived(slot(k.wx, 1), b + 1)
        k.arrived(slot(k.wy, 0), b + 2)

    def finish_far(self):
        k, b, slot = self.links, self.base, self.slot
        k.arrived(slot(k.wd, 0), b + 4)
        k.arrived(slot(k.wd, 1), b + 5)


class Sibling:
    def __init__(self, links, block, number):
        self.links, self.block = links, block
        self.base = links.take(number)
        self.out, self.come = 0, 0

    def send(self, w):
        b = self.block(w)
        self.links.go(b, b, self.base + self.out, self.base + self.out, wide=self.links.ws)
        self.out += 1

    def wait(self, w):
        self.links.arrived(self.block(w), self.base + self.come)
        self.come += 1


class Spread:
    def __init__(self, links, src, dst, peers=WIDE):
        self.links, self.src, self.dst = links, src, dst
        self.step = 1 if peers == WIDE else 2
        self.base = links.take(WIDE)

    def distances(self):
        return range(self.step, WIDE, self.step)

    def start(self):
        k = self.links
        for d in self.distances():
            to = lax.rem(k.w + d, WIDE)
            k.go(self.src(to), self.dst(k.w), self.base + d, self.base + d, wide=to)

    def wait(self, d):
        self.links.arrived(self.dst(lax.rem(self.links.w + WIDE - d, WIDE)), self.base + d)

    def finish(self):
        for d in self.distances():
            self.wait(d)


def row_scale(values):
    return lax.rsqrt(jnp.mean(values * values, axis=-1, keepdims=True) + EPS)


def row_chunks(rows, body, size=32):
    def step(r, carry):
        body(at(r * size, size))
        return carry

    lax.fori_loop(0, rows // size, step, 0)


def doc_mask(cols, rowdoc, decay, rows, block):
    tokens = decay.shape[-1]
    same = cols[rows, 0:1] == rowdoc[pl.ds(block, 1), :]
    i = lax.broadcasted_iota(jnp.int32, (tokens, tokens), 0)
    j = lax.broadcasted_iota(jnp.int32, (tokens, tokens), 1)
    return same & (i >= j)


def forward_kernel(
    x_ref, wq, wk, wv, wg, wo, fv, fg, dy, cols, rowdoc, passing, decay,
    xn_o, wqk_o, wvg_o, wo_o, fv_o, fg_o, dy_o, pre_o, qkv_o, sin_o, attn_o, gate_o, mixed_o,
    x1_o, x1n_o,
    xn, wqk, wvg, wout, pre, qkv, gates, sin, state, attn_s, attn, gate, mixed, x1, x1n,
    send, recv, here,
):
    k = Links(send, recv, here)
    w, n, core, chip = k.w, k.n, k.core, k.chip
    head_cols = 2 * HEAD
    tok = x_ref.shape[0]
    ff = fv_o.shape[-1]

    def wide_cols(index):
        return at(index * head_cols, head_cols)

    def chip_cols(index):
        return pl.ds(pl.multiple_of(index * ff, 128), ff)

    k.greet()
    own = [k.keep(wo, wout.at[w, n])]
    for m, (weight, to) in enumerate(((wq, wqk), (wk, wqk), (wv, wvg), (wg, wvg))):
        own.append(
            k.keep(weight.at[:, wide_cols(w)], to.at[w, n, :, pl.ds((m % 2) * head_cols, head_cols)])
        )
    own_ff = [
        k.keep(fv.at[:, chip_cols(chip)], fv_o.at[chip, core, n]),
        k.keep(fg.at[:, chip_cols(chip)], fg_o.at[chip, core, n]),
        k.keep(dy, dy_o.at[chip]),
    ]

    def norm_in(rows):
        v = x_ref[rows, :].astype(F32)
        xn[w, rows, :] = (v * row_scale(v)).astype(BF)

    row_chunks(tok, norm_in)
    k.met()

    line_out = Line(k, lambda i: wout.at[w, i])
    line_qk = Line(k, lambda i: wqk.at[:, i])
    line_vg = Line(k, lambda i: wvg.at[:, i])
    line_fv = Line(k, lambda i: fv_o.at[:, core, i])
    line_fg = Line(k, lambda i: fg_o.at[:, core, i])
    spreads = []
    for m, (weight, to) in enumerate(((wq, wqk), (wk, wqk), (wv, wvg), (wg, wvg))):
        lanes = pl.ds((m % 2) * head_cols, head_cols)
        spreads.append(
            Spread(
                k,
                lambda t, weight=weight: weight.at[:, wide_cols(t)],
                lambda s, to=to, lanes=lanes: to.at[s, n, :, lanes],
            )
        )
    spread_ff = [
        Spread(
            k,
            lambda t, weight=weight: weight.at[:, chip_cols(lax.div(t, 2))],
            lambda s, to=to: to.at[lax.div(s, 2), core, n],
            peers=CHIPS,
        )
        for weight, to in ((fv, fv_o), (fg, fg_o))
    ]
    half = tok // 2
    plane_xn = Plane(k, lambda s, h: xn.at[s, pl.ds(h * half, half)])
    plane_out = Plane(k, lambda s, h: wout.at[s, pl.ds(h * 2, 2)])
    plane_dy = Plane(k, lambda s, h: dy_o.at[lax.div(s, 2), pl.ds(h * half, half)])
    plane_x1n = Plane(k, lambda s, h: x1n_o.at[lax.div(s, 2), pl.ds(h * half, half)])
    twin_xn = Sibling(k, lambda s: xn.at[s], 4)
    twin_out = Sibling(k, lambda s: wout.at[s], 4)
    twin_fv = Sibling(k, lambda s: fv_o.at[:, s], 1)
    twin_fg = Sibling(k, lambda s: fg_o.at[:, s], 1)
    other = 1 - core

    for copy in own:
        copy.wait()
    line_out.start()
    spreads[0].start()
    spreads[1].start()
    plane_xn.start()
    spreads[2].start()
    spreads[3].start()
    twin_xn.send(w)
    spreads[0].finish()
    spreads[1].finish()
    line_qk.start()
    spreads[2].finish()
    spreads[3].finish()
    line_vg.start()
    for copy in own_ff:
        copy.wait()
    spread_ff[0].start()
    spread_ff[1].start()
    plane_xn.forward()
    plane_xn.finish_near()
    twin_xn.send(k.wx)
    twin_xn.send(k.wy)
    line_out.forward()
    line_out.finish()
    plane_out.start()
    twin_out.send(w)
    line_qk.forward()
    plane_xn.finish_far()
    twin_xn.send(k.wd)
    line_vg.forward()
    plane_out.forward()
    plane_out.finish_near()
    twin_out.send(k.wx)
    twin_out.send(k.wy)
    plane_out.finish_far()
    twin_out.send(k.wd)
    plane_dy.start()
    spread_ff[0].finish()
    spread_ff[1].finish()
    for s in (k.ws, k.wx + 1 - 2 * core, k.wy + 1 - 2 * core, k.wd + 1 - 2 * core):
        twin_xn.wait(s)
    keep_xn = k.keep(xn, xn_o)

    line_qk.finish()
    line_fv.start()

    def project_qk(t, carry):
        v = dot(xn[t], wqk[...].reshape(-1, 2 * head_cols))
        rows = at(t * tok, tok)
        pre[rows, :] = v
        qkv[rows, 0 : 2 * head_cols] = (v * jax.nn.sigmoid(v)).astype(BF)
        return carry

    lax.fori_loop(0, WIDE, project_qk, 0)
    keep_pre = k.keep(pre, pre_o)
    keep_wqk = k.keep(wqk, wqk_o)
    line_vg.finish()
    line_fg.start()

    def project_vg(t, carry):
        v = dot(xn[t], wvg[...].reshape(-1, 2 * head_cols)).astype(BF)
        qkv[at(t * tok, tok), 2 * head_cols : 3 * head_cols] = v[:, 0:head_cols]
        gates[t] = v[:, head_cols:]
        return carry

    lax.fori_loop(0, WIDE, project_vg, 0)
    keep_wvg = k.keep(wvg, wvg_o)
    keep_qkv = k.keep(qkv, qkv_o)
    spread_gate = Spread(k, lambda t: gates.at[t], lambda s: gate.at[:, wide_cols(s)])
    spread_gate.start()
    gate[:, wide_cols(w)] = gates[w]

    plane_dy.forward()
    state[...] = jnp.zeros_like(state)
    spread_attn = Spread(k, lambda t: attn_s.at[t], lambda s: attn.at[:, wide_cols(s)])

    def attend(b, carry):
        rows = at(b * BLOCK, BLOCK)
        mask = doc_mask(cols, rowdoc, decay, rows, b)
        for h in range(2):
            lanes = slice(h * HEAD, (h + 1) * HEAD)
            q = qkv[rows, h * HEAD : (h + 1) * HEAD]
            key = qkv[rows, head_cols + h * HEAD : head_cols + (h + 1) * HEAD]
            v = qkv[rows, 2 * head_cols + h * HEAD : 2 * head_cols + (h + 1) * HEAD]
            probs = jnp.where(mask, dot_rt(q, key) * decay[h], 0.0).astype(BF)
            before = state[h]
            before_bf = before.astype(BF)
            sin[b, h] = before_bf
            entry = cols[rows, 1 + h : 2 + h]
            tail = cols[rows, 3 + h : 4 + h]
            out = dot(probs, v) + entry * dot(q, before_bf)
            attn_s[b, :, lanes] = out.astype(BF)
            tailed = (key.astype(F32) * tail).astype(BF)
            state[h] = passing[pl.ds(2 * b + h, 1), :] * before + dot_lt(tailed, v)

        @pl.when(b != w)
        def _():
            d = lax.rem(b - w + WIDE, WIDE)
            base = spread_attn.base
            k.remote(attn_s.at[b], attn.at[:, wide_cols(w)], base + d, base + d, wide=b).start()

        @pl.when(b == w)
        def _():
            attn[:, wide_cols(w)] = attn_s[b]

        return carry

    lax.fori_loop(0, WIDE, attend, 0)
    for d in spread_attn.distances():
        to = lax.rem(w + d, WIDE)
        k.sent.append(
            k.remote(
                attn_s.at[to], attn.at[:, wide_cols(w)], spread_attn.base + d, spread_attn.base + d,
                wide=to,
            )
        )
    keep_sin = k.keep(sin, sin_o)
    for s in (k.ws, k.wx + 1 - 2 * core, k.wy + 1 - 2 * core, k.wd + 1 - 2 * core):
        twin_out.wait(s)
    keep_wo = k.keep(wout, wo_o)
    spread_gate.finish()
    spread_attn.finish()
    keep_attn = k.keep(attn, attn_o)
    keep_gate = k.keep(gate, gate_o)

    def mix(rows):
        a = attn[rows, :].astype(F32)
        mixed[rows, :] = (a * row_scale(a) * gate[rows, :].astype(F32)).astype(BF)

    row_chunks(tok, mix)
    keep_mixed = k.keep(mixed, mixed_o)

    def project_out(j, carry):
        lanes = at(j * 512, 512)
        part = dot(mixed[...], wout[:, :, :, lanes].reshape(-1, 512))
        x1[:, lanes] = x_ref[:, lanes].astype(F32) + part
        return carry

    lax.fori_loop(0, x1.shape[1] // 512, project_out, 0)
    keep_x1 = k.keep(x1, x1_o)

    def norm_mid(rows):
        v = x1[rows, :]
        x1n[rows, :] = (v * row_scale(v)).astype(BF)

    row_chunks(tok, norm_mid)
    k.keep(x1n, x1n_o.at[chip]).wait()
    plane_x1n.start()
    line_fv.forward()
    line_fg.forward()
    plane_x1n.forward()
    plane_dy.finish_near()
    plane_dy.finish_far()
    line_fv.finish()
    twin_fv.send(core)
    line_fg.finish()
    twin_fg.send(core)
    plane_x1n.finish_near()
    plane_x1n.finish_far()
    twin_fv.wait(other)
    twin_fg.wait(other)
    for copy in (
        keep_xn, keep_pre, keep_wqk, keep_wvg, keep_qkv, keep_sin, keep_wo, keep_attn, keep_gate,
        keep_mixed, keep_x1,
    ):
        copy.wait()
    k.drain()


def forward(tokens, weights, dy, cols, rowdoc, passing, decay):
    tok, width = tokens.shape
    shard = weights[0].shape[0]
    full = WIDE * tok
    ff = weights[5].shape[1] // CHIPS
    two = 2 * HEAD

    def hbm(shape, dtype=BF):
        return jax.ShapeDtypeStruct(shape, dtype)

    out_shape = (
        hbm((WIDE, tok, width)),
        hbm((WIDE, NARROW, shard, 2 * two)),
        hbm((WIDE, NARROW, shard, 2 * two)),
        hbm((WIDE, NARROW, shard, width)),
        hbm((CHIPS, 2, NARROW, shard, ff)),
        hbm((CHIPS, 2, NARROW, shard, ff)),
        hbm((CHIPS, tok, width)),
        hbm((full, 2 * two), F32),
        hbm((full, 3 * two)),
        hbm((WIDE, 2, HEAD, HEAD)),
        hbm((tok, width)),
        hbm((tok, width)),
        hbm((tok, width)),
        hbm((tok, width), F32),
        hbm((CHIPS, tok, width)),
    )
    scratch = [
        pltpu.VMEM((WIDE, tok, width), BF),
        pltpu.VMEM((WIDE, NARROW, shard, 2 * two), BF),
        pltpu.VMEM((WIDE, NARROW, shard, 2 * two), BF),
        pltpu.VMEM((WIDE, NARROW, shard, width), BF),
        pltpu.VMEM((full, 2 * two), F32),
        pltpu.VMEM((full, 3 * two), BF),
        pltpu.VMEM((WIDE, tok, two), BF),
        pltpu.VMEM((WIDE, 2, HEAD, HEAD), BF),
        pltpu.VMEM((2, HEAD, HEAD), F32),
        pltpu.VMEM((WIDE, tok, two), BF),
        pltpu.VMEM((tok, width), BF),
        pltpu.VMEM((tok, width), BF),
        pltpu.VMEM((tok, width), BF),
        pltpu.VMEM((tok, width), F32),
        pltpu.VMEM((tok, width), BF),
        pltpu.SemaphoreType.DMA((136,)),
        pltpu.SemaphoreType.DMA((136,)),
        pltpu.SemaphoreType.DMA((24,)),
    ]
    return pl.pallas_call(
        forward_kernel,
        out_shape=out_shape,
        in_specs=[VMEM] + [ANY] * 8 + [VMEM] * 4,
        out_specs=(ANY,) * len(out_shape),
        scratch_shapes=scratch,
        compiler_params=pltpu.CompilerParams(
            collective_id=0, has_side_effects=True, vmem_limit_bytes=60 * 2**20
        ),
        cost_estimate=pl.CostEstimate(flops=2 * 10**10, bytes_accessed=10**8, transcendentals=0),
    )(tokens, *weights, dy, cols, rowdoc, passing, decay)


def prepare(doc_starts, length):
    starts = lax.dynamic_slice_in_dim(doc_starts, lax.axis_index("narrow"), 1, 0)[0]
    blocks = length // BLOCK
    positions = jnp.arange(length, dtype=jnp.int32)
    doc_ids = jnp.sum((starts[None, :] <= positions[:, None]).astype(jnp.int32), axis=1)
    doc_ids = doc_ids.reshape(blocks, BLOCK).astype(F32)
    firsts = jnp.arange(blocks, dtype=jnp.int32) * BLOCK - 1
    prev_ids = jnp.sum((starts[None, :] <= firsts[:, None]).astype(jnp.int32), axis=1).astype(F32)
    slopes = lax.dynamic_slice_in_dim(head_slopes(), lax.axis_index("wide") * 2, 2, 0)
    offsets = jnp.arange(BLOCK, dtype=F32)
    lags = offsets[:, None] - offsets[None, :]
    decay = jnp.exp(-slopes[:, None, None] * jnp.maximum(lags, 0.0)[None])
    continues = (doc_ids == prev_ids[:, None]).astype(F32)
    entry = continues[..., None] * jnp.exp(-slopes[None, :] * (offsets[:, None] + 1.0))
    tail = (doc_ids == doc_ids[:, -1:]).astype(F32)[..., None] * jnp.exp(
        -slopes[None, :] * (BLOCK - 1.0 - offsets)[:, None]
    )
    passing = continues[:, -1:] * jnp.exp(-slopes * BLOCK)
    cols = jnp.concatenate([doc_ids[..., None], entry, tail], axis=-1).reshape(length, 5)
    cols = jnp.pad(cols, ((0, 0), (0, HEAD - 5)))
    passing = jnp.broadcast_to(passing.reshape(-1, 1), (2 * blocks, HEAD))
    return cols, doc_ids, passing, decay


TWINS = [[2 * i, 2 * i + 1] for i in range(CHIPS)]
SAME = [[2 * i + j for i in range(CHIPS)] for j in range(2)]


def local_box(
    tokens, doc_starts, wq, wk, wv, wg, wo, fv, fg, fo, cotangent,
):
    length = WIDE * tokens.shape[1]
    cols, rowdoc, passing, decay = prepare(doc_starts, length)
    (xn, wqk, wvg, w_out, fvw, fgw, dy, pre, qkv, sin, attn, gate, mixed, middle, x1n) = forward(
        tokens[0], (wq, wk, wv, wg, wo, fv, fg), cotangent[0], cols, rowdoc, passing, decay
    )
    two = 2 * HEAD
    blocks = WIDE

    def split_heads(values):
        return values.reshape(blocks, BLOCK, 2, HEAD)

    def to_heads(values):
        return lax.all_to_all(values, "wide", split_axis=1, concat_axis=0, tiled=True)

    normed_bf = xn.reshape(length, -1)
    wqk, wvg, w_out = (a.reshape(normed_bf.shape[1], -1) for a in (wqk, wvg, w_out))
    fvw, fgw = (a.reshape(normed_bf.shape[1], -1) for a in (fvw, fgw))
    inputs = tokens[0].astype(F32)
    normed, in_scale = normalize(inputs)
    middle_n, middle_scale = normalize(middle)
    attn_n, attn_scale = normalize(attn.astype(F32))
    upstream = cotangent[0]

    fow = lax.all_gather(fo, "narrow", axis=0, tiled=True)
    fow = lax.all_gather(fow, "wide", axis=0, tiled=True, axis_index_groups=TWINS)
    x4 = x1n.reshape(-1, normed_bf.shape[1])
    dy4 = dy.reshape(x4.shape)
    ffn_val, ffn_gat = matmul(x4, fvw), matmul(x4, fgw)
    ffn_mix = (ffn_val * ffn_gat).astype(BF)

    def scatter4(v):
        return lax.psum_scatter(
            v.astype(BF), "wide", scatter_dimension=0, tiled=True, axis_index_groups=SAME
        ).astype(F32)

    result = middle + scatter4(matmul(ffn_mix, fow))
    grad_fout = weight_grad(ffn_mix, dy4).astype(BF)
    d_mix = matmul_right_t(dy4, fow)
    d_val = (d_mix * ffn_gat).astype(BF)
    d_gat = (d_mix * ffn_val).astype(BF)
    d_middle_n = scatter4(matmul_right_t(d_val, fvw) + matmul_right_t(d_gat, fgw))
    d_middle = upstream.astype(F32) + normalize_back(middle_n, middle_scale, d_middle_n)
    d_branch = d_middle.astype(BF)
    grad_out = weight_grad(mixed, d_branch)
    d_mixed = matmul_right_t(d_branch, w_out)
    d_gate = to_heads((d_mixed * attn_n).astype(BF))
    d_attn = to_heads(
        normalize_back(attn_n, attn_scale, d_mixed * gate.astype(F32)).astype(BF)
    )

    doc_ids = rowdoc
    offsets = jnp.arange(BLOCK)
    within = (doc_ids[:, :, None] == doc_ids[:, None, :]) & (offsets[:, None] >= offsets[None, :])
    block_mask = jnp.where(within[:, None], decay[None], 0.0)
    entry_scale = cols[:, 1:3].reshape(blocks, BLOCK, 2)
    tail_scale = cols[:, 3:5].reshape(blocks, BLOCK, 2)
    passing = passing[:, 0].reshape(blocks, 2)
    queries, keys, values = (split_heads(qkv[:, i * two : (i + 1) * two]) for i in range(3))
    query_pre, key_pre = pre[:, :two], pre[:, two:]
    d_heads = split_heads(d_attn)
    probs = (ein("bihe,bjhe->bhij", queries, keys) * block_mask).astype(BF)
    tail_keys = (keys.astype(F32) * tail_scale[..., None]).astype(BF)
    d_probs = ein("bihe,bjhe->bhij", d_heads, values)
    d_scores = (d_probs * block_mask).astype(BF)
    d_query = ein("bhij,bjhe->bihe", d_scores, keys)
    d_key = ein("bhij,bihe->bjhe", d_scores, queries)
    d_value = ein("bhij,bihe->bjhe", probs, d_heads)
    d_query = d_query + entry_scale[..., None] * ein("bihf,bhef->bihe", d_heads, sin)
    entry_queries = (queries.astype(F32) * entry_scale[..., None]).astype(BF)
    grad_in = ein("bihe,bihf->bhef", entry_queries, d_heads)
    state = jnp.zeros((2, HEAD, HEAD), F32)
    leaving = [None] * blocks
    for b in reversed(range(blocks)):
        leaving[b] = state
        state = passing[b][:, None, None] * state + grad_in[b]
    block_out = jnp.stack(leaving).astype(BF)
    d_key = d_key + tail_scale[..., None] * ein("bjhf,bhef->bjhe", values, block_out)
    d_value = d_value + ein("bjhe,bhef->bjhf", tail_keys, block_out)
    dq_pre = (d_query.reshape(query_pre.shape) * silu_slope(query_pre)).astype(BF)
    dk_pre = (d_key.reshape(key_pre.shape) * silu_slope(key_pre)).astype(BF)
    dv_pre = d_value.reshape(query_pre.shape).astype(BF)
    d_qk = jnp.concatenate([dq_pre, dk_pre], axis=1)
    d_vg = jnp.concatenate([dv_pre, d_gate], axis=1)
    d_normed = lax.psum_scatter(
        (matmul_right_t(d_qk, wqk) + matmul_right_t(d_vg, wvg)).astype(BF),
        "wide", scatter_dimension=0, tiled=True,
    ).astype(F32)
    d_inputs = d_middle + normalize_back(normed, in_scale, d_normed)

    def narrow_sum(v):
        return lax.psum_scatter(v, "narrow", scatter_dimension=0, tiled=True)

    def head_grads(left, right):
        g = weight_grad(left, right).astype(BF).reshape(WIDE, NARROW, -1, right.shape[1])
        g = narrow_sum(g.swapaxes(0, 1).reshape(-1, right.shape[1]))
        g = lax.all_to_all(
            g.reshape(WIDE, -1, 2, two), "wide", split_axis=0, concat_axis=0, tiled=True
        ).reshape(WIDE, -1, 2, two)
        g = g.transpose(2, 1, 0, 3).astype(F32)
        return g[0].reshape(g.shape[1], -1), g[1].reshape(g.shape[1], -1)

    def ff_grads(left, right):
        g = weight_grad(left, right).astype(BF).reshape(CHIPS, 2, NARROW, -1, right.shape[1])
        g = g.transpose(1, 2, 0, 3, 4).reshape(-1, right.shape[1])
        g = lax.psum_scatter(g, "wide", scatter_dimension=0, tiled=True, axis_index_groups=TWINS)
        g = narrow_sum(g)
        return lax.all_to_all(
            g, "wide", split_axis=0, concat_axis=1, tiled=True, axis_index_groups=SAME
        ).astype(F32)

    g_query, g_key = head_grads(normed_bf, d_qk)
    g_value, g_gate = head_grads(normed_bf, d_vg)
    return (
        result.astype(BF)[None],
        d_inputs[None],
        g_query,
        g_key,
        g_value,
        g_gate,
        lax.psum_scatter(grad_out.astype(BF), BOTH, scatter_dimension=0, tiled=True).astype(F32),
        ff_grads(x4, d_val),
        ff_grads(x4, d_gat),
        narrow_sum(
            lax.psum_scatter(
                grad_fout, "wide", scatter_dimension=0, tiled=True, axis_index_groups=TWINS
            )
        ).astype(F32),
    )


def solution(mesh):
    box = (mesh.shape["wide"], mesh.shape["narrow"]) == (WIDE, NARROW)
    tok = P("narrow", "wide", None)
    row = P(BOTH, None)
    return jax.shard_map(
        local_box if box else local,
        mesh=mesh,
        in_specs=(tok, P()) + (row,) * 8 + (tok,),
        out_specs=(tok, tok) + (row,) * 8,
        check_vma=False,
    )
```

```python
import jax
import jax.numpy as jnp
from jax import lax
from jax.experimental import pallas as pl
from jax.experimental.pallas import tpu as pltpu
from jax.sharding import PartitionSpec as P

HEADS = 16
HEAD = 128
BLOCK = 256
LAYERS = 16
LAYER = 12

EPS = 1e-06
BOTH = ("wide", "narrow")
BF = jnp.bfloat16
F32 = jnp.float32


def normalize(values):
    scale = lax.rsqrt(jnp.mean(values * values, axis=-1, keepdims=True) + EPS)
    return (values * scale, scale)


def normalize_back(normed, scale, grad):
    return scale * (grad - normed * jnp.mean(grad * normed, axis=-1, keepdims=True))


def silu_slope(values):
    sigma = jax.nn.sigmoid(values)
    return sigma * (1.0 + values * (1.0 - sigma))


def matmul(left, right):
    return jnp.dot(left, right, preferred_element_type=F32)


def matmul_right_t(left, right):
    return lax.dot_general(left, right, (((1,), (1,)), ((), ())), preferred_element_type=F32)


def weight_grad(left, right):
    return lax.dot_general(left, right, (((0,), (0,)), ((), ())), preferred_element_type=F32)


def ein(spec, left, right):
    return jnp.einsum(spec, left, right, preferred_element_type=F32)


def head_slopes():
    order = jnp.arange(HEADS, dtype=F32)
    return jnp.exp2(-8.0 * (order + 1.0) / HEADS) * (1.0 - LAYER / (LAYERS - 1) + 1e-05)


def local(
    tokens,
    doc_starts,
    query_weight,
    key_weight,
    value_weight,
    gate_weight,
    out_weight,
    ffn_value_weight,
    ffn_gate_weight,
    ffn_out_weight,
    cotangent,
):
    wide, narrow = lax.axis_size("wide"), lax.axis_size("narrow")
    rows_here, width = tokens.shape[1:]
    length = rows_here * wide
    blocks = length // BLOCK
    heads_here = HEADS // wide
    shard = query_weight.shape[0]

    def reorder(values):
        return values.reshape(-1, wide, narrow, shard).swapaxes(1, 2).reshape(-1, width)

    def restore(values):
        return values.reshape(-1, narrow, wide, shard).swapaxes(1, 2).reshape(-1, width)

    def columns(weight):
        part = lax.all_to_all(weight, "wide", split_axis=1, concat_axis=0, tiled=True)
        return lax.all_gather(part, "narrow", axis=0, tiled=True)

    def gather_rows(values):
        return lax.all_gather(values, "wide", axis=0, tiled=True)

    def scatter_rows(values):
        return lax.psum_scatter(
            values.astype(BF), "wide", scatter_dimension=0, tiled=True
        ).astype(F32)

    def to_tokens(values):
        return lax.all_to_all(values, "wide", split_axis=0, concat_axis=1, tiled=True)

    def to_heads(values):
        return lax.all_to_all(values, "wide", split_axis=1, concat_axis=0, tiled=True)

    def column_sums(grad):
        part = lax.psum_scatter(grad.astype(BF), "narrow", scatter_dimension=0, tiled=True)
        return lax.all_to_all(part, "wide", split_axis=0, concat_axis=1, tiled=True).astype(F32)

    w_query, w_key, w_value, w_gate = map(
        columns, (query_weight, key_weight, value_weight, gate_weight)
    )
    w_out = lax.all_gather(out_weight, BOTH, axis=0, tiled=True)
    w_fval, w_fgate = map(columns, (ffn_value_weight, ffn_gate_weight))
    w_fout = lax.all_gather(ffn_out_weight, "narrow", axis=0, tiled=True)

    starts = lax.dynamic_slice_in_dim(doc_starts, lax.axis_index("narrow"), 1, 0)[0]
    positions = jnp.arange(length, dtype=jnp.int32)
    doc_ids = jnp.sum((starts[None, :] <= positions[:, None]).astype(jnp.int32), axis=1)
    doc_ids = doc_ids.reshape(blocks, BLOCK)
    firsts = jnp.arange(blocks, dtype=jnp.int32) * BLOCK - 1
    prev_ids = jnp.sum((starts[None, :] <= firsts[:, None]).astype(jnp.int32), axis=1)
    slopes = lax.dynamic_slice_in_dim(
        head_slopes(), lax.axis_index("wide") * heads_here, heads_here, 0
    )
    offsets = jnp.arange(BLOCK, dtype=F32)
    lags = offsets[:, None] - offsets[None, :]
    decays = jnp.exp(-slopes[:, None, None] * jnp.maximum(lags, 0.0)[None])
    within = (doc_ids[:, :, None] == doc_ids[:, None, :]) & (lags >= 0.0)
    block_mask = jnp.where(within[:, None], decays[None], 0.0)
    continues = (doc_ids == prev_ids[:, None]).astype(F32)
    entry_scale = continues[..., None] * jnp.exp(-slopes[None, :] * (offsets[:, None] + 1.0))
    tail_scale = (doc_ids == doc_ids[:, -1:]).astype(F32)[..., None] * jnp.exp(
        -slopes[None, :] * (BLOCK - 1.0 - offsets)[:, None]
    )
    passing = continues[:, -1:] * jnp.exp(-slopes * BLOCK)

    def split_heads(values):
        return values.reshape(blocks, BLOCK, heads_here, HEAD)

    inputs = tokens[0].astype(F32)
    normed, in_scale = normalize(inputs)
    normed_bf = gather_rows(reorder(normed.astype(BF)))
    query_pre = matmul(normed_bf, w_query)
    key_pre = matmul(normed_bf, w_key)
    queries = split_heads(jax.nn.silu(query_pre).astype(BF))
    keys = split_heads(jax.nn.silu(key_pre).astype(BF))
    values = split_heads(matmul(normed_bf, w_value).astype(BF))
    gate = matmul(normed_bf, w_gate)
    scores = ein("bihe,bjhe->bhij", queries, keys)
    probs = (scores * block_mask).astype(BF)
    inner = ein("bhij,bjhe->bihe", probs, values)
    tail_keys = (keys.astype(F32) * tail_scale[..., None]).astype(BF)
    fresh = ein("bjhe,bjhf->bhef", tail_keys, values)
    state = jnp.zeros((heads_here, HEAD, HEAD), F32)
    entering = []
    for b in range(blocks):
        entering.append(state)
        state = passing[b][:, None, None] * state + fresh[b]
    block_in = jnp.stack(entering).astype(BF)
    across = entry_scale[..., None] * ein("bihe,bhef->bihf", queries, block_in)
    attention = (inner + across).reshape(query_pre.shape)

    attn_tok = to_tokens(attention)
    gate_tok = to_tokens(gate)
    attn_n, attn_scale = normalize(attn_tok)
    mixed = (attn_n * gate_tok).astype(BF)
    middle = inputs + matmul(mixed, w_out)
    middle_n, middle_scale = normalize(middle)
    middle_bf = gather_rows(reorder(middle_n.astype(BF)))
    ffn_val = matmul(middle_bf, w_fval)
    ffn_gat = matmul(middle_bf, w_fgate)
    ffn_mix = (ffn_val * ffn_gat).astype(BF)
    result = middle + scatter_rows(matmul(ffn_mix, w_fout))

    upstream = cotangent[0]
    up_all = gather_rows(upstream)
    grad_fout = weight_grad(ffn_mix, up_all)
    d_mix = matmul_right_t(up_all, w_fout)
    d_val = (d_mix * ffn_gat).astype(BF)
    d_gat = (d_mix * ffn_val).astype(BF)
    grad_fval = weight_grad(middle_bf, d_val)
    grad_fgate = weight_grad(middle_bf, d_gat)
    d_middle_n = restore(
        scatter_rows(matmul_right_t(d_val, w_fval) + matmul_right_t(d_gat, w_fgate))
    )
    d_middle = upstream.astype(F32) + normalize_back(middle_n, middle_scale, d_middle_n)
    d_branch = d_middle.astype(BF)
    grad_out = weight_grad(mixed, d_branch)
    d_mixed = matmul_right_t(d_branch, w_out)
    d_gate = to_heads((d_mixed * attn_n).astype(BF))
    d_attn = to_heads(normalize_back(attn_n, attn_scale, d_mixed * gate_tok).astype(BF))

    d_heads = split_heads(d_attn)
    d_probs = ein("bihe,bjhe->bhij", d_heads, values)
    d_scores = (d_probs * block_mask).astype(BF)
    d_query = ein("bhij,bjhe->bihe", d_scores, keys)
    d_key = ein("bhij,bihe->bjhe", d_scores, queries)
    d_value = ein("bhij,bihe->bjhe", probs, d_heads)
    d_query = d_query + entry_scale[..., None] * ein("bihf,bhef->bihe", d_heads, block_in)
    entry_queries = (queries.astype(F32) * entry_scale[..., None]).astype(BF)
    grad_in = ein("bihe,bihf->bhef", entry_queries, d_heads)
    state = jnp.zeros((heads_here, HEAD, HEAD), F32)
    leaving = [None] * blocks
    for b in reversed(range(blocks)):
        leaving[b] = state
        state = passing[b][:, None, None] * state + grad_in[b]
    block_out = jnp.stack(leaving).astype(BF)
    d_key = d_key + tail_scale[..., None] * ein("bjhf,bhef->bjhe", values, block_out)
    d_value = d_value + ein("bjhe,bhef->bjhf", tail_keys, block_out)
    dq_pre = (d_query.reshape(query_pre.shape) * silu_slope(query_pre)).astype(BF)
    dk_pre = (d_key.reshape(key_pre.shape) * silu_slope(key_pre)).astype(BF)
    dv_pre = d_value.reshape(query_pre.shape).astype(BF)
    grad_query = weight_grad(normed_bf, dq_pre)
    grad_key = weight_grad(normed_bf, dk_pre)
    grad_value = weight_grad(normed_bf, dv_pre)
    grad_gate = weight_grad(normed_bf, d_gate)
    d_normed = restore(
        scatter_rows(
            matmul_right_t(dq_pre, w_query)
            + matmul_right_t(dk_pre, w_key)
            + matmul_right_t(dv_pre, w_value)
            + matmul_right_t(d_gate, w_gate)
        )
    )
    d_inputs = d_middle + normalize_back(normed, in_scale, d_normed)
    return (
        result.astype(BF)[None],
        d_inputs[None],
        column_sums(grad_query),
        column_sums(grad_key),
        column_sums(grad_value),
        column_sums(grad_gate),
        lax.psum_scatter(grad_out.astype(BF), BOTH, scatter_dimension=0, tiled=True).astype(F32),
        column_sums(grad_fval),
        column_sums(grad_fgate),
        lax.psum_scatter(grad_fout.astype(BF), "narrow", scatter_dimension=0, tiled=True).astype(
            F32
        ),
    )


MESH = pl.DeviceIdType.MESH
ANY = pl.BlockSpec(memory_space=pl.ANY)
VMEM = pl.BlockSpec(memory_space=pltpu.VMEM)
WIDE, NARROW = 8, 4
CHIPS = WIDE // 2


def dot(left, right):
    return jnp.dot(left, right, preferred_element_type=F32)


def dot_rt(left, right):
    return lax.dot_general(left, right, (((1,), (1,)), ((), ())), preferred_element_type=F32)


def dot_lt(left, right):
    return lax.dot_general(left, right, (((0,), (0,)), ((), ())), preferred_element_type=F32)


def at(start, size):
    return pl.ds(pl.multiple_of(start, size), size)


class Links:
    def __init__(self, send, recv, here):
        self.send, self.recv, self.here = send, recv, here
        self.count = 0
        self.sent, self.kept = [], []
        w = lax.axis_index("wide")
        n = lax.axis_index("narrow")
        self.w, self.n = w, n
        self.core = lax.rem(w, 2)
        self.chip = lax.div(w, 2)
        x, y = lax.rem(self.chip, 2), lax.div(self.chip, 2)
        self.wx = w + 2 - 4 * x
        self.wy = w + 4 - 8 * y
        self.wd = w + 6 - 4 * x - 8 * y
        self.ws = w + 1 - 2 * self.core
        self.px = self.chip + 1 - 2 * x
        self.py = self.chip + 2 - 4 * y
        self.pd = 3 - self.chip
        self.mid = lax.rem(lax.div(n + 1, 2), 2)
        self.pair = n + 1 - 2 * lax.rem(n, 2)
        self.cross = 2 - lax.div(n, 2)
        self.far = 3 - 3 * lax.div(n, 2)
        self.end_to = 3 * lax.rem(n + 1, 2)
        self.end_part = lax.rem(2 * n, 3) + 3 * lax.div(n, 3)

    def greet(self):
        barrier = pltpu.get_barrier_semaphore()
        for d in range(1, WIDE):
            pl.semaphore_signal(
                barrier, inc=1, device_id=(lax.rem(self.w + d, WIDE), self.n), device_id_type=MESH
            )
        for d in range(1, NARROW):
            pl.semaphore_signal(
                barrier, inc=1, device_id=(self.w, lax.rem(self.n + d, NARROW)), device_id_type=MESH
            )

    def met(self):
        pl.semaphore_wait(pltpu.get_barrier_semaphore(), WIDE + NARROW - 2)

    def take(self, number):
        base = self.count
        self.count += number
        return base

    def remote(self, src, dst, send, recv, wide=None, narrow=None):
        return pltpu.make_async_remote_copy(
            src_ref=src,
            dst_ref=dst,
            send_sem=self.send.at[send],
            recv_sem=self.recv.at[recv],
            device_id=(self.w if wide is None else wide, self.n if narrow is None else narrow),
            device_id_type=MESH,
        )

    def go(self, src, dst, send, recv, wide=None, narrow=None, record=True):
        copy = self.remote(src, dst, send, recv, wide, narrow)
        copy.start()
        if record:
            self.sent.append(copy)

    def arrived(self, ref, recv):
        self.remote(ref, ref, recv, recv, wide=self.ws).wait_recv()

    def keep(self, src, dst):
        copy = pltpu.make_async_copy(src, dst, self.here.at[len(self.kept)])
        copy.start()
        self.kept.append(copy)
        return copy

    def drain(self):
        for copy in self.sent:
            copy.wait_send()


class Line:
    def __init__(self, links, part):
        self.links, self.part = links, part
        self.base = links.take(4)

    def start(self):
        k, b, mine = self.links, self.base, self.part(self.links.n)
        k.go(mine, mine, b, b + k.n, narrow=k.pair)
        k.go(mine, mine, b + 1, b + k.n, narrow=k.cross)
        last = self.part(k.end_part)
        self.last = k.remote(last, last, b + 2, b + k.end_part, narrow=k.end_to)

        @pl.when(k.mid == 0)
        def _():
            self.last.start()

    def wait(self, index):
        self.links.arrived(self.part(index), self.base + index)

    def forward(self):
        @pl.when(self.links.mid == 1)
        def _():
            self.wait(self.links.cross)
            self.last.start()

    def finish(self):
        k = self.links
        self.wait(k.pair)
        self.wait(k.far)

        @pl.when(k.mid == 0)
        def _():
            self.wait(k.cross)

        k.sent.append(self.last)


class Plane:
    def __init__(self, links, slot):
        self.links, self.slot = links, slot
        self.base = links.take(6)

    def start(self):
        k, b, slot = self.links, self.base, self.slot
        k.go(slot(k.w, 0), slot(k.w, 0), b, b, wide=k.wx)
        k.go(slot(k.w, 1), slot(k.w, 1), b + 3, b + 3, wide=k.wy)
        k.go(slot(k.w, 1), slot(k.w, 1), b + 1, b + 1, wide=k.wx)
        k.go(slot(k.w, 0), slot(k.w, 0), b + 2, b + 2, wide=k.wy)

    def forward(self):
        k, b, slot = self.links, self.base, self.slot
        k.arrived(slot(k.wx, 0), b)
        k.go(slot(k.wx, 0), slot(k.wx, 0), b + 4, b + 4, wide=k.wy)
        k.arrived(slot(k.wy, 1), b + 3)
        k.go(slot(k.wy, 1), slot(k.wy, 1), b + 5, b + 5, wide=k.wx)

    def finish_near(self):
        k, b, slot = self.links, self.base, self.slot
        k.arrived(slot(k.wx, 1), b + 1)
        k.arrived(slot(k.wy, 0), b + 2)

    def finish_far(self):
        k, b, slot = self.links, self.base, self.slot
        k.arrived(slot(k.wd, 0), b + 4)
        k.arrived(slot(k.wd, 1), b + 5)


class Sibling:
    def __init__(self, links, block, number):
        self.links, self.block = links, block
        self.base = links.take(number)
        self.out, self.come = 0, 0

    def send(self, w):
        b = self.block(w)
        self.links.go(b, b, self.base + self.out, self.base + self.out, wide=self.links.ws)
        self.out += 1

    def wait(self, w):
        self.links.arrived(self.block(w), self.base + self.come)
        self.come += 1


class Spread:
    def __init__(self, links, src, dst, peers=WIDE, record=True):
        self.links, self.src, self.dst, self.record = links, src, dst, record
        self.step = 1 if peers == WIDE else 2
        self.base = links.take(WIDE)

    def distances(self):
        return range(self.step, WIDE, self.step)

    def start(self):
        k = self.links
        for d in self.distances():
            to = lax.rem(k.w + d, WIDE)
            k.go(self.src(to), self.dst(k.w), self.base + d, self.base + d, to, None, self.record)

    def drain(self):
        k = self.links
        for d in self.distances():
            to = lax.rem(k.w + d, WIDE)
            k.remote(self.src(to), self.dst(k.w), self.base + d, self.base + d, to).wait_send()

    def wait(self, d):
        self.links.arrived(self.dst(lax.rem(self.links.w + WIDE - d, WIDE)), self.base + d)

    def finish(self):
        for d in self.distances():
            self.wait(d)


def row_scale(values):
    return lax.rsqrt(jnp.mean(values * values, axis=-1, keepdims=True) + EPS)


def row_chunks(rows, body, size=32):
    def step(r, carry):
        body(at(r * size, size))
        return carry

    lax.fori_loop(0, rows // size, step, 0)


def doc_mask(cols, rowdoc, decay, rows, block):
    tokens = decay.shape[-1]
    same = cols[rows, 0:1] == rowdoc[pl.ds(block, 1), :]
    i = lax.broadcasted_iota(jnp.int32, (tokens, tokens), 0)
    j = lax.broadcasted_iota(jnp.int32, (tokens, tokens), 1)
    return same & (i >= j)


def forward_kernel(
    x_ref, wq, wk, wv, wg, wo, fv, fg, fo, dy, cols, rowdoc, passing, decay,
    xn_o, wqk_o, wvg_o, wo_o, fv_o, fg_o, fo_o, dy_o, slope_o, qkv_o, sin_o, attn_o, gate_o, mixed_o,
    x1_o, x1n_o,
    xn, wqk, wvg, wout, slope, qkv, gates, sin, state, attn_s, attn, gate, mixed, x1, x1n,
    send, recv, here,
):
    k = Links(send, recv, here)
    w, n, core, chip = k.w, k.n, k.core, k.chip
    head_cols = 2 * HEAD
    tok = x_ref.shape[0]
    ff = fv_o.shape[-1]

    def wide_cols(index):
        return at(index * head_cols, head_cols)

    def chip_cols(index):
        return pl.ds(pl.multiple_of(index * ff, 128), ff)

    k.greet()
    own = [k.keep(wo, wout.at[w, n])]
    for m, (weight, to) in enumerate(((wq, wqk), (wk, wqk), (wv, wvg), (wg, wvg))):
        own.append(
            k.keep(weight.at[:, wide_cols(w)], to.at[w, n, :, pl.ds((m % 2) * head_cols, head_cols)])
        )
    own_ff = [
        k.keep(fv.at[:, chip_cols(chip)], fv_o.at[chip, core, n]),
        k.keep(fg.at[:, chip_cols(chip)], fg_o.at[chip, core, n]),
        k.keep(fo, fo_o.at[core, n]),
        k.keep(dy, dy_o.at[chip]),
    ]

    def norm_in(rows):
        v = x_ref[rows, :].astype(F32)
        xn[w, rows, :] = (v * row_scale(v)).astype(BF)

    row_chunks(tok, norm_in)
    k.met()

    line_out = Line(k, lambda i: wout.at[w, i])
    line_qk = Line(k, lambda i: wqk.at[:, i])
    line_vg = Line(k, lambda i: wvg.at[:, i])
    line_fv = Line(k, lambda i: fv_o.at[:, core, i])
    line_fg = Line(k, lambda i: fg_o.at[:, core, i])
    line_fo = Line(k, lambda i: fo_o.at[core, i])
    spreads = []
    for m, (weight, to) in enumerate(((wq, wqk), (wk, wqk), (wv, wvg), (wg, wvg))):
        lanes = pl.ds((m % 2) * head_cols, head_cols)
        spreads.append(
            Spread(
                k,
                lambda t, weight=weight: weight.at[:, wide_cols(t)],
                lambda s, to=to, lanes=lanes: to.at[s, n, :, lanes],
            )
        )
    spread_ff = [
        Spread(
            k,
            lambda t, weight=weight: weight.at[:, chip_cols(lax.div(t, 2))],
            lambda s, to=to: to.at[lax.div(s, 2), core, n],
            peers=CHIPS,
        )
        for weight, to in ((fv, fv_o), (fg, fg_o))
    ]
    half = tok // 2
    plane_xn = Plane(k, lambda s, h: xn.at[s, pl.ds(h * half, half)])
    plane_out = Plane(k, lambda s, h: wout.at[s, pl.ds(h * 2, 2)])
    plane_dy = Plane(k, lambda s, h: dy_o.at[lax.div(s, 2), pl.ds(h * half, half)])
    plane_x1n = Plane(k, lambda s, h: x1n_o.at[lax.div(s, 2), pl.ds(h * half, half)])
    twin_xn = Sibling(k, lambda s: xn.at[s], 4)
    twin_out = Sibling(k, lambda s: wout.at[s], 4)
    twin_fv = Sibling(k, lambda s: fv_o.at[:, s], 1)
    twin_fg = Sibling(k, lambda s: fg_o.at[:, s], 1)
    twin_fo = Sibling(k, lambda s: fo_o.at[s], 1)
    other = 1 - core

    for copy in own:
        copy.wait()
    line_out.start()
    spreads[0].start()
    spreads[1].start()
    plane_xn.start()
    spreads[2].start()
    spreads[3].start()
    twin_xn.send(w)
    spreads[0].finish()
    spreads[1].finish()
    line_qk.start()
    spreads[2].finish()
    spreads[3].finish()
    line_vg.start()
    for copy in own_ff:
        copy.wait()
    spread_ff[0].start()
    spread_ff[1].start()
    plane_xn.forward()
    plane_xn.finish_near()
    twin_xn.send(k.wx)
    twin_xn.send(k.wy)
    line_out.forward()
    line_out.finish()
    plane_out.start()
    twin_out.send(w)
    line_qk.forward()
    plane_xn.finish_far()
    twin_xn.send(k.wd)
    line_vg.forward()
    plane_out.forward()
    plane_out.finish_near()
    twin_out.send(k.wx)
    twin_out.send(k.wy)
    plane_out.finish_far()
    twin_out.send(k.wd)
    plane_dy.start()
    spread_ff[0].finish()
    spread_ff[1].finish()
    for s in (k.ws, k.wx + 1 - 2 * core, k.wy + 1 - 2 * core, k.wd + 1 - 2 * core):
        twin_xn.wait(s)
    keep_xn = k.keep(xn, xn_o)

    line_qk.finish()
    line_fv.start()

    def project_qk(t, carry):
        v = dot(xn[t], wqk[...].reshape(-1, 2 * head_cols))
        rows = at(t * tok, tok)
        sigma = jax.nn.sigmoid(v)
        slope[rows, :] = (sigma * (1.0 + v * (1.0 - sigma))).astype(BF)
        qkv[rows, 0 : 2 * head_cols] = (v * sigma).astype(BF)
        return carry

    lax.fori_loop(0, WIDE, project_qk, 0)
    keep_slope = k.keep(slope, slope_o)
    keep_wqk = k.keep(wqk, wqk_o)
    line_vg.finish()
    line_fg.start()
    line_fo.start()

    def project_vg(t, carry):
        v = dot(xn[t], wvg[...].reshape(-1, 2 * head_cols)).astype(BF)
        qkv[at(t * tok, tok), 2 * head_cols : 3 * head_cols] = v[:, 0:head_cols]
        gates[t] = v[:, head_cols:]
        return carry

    lax.fori_loop(0, WIDE, project_vg, 0)
    keep_wvg = k.keep(wvg, wvg_o)
    keep_qkv = k.keep(qkv, qkv_o)
    spread_gate = Spread(k, lambda t: gates.at[t], lambda s: gate.at[:, wide_cols(s)])
    spread_gate.start()
    gate[:, wide_cols(w)] = gates[w]

    plane_dy.forward()
    state[...] = jnp.zeros_like(state)
    spread_attn = Spread(k, lambda t: attn_s.at[t], lambda s: attn.at[:, wide_cols(s)])

    def attend(b, carry):
        rows = at(b * BLOCK, BLOCK)
        mask = doc_mask(cols, rowdoc, decay, rows, b)
        for h in range(2):
            lanes = slice(h * HEAD, (h + 1) * HEAD)
            q = qkv[rows, h * HEAD : (h + 1) * HEAD]
            key = qkv[rows, head_cols + h * HEAD : head_cols + (h + 1) * HEAD]
            v = qkv[rows, 2 * head_cols + h * HEAD : 2 * head_cols + (h + 1) * HEAD]
            probs = jnp.where(mask, dot_rt(q, key) * decay[h], 0.0).astype(BF)
            before = state[h]
            before_bf = before.astype(BF)
            sin[b, h] = before_bf
            entry = cols[rows, 1 + h : 2 + h]
            tail = cols[rows, 3 + h : 4 + h]
            out = dot(probs, v) + entry * dot(q, before_bf)
            attn_s[b, :, lanes] = out.astype(BF)
            tailed = (key.astype(F32) * tail).astype(BF)
            state[h] = passing[pl.ds(2 * b + h, 1), :] * before + dot_lt(tailed, v)

        @pl.when(b != w)
        def _():
            d = lax.rem(b - w + WIDE, WIDE)
            base = spread_attn.base
            k.remote(attn_s.at[b], attn.at[:, wide_cols(w)], base + d, base + d, wide=b).start()

        @pl.when(b == w)
        def _():
            attn[:, wide_cols(w)] = attn_s[b]

        return carry

    lax.fori_loop(0, WIDE, attend, 0)
    for d in spread_attn.distances():
        to = lax.rem(w + d, WIDE)
        k.sent.append(
            k.remote(
                attn_s.at[to], attn.at[:, wide_cols(w)], spread_attn.base + d, spread_attn.base + d,
                wide=to,
            )
        )
    keep_sin = k.keep(sin, sin_o)
    for s in (k.ws, k.wx + 1 - 2 * core, k.wy + 1 - 2 * core, k.wd + 1 - 2 * core):
        twin_out.wait(s)
    keep_wo = k.keep(wout, wo_o)
    spread_gate.finish()
    spread_attn.finish()
    keep_attn = k.keep(attn, attn_o)
    keep_gate = k.keep(gate, gate_o)

    def mix(rows):
        a = attn[rows, :].astype(F32)
        mixed[rows, :] = (a * row_scale(a) * gate[rows, :].astype(F32)).astype(BF)

    row_chunks(tok, mix)
    keep_mixed = k.keep(mixed, mixed_o)

    def project_out(j, carry):
        lanes = at(j * 512, 512)
        part = dot(mixed[...], wout[:, :, :, lanes].reshape(-1, 512))
        x1[:, lanes] = x_ref[:, lanes].astype(F32) + part
        return carry

    lax.fori_loop(0, x1.shape[1] // 512, project_out, 0)
    keep_x1 = k.keep(x1, x1_o)

    def norm_mid(rows):
        v = x1[rows, :]
        x1n[rows, :] = (v * row_scale(v)).astype(BF)

    row_chunks(tok, norm_mid)
    k.keep(x1n, x1n_o.at[chip]).wait()
    plane_x1n.start()
    line_fv.forward()
    line_fg.forward()
    line_fo.forward()
    plane_x1n.forward()
    plane_dy.finish_near()
    plane_dy.finish_far()
    line_fv.finish()
    twin_fv.send(core)
    line_fg.finish()
    twin_fg.send(core)
    line_fo.finish()
    twin_fo.send(core)
    plane_x1n.finish_near()
    plane_x1n.finish_far()
    twin_fv.wait(other)
    twin_fg.wait(other)
    twin_fo.wait(other)
    for copy in (
        keep_xn, keep_slope, keep_wqk, keep_wvg, keep_qkv, keep_sin, keep_wo, keep_attn, keep_gate,
        keep_mixed, keep_x1,
    ):
        copy.wait()
    k.drain()


def forward(tokens, weights, dy, cols, rowdoc, passing, decay):
    tok, width = tokens.shape
    shard = weights[0].shape[0]
    full = WIDE * tok
    ff = weights[5].shape[1] // CHIPS
    fo_rows = weights[7].shape[0]
    two = 2 * HEAD

    def hbm(shape, dtype=BF):
        return jax.ShapeDtypeStruct(shape, dtype)

    out_shape = (
        hbm((WIDE, tok, width)),
        hbm((WIDE, NARROW, shard, 2 * two)),
        hbm((WIDE, NARROW, shard, 2 * two)),
        hbm((WIDE, NARROW, shard, width)),
        hbm((CHIPS, 2, NARROW, shard, ff)),
        hbm((CHIPS, 2, NARROW, shard, ff)),
        hbm((2, NARROW, fo_rows, width)),
        hbm((CHIPS, tok, width)),
        hbm((full, 2 * two)),
        hbm((full, 3 * two)),
        hbm((WIDE, 2, HEAD, HEAD)),
        hbm((tok, width)),
        hbm((tok, width)),
        hbm((tok, width)),
        hbm((tok, width), F32),
        hbm((CHIPS, tok, width)),
    )
    scratch = [
        pltpu.VMEM((WIDE, tok, width), BF),
        pltpu.VMEM((WIDE, NARROW, shard, 2 * two), BF),
        pltpu.VMEM((WIDE, NARROW, shard, 2 * two), BF),
        pltpu.VMEM((WIDE, NARROW, shard, width), BF),
        pltpu.VMEM((full, 2 * two), BF),
        pltpu.VMEM((full, 3 * two), BF),
        pltpu.VMEM((WIDE, tok, two), BF),
        pltpu.VMEM((WIDE, 2, HEAD, HEAD), BF),
        pltpu.VMEM((2, HEAD, HEAD), F32),
        pltpu.VMEM((WIDE, tok, two), BF),
        pltpu.VMEM((tok, width), BF),
        pltpu.VMEM((tok, width), BF),
        pltpu.VMEM((tok, width), BF),
        pltpu.VMEM((tok, width), F32),
        pltpu.VMEM((tok, width), BF),
        pltpu.SemaphoreType.DMA((136,)),
        pltpu.SemaphoreType.DMA((136,)),
        pltpu.SemaphoreType.DMA((24,)),
    ]
    return pl.pallas_call(
        forward_kernel,
        out_shape=out_shape,
        in_specs=[VMEM] + [ANY] * 9 + [VMEM] * 4,
        out_specs=(ANY,) * len(out_shape),
        scratch_shapes=scratch,
        compiler_params=pltpu.CompilerParams(
            collective_id=0, has_side_effects=True, vmem_limit_bytes=60 * 2**20
        ),
        cost_estimate=pl.CostEstimate(flops=2 * 10**10, bytes_accessed=10**8, transcendentals=0),
    )(tokens, *weights, dy, cols, rowdoc, passing, decay)


class LineSum:
    def __init__(self, links, part, land):
        self.links, self.part, self.land = links, part, land
        self.base = links.take(3)
        self.over = 1 + lax.rem(links.n, 2)

    def relay(self, slot):
        k, b = self.links, self.base
        return k.remote(self.part(k.cross), self.land(slot), b, b + slot, narrow=self.over)

    def near(self):
        k, b = self.links, self.base
        return k.remote(self.part(k.pair), self.land(0), b + 1, b, narrow=k.pair)

    def distant(self):
        k, b = self.links, self.base
        slot = 2 - k.mid
        return k.remote(self.part(k.far), self.land(slot), b + 2, b + slot, narrow=k.far)

    def start(self):
        @pl.when(self.links.mid == 0)
        def _():
            self.relay(1).start()

        self.distant().start()
        self.near().start()

    def forward(self, add):
        k = self.links

        @pl.when(k.mid == 1)
        def _():
            k.arrived(self.land(1), self.base + 1)
            add(self.part(k.cross), self.land(1))
            self.relay(2).start()

    def finish(self):
        k = self.links
        k.arrived(self.land(0), self.base)
        k.arrived(self.land(2), self.base + 2)

        @pl.when(k.mid == 0)
        def _():
            k.arrived(self.land(1), self.base + 1)

    def drain(self):
        self.relay(1).wait_send()
        self.distant().wait_send()
        self.near().wait_send()


class PlaneSum:
    def __init__(self, links, block, corner, near, half):
        self.links, self.block, self.corner, self.near, self.half = links, block, corner, near, half
        self.base = links.take(6)

    def rows(self, h):
        return pl.ds(h * self.half, self.half)

    def copy(self, index):
        k = self.links
        chip, h, land, to = (
            (k.pd, 0, self.corner.at[0], k.wx),
            (k.pd, 1, self.corner.at[1], k.wy),
            (k.px, 0, self.near.at[0, self.rows(0)], k.wx),
            (k.py, 1, self.near.at[1, self.rows(1)], k.wy),
            (k.px, 1, self.near.at[0, self.rows(1)], k.wx),
            (k.py, 0, self.near.at[1, self.rows(0)], k.wy),
        )[index]
        sem = self.base + index
        return k.remote(self.block(chip).at[self.rows(h)], land, sem, sem, wide=to)

    def send_far(self):
        self.copy(0).start()
        self.copy(1).start()

    def send_x(self):
        self.copy(2).start()

    def send_y(self):
        self.copy(3).start()

    def combine(self, add):
        k = self.links
        self.copy(1).wait_recv()
        add(self.block(k.px).at[self.rows(1)], self.corner.at[1])
        self.copy(4).start()
        self.copy(0).wait_recv()
        add(self.block(k.py).at[self.rows(0)], self.corner.at[0])
        self.copy(5).start()

    def finish(self):
        for index in range(2, 6):
            self.copy(index).wait_recv()

    def drain(self):
        for index in range(6):
            self.copy(index).wait_send()


def backward_kernel(
    x_in, xn_in, wqk_in, wvg_in, wo_in, fv_in, fg_in, fo_in, dy_in, slope_in, qkv_in, sin_in,
    attn_in, gate_in, mixed_in, x1_in, x1n_in, cols_in, decay_in, rowdoc, passing,
    result_o, dx_o, gq_o, gk_o, gv_o, gg_o, go_o, gfv_o, gfg_o, gfo_o,
    corner, near, twin_fo, twin_ff, twin_wo, twin_xn, land_fo, land_ff, land_wo, land_qk, turn_ff,
    turn_qk, a_land, g_land,
    g_fo, g_fv, g_fg, stage, acc, tmp, tmp_ff,
    send, recv, here,
):
    k = Links(send, recv, here)
    w, n, core, chip = k.w, k.n, k.core, k.chip
    other = 1 - core
    tok, width = acc.shape
    ff = g_fv.shape[-1]
    fo_rows = land_fo.shape[1]
    half = tok // 2
    two = 2 * HEAD
    order = (k.pd, k.px, k.py, chip)

    def nth(j):
        flip_x, flip_y = 1 - lax.div(j, 2), 1 - lax.rem(j, 2)
        return (
            chip + flip_x * (1 - 2 * lax.rem(chip, 2)) + flip_y * (2 - 4 * lax.div(chip, 2))
        )

    def fetch(src, dst):
        copy = pltpu.make_async_copy(src, dst, here.at[0])
        copy.start()
        copy.wait()

    def adder(spot):
        def add(to, land):
            fetch(land, spot)
            to[...] = (to[...].astype(F32) + spot[...].astype(F32)).astype(BF)

        return add

    add_half = adder(tmp.at[pl.ds(0, half)])
    add_fo = adder(tmp.at[pl.ds(0, fo_rows)])
    add_wo = adder(tmp.at[pl.ds(0, 64)])
    add_ff = adder(tmp_ff)
    k.kept.append(None)

    def fo_part(owner, i):
        return g_fo.at[pl.ds(pl.multiple_of((owner * NARROW + i) * fo_rows, 16), fo_rows)]

    line_fo = LineSum(k, lambda i: fo_part(core, i), lambda s: land_fo.at[s])
    line_ff = [
        LineSum(k, lambda i, g=g: g.at[:, i], lambda s, m=m: land_ff.at[m, s])
        for m, g in enumerate((g_fv, g_fg))
    ]
    planes = [
        PlaneSum(k, lambda q: stage.at[q], corner.at[m], near.at[m], half) for m in range(4)
    ]
    plane_mid, plane_res, plane_out, plane_in = planes
    twin_base = k.take(4 * 5)

    def twin(m, j, src, dst):
        sem = twin_base + 4 * m + j
        return k.remote(src, dst, sem, sem, wide=k.ws)

    k.greet()

    def ffn(x1n, dy, fvw, fgw, fow, mix, val, gat, side):
        loads = [
            k.keep(x1n_in, x1n), k.keep(fv_in, fvw), k.keep(fg_in, fgw), k.keep(dy_in, dy),
            k.keep(fo_in, fow),
        ]
        for copy in loads:
            copy.wait()
        k.met()

        def up(j, carry):
            v = dot(x1n[j], fvw[...].reshape(width, ff))
            g = dot(x1n[j], fgw[...].reshape(width, ff))
            mix[j] = (v * g).astype(BF)
            val[j] = v.astype(BF)
            gat[j] = g.astype(BF)
            return carry

        lax.fori_loop(0, CHIPS, up, 0)

        def fo_grad(rows):
            left = mix[:, :, rows].reshape(CHIPS * tok, -1)
            for h in range(2):
                lanes = slice(h * width // 2, (h + 1) * width // 2)
                right = dy[:, :, lanes].reshape(CHIPS * tok, -1)
                g_fo[rows, lanes] = dot_lt(left, right).astype(BF)

        def fo_step(j, carry):
            fo_grad(at(j * 256, 256))
            return carry

        lax.fori_loop(0, ff // 256, fo_step, 0)
        if ff % 256:
            fo_grad(pl.ds(ff - ff % 256, ff % 256))
        for i in range(NARROW):
            twin(0, i, fo_part(other, i), twin_fo.at[i]).start()
        for i in range(NARROW):
            copy = twin(0, i, fo_part(other, i), twin_fo.at[i])
            copy.wait_recv()
            add_fo(fo_part(core, i), twin_fo.at[i])
            copy.wait_send()
        line_fo.start()

        def down(j, carry):
            q = nth(j)
            d_mix = dot_rt(dy[q], fow[...].reshape(ff, width))
            d_val = (d_mix * gat[q].astype(F32)).astype(BF)
            d_gat = (d_mix * val[q].astype(F32)).astype(BF)
            val[q] = d_val
            gat[q] = d_gat

            def back(i, carry):
                lanes = at(i * 512, 512)
                d_x = dot_rt(val[q], fvw[i].reshape(512, ff)) + dot_rt(
                    gat[q], fgw[i].reshape(512, ff)
                )
                stage[q, :, lanes] = d_x.astype(BF)

                @pl.when(j == 3)
                def _():
                    acc[:, lanes] = d_x

                return carry

            lax.fori_loop(0, width // 512, back, 0)

            for step, push in enumerate((plane_mid.send_far, plane_mid.send_x, plane_mid.send_y)):
                pl.when(j == step)(push)

            return carry

        lax.fori_loop(0, CHIPS, down, 0)
        plane_mid.combine(add_half)
        line_fo.forward(add_fo)

        for m, (d_ff, g_ff) in enumerate(((val, g_fv), (gat, g_fg))):

            def ff_grad(owner):
                left = x1n[:, :, at(owner * tok, tok)].reshape(CHIPS * tok, tok)
                g = dot_lt(left, d_ff[...].reshape(CHIPS * tok, ff)).astype(BF)
                return g.reshape(NARROW, -1, ff)

            def side_step(q, carry):
                slot = lax.rem(q, 2)

                @pl.when(q >= 2)
                def _():
                    twin(1 + m, q - 2, side.at[slot], twin_ff.at[m, q]).wait_send()

                side[slot] = ff_grad(2 * q + other)
                twin(1 + m, q, side.at[slot], twin_ff.at[m, q]).start()
                return carry

            def own_step(q, carry):
                g_ff[q] = ff_grad(2 * q + core)
                return carry

            lax.fori_loop(0, CHIPS, side_step, 0)
            lax.fori_loop(0, CHIPS, own_step, 0)
            for q in range(CHIPS):
                copy = twin(1 + m, q, side.at[q % 2], twin_ff.at[m, q])
                copy.wait_recv()
                add_ff(g_ff.at[q], twin_ff.at[m, q])
                if q >= 2:
                    copy.wait_send()
            line_ff[m].start()

        plane_mid.drain()

        def out_step(j, carry):
            q = nth(j)
            stage[q] = dot(mix[q], fow[...].reshape(ff, width)).astype(BF)
            for step, push in enumerate((plane_res.send_far, plane_res.send_x, plane_res.send_y)):
                pl.when(j == step)(push)
            return carry

        lax.fori_loop(0, CHIPS, out_step, 0)
        plane_res.combine(add_half)

    pl.run_scoped(
        ffn,
        pltpu.VMEM((CHIPS, tok, width), BF),
        pltpu.VMEM((CHIPS, tok, width), BF),
        pltpu.VMEM(fv_in.shape, BF),
        pltpu.VMEM(fg_in.shape, BF),
        pltpu.VMEM(fo_in.shape, BF),
        pltpu.VMEM((CHIPS, tok, ff), BF),
        pltpu.VMEM((CHIPS, tok, ff), BF),
        pltpu.VMEM((CHIPS, tok, ff), BF),
        pltpu.VMEM((2, *g_fv.shape[1:]), BF),
    )

    def rest(d_x1, d_branch, mixed, da_src, dg_src, side, g_wo, g_qk, g_vg):
        line_wo = LineSum(k, lambda i: g_wo.at[i], lambda s: land_wo.at[s])
        line_qk = [
            LineSum(k, lambda i, g=g: g.at[:, i], lambda s, m=m: land_qk.at[m, s])
            for m, g in enumerate((g_qk, g_vg))
        ]
        spread_a = Spread(
            k, lambda t: da_src.at[:, at(t * two, two)], lambda s: a_land.at[s], record=False
        )
        spread_g = Spread(
            k, lambda t: dg_src.at[:, at(t * two, two)], lambda s: g_land.at[s], record=False
        )

        def middle(wo, x1, attn, gate, dy, d_mixed, pair):
            load_wo = k.keep(wo_in, wo)
            load_mixed = k.keep(mixed_in, mixed)
            loads = [
                k.keep(x1_in, x1), k.keep(attn_in, attn), k.keep(gate_in, gate),
                k.keep(dy_in.at[chip], dy),
            ]
            for copy in loads:
                copy.wait()
            plane_mid.finish()
            fetch(near.at[0], pair)

            def norm_back(rows):
                g = acc[rows, :] + pair[0, rows, :].astype(F32) + pair[1, rows, :].astype(F32)
                v = x1[rows, :]
                r = row_scale(v)
                u = v * r
                d = dy[rows, :].astype(F32) + r * (g - u * jnp.mean(g * u, axis=-1, keepdims=True))
                d_x1[rows, :] = d
                d_branch[rows, :] = d.astype(BF)

            row_chunks(tok, norm_back)
            load_wo.wait()

            def mixed_step(j, carry):
                d_mixed[:, at(j * 512, 512)] = dot_rt(
                    d_branch[...], wo[pl.ds(2 * j, 2)].reshape(512, width)
                )
                return carry

            lax.fori_loop(0, width // 512, mixed_step, 0)

            def attn_back(rows):
                a = attn[rows, :].astype(F32)
                s = row_scale(a)
                u = a * s
                d = d_mixed[rows, :]
                dg_src[rows, :] = (d * u).astype(BF)
                g = d * gate[rows, :].astype(F32)
                da_src[rows, :] = (
                    s * (g - u * jnp.mean(g * u, axis=-1, keepdims=True))
                ).astype(BF)

            row_chunks(tok, attn_back)
            spread_a.start()
            spread_g.start()
            own = [
                k.keep(da_src.at[:, at(w * two, two)], a_land.at[w]),
                k.keep(dg_src.at[:, at(w * two, two)], g_land.at[w]),
            ]

            plane_res.finish()
            fetch(near.at[1], pair)

            def add_up(rows):
                v = x1[rows, :] + stage[chip, rows, :].astype(F32)
                v = v + pair[0, rows, :].astype(F32) + pair[1, rows, :].astype(F32)
                dy[rows, :] = v.astype(BF)

            row_chunks(tok, add_up)
            store = k.keep(dy, result_o)
            for copy in (load_mixed, store, *own):
                copy.wait()

        pl.run_scoped(
            middle,
            pltpu.VMEM((WIDE, tok, width), BF),
            pltpu.VMEM((tok, width), F32),
            pltpu.VMEM((tok, width), BF),
            pltpu.VMEM((tok, width), BF),
            pltpu.VMEM((tok, width), BF),
            pltpu.VMEM((tok, width), F32),
            pltpu.VMEM((2, tok, width), BF),
        )
        line_ff[0].forward(add_ff)
        plane_res.drain()

        def eight_way(plane, twin_index, landing, term):
            def side_step(j, carry):
                q = nth(j)
                side[q] = term(2 * q + other).astype(BF)
                twin(twin_index, j, side.at[q], landing.at[q]).start()
                return carry

            lax.fori_loop(0, CHIPS, side_step, 0)

            def own_step(j, carry):
                q = nth(j)
                v = term(2 * q + core)
                twin(twin_index, j, side.at[q], landing.at[q]).wait_recv()
                fetch(landing.at[q], tmp)
                v = v + tmp[...].astype(F32)

                @pl.when(j < 3)
                def _():
                    stage[q] = v.astype(BF)

                for step, push in enumerate((plane.send_far, plane.send_x, plane.send_y)):
                    pl.when(j == step)(push)

                @pl.when(j == 3)
                def _():
                    acc[...] = v

                return carry

            lax.fori_loop(0, CHIPS, own_step, 0)
            plane.combine(add_half)
            for j in range(CHIPS):
                twin(twin_index, j, side.at[order[j]], landing.at[order[j]]).wait_send()

        eight_way(
            plane_out,
            3,
            twin_wo,
            lambda owner: dot_lt(mixed[:, at(owner * tok, tok)], d_branch[...]),
        )
        line_ff[1].forward(add_ff)

        def attention(xn, d_qk, d_vg, state):
            load_xn = k.keep(xn_in, xn)
            state[...] = jnp.zeros_like(state)

            def heads(slope, qkv, sin, cols, decay, d_attn, d_gate):
                loads = [
                    k.keep(qkv_in, qkv), k.keep(sin_in, sin), k.keep(slope_in, slope),
                    k.keep(cols_in, cols), k.keep(decay_in, decay),
                ]
                for copy in loads:
                    copy.wait()
                spread_a.finish()
                spread_g.finish()
                loads = [k.keep(a_land, d_attn), k.keep(g_land, d_gate)]
                for copy in loads:
                    copy.wait()

                def step(i, carry):
                    b = WIDE - 1 - i
                    rows = at(b * BLOCK, BLOCK)
                    mask = doc_mask(cols, rowdoc, decay, rows, b)
                    for h in range(2):
                        lanes = slice(h * HEAD, (h + 1) * HEAD)
                        key_lanes = slice(two + h * HEAD, two + (h + 1) * HEAD)
                        q = qkv[rows, lanes]
                        key = qkv[rows, key_lanes]
                        v = qkv[rows, 2 * two + h * HEAD : 2 * two + (h + 1) * HEAD]
                        d_o = d_attn[b, :, lanes]
                        factor = jnp.where(mask, decay[h], 0.0)
                        probs = (dot_rt(q, key) * factor).astype(BF)
                        d_probs = (dot_rt(d_o, v) * factor).astype(BF)
                        entry = cols[rows, 1 + h : 2 + h]
                        tail = cols[rows, 3 + h : 4 + h]
                        before = sin[b, h]
                        after = state[h]
                        after_bf = after.astype(BF)
                        tailed = (key.astype(F32) * tail).astype(BF)
                        entered = (q.astype(F32) * entry).astype(BF)
                        d_q = dot(d_probs, key) + entry * dot_rt(d_o, before)
                        d_k = dot_lt(d_probs, q) + tail * dot_rt(v, after_bf)
                        d_v = dot_lt(probs, d_o) + dot(tailed, after_bf)
                        d_qk[rows, lanes] = (d_q * slope[rows, lanes].astype(F32)).astype(BF)
                        d_qk[rows, key_lanes] = (d_k * slope[rows, key_lanes].astype(F32)).astype(BF)
                        d_vg[rows, lanes] = d_v.astype(BF)
                        state[h] = passing[pl.ds(2 * b + h, 1), :] * after + dot_lt(entered, d_o)
                    d_vg[rows, two:] = d_gate[b]
                    return carry

                lax.fori_loop(0, WIDE, step, 0)

            pl.run_scoped(
                heads,
                pltpu.VMEM(slope_in.shape, BF),
                pltpu.VMEM(qkv_in.shape, BF),
                pltpu.VMEM(sin_in.shape, BF),
                pltpu.VMEM(cols_in.shape, F32),
                pltpu.VMEM(decay_in.shape, F32),
                pltpu.VMEM((WIDE, tok, two), BF),
                pltpu.VMEM((WIDE, tok, two), BF),
            )

            plane_out.finish()
            for side_index in range(2):
                fetch(near.at[2, side_index], tmp)
                acc[...] = acc[...] + tmp[...].astype(F32)
            g_wo[...] = acc[...].astype(BF).reshape(g_wo.shape)
            line_wo.start()
            plane_out.drain()
            load_xn.wait()

            for m, (d_in, g_in) in enumerate(((d_qk, g_qk), (d_vg, g_vg))):

                def in_grad(s, carry):
                    left = xn[:, :, at(s * tok, tok)].reshape(WIDE * tok, tok)
                    g_in[s] = dot_lt(left, d_in[...]).astype(BF).reshape(NARROW, -1, 2 * two)
                    return carry

                lax.fori_loop(0, WIDE, in_grad, 0)
                line_qk[m].start()

            def spread_in(wqk, wvg):
                loads = [k.keep(wqk_in, wqk), k.keep(wvg_in, wvg)]
                for copy in loads:
                    copy.wait()

                def term(owner):
                    rows = at(owner * tok, tok)
                    return dot_rt(d_qk[rows, :], wqk[...].reshape(width, 2 * two)) + dot_rt(
                        d_vg[rows, :], wvg[...].reshape(width, 2 * two)
                    )

                eight_way(plane_in, 4, twin_xn, term)

            pl.run_scoped(spread_in, pltpu.VMEM(wqk_in.shape, BF), pltpu.VMEM(wvg_in.shape, BF))

        pl.run_scoped(
            attention,
            pltpu.VMEM((WIDE, tok, width), BF),
            pltpu.VMEM((WIDE * tok, 2 * two), BF),
            pltpu.VMEM((WIDE * tok, 2 * two), BF),
            pltpu.VMEM((2, HEAD, HEAD), F32),
        )

        def last(x, pair, three, three_ff, three_qk, ff_src, qk_src, ff_all, qk_all, ff_f32, w_f32, tmp_qk):
            add_qk = adder(tmp_qk)
            load_x = k.keep(x_in, x)
            line_wo.forward(add_wo)

            def total(part, lands):
                extra = jnp.where(k.mid == 0, lands[1].astype(F32), 0.0)
                return part.astype(F32) + lands[0].astype(F32) + lands[2].astype(F32) + extra

            turns = []
            for m, g_ff in enumerate((g_fv, g_fg)):
                line_ff[m].finish()
                fetch(land_ff.at[m], three_ff)
                for q in range(CHIPS):
                    ff_src[m, q] = total(g_ff[q, n], [three_ff[s, q] for s in range(3)]).astype(BF)
                turn = Spread(
                    k,
                    lambda t, m=m: ff_src.at[m, lax.div(t, 2)],
                    lambda s, m=m: turn_ff.at[m, lax.div(s, 2)],
                    peers=CHIPS,
                    record=False,
                )
                turn.start()
                turns.append(turn)
            load_x.wait()
            plane_in.finish()
            fetch(near.at[3], pair)

            def input_back(rows):
                g = acc[rows, :] + pair[0, rows, :].astype(F32) + pair[1, rows, :].astype(F32)
                v = x[rows, :].astype(F32)
                r = row_scale(v)
                u = v * r
                d_x1[rows, :] = d_x1[rows, :] + r * (
                    g - u * jnp.mean(g * u, axis=-1, keepdims=True)
                )

            row_chunks(tok, input_back)
            stores = [k.keep(d_x1, dx_o)]
            line_qk[0].forward(add_qk)
            line_fo.finish()
            fetch(land_fo, three.at[:, pl.ds(0, fo_rows)])
            for r in range(0, fo_rows, 16):
                rows = pl.ds(r, 16)
                part = g_fo[pl.ds(pl.multiple_of((core * NARROW + n) * fo_rows + r, 16), 16), :]
                acc[rows, :] = total(part, [three[s, rows, :] for s in range(3)])
            store_fo = k.keep(acc.at[pl.ds(0, fo_rows)], gfo_o)
            line_wo.finish()
            fetch(land_wo, three.at[:, pl.ds(0, 64)])
            w_f32[4] = total(g_wo[n], [three[s, 0:64, :] for s in range(3)])
            stores.append(k.keep(w_f32.at[4], go_o))
            for m, turn in enumerate(turns):
                ff_all[chip] = ff_src[m, chip]
                turn.finish()
                for d in turn.distances():
                    q = lax.rem(chip + CHIPS - d // 2, CHIPS)
                    fetch(turn_ff.at[m, q], ff_all.at[q])
                for q in range(CHIPS):
                    ff_f32[m, :, q * ff : (q + 1) * ff] = ff_all[q].astype(F32)
                stores.append(k.keep(ff_f32.at[m], (gfv_o, gfg_o)[m]))
            line_qk[1].forward(add_qk)
            ff_turns, turns = turns, []
            for m, g_in in enumerate((g_qk, g_vg)):
                line_qk[m].finish()
                fetch(land_qk.at[m], three_qk)
                for s in range(WIDE):
                    qk_src[m, s] = total(g_in[s, n], [three_qk[i, s] for i in range(3)]).astype(BF)
                turn = Spread(
                    k,
                    lambda t, m=m: qk_src.at[m, t],
                    lambda s, m=m: turn_qk.at[m, s],
                    record=False,
                )
                turn.start()
                turns.append(turn)
            for m, turn in enumerate(turns):
                qk_all[m, w] = qk_src[m, w]
                turn.finish()
                for d in turn.distances():
                    s = lax.rem(w + WIDE - d, WIDE)
                    fetch(turn_qk.at[m, s], qk_all.at[m, s])
                for s in range(WIDE):
                    lanes = slice(s * two, (s + 1) * two)
                    w_f32[2 * m, :, lanes] = qk_all[m, s, :, 0:two].astype(F32)
                    w_f32[2 * m + 1, :, lanes] = qk_all[m, s, :, two:].astype(F32)
                outs = ((gq_o, gk_o), (gv_o, gg_o))[m]
                stores.append(k.keep(w_f32.at[2 * m], outs[0]))
                stores.append(k.keep(w_f32.at[2 * m + 1], outs[1]))
            for copy in stores + [store_fo]:
                copy.wait()
            plane_in.drain()
            for sums in (line_fo, line_wo, *line_ff, *line_qk, spread_a, spread_g, *ff_turns, *turns):
                sums.drain()

        pl.run_scoped(
            last,
            pltpu.VMEM((tok, width), BF),
            pltpu.VMEM((2, tok, width), BF),
            pltpu.VMEM((3, tok, width), BF),
            pltpu.VMEM(land_ff.shape[1:], BF),
            pltpu.VMEM(land_qk.shape[1:], BF),
            pltpu.VMEM((2, CHIPS, 64, ff), BF),
            pltpu.VMEM((2, WIDE, 64, 2 * two), BF),
            pltpu.VMEM((CHIPS, 64, ff), BF),
            pltpu.VMEM((2, WIDE, 64, 2 * two), BF),
            pltpu.VMEM((2, 64, CHIPS * ff), F32),
            pltpu.VMEM((5, 64, width), F32),
            pltpu.VMEM(g_qk.shape[:1] + g_qk.shape[2:], BF),
        )

    pl.run_scoped(
        rest,
        pltpu.VMEM((tok, width), F32),
        pltpu.VMEM((tok, width), BF),
        pltpu.VMEM((tok, width), BF),
        pltpu.VMEM((tok, width), BF),
        pltpu.VMEM((tok, width), BF),
        pltpu.VMEM((CHIPS, tok, width), BF),
        pltpu.VMEM((NARROW, 64, width), BF),
        pltpu.VMEM((WIDE, NARROW, 64, 2 * two), BF),
        pltpu.VMEM((WIDE, NARROW, 64, 2 * two), BF),
    )


def backward(tokens, kept, cols, rowdoc, passing, decay):
    tok, width = tokens.shape
    fv, fo = kept[4], kept[6]
    shard, ff, fo_rows = fv.shape[3], fv.shape[4], fo.shape[2]
    two = 2 * HEAD

    def arr(*shape, dtype=BF):
        return jax.ShapeDtypeStruct(shape, dtype)

    square = [arr(shard, width, dtype=F32)] * 5
    out_shape = (
        arr(tok, width),
        arr(tok, width, dtype=F32),
        *square,
        arr(shard, CHIPS * ff, dtype=F32),
        arr(shard, CHIPS * ff, dtype=F32),
        arr(fo_rows, width, dtype=F32),
        arr(4, 2, tok // 2, width),
        arr(4, 2, tok, width),
        arr(NARROW, fo_rows, width),
        arr(2, CHIPS, NARROW, shard, ff),
        arr(CHIPS, tok, width),
        arr(CHIPS, tok, width),
        arr(3, fo_rows, width),
        arr(2, 3, CHIPS, shard, ff),
        arr(3, shard, width),
        arr(2, 3, WIDE, shard, 2 * two),
        arr(2, CHIPS, shard, ff),
        arr(2, WIDE, shard, 2 * two),
        arr(WIDE, tok, two),
        arr(WIDE, tok, two),
    )
    scratch = [
        pltpu.VMEM((CHIPS * ff // CHIPS, width), BF),
        pltpu.VMEM((CHIPS, NARROW, shard, ff), BF),
        pltpu.VMEM((CHIPS, NARROW, shard, ff), BF),
        pltpu.VMEM((CHIPS, tok, width), BF),
        pltpu.VMEM((tok, width), F32),
        pltpu.VMEM((tok, width), BF),
        pltpu.VMEM((CHIPS, shard, ff), BF),
        pltpu.SemaphoreType.DMA((112,)),
        pltpu.SemaphoreType.DMA((112,)),
        pltpu.SemaphoreType.DMA((48,)),
    ]
    outs = pl.pallas_call(
        backward_kernel,
        out_shape=out_shape,
        in_specs=[ANY] * 19 + [VMEM] * 2,
        out_specs=(ANY,) * len(out_shape),
        scratch_shapes=scratch,
        compiler_params=pltpu.CompilerParams(
            collective_id=1, has_side_effects=True, vmem_limit_bytes=63 * 2**20
        ),
        cost_estimate=pl.CostEstimate(flops=6 * 10**10, bytes_accessed=2 * 10**8, transcendentals=0),
    )(tokens, *kept, cols, decay, rowdoc, passing)
    return outs[:10]


def prepare(doc_starts, length):
    starts = lax.dynamic_slice_in_dim(doc_starts, lax.axis_index("narrow"), 1, 0)[0]
    blocks = length // BLOCK
    positions = jnp.arange(length, dtype=jnp.int32)
    doc_ids = jnp.sum((starts[None, :] <= positions[:, None]).astype(jnp.int32), axis=1)
    doc_ids = doc_ids.reshape(blocks, BLOCK).astype(F32)
    firsts = jnp.arange(blocks, dtype=jnp.int32) * BLOCK - 1
    prev_ids = jnp.sum((starts[None, :] <= firsts[:, None]).astype(jnp.int32), axis=1).astype(F32)
    slopes = lax.dynamic_slice_in_dim(head_slopes(), lax.axis_index("wide") * 2, 2, 0)
    offsets = jnp.arange(BLOCK, dtype=F32)
    lags = offsets[:, None] - offsets[None, :]
    decay = jnp.exp(-slopes[:, None, None] * jnp.maximum(lags, 0.0)[None])
    continues = (doc_ids == prev_ids[:, None]).astype(F32)
    entry = continues[..., None] * jnp.exp(-slopes[None, :] * (offsets[:, None] + 1.0))
    tail = (doc_ids == doc_ids[:, -1:]).astype(F32)[..., None] * jnp.exp(
        -slopes[None, :] * (BLOCK - 1.0 - offsets)[:, None]
    )
    passing = continues[:, -1:] * jnp.exp(-slopes * BLOCK)
    cols = jnp.concatenate([doc_ids[..., None], entry, tail], axis=-1).reshape(length, 5)
    cols = jnp.pad(cols, ((0, 0), (0, HEAD - 5)))
    passing = jnp.broadcast_to(passing.reshape(-1, 1), (2 * blocks, HEAD))
    return cols, doc_ids, passing, decay


def local_box(tokens, doc_starts, wq, wk, wv, wg, wo, fv, fg, fo, cotangent):
    tok, width = tokens.shape[1:]
    tables = prepare(doc_starts, WIDE * tok)
    kept = list(
        forward(tokens[0], (wq, wk, wv, wg, wo, fv, fg, fo), cotangent[0], *tables)
    )
    kept[3] = kept[3].reshape(WIDE, tok, width)
    outs = backward(tokens[0], kept, *tables)
    return (outs[0][None], outs[1][None]) + tuple(outs[2:])


def solution(mesh):
    box = (mesh.shape["wide"], mesh.shape["narrow"]) == (WIDE, NARROW)
    tok = P("narrow", "wide", None)
    row = P(BOTH, None)
    return jax.shard_map(
        local_box if box else local,
        mesh=mesh,
        in_specs=(tok, P()) + (row,) * 8 + (tok,),
        out_specs=(tok, tok) + (row,) * 8,
        check_vma=False,
    )
```

```python
import jax
import jax.numpy as jnp
from jax import lax
from jax.experimental import pallas as pl
from jax.experimental.pallas import tpu as pltpu
from jax.sharding import PartitionSpec as P

HEADS = 16
HEAD = 128
BLOCK = 256
LAYERS = 16
LAYER = 12

EPS = 1e-06
BOTH = ("wide", "narrow")
BF = jnp.bfloat16
F32 = jnp.float32


def normalize(values):
    scale = lax.rsqrt(jnp.mean(values * values, axis=-1, keepdims=True) + EPS)
    return (values * scale, scale)


def normalize_back(normed, scale, grad):
    return scale * (grad - normed * jnp.mean(grad * normed, axis=-1, keepdims=True))


def silu_slope(values):
    sigma = jax.nn.sigmoid(values)
    return sigma * (1.0 + values * (1.0 - sigma))


def matmul(left, right):
    return jnp.dot(left, right, preferred_element_type=F32)


def matmul_right_t(left, right):
    return lax.dot_general(left, right, (((1,), (1,)), ((), ())), preferred_element_type=F32)


def weight_grad(left, right):
    return lax.dot_general(left, right, (((0,), (0,)), ((), ())), preferred_element_type=F32)


def ein(spec, left, right):
    return jnp.einsum(spec, left, right, preferred_element_type=F32)


def head_slopes():
    order = jnp.arange(HEADS, dtype=F32)
    return jnp.exp2(-8.0 * (order + 1.0) / HEADS) * (1.0 - LAYER / (LAYERS - 1) + 1e-05)


def local(
    tokens,
    doc_starts,
    query_weight,
    key_weight,
    value_weight,
    gate_weight,
    out_weight,
    ffn_value_weight,
    ffn_gate_weight,
    ffn_out_weight,
    cotangent,
):
    wide, narrow = lax.axis_size("wide"), lax.axis_size("narrow")
    rows_here, width = tokens.shape[1:]
    length = rows_here * wide
    blocks = length // BLOCK
    heads_here = HEADS // wide
    shard = query_weight.shape[0]

    def reorder(values):
        return values.reshape(-1, wide, narrow, shard).swapaxes(1, 2).reshape(-1, width)

    def restore(values):
        return values.reshape(-1, narrow, wide, shard).swapaxes(1, 2).reshape(-1, width)

    def columns(weight):
        part = lax.all_to_all(weight, "wide", split_axis=1, concat_axis=0, tiled=True)
        return lax.all_gather(part, "narrow", axis=0, tiled=True)

    def gather_rows(values):
        return lax.all_gather(values, "wide", axis=0, tiled=True)

    def scatter_rows(values):
        return lax.psum_scatter(
            values.astype(BF), "wide", scatter_dimension=0, tiled=True
        ).astype(F32)

    def to_tokens(values):
        return lax.all_to_all(values, "wide", split_axis=0, concat_axis=1, tiled=True)

    def to_heads(values):
        return lax.all_to_all(values, "wide", split_axis=1, concat_axis=0, tiled=True)

    def column_sums(grad):
        part = lax.psum_scatter(grad.astype(BF), "narrow", scatter_dimension=0, tiled=True)
        return lax.all_to_all(part, "wide", split_axis=0, concat_axis=1, tiled=True).astype(F32)

    w_query, w_key, w_value, w_gate = map(
        columns, (query_weight, key_weight, value_weight, gate_weight)
    )
    w_out = lax.all_gather(out_weight, BOTH, axis=0, tiled=True)
    w_fval, w_fgate = map(columns, (ffn_value_weight, ffn_gate_weight))
    w_fout = lax.all_gather(ffn_out_weight, "narrow", axis=0, tiled=True)

    starts = lax.dynamic_slice_in_dim(doc_starts, lax.axis_index("narrow"), 1, 0)[0]
    positions = jnp.arange(length, dtype=jnp.int32)
    doc_ids = jnp.sum((starts[None, :] <= positions[:, None]).astype(jnp.int32), axis=1)
    doc_ids = doc_ids.reshape(blocks, BLOCK)
    firsts = jnp.arange(blocks, dtype=jnp.int32) * BLOCK - 1
    prev_ids = jnp.sum((starts[None, :] <= firsts[:, None]).astype(jnp.int32), axis=1)
    slopes = lax.dynamic_slice_in_dim(
        head_slopes(), lax.axis_index("wide") * heads_here, heads_here, 0
    )
    offsets = jnp.arange(BLOCK, dtype=F32)
    lags = offsets[:, None] - offsets[None, :]
    decays = jnp.exp(-slopes[:, None, None] * jnp.maximum(lags, 0.0)[None])
    within = (doc_ids[:, :, None] == doc_ids[:, None, :]) & (lags >= 0.0)
    block_mask = jnp.where(within[:, None], decays[None], 0.0)
    continues = (doc_ids == prev_ids[:, None]).astype(F32)
    entry_scale = continues[..., None] * jnp.exp(-slopes[None, :] * (offsets[:, None] + 1.0))
    tail_scale = (doc_ids == doc_ids[:, -1:]).astype(F32)[..., None] * jnp.exp(
        -slopes[None, :] * (BLOCK - 1.0 - offsets)[:, None]
    )
    passing = continues[:, -1:] * jnp.exp(-slopes * BLOCK)

    def split_heads(values):
        return values.reshape(blocks, BLOCK, heads_here, HEAD)

    inputs = tokens[0].astype(F32)
    normed, in_scale = normalize(inputs)
    normed_bf = gather_rows(reorder(normed.astype(BF)))
    query_pre = matmul(normed_bf, w_query)
    key_pre = matmul(normed_bf, w_key)
    queries = split_heads(jax.nn.silu(query_pre).astype(BF))
    keys = split_heads(jax.nn.silu(key_pre).astype(BF))
    values = split_heads(matmul(normed_bf, w_value).astype(BF))
    gate = matmul(normed_bf, w_gate)
    scores = ein("bihe,bjhe->bhij", queries, keys)
    probs = (scores * block_mask).astype(BF)
    inner = ein("bhij,bjhe->bihe", probs, values)
    tail_keys = (keys.astype(F32) * tail_scale[..., None]).astype(BF)
    fresh = ein("bjhe,bjhf->bhef", tail_keys, values)
    state = jnp.zeros((heads_here, HEAD, HEAD), F32)
    entering = []
    for b in range(blocks):
        entering.append(state)
        state = passing[b][:, None, None] * state + fresh[b]
    block_in = jnp.stack(entering).astype(BF)
    across = entry_scale[..., None] * ein("bihe,bhef->bihf", queries, block_in)
    attention = (inner + across).reshape(query_pre.shape)

    attn_tok = to_tokens(attention)
    gate_tok = to_tokens(gate)
    attn_n, attn_scale = normalize(attn_tok)
    mixed = (attn_n * gate_tok).astype(BF)
    middle = inputs + matmul(mixed, w_out)
    middle_n, middle_scale = normalize(middle)
    middle_bf = gather_rows(reorder(middle_n.astype(BF)))
    ffn_val = matmul(middle_bf, w_fval)
    ffn_gat = matmul(middle_bf, w_fgate)
    ffn_mix = (ffn_val * ffn_gat).astype(BF)
    result = middle + scatter_rows(matmul(ffn_mix, w_fout))

    upstream = cotangent[0]
    up_all = gather_rows(upstream)
    grad_fout = weight_grad(ffn_mix, up_all)
    d_mix = matmul_right_t(up_all, w_fout)
    d_val = (d_mix * ffn_gat).astype(BF)
    d_gat = (d_mix * ffn_val).astype(BF)
    grad_fval = weight_grad(middle_bf, d_val)
    grad_fgate = weight_grad(middle_bf, d_gat)
    d_middle_n = restore(
        scatter_rows(matmul_right_t(d_val, w_fval) + matmul_right_t(d_gat, w_fgate))
    )
    d_middle = upstream.astype(F32) + normalize_back(middle_n, middle_scale, d_middle_n)
    d_branch = d_middle.astype(BF)
    grad_out = weight_grad(mixed, d_branch)
    d_mixed = matmul_right_t(d_branch, w_out)
    d_gate = to_heads((d_mixed * attn_n).astype(BF))
    d_attn = to_heads(normalize_back(attn_n, attn_scale, d_mixed * gate_tok).astype(BF))

    d_heads = split_heads(d_attn)
    d_probs = ein("bihe,bjhe->bhij", d_heads, values)
    d_scores = (d_probs * block_mask).astype(BF)
    d_query = ein("bhij,bjhe->bihe", d_scores, keys)
    d_key = ein("bhij,bihe->bjhe", d_scores, queries)
    d_value = ein("bhij,bihe->bjhe", probs, d_heads)
    d_query = d_query + entry_scale[..., None] * ein("bihf,bhef->bihe", d_heads, block_in)
    entry_queries = (queries.astype(F32) * entry_scale[..., None]).astype(BF)
    grad_in = ein("bihe,bihf->bhef", entry_queries, d_heads)
    state = jnp.zeros((heads_here, HEAD, HEAD), F32)
    leaving = [None] * blocks
    for b in reversed(range(blocks)):
        leaving[b] = state
        state = passing[b][:, None, None] * state + grad_in[b]
    block_out = jnp.stack(leaving).astype(BF)
    d_key = d_key + tail_scale[..., None] * ein("bjhf,bhef->bjhe", values, block_out)
    d_value = d_value + ein("bjhe,bhef->bjhf", tail_keys, block_out)
    dq_pre = (d_query.reshape(query_pre.shape) * silu_slope(query_pre)).astype(BF)
    dk_pre = (d_key.reshape(key_pre.shape) * silu_slope(key_pre)).astype(BF)
    dv_pre = d_value.reshape(query_pre.shape).astype(BF)
    grad_query = weight_grad(normed_bf, dq_pre)
    grad_key = weight_grad(normed_bf, dk_pre)
    grad_value = weight_grad(normed_bf, dv_pre)
    grad_gate = weight_grad(normed_bf, d_gate)
    d_normed = restore(
        scatter_rows(
            matmul_right_t(dq_pre, w_query)
            + matmul_right_t(dk_pre, w_key)
            + matmul_right_t(dv_pre, w_value)
            + matmul_right_t(d_gate, w_gate)
        )
    )
    d_inputs = d_middle + normalize_back(normed, in_scale, d_normed)
    return (
        result.astype(BF)[None],
        d_inputs[None],
        column_sums(grad_query),
        column_sums(grad_key),
        column_sums(grad_value),
        column_sums(grad_gate),
        lax.psum_scatter(grad_out.astype(BF), BOTH, scatter_dimension=0, tiled=True).astype(F32),
        column_sums(grad_fval),
        column_sums(grad_fgate),
        lax.psum_scatter(grad_fout.astype(BF), "narrow", scatter_dimension=0, tiled=True).astype(
            F32
        ),
    )


MESH = pl.DeviceIdType.MESH
ANY = pl.BlockSpec(memory_space=pl.ANY)
VMEM = pl.BlockSpec(memory_space=pltpu.VMEM)
WIDE, NARROW = 8, 4
CHIPS = WIDE // 2


def dot(left, right):
    return jnp.dot(left, right, preferred_element_type=F32)


def dot_rt(left, right):
    return lax.dot_general(left, right, (((1,), (1,)), ((), ())), preferred_element_type=F32)


def dot_lt(left, right):
    return lax.dot_general(left, right, (((0,), (0,)), ((), ())), preferred_element_type=F32)


def at(start, size):
    return pl.ds(pl.multiple_of(start, size), size)


class Links:
    def __init__(self, send, recv, here):
        self.send, self.recv, self.here = send, recv, here
        self.count = 0
        self.sent, self.kept = [], []
        w = lax.axis_index("wide")
        n = lax.axis_index("narrow")
        self.w, self.n = w, n
        self.core = lax.rem(w, 2)
        self.chip = lax.div(w, 2)
        x, y = lax.rem(self.chip, 2), lax.div(self.chip, 2)
        self.wx = w + 2 - 4 * x
        self.wy = w + 4 - 8 * y
        self.wd = w + 6 - 4 * x - 8 * y
        self.ws = w + 1 - 2 * self.core
        self.px = self.chip + 1 - 2 * x
        self.py = self.chip + 2 - 4 * y
        self.pd = 3 - self.chip
        self.mid = lax.rem(lax.div(n + 1, 2), 2)
        self.pair = n + 1 - 2 * lax.rem(n, 2)
        self.cross = 2 - lax.div(n, 2)
        self.far = 3 - 3 * lax.div(n, 2)
        self.end_to = 3 * lax.rem(n + 1, 2)
        self.end_part = lax.rem(2 * n, 3) + 3 * lax.div(n, 3)

    def greet(self):
        barrier = pltpu.get_barrier_semaphore()
        for d in range(1, WIDE):
            pl.semaphore_signal(
                barrier, inc=1, device_id=(lax.rem(self.w + d, WIDE), self.n), device_id_type=MESH
            )
        for d in range(1, NARROW):
            pl.semaphore_signal(
                barrier, inc=1, device_id=(self.w, lax.rem(self.n + d, NARROW)), device_id_type=MESH
            )

    def met(self):
        pl.semaphore_wait(pltpu.get_barrier_semaphore(), WIDE + NARROW - 2)

    def take(self, number):
        base = self.count
        self.count += number
        return base

    def remote(self, src, dst, send, recv, wide=None, narrow=None):
        return pltpu.make_async_remote_copy(
            src_ref=src,
            dst_ref=dst,
            send_sem=self.send.at[send],
            recv_sem=self.recv.at[recv],
            device_id=(self.w if wide is None else wide, self.n if narrow is None else narrow),
            device_id_type=MESH,
        )

    def go(self, src, dst, send, recv, wide=None, narrow=None, record=True):
        copy = self.remote(src, dst, send, recv, wide, narrow)
        copy.start()
        if record:
            self.sent.append(copy)

    def arrived(self, ref, recv):
        self.remote(ref, ref, recv, recv, wide=self.ws).wait_recv()

    def keep(self, src, dst):
        copy = pltpu.make_async_copy(src, dst, self.here.at[len(self.kept)])
        copy.start()
        self.kept.append(copy)
        return copy

    def drain(self):
        for copy in self.sent:
            copy.wait_send()


class Line:
    def __init__(self, links, part):
        self.links, self.part = links, part
        self.base = links.take(4)

    def start(self):
        k, b, mine = self.links, self.base, self.part(self.links.n)
        k.go(mine, mine, b + 1, b + k.n, narrow=k.cross)
        k.go(mine, mine, b, b + k.n, narrow=k.pair)
        last = self.part(k.end_part)
        self.last = k.remote(last, last, b + 2, b + k.end_part, narrow=k.end_to)

        @pl.when(k.mid == 0)
        def _():
            self.last.start()

    def wait(self, index):
        self.links.arrived(self.part(index), self.base + index)

    def forward(self):
        @pl.when(self.links.mid == 1)
        def _():
            self.wait(self.links.cross)
            self.last.start()

    def finish(self):
        k = self.links
        self.wait(k.pair)
        self.wait(k.far)

        @pl.when(k.mid == 0)
        def _():
            self.wait(k.cross)

        k.sent.append(self.last)


class Plane:
    def __init__(self, links, slot):
        self.links, self.slot = links, slot
        self.base = links.take(6)

    def start(self):
        k, b, slot = self.links, self.base, self.slot
        k.go(slot(k.w, 0), slot(k.w, 0), b, b, wide=k.wx)
        k.go(slot(k.w, 1), slot(k.w, 1), b + 3, b + 3, wide=k.wy)
        k.go(slot(k.w, 1), slot(k.w, 1), b + 1, b + 1, wide=k.wx)
        k.go(slot(k.w, 0), slot(k.w, 0), b + 2, b + 2, wide=k.wy)

    def forward(self):
        k, b, slot = self.links, self.base, self.slot
        k.arrived(slot(k.wx, 0), b)
        k.go(slot(k.wx, 0), slot(k.wx, 0), b + 4, b + 4, wide=k.wy)
        k.arrived(slot(k.wy, 1), b + 3)
        k.go(slot(k.wy, 1), slot(k.wy, 1), b + 5, b + 5, wide=k.wx)

    def finish_near(self):
        k, b, slot = self.links, self.base, self.slot
        k.arrived(slot(k.wx, 1), b + 1)
        k.arrived(slot(k.wy, 0), b + 2)

    def finish_far(self):
        k, b, slot = self.links, self.base, self.slot
        k.arrived(slot(k.wd, 0), b + 4)
        k.arrived(slot(k.wd, 1), b + 5)


class Sibling:
    def __init__(self, links, block, number):
        self.links, self.block = links, block
        self.base = links.take(number)
        self.out, self.come = 0, 0

    def send(self, w):
        b = self.block(w)
        self.links.go(b, b, self.base + self.out, self.base + self.out, wide=self.links.ws)
        self.out += 1

    def wait(self, w):
        self.links.arrived(self.block(w), self.base + self.come)
        self.come += 1


class Spread:
    def __init__(self, links, src, dst, peers=WIDE, record=True):
        self.links, self.src, self.dst, self.record = links, src, dst, record
        self.step = 1 if peers == WIDE else 2
        self.base = links.take(WIDE)

    def distances(self):
        return range(self.step, WIDE, self.step)

    def start(self):
        k = self.links
        for d in self.distances():
            to = lax.rem(k.w + d, WIDE)
            k.go(self.src(to), self.dst(k.w), self.base + d, self.base + d, to, None, self.record)

    def drain(self):
        k = self.links
        for d in self.distances():
            to = lax.rem(k.w + d, WIDE)
            k.remote(self.src(to), self.dst(k.w), self.base + d, self.base + d, to).wait_send()

    def wait(self, d):
        self.links.arrived(self.dst(lax.rem(self.links.w + WIDE - d, WIDE)), self.base + d)

    def finish(self):
        for d in self.distances():
            self.wait(d)


def row_scale(values):
    return lax.rsqrt(jnp.mean(values * values, axis=-1, keepdims=True) + EPS)


def row_chunks(rows, body, size=32):
    def step(r, carry):
        body(at(r * size, size))
        return carry

    lax.fori_loop(0, rows // size, step, 0)


def doc_mask(cols, rowdoc, decay, rows, block):
    tokens = decay.shape[-1]
    same = cols[rows, 0:1] == rowdoc[pl.ds(block, 1), :]
    i = lax.broadcasted_iota(jnp.int32, (tokens, tokens), 0)
    j = lax.broadcasted_iota(jnp.int32, (tokens, tokens), 1)
    return same & (i >= j)


def forward_kernel(
    x_ref, wq, wk, wv, wg, wo, fv, fg, fo, dy, cols, rowdoc, passing, decay,
    xn_o, wqk_o, wvg_o, wo_o, fv_o, fg_o, fo_o, dy_o, slope_o, qkv_o, sin_o, attn_o, gate_o, mixed_o,
    x1_o, x1n_o,
    xn, wqk, wvg, wout, slope, qkv, gates, sin, state, attn_s, attn, gate, mixed, x1, x1n,
    send, recv, here,
):
    k = Links(send, recv, here)
    w, n, core, chip = k.w, k.n, k.core, k.chip
    head_cols = 2 * HEAD
    tok = x_ref.shape[0]
    ff = fv_o.shape[-1]

    def wide_cols(index):
        return at(index * head_cols, head_cols)

    def chip_cols(index):
        return pl.ds(pl.multiple_of(index * ff, 128), ff)

    k.greet()
    own = [k.keep(wo, wout.at[w, n])]
    for m, (weight, to) in enumerate(((wq, wqk), (wk, wqk), (wv, wvg), (wg, wvg))):
        own.append(
            k.keep(weight.at[:, wide_cols(w)], to.at[w, n, :, pl.ds((m % 2) * head_cols, head_cols)])
        )
    own_ff = [
        k.keep(fv.at[:, chip_cols(chip)], fv_o.at[chip, core, n]),
        k.keep(fg.at[:, chip_cols(chip)], fg_o.at[chip, core, n]),
        k.keep(fo, fo_o.at[core, n]),
        k.keep(dy, dy_o.at[chip]),
    ]

    def norm_in(rows):
        v = x_ref[rows, :].astype(F32)
        xn[w, rows, :] = (v * row_scale(v)).astype(BF)

    row_chunks(tok, norm_in)
    k.met()

    line_out = Line(k, lambda i: wout.at[w, i])
    line_qk = Line(k, lambda i: wqk.at[:, i])
    line_vg = Line(k, lambda i: wvg.at[:, i])
    line_fv = Line(k, lambda i: fv_o.at[:, core, i])
    line_fg = Line(k, lambda i: fg_o.at[:, core, i])
    line_fo = Line(k, lambda i: fo_o.at[core, i])
    spreads = []
    for m, (weight, to) in enumerate(((wq, wqk), (wk, wqk), (wv, wvg), (wg, wvg))):
        lanes = pl.ds((m % 2) * head_cols, head_cols)
        spreads.append(
            Spread(
                k,
                lambda t, weight=weight: weight.at[:, wide_cols(t)],
                lambda s, to=to, lanes=lanes: to.at[s, n, :, lanes],
            )
        )
    spread_ff = [
        Spread(
            k,
            lambda t, weight=weight: weight.at[:, chip_cols(lax.div(t, 2))],
            lambda s, to=to: to.at[lax.div(s, 2), core, n],
            peers=CHIPS,
        )
        for weight, to in ((fv, fv_o), (fg, fg_o))
    ]
    half = tok // 2
    plane_xn = Plane(k, lambda s, h: xn.at[s, pl.ds(h * half, half)])
    plane_out = Plane(k, lambda s, h: wout.at[s, pl.ds(h * 2, 2)])
    plane_dy = Plane(k, lambda s, h: dy_o.at[lax.div(s, 2), pl.ds(h * half, half)])
    plane_x1n = Plane(k, lambda s, h: x1n_o.at[lax.div(s, 2), pl.ds(h * half, half)])
    twin_xn = Sibling(k, lambda s: xn.at[s], 4)
    twin_out = Sibling(k, lambda s: wout.at[s], 4)
    twin_fv = Sibling(k, lambda s: fv_o.at[:, s], 1)
    twin_fg = Sibling(k, lambda s: fg_o.at[:, s], 1)
    twin_fo = Sibling(k, lambda s: fo_o.at[s], 1)
    other = 1 - core

    for copy in own:
        copy.wait()
    line_out.start()
    for spread in spreads:
        spread.start()
    plane_xn.start()
    twin_xn.send(w)
    for spread in spread_ff:
        spread.start()
    spreads[0].finish()
    spreads[1].finish()
    line_qk.start()
    spreads[2].finish()
    spreads[3].finish()
    line_vg.start()
    line_out.forward()
    plane_xn.forward()
    line_out.finish()
    plane_out.start()
    twin_out.send(w)
    plane_xn.finish_near()
    twin_xn.send(k.wx)
    twin_xn.send(k.wy)
    line_qk.forward()
    plane_xn.finish_far()
    twin_xn.send(k.wd)
    spread_ff[0].finish()
    spread_ff[1].finish()
    for copy in own_ff:
        copy.wait()
    line_fv.start()
    line_fg.start()
    line_fo.start()
    line_vg.forward()
    plane_out.forward()
    for s in (k.ws, k.wx + 1 - 2 * core, k.wy + 1 - 2 * core, k.wd + 1 - 2 * core):
        twin_xn.wait(s)
    keep_xn = k.keep(xn, xn_o)
    line_qk.finish()

    def project_qk(t, carry):
        v = dot(xn[t], wqk[...].reshape(-1, 2 * head_cols))
        rows = at(t * tok, tok)
        sigma = jax.nn.sigmoid(v)
        slope[rows, :] = (sigma * (1.0 + v * (1.0 - sigma))).astype(BF)
        qkv[rows, 0 : 2 * head_cols] = (v * sigma).astype(BF)
        return carry

    lax.fori_loop(0, WIDE, project_qk, 0)
    keep_slope = k.keep(slope, slope_o)
    keep_wqk = k.keep(wqk, wqk_o)
    plane_out.finish_near()
    twin_out.send(k.wx)
    twin_out.send(k.wy)
    line_vg.finish()

    def project_vg(t, carry):
        v = dot(xn[t], wvg[...].reshape(-1, 2 * head_cols)).astype(BF)
        qkv[at(t * tok, tok), 2 * head_cols : 3 * head_cols] = v[:, 0:head_cols]
        gates[t] = v[:, head_cols:]
        return carry

    lax.fori_loop(0, WIDE, project_vg, 0)
    keep_wvg = k.keep(wvg, wvg_o)
    keep_qkv = k.keep(qkv, qkv_o)
    spread_gate = Spread(k, lambda t: gates.at[t], lambda s: gate.at[:, wide_cols(s)])
    spread_gate.start()
    gate[:, wide_cols(w)] = gates[w]

    state[...] = jnp.zeros_like(state)
    spread_attn = Spread(k, lambda t: attn_s.at[t], lambda s: attn.at[:, wide_cols(s)])

    def attend(b, carry):
        rows = at(b * BLOCK, BLOCK)
        mask = doc_mask(cols, rowdoc, decay, rows, b)
        for h in range(2):
            lanes = slice(h * HEAD, (h + 1) * HEAD)
            q = qkv[rows, h * HEAD : (h + 1) * HEAD]
            key = qkv[rows, head_cols + h * HEAD : head_cols + (h + 1) * HEAD]
            v = qkv[rows, 2 * head_cols + h * HEAD : 2 * head_cols + (h + 1) * HEAD]
            probs = jnp.where(mask, dot_rt(q, key) * decay[h], 0.0).astype(BF)
            before = state[h]
            before_bf = before.astype(BF)
            sin[b, h] = before_bf
            entry = cols[rows, 1 + h : 2 + h]
            tail = cols[rows, 3 + h : 4 + h]
            out = dot(probs, v) + entry * dot(q, before_bf)
            attn_s[b, :, lanes] = out.astype(BF)
            tailed = (key.astype(F32) * tail).astype(BF)
            state[h] = passing[pl.ds(2 * b + h, 1), :] * before + dot_lt(tailed, v)

        @pl.when(b != w)
        def _():
            d = lax.rem(b - w + WIDE, WIDE)
            base = spread_attn.base
            k.remote(attn_s.at[b], attn.at[:, wide_cols(w)], base + d, base + d, wide=b).start()

        @pl.when(b == w)
        def _():
            attn[:, wide_cols(w)] = attn_s[b]

        return carry

    lax.fori_loop(0, WIDE, attend, 0)
    for d in spread_attn.distances():
        to = lax.rem(w + d, WIDE)
        k.sent.append(
            k.remote(
                attn_s.at[to], attn.at[:, wide_cols(w)], spread_attn.base + d, spread_attn.base + d,
                wide=to,
            )
        )
    keep_sin = k.keep(sin, sin_o)
    plane_out.finish_far()
    twin_out.send(k.wd)
    plane_dy.start()
    for s in (k.ws, k.wx + 1 - 2 * core, k.wy + 1 - 2 * core, k.wd + 1 - 2 * core):
        twin_out.wait(s)
    keep_wo = k.keep(wout, wo_o)
    spread_gate.finish()
    spread_attn.finish()
    keep_attn = k.keep(attn, attn_o)
    keep_gate = k.keep(gate, gate_o)

    def mix(rows):
        a = attn[rows, :].astype(F32)
        mixed[rows, :] = (a * row_scale(a) * gate[rows, :].astype(F32)).astype(BF)

    row_chunks(tok, mix)
    keep_mixed = k.keep(mixed, mixed_o)

    def project_out(j, carry):
        lanes = at(j * 512, 512)
        part = dot(mixed[...], wout[:, :, :, lanes].reshape(-1, 512))
        x1[:, lanes] = x_ref[:, lanes].astype(F32) + part
        return carry

    lax.fori_loop(0, x1.shape[1] // 512, project_out, 0)
    keep_x1 = k.keep(x1, x1_o)

    def norm_mid(rows):
        v = x1[rows, :]
        x1n[rows, :] = (v * row_scale(v)).astype(BF)

    row_chunks(tok, norm_mid)
    k.keep(x1n, x1n_o.at[chip]).wait()
    plane_x1n.start()
    line_fv.forward()
    plane_dy.forward()
    plane_x1n.forward()
    line_fg.forward()
    line_fo.forward()
    plane_dy.finish_near()
    plane_dy.finish_far()
    line_fv.finish()
    twin_fv.send(core)
    line_fg.finish()
    twin_fg.send(core)
    line_fo.finish()
    twin_fo.send(core)
    plane_x1n.finish_near()
    plane_x1n.finish_far()
    twin_fv.wait(other)
    twin_fg.wait(other)
    twin_fo.wait(other)
    for copy in (
        keep_xn, keep_slope, keep_wqk, keep_wvg, keep_qkv, keep_sin, keep_wo, keep_attn, keep_gate,
        keep_mixed, keep_x1,
    ):
        copy.wait()
    k.drain()


def forward(tokens, weights, dy, cols, rowdoc, passing, decay):
    tok, width = tokens.shape
    shard = weights[0].shape[0]
    full = WIDE * tok
    ff = weights[5].shape[1] // CHIPS
    fo_rows = weights[7].shape[0]
    two = 2 * HEAD

    def hbm(shape, dtype=BF):
        return jax.ShapeDtypeStruct(shape, dtype)

    out_shape = (
        hbm((WIDE, tok, width)),
        hbm((WIDE, NARROW, shard, 2 * two)),
        hbm((WIDE, NARROW, shard, 2 * two)),
        hbm((WIDE, NARROW, shard, width)),
        hbm((CHIPS, 2, NARROW, shard, ff)),
        hbm((CHIPS, 2, NARROW, shard, ff)),
        hbm((2, NARROW, fo_rows, width)),
        hbm((CHIPS, tok, width)),
        hbm((full, 2 * two)),
        hbm((full, 3 * two)),
        hbm((WIDE, 2, HEAD, HEAD)),
        hbm((tok, width)),
        hbm((tok, width)),
        hbm((tok, width)),
        hbm((tok, width), F32),
        hbm((CHIPS, tok, width)),
    )
    scratch = [
        pltpu.VMEM((WIDE, tok, width), BF),
        pltpu.VMEM((WIDE, NARROW, shard, 2 * two), BF),
        pltpu.VMEM((WIDE, NARROW, shard, 2 * two), BF),
        pltpu.VMEM((WIDE, NARROW, shard, width), BF),
        pltpu.VMEM((full, 2 * two), BF),
        pltpu.VMEM((full, 3 * two), BF),
        pltpu.VMEM((WIDE, tok, two), BF),
        pltpu.VMEM((WIDE, 2, HEAD, HEAD), BF),
        pltpu.VMEM((2, HEAD, HEAD), F32),
        pltpu.VMEM((WIDE, tok, two), BF),
        pltpu.VMEM((tok, width), BF),
        pltpu.VMEM((tok, width), BF),
        pltpu.VMEM((tok, width), BF),
        pltpu.VMEM((tok, width), F32),
        pltpu.VMEM((tok, width), BF),
        pltpu.SemaphoreType.DMA((136,)),
        pltpu.SemaphoreType.DMA((136,)),
        pltpu.SemaphoreType.DMA((24,)),
    ]
    return pl.pallas_call(
        forward_kernel,
        out_shape=out_shape,
        in_specs=[VMEM] + [ANY] * 9 + [VMEM] * 4,
        out_specs=(ANY,) * len(out_shape),
        scratch_shapes=scratch,
        compiler_params=pltpu.CompilerParams(
            collective_id=0, has_side_effects=True, vmem_limit_bytes=60 * 2**20
        ),
        cost_estimate=pl.CostEstimate(flops=2 * 10**10, bytes_accessed=10**8, transcendentals=0),
    )(tokens, *weights, dy, cols, rowdoc, passing, decay)


class LineSum:
    def __init__(self, links, part, land):
        self.links, self.part, self.land = links, part, land
        self.base = links.take(3)
        self.over = 1 + lax.rem(links.n, 2)

    def relay(self, slot):
        k, b = self.links, self.base
        return k.remote(self.part(k.cross), self.land(slot), b, b + slot, narrow=self.over)

    def near(self):
        k, b = self.links, self.base
        return k.remote(self.part(k.pair), self.land(0), b + 1, b, narrow=k.pair)

    def distant(self):
        k, b = self.links, self.base
        slot = 2 - k.mid
        return k.remote(self.part(k.far), self.land(slot), b + 2, b + slot, narrow=k.far)

    def start(self):
        @pl.when(self.links.mid == 0)
        def _():
            self.relay(1).start()

        self.distant().start()
        self.near().start()

    def forward(self, add):
        k = self.links

        @pl.when(k.mid == 1)
        def _():
            k.arrived(self.land(1), self.base + 1)
            add(self.part(k.cross), self.land(1))
            self.relay(2).start()

    def finish(self):
        k = self.links
        k.arrived(self.land(0), self.base)
        k.arrived(self.land(2), self.base + 2)

        @pl.when(k.mid == 0)
        def _():
            k.arrived(self.land(1), self.base + 1)

    def drain(self):
        self.relay(1).wait_send()
        self.distant().wait_send()
        self.near().wait_send()


class PlaneSum:
    def __init__(self, links, block, corner, near, half):
        self.links, self.block, self.corner, self.near, self.half = links, block, corner, near, half
        self.base = links.take(6)

    def rows(self, h):
        return pl.ds(h * self.half, self.half)

    def copy(self, index):
        k = self.links
        chip, h, land, to = (
            (k.pd, 0, self.corner.at[0], k.wx),
            (k.pd, 1, self.corner.at[1], k.wy),
            (k.px, 0, self.near.at[0, self.rows(0)], k.wx),
            (k.py, 1, self.near.at[1, self.rows(1)], k.wy),
            (k.px, 1, self.near.at[0, self.rows(1)], k.wx),
            (k.py, 0, self.near.at[1, self.rows(0)], k.wy),
        )[index]
        sem = self.base + index
        return k.remote(self.block(chip).at[self.rows(h)], land, sem, sem, wide=to)

    def send_far(self):
        self.copy(0).start()
        self.copy(1).start()

    def send_x(self):
        self.copy(2).start()

    def send_y(self):
        self.copy(3).start()

    def combine(self, add):
        k = self.links
        self.copy(1).wait_recv()
        add(self.block(k.px).at[self.rows(1)], self.corner.at[1])
        self.copy(4).start()
        self.copy(0).wait_recv()
        add(self.block(k.py).at[self.rows(0)], self.corner.at[0])
        self.copy(5).start()

    def finish(self):
        for index in range(2, 6):
            self.copy(index).wait_recv()

    def drain(self):
        for index in range(6):
            self.copy(index).wait_send()


def backward_kernel(
    x_in, xn_in, wqk_in, wvg_in, wo_in, fv_in, fg_in, fo_in, dy_in, slope_in, qkv_in, sin_in,
    attn_in, gate_in, mixed_in, x1_in, x1n_in, cols_in, decay_in, rowdoc, passing,
    result_o, dx_o, gq_o, gk_o, gv_o, gg_o, go_o, gfv_o, gfg_o, gfo_o,
    corner, near, twin_fo, twin_ff, twin_wo, twin_xn, land_fo, land_ff, land_wo, land_qk, turn_ff,
    turn_qk, a_land, g_land,
    g_fo, g_fv, g_fg, stage, acc, tmp, tmp_ff,
    send, recv, here,
):
    k = Links(send, recv, here)
    w, n, core, chip = k.w, k.n, k.core, k.chip
    other = 1 - core
    tok, width = acc.shape
    ff = g_fv.shape[-1]
    fo_rows = land_fo.shape[1]
    half = tok // 2
    two = 2 * HEAD
    order = (k.pd, k.px, k.py, chip)

    def nth(j):
        flip_x, flip_y = 1 - lax.div(j, 2), 1 - lax.rem(j, 2)
        return (
            chip + flip_x * (1 - 2 * lax.rem(chip, 2)) + flip_y * (2 - 4 * lax.div(chip, 2))
        )

    def fetch(src, dst):
        copy = pltpu.make_async_copy(src, dst, here.at[0])
        copy.start()
        copy.wait()

    def adder(spot):
        def add(to, land):
            fetch(land, spot)
            to[...] = (to[...].astype(F32) + spot[...].astype(F32)).astype(BF)

        return add

    add_half = adder(tmp.at[pl.ds(0, half)])
    add_fo = adder(tmp.at[pl.ds(0, fo_rows)])
    add_wo = adder(tmp.at[pl.ds(0, 64)])
    add_ff = adder(tmp_ff)
    k.kept.append(None)

    def fo_part(owner, i):
        return g_fo.at[pl.ds(pl.multiple_of((owner * NARROW + i) * fo_rows, 16), fo_rows)]

    line_fo = LineSum(k, lambda i: fo_part(core, i), lambda s: land_fo.at[s])
    line_ff = [
        LineSum(k, lambda i, g=g: g.at[:, i], lambda s, m=m: land_ff.at[m, s])
        for m, g in enumerate((g_fv, g_fg))
    ]
    def plane_sum(m, blocks):
        return PlaneSum(k, lambda q: blocks.at[q], corner.at[m], near.at[m], half)

    plane_mid, plane_res, plane_in = (plane_sum(m, stage) for m in (0, 1, 3))
    twin_base = k.take(4 * 5)

    def twin(m, j, src, dst):
        sem = twin_base + 4 * m + j
        return k.remote(src, dst, sem, sem, wide=k.ws)

    k.greet()

    def ffn(x1n, dy, fvw, fgw, fow, mix, val, gat, side):
        loads = [
            k.keep(x1n_in, x1n), k.keep(fv_in, fvw), k.keep(fg_in, fgw), k.keep(dy_in, dy),
            k.keep(fo_in, fow),
        ]
        for copy in loads[:3]:
            copy.wait()
        k.met()

        def up(j, carry):
            v = dot(x1n[j], fvw[...].reshape(width, ff))
            g = dot(x1n[j], fgw[...].reshape(width, ff))
            mix[j] = (v * g).astype(BF)
            val[j] = v.astype(BF)
            gat[j] = g.astype(BF)
            return carry

        lax.fori_loop(0, CHIPS, up, 0)

        for copy in loads[3:]:
            copy.wait()

        def fo_grad(j, carry):
            chunk = lax.rem(j + 2 * other, chunks)
            rows = pl.ds(pl.multiple_of(jnp.minimum(chunk * 256, ff - 256), 128), 256)
            left = mix[:, :, rows].reshape(CHIPS * tok, 256)
            for h in range(2):
                lanes = slice(h * width // 2, (h + 1) * width // 2)
                right = dy[:, :, lanes].reshape(CHIPS * tok, -1)
                g_fo[rows, lanes] = dot_lt(left, right).astype(BF)
            return carry

        chunks = pl.cdiv(ff, 256)
        lax.fori_loop(0, 4, fo_grad, 0)
        for i in range(NARROW):
            twin(0, i, fo_part(other, i), twin_fo.at[i]).start()
        lax.fori_loop(4, chunks, fo_grad, 0)
        for i in range(NARROW):
            copy = twin(0, i, fo_part(other, i), twin_fo.at[i])
            copy.wait_recv()
            add_fo(fo_part(core, i), twin_fo.at[i])
            copy.wait_send()
        line_fo.start()

        def down(j, carry):
            q = nth(j)
            d_mix = dot_rt(dy[q], fow[...].reshape(ff, width))
            d_val = (d_mix * gat[q].astype(F32)).astype(BF)
            d_gat = (d_mix * val[q].astype(F32)).astype(BF)
            val[q] = d_val
            gat[q] = d_gat

            def back(i, carry):
                lanes = at(i * 512, 512)
                d_x = dot_rt(val[q], fvw[i].reshape(512, ff)) + dot_rt(
                    gat[q], fgw[i].reshape(512, ff)
                )
                stage[q, :, lanes] = d_x.astype(BF)

                @pl.when(j == 3)
                def _():
                    acc[:, lanes] = d_x

                return carry

            lax.fori_loop(0, width // 512, back, 0)

            for step, push in enumerate((plane_mid.send_far, plane_mid.send_x, plane_mid.send_y)):
                pl.when(j == step)(push)

            return carry

        lax.fori_loop(0, CHIPS, down, 0)
        plane_mid.combine(add_half)
        line_fo.forward(add_fo)

        for m, (d_ff, g_ff) in enumerate(((val, g_fv), (gat, g_fg))):

            def ff_grad(owner):
                left = x1n[:, :, at(owner * tok, tok)].reshape(CHIPS * tok, tok)
                g = dot_lt(left, d_ff[...].reshape(CHIPS * tok, ff)).astype(BF)
                return g.reshape(NARROW, -1, ff)

            def side_step(q, carry):
                slot = lax.rem(q, 2)

                @pl.when(q >= 2)
                def _():
                    twin(1 + m, q - 2, side.at[slot], twin_ff.at[m, q]).wait_send()

                side[slot] = ff_grad(2 * q + other)
                twin(1 + m, q, side.at[slot], twin_ff.at[m, q]).start()
                return carry

            def own_step(q, carry):
                g_ff[q] = ff_grad(2 * q + core)
                return carry

            lax.fori_loop(0, CHIPS, side_step, 0)
            lax.fori_loop(0, CHIPS, own_step, 0)
            for q in range(CHIPS):
                copy = twin(1 + m, q, side.at[q % 2], twin_ff.at[m, q])
                copy.wait_recv()
                add_ff(g_ff.at[q], twin_ff.at[m, q])
                if q >= 2:
                    copy.wait_send()
            line_ff[m].start()

        plane_mid.drain()

        def out_step(j, carry):
            q = nth(j)
            stage[q] = dot(mix[q], fow[...].reshape(ff, width)).astype(BF)
            for step, push in enumerate((plane_res.send_far, plane_res.send_x, plane_res.send_y)):
                pl.when(j == step)(push)
            return carry

        lax.fori_loop(0, CHIPS, out_step, 0)

    pl.run_scoped(
        ffn,
        pltpu.VMEM((CHIPS, tok, width), BF),
        pltpu.VMEM((CHIPS, tok, width), BF),
        pltpu.VMEM(fv_in.shape, BF),
        pltpu.VMEM(fg_in.shape, BF),
        pltpu.VMEM(fo_in.shape, BF),
        pltpu.VMEM((CHIPS, tok, ff), BF),
        pltpu.VMEM((CHIPS, tok, ff), BF),
        pltpu.VMEM((CHIPS, tok, ff), BF),
        pltpu.VMEM((2, *g_fv.shape[1:]), BF),
    )

    def rest(d_x1, d_branch, mixed, da_src, dg_src, side, stage_wo, own_res, g_wo, g_qk, g_vg):
        plane_out = plane_sum(2, stage_wo)
        own_res[...] = stage[chip]
        line_wo = LineSum(k, lambda i: g_wo.at[i], lambda s: land_wo.at[s])
        line_qk = [
            LineSum(k, lambda i, g=g: g.at[:, i], lambda s, m=m: land_qk.at[m, s])
            for m, g in enumerate((g_qk, g_vg))
        ]
        spread_a = Spread(
            k, lambda t: da_src.at[:, at(t * two, two)], lambda s: a_land.at[s], record=False
        )
        spread_g = Spread(
            k, lambda t: dg_src.at[:, at(t * two, two)], lambda s: g_land.at[s], record=False
        )

        def middle(wo, x1, attn, gate, dy, d_mixed, pair):
            loads = [k.keep(x1_in, x1), k.keep(dy_in.at[chip], dy)]
            late = [
                k.keep(attn_in, attn), k.keep(gate_in, gate), k.keep(wo_in, wo),
                k.keep(mixed_in, mixed),
            ]
            plane_mid.finish()
            fetch(near.at[0], pair)
            for copy in loads:
                copy.wait()

            def norm_back(rows):
                g = acc[rows, :] + pair[0, rows, :].astype(F32) + pair[1, rows, :].astype(F32)
                v = x1[rows, :]
                r = row_scale(v)
                u = v * r
                d = dy[rows, :].astype(F32) + r * (g - u * jnp.mean(g * u, axis=-1, keepdims=True))
                d_x1[rows, :] = d
                d_branch[rows, :] = d.astype(BF)

            row_chunks(tok, norm_back)
            for copy in late:
                copy.wait()

            def mixed_step(j, carry):
                d_mixed[:, at(j * 512, 512)] = dot_rt(
                    d_branch[...], wo[pl.ds(2 * j, 2)].reshape(512, width)
                )
                return carry

            lax.fori_loop(0, width // 512, mixed_step, 0)

            def attn_back(rows):
                a = attn[rows, :].astype(F32)
                s = row_scale(a)
                u = a * s
                d = d_mixed[rows, :]
                dg_src[rows, :] = (d * u).astype(BF)
                g = d * gate[rows, :].astype(F32)
                da_src[rows, :] = (
                    s * (g - u * jnp.mean(g * u, axis=-1, keepdims=True))
                ).astype(BF)

            row_chunks(tok, attn_back)
            spread_a.start()
            spread_g.start()
            own = [
                k.keep(da_src.at[:, at(w * two, two)], a_land.at[w]),
                k.keep(dg_src.at[:, at(w * two, two)], g_land.at[w]),
            ]

            for copy in own:
                copy.wait()

        pl.run_scoped(
            middle,
            pltpu.VMEM((WIDE, tok, width), BF),
            pltpu.VMEM((tok, width), F32),
            pltpu.VMEM((tok, width), BF),
            pltpu.VMEM((tok, width), BF),
            pltpu.VMEM((tok, width), BF),
            pltpu.VMEM((tok, width), F32),
            pltpu.VMEM((2, tok, width), BF),
        )
        plane_res.combine(add_half)

        def eight_way(plane, twin_index, landing, blocks, term):
            def side_step(j, carry):
                q = nth(j)
                side[q] = term(2 * q + other).astype(BF)
                twin(twin_index, j, side.at[q], landing.at[q]).start()
                return carry

            lax.fori_loop(0, CHIPS, side_step, 0)

            def own_step(j, carry):
                q = nth(j)
                v = term(2 * q + core)
                twin(twin_index, j, side.at[q], landing.at[q]).wait_recv()
                fetch(landing.at[q], tmp)
                v = v + tmp[...].astype(F32)

                @pl.when(j < 3)
                def _():
                    blocks[q] = v.astype(BF)

                for step, push in enumerate((plane.send_far, plane.send_x, plane.send_y)):
                    pl.when(j == step)(push)

                @pl.when(j == 3)
                def _():
                    acc[...] = v

                return carry

            lax.fori_loop(0, CHIPS, own_step, 0)
            for j in range(CHIPS):
                twin(twin_index, j, side.at[order[j]], landing.at[order[j]]).wait_send()

        eight_way(
            plane_out,
            3,
            twin_wo,
            stage_wo,
            lambda owner: dot_lt(mixed[:, at(owner * tok, tok)], d_branch[...]),
        )
        line_ff[0].forward(add_ff)

        def attention(xn, d_qk, d_vg, state):
            state[...] = jnp.zeros_like(state)

            def heads(slope, qkv, sin, cols, decay, d_attn, d_gate):
                loads = [
                    k.keep(qkv_in, qkv), k.keep(sin_in, sin), k.keep(slope_in, slope),
                    k.keep(cols_in, cols), k.keep(decay_in, decay),
                ]
                load_xn = k.keep(xn_in, xn)
                for copy in loads:
                    copy.wait()
                spread_a.finish()
                spread_g.finish()
                loads = [k.keep(a_land, d_attn), k.keep(g_land, d_gate)]
                for copy in loads:
                    copy.wait()

                def step(i, carry):
                    b = WIDE - 1 - i
                    rows = at(b * BLOCK, BLOCK)
                    mask = doc_mask(cols, rowdoc, decay, rows, b)
                    for h in range(2):
                        lanes = slice(h * HEAD, (h + 1) * HEAD)
                        key_lanes = slice(two + h * HEAD, two + (h + 1) * HEAD)
                        q = qkv[rows, lanes]
                        key = qkv[rows, key_lanes]
                        v = qkv[rows, 2 * two + h * HEAD : 2 * two + (h + 1) * HEAD]
                        d_o = d_attn[b, :, lanes]
                        factor = jnp.where(mask, decay[h], 0.0)
                        probs = (dot_rt(q, key) * factor).astype(BF)
                        d_probs = (dot_rt(d_o, v) * factor).astype(BF)
                        entry = cols[rows, 1 + h : 2 + h]
                        tail = cols[rows, 3 + h : 4 + h]
                        before = sin[b, h]
                        after = state[h]
                        after_bf = after.astype(BF)
                        tailed = (key.astype(F32) * tail).astype(BF)
                        entered = (q.astype(F32) * entry).astype(BF)
                        d_q = dot(d_probs, key) + entry * dot_rt(d_o, before)
                        d_k = dot_lt(d_probs, q) + tail * dot_rt(v, after_bf)
                        d_v = dot_lt(probs, d_o) + dot(tailed, after_bf)
                        d_qk[rows, lanes] = (d_q * slope[rows, lanes].astype(F32)).astype(BF)
                        d_qk[rows, key_lanes] = (d_k * slope[rows, key_lanes].astype(F32)).astype(BF)
                        d_vg[rows, lanes] = d_v.astype(BF)
                        state[h] = passing[pl.ds(2 * b + h, 1), :] * after + dot_lt(entered, d_o)
                    d_vg[rows, two:] = d_gate[b]
                    return carry

                lax.fori_loop(0, WIDE, step, 0)
                load_xn.wait()

            pl.run_scoped(
                heads,
                pltpu.VMEM(slope_in.shape, BF),
                pltpu.VMEM(qkv_in.shape, BF),
                pltpu.VMEM(sin_in.shape, BF),
                pltpu.VMEM(cols_in.shape, F32),
                pltpu.VMEM(decay_in.shape, F32),
                pltpu.VMEM((WIDE, tok, two), BF),
                pltpu.VMEM((WIDE, tok, two), BF),
            )

            plane_out.combine(add_half)
            for m, (d_in, g_in) in enumerate(((d_qk, g_qk), (d_vg, g_vg))):

                def in_grad(s, carry):
                    left = xn[:, :, at(s * tok, tok)].reshape(WIDE * tok, tok)
                    g_in[s] = dot_lt(left, d_in[...]).astype(BF).reshape(NARROW, -1, 2 * two)
                    return carry

                lax.fori_loop(0, WIDE, in_grad, 0)
                line_qk[m].start()

            line_ff[1].forward(add_ff)
            plane_out.finish()
            for side_index in range(2):
                fetch(near.at[2, side_index], tmp)
                acc[...] = acc[...] + tmp[...].astype(F32)
            g_wo[...] = acc[...].astype(BF).reshape(g_wo.shape)
            line_wo.start()
            plane_out.drain()
            plane_res.drain()

            def spread_in(wqk, wvg):
                loads = [k.keep(wqk_in, wqk), k.keep(wvg_in, wvg)]
                for copy in loads:
                    copy.wait()

                def term(owner):
                    rows = at(owner * tok, tok)
                    return dot_rt(d_qk[rows, :], wqk[...].reshape(width, 2 * two)) + dot_rt(
                        d_vg[rows, :], wvg[...].reshape(width, 2 * two)
                    )

                eight_way(plane_in, 4, twin_xn, stage, term)

            pl.run_scoped(spread_in, pltpu.VMEM(wqk_in.shape, BF), pltpu.VMEM(wvg_in.shape, BF))

        pl.run_scoped(
            attention,
            pltpu.VMEM((WIDE, tok, width), BF),
            pltpu.VMEM((WIDE * tok, 2 * two), BF),
            pltpu.VMEM((WIDE * tok, 2 * two), BF),
            pltpu.VMEM((2, HEAD, HEAD), F32),
        )

        def last(
            x, x1, pair, three, three_ff, three_qk, ff_src, qk_src, ff_all, qk_all, ff_f32, w_f32, w_fo, tmp_qk
        ):
            add_qk = adder(tmp_qk)
            load_x, load_x1 = k.keep(x_in, x), k.keep(x1_in, x1)

            def total(part, lands):
                extra = jnp.where(k.mid == 0, lands[1].astype(F32), 0.0)
                return part.astype(F32) + lands[0].astype(F32) + lands[2].astype(F32) + extra

            ff_turns = []
            for m, g_ff in enumerate((g_fv, g_fg)):
                line_ff[m].finish()
                fetch(land_ff.at[m], three_ff)
                for q in range(CHIPS):
                    ff_src[m, q] = total(g_ff[q, n], [three_ff[s, q] for s in range(3)]).astype(BF)
                turn = Spread(
                    k,
                    lambda t, m=m: ff_src.at[m, lax.div(t, 2)],
                    lambda s, m=m: turn_ff.at[m, lax.div(s, 2)],
                    peers=CHIPS,
                    record=False,
                )
                turn.start()
                ff_turns.append((turn, k.keep(ff_src.at[m, chip], turn_ff.at[m, chip])))
            plane_in.combine(add_half)
            line_fo.finish()
            fetch(land_fo, three.at[:, pl.ds(0, fo_rows)])
            own = fo_part(core, n)
            for r in range(0, fo_rows, 16):
                rows = pl.ds(r, 16)
                w_fo[rows, :] = total(own[rows, :], [three[s, rows, :] for s in range(3)])
            stores = [k.keep(w_fo, gfo_o)]
            line_qk[0].forward(add_qk)

            plane_res.finish()
            fetch(near.at[1], pair)
            load_x1.wait()

            def add_up(rows):
                v = x1[rows, :] + own_res[rows, :].astype(F32)
                v = v + pair[0, rows, :].astype(F32) + pair[1, rows, :].astype(F32)
                own_res[rows, :] = v.astype(BF)

            row_chunks(tok, add_up)
            stores.append(k.keep(own_res, result_o))
            load_x.wait()
            plane_in.finish()
            fetch(near.at[3], pair)

            def input_back(rows):
                g = acc[rows, :] + pair[0, rows, :].astype(F32) + pair[1, rows, :].astype(F32)
                v = x[rows, :].astype(F32)
                r = row_scale(v)
                u = v * r
                d_x1[rows, :] = d_x1[rows, :] + r * (
                    g - u * jnp.mean(g * u, axis=-1, keepdims=True)
                )

            row_chunks(tok, input_back)
            stores.append(k.keep(d_x1, dx_o))
            for m, (turn, copy) in enumerate(ff_turns):
                turn.finish()
                copy.wait()
                fetch(turn_ff.at[m], ff_all)
                for q in range(CHIPS):
                    ff_f32[m, :, q * ff : (q + 1) * ff] = ff_all[q].astype(F32)
                stores.append(k.keep(ff_f32.at[m], (gfv_o, gfg_o)[m]))
            line_qk[1].forward(add_qk)
            qk_turns = []
            for m, g_in in enumerate((g_qk, g_vg)):
                line_qk[m].finish()
                fetch(land_qk.at[m], three_qk)
                for s in range(WIDE):
                    qk_src[m, s] = total(g_in[s, n], [three_qk[i, s] for i in range(3)]).astype(BF)
                turn = Spread(
                    k,
                    lambda t, m=m: qk_src.at[m, t],
                    lambda s, m=m: turn_qk.at[m, s],
                    record=False,
                )
                turn.start()
                qk_turns.append((turn, k.keep(qk_src.at[m, w], turn_qk.at[m, w])))
                if m == 0:
                    line_wo.forward(add_wo)
            line_wo.finish()
            fetch(land_wo, three.at[:, pl.ds(0, 64)])
            w_f32[4] = total(g_wo[n], [three[s, 0:64, :] for s in range(3)])
            stores.append(k.keep(w_f32.at[4], go_o))
            for m, (turn, copy) in enumerate(qk_turns):
                turn.finish()
                copy.wait()
                fetch(turn_qk.at[m], qk_all)
                for s in range(WIDE):
                    lanes = slice(s * two, (s + 1) * two)
                    w_f32[2 * m, :, lanes] = qk_all[s, :, 0:two].astype(F32)
                    w_f32[2 * m + 1, :, lanes] = qk_all[s, :, two:].astype(F32)
                outs = ((gq_o, gk_o), (gv_o, gg_o))[m]
                stores.append(k.keep(w_f32.at[2 * m], outs[0]))
                stores.append(k.keep(w_f32.at[2 * m + 1], outs[1]))
            for copy in stores:
                copy.wait()
            plane_in.drain()
            turns = [turn for turn, copy in ff_turns + qk_turns]
            for sums in (line_fo, line_wo, *line_ff, *line_qk, spread_a, spread_g, *turns):
                sums.drain()

        pl.run_scoped(
            last,
            pltpu.VMEM((tok, width), BF),
            pltpu.VMEM((tok, width), F32),
            pltpu.VMEM((2, tok, width), BF),
            pltpu.VMEM((3, tok, width), BF),
            pltpu.VMEM(land_ff.shape[1:], BF),
            pltpu.VMEM(land_qk.shape[1:], BF),
            pltpu.VMEM((2, CHIPS, 64, ff), BF),
            pltpu.VMEM((2, WIDE, 64, 2 * two), BF),
            pltpu.VMEM((CHIPS, 64, ff), BF),
            pltpu.VMEM((WIDE, 64, 2 * two), BF),
            pltpu.VMEM((2, 64, CHIPS * ff), F32),
            pltpu.VMEM((5, 64, width), F32),
            pltpu.VMEM((fo_rows, width), F32),
            pltpu.VMEM((WIDE, 64, 2 * two), BF),
        )

    pl.run_scoped(
        rest,
        pltpu.VMEM((tok, width), F32),
        pltpu.VMEM((tok, width), BF),
        pltpu.VMEM((tok, width), BF),
        pltpu.VMEM((tok, width), BF),
        pltpu.VMEM((tok, width), BF),
        pltpu.VMEM((CHIPS, tok, width), BF),
        pltpu.VMEM((CHIPS, tok, width), BF),
        pltpu.VMEM((tok, width), BF),
        pltpu.VMEM((NARROW, 64, width), BF),
        pltpu.VMEM((WIDE, NARROW, 64, 2 * two), BF),
        pltpu.VMEM((WIDE, NARROW, 64, 2 * two), BF),
    )


def backward(tokens, kept, cols, rowdoc, passing, decay):
    tok, width = tokens.shape
    fv, fo = kept[4], kept[6]
    shard, ff, fo_rows = fv.shape[3], fv.shape[4], fo.shape[2]
    two = 2 * HEAD

    def arr(*shape, dtype=BF):
        return jax.ShapeDtypeStruct(shape, dtype)

    square = [arr(shard, width, dtype=F32)] * 5
    out_shape = (
        arr(tok, width),
        arr(tok, width, dtype=F32),
        *square,
        arr(shard, CHIPS * ff, dtype=F32),
        arr(shard, CHIPS * ff, dtype=F32),
        arr(fo_rows, width, dtype=F32),
        arr(4, 2, tok // 2, width),
        arr(4, 2, tok, width),
        arr(NARROW, fo_rows, width),
        arr(2, CHIPS, NARROW, shard, ff),
        arr(CHIPS, tok, width),
        arr(CHIPS, tok, width),
        arr(3, fo_rows, width),
        arr(2, 3, CHIPS, shard, ff),
        arr(3, shard, width),
        arr(2, 3, WIDE, shard, 2 * two),
        arr(2, CHIPS, shard, ff),
        arr(2, WIDE, shard, 2 * two),
        arr(WIDE, tok, two),
        arr(WIDE, tok, two),
    )
    scratch = [
        pltpu.VMEM((CHIPS * ff // CHIPS, width), BF),
        pltpu.VMEM((CHIPS, NARROW, shard, ff), BF),
        pltpu.VMEM((CHIPS, NARROW, shard, ff), BF),
        pltpu.VMEM((CHIPS, tok, width), BF),
        pltpu.VMEM((tok, width), F32),
        pltpu.VMEM((tok, width), BF),
        pltpu.VMEM((CHIPS, shard, ff), BF),
        pltpu.SemaphoreType.DMA((112,)),
        pltpu.SemaphoreType.DMA((112,)),
        pltpu.SemaphoreType.DMA((48,)),
    ]
    outs = pl.pallas_call(
        backward_kernel,
        out_shape=out_shape,
        in_specs=[ANY] * 19 + [VMEM] * 2,
        out_specs=(ANY,) * len(out_shape),
        scratch_shapes=scratch,
        compiler_params=pltpu.CompilerParams(
            collective_id=1, has_side_effects=True, vmem_limit_bytes=63 * 2**20
        ),
        cost_estimate=pl.CostEstimate(flops=6 * 10**10, bytes_accessed=2 * 10**8, transcendentals=0),
    )(tokens, *kept, cols, decay, rowdoc, passing)
    return outs[:10]


def prepare(doc_starts, length):
    starts = lax.dynamic_slice_in_dim(doc_starts, lax.axis_index("narrow"), 1, 0)[0]
    blocks = length // BLOCK
    positions = jnp.arange(length, dtype=jnp.int32)
    doc_ids = jnp.sum((starts[None, :] <= positions[:, None]).astype(jnp.int32), axis=1)
    doc_ids = doc_ids.reshape(blocks, BLOCK).astype(F32)
    firsts = jnp.arange(blocks, dtype=jnp.int32) * BLOCK - 1
    prev_ids = jnp.sum((starts[None, :] <= firsts[:, None]).astype(jnp.int32), axis=1).astype(F32)
    slopes = lax.dynamic_slice_in_dim(head_slopes(), lax.axis_index("wide") * 2, 2, 0)
    offsets = jnp.arange(BLOCK, dtype=F32)
    lags = offsets[:, None] - offsets[None, :]
    decay = jnp.exp(-slopes[:, None, None] * jnp.maximum(lags, 0.0)[None])
    continues = (doc_ids == prev_ids[:, None]).astype(F32)
    entry = continues[..., None] * jnp.exp(-slopes[None, :] * (offsets[:, None] + 1.0))
    tail = (doc_ids == doc_ids[:, -1:]).astype(F32)[..., None] * jnp.exp(
        -slopes[None, :] * (BLOCK - 1.0 - offsets)[:, None]
    )
    passing = continues[:, -1:] * jnp.exp(-slopes * BLOCK)
    cols = jnp.concatenate([doc_ids[..., None], entry, tail], axis=-1).reshape(length, 5)
    cols = jnp.pad(cols, ((0, 0), (0, HEAD - 5)))
    passing = jnp.broadcast_to(passing.reshape(-1, 1), (2 * blocks, HEAD))
    return cols, doc_ids, passing, decay


def local_box(tokens, doc_starts, wq, wk, wv, wg, wo, fv, fg, fo, cotangent):
    tok, width = tokens.shape[1:]
    tables = prepare(doc_starts, WIDE * tok)
    kept = list(
        forward(tokens[0], (wq, wk, wv, wg, wo, fv, fg, fo), cotangent[0], *tables)
    )
    kept[3] = kept[3].reshape(WIDE, tok, width)
    outs = backward(tokens[0], kept, *tables)
    return (outs[0][None], outs[1][None]) + tuple(outs[2:])


def solution(mesh):
    box = (mesh.shape["wide"], mesh.shape["narrow"]) == (WIDE, NARROW)
    tok = P("narrow", "wide", None)
    row = P(BOTH, None)
    return jax.shard_map(
        local_box if box else local,
        mesh=mesh,
        in_specs=(tok, P()) + (row,) * 8 + (tok,),
        out_specs=(tok, tok) + (row,) * 8,
        check_vma=False,
    )
```

```python
import jax
import jax.numpy as jnp
from jax import lax
from jax.experimental import pallas as pl
from jax.experimental.pallas import tpu as pltpu
from jax.sharding import PartitionSpec as P

HEADS = 16
HEAD = 128
BLOCK = 256
LAYERS = 16
LAYER = 12

EPS = 1e-06
BOTH = ("wide", "narrow")
BF = jnp.bfloat16
F32 = jnp.float32


def normalize(values):
    scale = lax.rsqrt(jnp.mean(values * values, axis=-1, keepdims=True) + EPS)
    return (values * scale, scale)


def normalize_back(normed, scale, grad):
    return scale * (grad - normed * jnp.mean(grad * normed, axis=-1, keepdims=True))


def silu_slope(values):
    sigma = jax.nn.sigmoid(values)
    return sigma * (1.0 + values * (1.0 - sigma))


def matmul(left, right):
    return jnp.dot(left, right, preferred_element_type=F32)


def matmul_right_t(left, right):
    return lax.dot_general(left, right, (((1,), (1,)), ((), ())), preferred_element_type=F32)


def weight_grad(left, right):
    return lax.dot_general(left, right, (((0,), (0,)), ((), ())), preferred_element_type=F32)


def ein(spec, left, right):
    return jnp.einsum(spec, left, right, preferred_element_type=F32)


def head_slopes():
    order = jnp.arange(HEADS, dtype=F32)
    return jnp.exp2(-8.0 * (order + 1.0) / HEADS) * (1.0 - LAYER / (LAYERS - 1) + 1e-05)


def local(
    tokens,
    doc_starts,
    query_weight,
    key_weight,
    value_weight,
    gate_weight,
    out_weight,
    ffn_value_weight,
    ffn_gate_weight,
    ffn_out_weight,
    cotangent,
):
    wide, narrow = lax.axis_size("wide"), lax.axis_size("narrow")
    rows_here, width = tokens.shape[1:]
    length = rows_here * wide
    blocks = length // BLOCK
    heads_here = HEADS // wide
    shard = query_weight.shape[0]

    def reorder(values):
        return values.reshape(-1, wide, narrow, shard).swapaxes(1, 2).reshape(-1, width)

    def restore(values):
        return values.reshape(-1, narrow, wide, shard).swapaxes(1, 2).reshape(-1, width)

    def columns(weight):
        part = lax.all_to_all(weight, "wide", split_axis=1, concat_axis=0, tiled=True)
        return lax.all_gather(part, "narrow", axis=0, tiled=True)

    def gather_rows(values):
        return lax.all_gather(values, "wide", axis=0, tiled=True)

    def scatter_rows(values):
        return lax.psum_scatter(
            values.astype(BF), "wide", scatter_dimension=0, tiled=True
        ).astype(F32)

    def to_tokens(values):
        return lax.all_to_all(values, "wide", split_axis=0, concat_axis=1, tiled=True)

    def to_heads(values):
        return lax.all_to_all(values, "wide", split_axis=1, concat_axis=0, tiled=True)

    def column_sums(grad):
        part = lax.psum_scatter(grad.astype(BF), "narrow", scatter_dimension=0, tiled=True)
        return lax.all_to_all(part, "wide", split_axis=0, concat_axis=1, tiled=True).astype(F32)

    w_query, w_key, w_value, w_gate = map(
        columns, (query_weight, key_weight, value_weight, gate_weight)
    )
    w_out = lax.all_gather(out_weight, BOTH, axis=0, tiled=True)
    w_fval, w_fgate = map(columns, (ffn_value_weight, ffn_gate_weight))
    w_fout = lax.all_gather(ffn_out_weight, "narrow", axis=0, tiled=True)

    starts = lax.dynamic_slice_in_dim(doc_starts, lax.axis_index("narrow"), 1, 0)[0]
    positions = jnp.arange(length, dtype=jnp.int32)
    doc_ids = jnp.sum((starts[None, :] <= positions[:, None]).astype(jnp.int32), axis=1)
    doc_ids = doc_ids.reshape(blocks, BLOCK)
    firsts = jnp.arange(blocks, dtype=jnp.int32) * BLOCK - 1
    prev_ids = jnp.sum((starts[None, :] <= firsts[:, None]).astype(jnp.int32), axis=1)
    slopes = lax.dynamic_slice_in_dim(
        head_slopes(), lax.axis_index("wide") * heads_here, heads_here, 0
    )
    offsets = jnp.arange(BLOCK, dtype=F32)
    lags = offsets[:, None] - offsets[None, :]
    decays = jnp.exp(-slopes[:, None, None] * jnp.maximum(lags, 0.0)[None])
    within = (doc_ids[:, :, None] == doc_ids[:, None, :]) & (lags >= 0.0)
    block_mask = jnp.where(within[:, None], decays[None], 0.0)
    continues = (doc_ids == prev_ids[:, None]).astype(F32)
    entry_scale = continues[..., None] * jnp.exp(-slopes[None, :] * (offsets[:, None] + 1.0))
    tail_scale = (doc_ids == doc_ids[:, -1:]).astype(F32)[..., None] * jnp.exp(
        -slopes[None, :] * (BLOCK - 1.0 - offsets)[:, None]
    )
    passing = continues[:, -1:] * jnp.exp(-slopes * BLOCK)

    def split_heads(values):
        return values.reshape(blocks, BLOCK, heads_here, HEAD)

    inputs = tokens[0].astype(F32)
    normed, in_scale = normalize(inputs)
    normed_bf = gather_rows(reorder(normed.astype(BF)))
    query_pre = matmul(normed_bf, w_query)
    key_pre = matmul(normed_bf, w_key)
    queries = split_heads(jax.nn.silu(query_pre).astype(BF))
    keys = split_heads(jax.nn.silu(key_pre).astype(BF))
    values = split_heads(matmul(normed_bf, w_value).astype(BF))
    gate = matmul(normed_bf, w_gate)
    scores = ein("bihe,bjhe->bhij", queries, keys)
    probs = (scores * block_mask).astype(BF)
    inner = ein("bhij,bjhe->bihe", probs, values)
    tail_keys = (keys.astype(F32) * tail_scale[..., None]).astype(BF)
    fresh = ein("bjhe,bjhf->bhef", tail_keys, values)
    state = jnp.zeros((heads_here, HEAD, HEAD), F32)
    entering = []
    for b in range(blocks):
        entering.append(state)
        state = passing[b][:, None, None] * state + fresh[b]
    block_in = jnp.stack(entering).astype(BF)
    across = entry_scale[..., None] * ein("bihe,bhef->bihf", queries, block_in)
    attention = (inner + across).reshape(query_pre.shape)

    attn_tok = to_tokens(attention)
    gate_tok = to_tokens(gate)
    attn_n, attn_scale = normalize(attn_tok)
    mixed = (attn_n * gate_tok).astype(BF)
    middle = inputs + matmul(mixed, w_out)
    middle_n, middle_scale = normalize(middle)
    middle_bf = gather_rows(reorder(middle_n.astype(BF)))
    ffn_val = matmul(middle_bf, w_fval)
    ffn_gat = matmul(middle_bf, w_fgate)
    ffn_mix = (ffn_val * ffn_gat).astype(BF)
    result = middle + scatter_rows(matmul(ffn_mix, w_fout))

    upstream = cotangent[0]
    up_all = gather_rows(upstream)
    grad_fout = weight_grad(ffn_mix, up_all)
    d_mix = matmul_right_t(up_all, w_fout)
    d_val = (d_mix * ffn_gat).astype(BF)
    d_gat = (d_mix * ffn_val).astype(BF)
    grad_fval = weight_grad(middle_bf, d_val)
    grad_fgate = weight_grad(middle_bf, d_gat)
    d_middle_n = restore(
        scatter_rows(matmul_right_t(d_val, w_fval) + matmul_right_t(d_gat, w_fgate))
    )
    d_middle = upstream.astype(F32) + normalize_back(middle_n, middle_scale, d_middle_n)
    d_branch = d_middle.astype(BF)
    grad_out = weight_grad(mixed, d_branch)
    d_mixed = matmul_right_t(d_branch, w_out)
    d_gate = to_heads((d_mixed * attn_n).astype(BF))
    d_attn = to_heads(normalize_back(attn_n, attn_scale, d_mixed * gate_tok).astype(BF))

    d_heads = split_heads(d_attn)
    d_probs = ein("bihe,bjhe->bhij", d_heads, values)
    d_scores = (d_probs * block_mask).astype(BF)
    d_query = ein("bhij,bjhe->bihe", d_scores, keys)
    d_key = ein("bhij,bihe->bjhe", d_scores, queries)
    d_value = ein("bhij,bihe->bjhe", probs, d_heads)
    d_query = d_query + entry_scale[..., None] * ein("bihf,bhef->bihe", d_heads, block_in)
    entry_queries = (queries.astype(F32) * entry_scale[..., None]).astype(BF)
    grad_in = ein("bihe,bihf->bhef", entry_queries, d_heads)
    state = jnp.zeros((heads_here, HEAD, HEAD), F32)
    leaving = [None] * blocks
    for b in reversed(range(blocks)):
        leaving[b] = state
        state = passing[b][:, None, None] * state + grad_in[b]
    block_out = jnp.stack(leaving).astype(BF)
    d_key = d_key + tail_scale[..., None] * ein("bjhf,bhef->bjhe", values, block_out)
    d_value = d_value + ein("bjhe,bhef->bjhf", tail_keys, block_out)
    dq_pre = (d_query.reshape(query_pre.shape) * silu_slope(query_pre)).astype(BF)
    dk_pre = (d_key.reshape(key_pre.shape) * silu_slope(key_pre)).astype(BF)
    dv_pre = d_value.reshape(query_pre.shape).astype(BF)
    grad_query = weight_grad(normed_bf, dq_pre)
    grad_key = weight_grad(normed_bf, dk_pre)
    grad_value = weight_grad(normed_bf, dv_pre)
    grad_gate = weight_grad(normed_bf, d_gate)
    d_normed = restore(
        scatter_rows(
            matmul_right_t(dq_pre, w_query)
            + matmul_right_t(dk_pre, w_key)
            + matmul_right_t(dv_pre, w_value)
            + matmul_right_t(d_gate, w_gate)
        )
    )
    d_inputs = d_middle + normalize_back(normed, in_scale, d_normed)
    return (
        result.astype(BF)[None],
        d_inputs[None],
        column_sums(grad_query),
        column_sums(grad_key),
        column_sums(grad_value),
        column_sums(grad_gate),
        lax.psum_scatter(grad_out.astype(BF), BOTH, scatter_dimension=0, tiled=True).astype(F32),
        column_sums(grad_fval),
        column_sums(grad_fgate),
        lax.psum_scatter(grad_fout.astype(BF), "narrow", scatter_dimension=0, tiled=True).astype(
            F32
        ),
    )


MESH = pl.DeviceIdType.MESH
ANY = pl.BlockSpec(memory_space=pl.ANY)
VMEM = pl.BlockSpec(memory_space=pltpu.VMEM)
WIDE, NARROW = 8, 4
CHIPS = WIDE // 2


def dot(left, right):
    return jnp.dot(left, right, preferred_element_type=F32)


def dot_rt(left, right):
    return lax.dot_general(left, right, (((1,), (1,)), ((), ())), preferred_element_type=F32)


def dot_lt(left, right):
    return lax.dot_general(left, right, (((0,), (0,)), ((), ())), preferred_element_type=F32)


def at(start, size):
    return pl.ds(pl.multiple_of(start, size), size)


class Links:
    def __init__(self, send, recv, here):
        self.send, self.recv, self.here = send, recv, here
        self.count, self.kept = 0, 1
        w = lax.axis_index("wide")
        n = lax.axis_index("narrow")
        self.w, self.n = w, n
        self.core = lax.rem(w, 2)
        self.chip = lax.div(w, 2)
        x, y = lax.rem(self.chip, 2), lax.div(self.chip, 2)
        self.wx = w + 2 - 4 * x
        self.wy = w + 4 - 8 * y
        self.wd = w + 6 - 4 * x - 8 * y
        self.ws = w + 1 - 2 * self.core
        self.px = self.chip + 1 - 2 * x
        self.py = self.chip + 2 - 4 * y
        self.pd = 3 - self.chip
        self.mid = lax.rem(lax.div(n + 1, 2), 2)
        self.pair = n + 1 - 2 * lax.rem(n, 2)
        self.cross = 2 - lax.div(n, 2)
        self.far = 3 - 3 * lax.div(n, 2)
        self.end_to = 3 * lax.rem(n + 1, 2)
        self.end_part = lax.rem(2 * n, 3) + 3 * lax.div(n, 3)

    def greet(self):
        barrier = pltpu.get_barrier_semaphore()
        for d in range(1, WIDE):
            pl.semaphore_signal(
                barrier, inc=1, device_id=(lax.rem(self.w + d, WIDE), self.n), device_id_type=MESH
            )
        for d in range(1, NARROW):
            pl.semaphore_signal(
                barrier, inc=1, device_id=(self.w, lax.rem(self.n + d, NARROW)), device_id_type=MESH
            )

    def met(self):
        pl.semaphore_wait(pltpu.get_barrier_semaphore(), WIDE + NARROW - 2)

    def take(self, number):
        base = self.count
        self.count += number
        return base

    def remote(self, src, dst, send, recv, wide=None, narrow=None):
        return pltpu.make_async_remote_copy(
            src_ref=src,
            dst_ref=dst,
            send_sem=self.send.at[send],
            recv_sem=self.recv.at[recv],
            device_id=(self.w if wide is None else wide, self.n if narrow is None else narrow),
            device_id_type=MESH,
        )

    def arrived(self, ref, recv):
        self.remote(ref, ref, recv, recv, wide=self.ws).wait_recv()

    def keep(self, src, dst):
        copy = pltpu.make_async_copy(src, dst, self.here.at[self.kept])
        self.kept += 1
        copy.start()
        return copy


class Line:
    def __init__(self, links, part):
        self.links, self.part = links, part
        self.base = links.take(5)

    def copy(self, index):
        k, b = self.links, self.base
        which, to = (
            (k.n, k.pair),
            (k.n, k.cross),
            (k.pair, k.cross),
            (k.cross, k.pair),
            (k.far, k.pair),
        )[index]
        ref = self.part(which)
        return k.remote(ref, ref, b + index, b + which, narrow=to)

    def start(self):
        self.start_away()
        pl.when(self.links.mid == 1)(lambda: self.copy(0).start())

    def start_away(self):
        pl.when(self.links.mid == 1)(lambda: self.copy(1).start())
        pl.when(self.links.mid == 0)(lambda: self.copy(0).start())

    def start_home(self):
        pl.when(self.links.mid == 1)(lambda: self.copy(0).start())

    def wait(self, index):
        self.links.arrived(self.part(index), self.base + index)

    def forward(self):
        @pl.when(self.links.mid == 1)
        def _():
            self.wait(self.links.cross)
            self.copy(3).start()
            self.wait(self.links.pair)
            self.copy(2).start()

    def forward_far(self):
        @pl.when(self.links.mid == 1)
        def _():
            self.wait(self.links.far)
            self.copy(4).start()

    def finish(self, then=lambda place: None):
        k = self.links
        then(0)
        for place, index in enumerate((k.pair, k.cross, k.far)):
            pl.when(k.mid == 0)(lambda index=index: self.wait(index))
            then(place + 1)

    def drain(self):
        self.copy(0).wait_send()

        @pl.when(self.links.mid == 1)
        def _():
            for index in range(1, 5):
                self.copy(index).wait_send()


class Plane:
    def __init__(self, links, slot):
        self.links, self.slot = links, slot
        self.base = links.take(6)

    def copy(self, index):
        k, b = self.links, self.base
        owner, half, to = (
            (k.w, 0, k.wx),
            (k.w, 1, k.wy),
            (k.w, 1, k.wx),
            (k.w, 0, k.wy),
            (k.wx, 0, k.wy),
            (k.wy, 1, k.wx),
        )[index]
        ref = self.slot(owner, half)
        return k.remote(ref, ref, b + index, b + index, wide=to)

    def start(self):
        for index in range(4):
            self.copy(index).start()

    def forward(self):
        k, b, slot = self.links, self.base, self.slot
        k.arrived(slot(k.wx, 0), b)
        self.copy(4).start()
        k.arrived(slot(k.wy, 1), b + 1)
        self.copy(5).start()

    def finish_near(self):
        k, b, slot = self.links, self.base, self.slot
        k.arrived(slot(k.wx, 1), b + 2)
        k.arrived(slot(k.wy, 0), b + 3)

    def finish_far(self):
        k, b, slot = self.links, self.base, self.slot
        k.arrived(slot(k.wd, 0), b + 4)
        k.arrived(slot(k.wd, 1), b + 5)

    def drain(self):
        for index in range(6):
            self.copy(index).wait_send()


class Sibling:
    def __init__(self, links, block, twin, number):
        self.links, self.block, self.twin, self.number = links, block, twin, number
        self.base = links.take(number)

    def copy(self, index):
        k, b = self.links, self.base + index
        ref = self.block(index)
        return k.remote(ref, ref, b, b, wide=k.ws)

    def send(self, index):
        self.copy(index).start()

    def wait(self, index):
        self.links.arrived(self.twin(index), self.base + index)

    def drain(self):
        for index in range(self.number):
            self.copy(index).wait_send()


class Spread:
    def __init__(self, links, src, dst, peers=WIDE):
        self.links, self.src, self.dst = links, src, dst
        self.step = 1 if peers == WIDE else 2
        self.base = links.take(WIDE)

    def distances(self):
        return range(self.step, WIDE, self.step)

    def copy(self, d, to):
        k, b = self.links, self.base + d
        return k.remote(self.src(to), self.dst(k.w), b, b, wide=to)

    def start(self):
        for d in self.distances():
            self.copy(d, lax.rem(self.links.w + d, WIDE)).start()

    def finish(self):
        k = self.links
        for d in self.distances():
            k.arrived(self.dst(lax.rem(k.w + WIDE - d, WIDE)), self.base + d)

    def drain(self):
        for d in self.distances():
            self.copy(d, lax.rem(self.links.w + d, WIDE)).wait_send()


def row_scale(values):
    return lax.rsqrt(jnp.mean(values * values, axis=-1, keepdims=True) + EPS)


def row_chunks(rows, body, size=32):
    def step(r, carry):
        body(at(r * size, size))
        return carry

    lax.fori_loop(0, rows // size, step, 0)


def doc_mask(cols, rowdoc, decay, rows, block):
    tokens = decay.shape[-1]
    same = cols[rows, 0:1] == rowdoc[pl.ds(block, 1), :]
    i = lax.broadcasted_iota(jnp.int32, (tokens, tokens), 0)
    j = lax.broadcasted_iota(jnp.int32, (tokens, tokens), 1)
    return same & (i >= j)


class LineSum:
    def __init__(self, links, part, land):
        self.links, self.part, self.land = links, part, land
        self.base = links.take(5)
        self.onward = links.pair + links.mid * (links.cross - links.pair)

    def copy(self, index):
        k, b = self.links, self.base
        which, slot, to = (
            (k.far, 3 * k.mid, self.onward),
            (k.cross, 1 + 3 * k.mid, self.onward),
            (k.pair, 2 - 2 * k.mid, k.pair),
        )[index]
        return k.remote(self.part(which), self.land(slot), b + index, b + slot, narrow=to)

    def start(self):
        @pl.when(self.links.mid == 0)
        def _():
            for index in range(3):
                self.copy(index).start()

    def wait(self, slot):
        self.links.arrived(self.land(slot), self.base + slot)

    def forward(self, add):
        k = self.links

        @pl.when(k.mid == 1)
        def _():
            self.wait(0)
            add(self.part(k.far), self.land(0))
            self.copy(0).start()
            self.wait(1)
            add(self.part(k.cross), self.land(1))
            self.copy(1).start()

    def forward_near(self, add):
        k = self.links

        @pl.when(k.mid == 1)
        def _():
            self.wait(3)
            add(self.part(k.pair), self.land(3))
            self.copy(2).start()

    def finish(self, fetch, spots):
        k = self.links
        pl.when(k.mid == 0)(lambda: self.wait(0))

        @pl.when(k.mid == 1)
        def _():
            self.wait(2)
            self.wait(4)
            fetch(self.land(4), spots.at[1])

        fetch(self.land(2 * k.mid), spots.at[0])

        @pl.when(k.mid == 0)
        def _():
            spots[1] = jnp.zeros(spots.shape[1:], spots.dtype)

    def drain(self):
        for index in range(3):
            self.copy(index).wait_send()


class PlaneSum:
    def __init__(self, links, block, corner, near, half):
        self.links, self.block, self.corner, self.near, self.half = links, block, corner, near, half
        self.base = links.take(6)

    def rows(self, h):
        return pl.ds(h * self.half, self.half)

    def copy(self, index):
        k = self.links
        chip, h, land, to = (
            (k.pd, 0, self.corner.at[0], k.wx),
            (k.pd, 1, self.corner.at[1], k.wy),
            (k.px, 0, self.near.at[0, self.rows(0)], k.wx),
            (k.py, 1, self.near.at[1, self.rows(1)], k.wy),
            (k.px, 1, self.near.at[0, self.rows(1)], k.wx),
            (k.py, 0, self.near.at[1, self.rows(0)], k.wy),
        )[index]
        sem = self.base + index
        return k.remote(self.block(chip).at[self.rows(h)], land, sem, sem, wide=to)

    def send_far(self):
        self.copy(0).start()
        self.copy(1).start()

    def send_x(self):
        self.copy(2).start()

    def send_y(self):
        self.copy(3).start()

    def combine(self, add):
        k = self.links
        self.copy(1).wait_recv()
        add(self.block(k.px).at[self.rows(1)], self.corner.at[1])
        self.copy(4).start()
        self.copy(0).wait_recv()
        add(self.block(k.py).at[self.rows(0)], self.corner.at[0])
        self.copy(5).start()

    def finish(self):
        for index in range(2, 6):
            self.copy(index).wait_recv()

    def drain(self):
        for index in range(6):
            self.copy(index).wait_send()


def layer_kernel(
    x_in, wq, wk, wv, wg, wo, fv, fg, fo, dy_arg, cols_in, decay_in, rowdoc, passing,
    result_o, dx_o, gq_o, gk_o, gv_o, gg_o, go_o, gfv_o, gfg_o, gfo_o,
    xn_in, wqk_in, wvg_in, wo_in, fv_in, fg_in, fo_in, dy_in, slope_in, qkv_in, sin_in, attn_in,
    gate_in, mixed_in, x1_in, x1n_in,
    corner, near, twin_fo_land, twin_ff, twin_wo, twin_xn_land, land_fo, land_ff, land_wo, land_qk,
    turn_ff, turn_qk, a_land, g_land,
    g_fo, g_fv, g_fg, stage, acc, tmp, tmp_ff,
    send, recv, here,
):
    k = Links(send, recv, here)
    w, n, core, chip = k.w, k.n, k.core, k.chip
    other = 1 - core
    tok, width = acc.shape
    ff = g_fv.shape[-1]
    fo_rows = land_fo.shape[1]
    half = tok // 2
    two = 2 * HEAD
    order = (k.pd, k.px, k.py, chip)

    def nth(j):
        flip_x, flip_y = 1 - lax.div(j, 2), 1 - lax.rem(j, 2)
        return (
            chip + flip_x * (1 - 2 * lax.rem(chip, 2)) + flip_y * (2 - 4 * lax.div(chip, 2))
        )

    def fetch(src, dst):
        copy = pltpu.make_async_copy(src, dst, here.at[0])
        copy.start()
        copy.wait()

    def adder(spot):
        def add(to, land):
            fetch(land, spot)
            to[...] = (to[...].astype(F32) + spot[...].astype(F32)).astype(BF)

        return add

    add_half = adder(tmp.at[pl.ds(0, half)])
    add_fo = adder(tmp.at[pl.ds(0, fo_rows)])
    add_wo = adder(tmp.at[pl.ds(0, 64)])
    add_ff = adder(tmp_ff)
    def fo_part(owner, i):
        return g_fo.at[pl.ds(pl.multiple_of((owner * NARROW + i) * fo_rows, 16), fo_rows)]

    sum_fo = LineSum(k, lambda i: fo_part(core, i), lambda s: land_fo.at[s])
    sum_ff = [
        LineSum(k, lambda i, g=g: g.at[:, i], lambda s, m=m: land_ff.at[m, s])
        for m, g in enumerate((g_fv, g_fg))
    ]
    def plane_sum(m, blocks):
        return PlaneSum(k, lambda q: blocks.at[q], corner.at[m], near.at[m], half)

    plane_mid, plane_res, plane_in = (plane_sum(m, stage) for m in (0, 1, 3))
    twin_base = k.take(4 * 5)

    def twin(m, j, src, dst):
        sem = twin_base + 4 * m + j
        return k.remote(src, dst, sem, sem, wide=k.ws)

    def wide_cols(index):
        return at(index * two, two)

    def chip_cols(index):
        return pl.ds(pl.multiple_of(index * ff, 128), ff)

    projections = ((wq, wqk_in), (wk, wqk_in), (wv, wvg_in), (wg, wvg_in))
    lines = line_out, line_qk, line_vg, line_fv, line_fg, line_fo = (
        Line(k, lambda i: wo_in.at[w, i]),
        Line(k, lambda i: wqk_in.at[:, i]),
        Line(k, lambda i: wvg_in.at[:, i]),
        Line(k, lambda i: fv_in.at[:, core, i]),
        Line(k, lambda i: fg_in.at[:, core, i]),
        Line(k, lambda i: fo_in.at[core, i]),
    )
    spreads = [
        Spread(
            k,
            lambda t, weight=weight: weight.at[:, wide_cols(t)],
            lambda s, m=m, to=to: to.at[s, n, :, pl.ds((m % 2) * two, two)],
        )
        for m, (weight, to) in enumerate(projections)
    ]
    spread_ff = [
        Spread(
            k,
            lambda t, weight=weight: weight.at[:, chip_cols(lax.div(t, 2))],
            lambda s, to=to: to.at[lax.div(s, 2), core, n],
            peers=CHIPS,
        )
        for weight, to in ((fv, fv_in), (fg, fg_in))
    ]
    planes = plane_xn, plane_out, plane_dy, plane_x1n = (
        Plane(k, lambda s, h: xn_in.at[s, pl.ds(h * half, half)]),
        Plane(k, lambda s, h: wo_in.at[s, pl.ds(h * 2, 2)]),
        Plane(k, lambda s, h: dy_in.at[lax.div(s, 2), pl.ds(h * half, half)]),
        Plane(k, lambda s, h: x1n_in.at[lax.div(s, 2), pl.ds(h * half, half)]),
    )
    here4 = (w, k.wx, k.wy, k.wd)
    there4 = tuple(s + 1 - 2 * core for s in here4)
    near4 = (n, k.pair, k.cross, k.far)
    twins = twin_xn, twin_out, twin_fv, twin_fg, twin_fo = (
        Sibling(k, lambda i: xn_in.at[here4[i]], lambda i: xn_in.at[there4[i]], 4),
        Sibling(k, lambda i: wo_in.at[here4[i]], lambda i: wo_in.at[there4[i]], 4),
        Sibling(k, lambda i: fv_in.at[:, core, near4[i]], lambda i: fv_in.at[:, other, near4[i]], 4),
        Sibling(k, lambda i: fg_in.at[:, core, near4[i]], lambda i: fg_in.at[:, other, near4[i]], 4),
        Sibling(k, lambda i: fo_in.at[core, near4[i]], lambda i: fo_in.at[other, near4[i]], 4),
    )

    k.greet()
    own_out = k.keep(wo, wo_in.at[w, n])
    own_in = [
        k.keep(weight.at[:, wide_cols(w)], to.at[w, n, :, pl.ds((m % 2) * two, two)])
        for m, (weight, to) in enumerate(projections)
    ]
    own_ff = [
        k.keep(fv.at[:, chip_cols(chip)], fv_in.at[chip, core, n]),
        k.keep(fg.at[:, chip_cols(chip)], fg_in.at[chip, core, n]),
        k.keep(fo, fo_in.at[core, n]),
        k.keep(dy_arg, dy_in.at[chip]),
    ]

    def before(
        x, xn, wqk, wvg, wout, slope, qkv, gates, sin, state, attn_s, attn, gate, mixed, x1, x1n,
        cols, decay,
    ):
        k.keep(x_in, x).wait()

        def norm_in(rows):
            v = x[rows, :].astype(F32)
            x1n[rows, :] = (v * row_scale(v)).astype(BF)

        row_chunks(tok, norm_in)
        own_xn = k.keep(x1n, xn_in.at[w])
        load_cols, load_decay = k.keep(cols_in, cols), k.keep(decay_in, decay)
        k.met()
        own_out.wait()
        line_out.start()
        for spread in spreads:
            spread.start()
        own_xn.wait()
        plane_xn.start()
        twin_xn.send(0)
        for spread in spread_ff:
            spread.start()
        for copy in own_in:
            copy.wait()
        spreads[0].finish()
        spreads[1].finish()
        line_qk.start()
        spreads[2].finish()
        spreads[3].finish()
        line_vg.start()
        line_out.forward()
        plane_xn.forward()
        line_out.forward_far()
        line_qk.forward()
        plane_xn.finish_near()
        twin_xn.send(1)
        twin_xn.send(2)
        line_vg.forward()
        line_qk.forward_far()
        line_out.finish()
        plane_out.start()
        twin_out.send(0)
        plane_xn.finish_far()
        twin_xn.send(3)
        line_vg.forward_far()
        spread_ff[0].finish()
        spread_ff[1].finish()
        for copy in own_ff:
            copy.wait()
        line_fv.start()
        for i in range(4):
            twin_xn.wait(i)
        load_xn = k.keep(xn_in, xn)
        plane_out.forward()
        line_qk.finish()
        load_qk = k.keep(wqk_in, wqk)
        load_xn.wait()
        load_qk.wait()

        def project_qk(t, carry):
            v = dot(xn[t], wqk[...].reshape(width, 2 * two))
            rows = at(t * tok, tok)
            sigma = jax.nn.sigmoid(v)
            slope[rows, :] = (sigma * (1.0 + v * (1.0 - sigma))).astype(BF)
            qkv[rows, 0 : 2 * two] = (v * sigma).astype(BF)
            return carry

        lax.fori_loop(0, WIDE, project_qk, 0)
        stores = [k.keep(slope, slope_in)]
        plane_out.finish_near()
        twin_out.send(1)
        twin_out.send(2)
        line_vg.finish()
        k.keep(wvg_in, wvg).wait()

        def project_vg(t, carry):
            v = dot(xn[t], wvg[...].reshape(width, 2 * two)).astype(BF)
            qkv[at(t * tok, tok), 2 * two : 3 * two] = v[:, 0:two]
            gates[t] = v[:, two:]
            return carry

        lax.fori_loop(0, WIDE, project_vg, 0)
        line_fv.forward()
        line_fg.start()
        stores.append(k.keep(qkv, qkv_in))
        spread_gate = Spread(k, lambda t: gates.at[t], lambda s: gate_in.at[:, wide_cols(s)])
        spread_gate.start()
        own = [k.keep(gates.at[w], gate_in.at[:, wide_cols(w)])]
        load_cols.wait()
        load_decay.wait()
        state[...] = jnp.zeros_like(state)
        spread_attn = Spread(k, lambda t: attn_s.at[t], lambda s: attn_in.at[:, wide_cols(s)])

        def attend(b, carry):
            rows = at(b * BLOCK, BLOCK)
            mask = doc_mask(cols, rowdoc, decay, rows, b)
            for h in range(2):
                lanes = slice(h * HEAD, (h + 1) * HEAD)
                q = qkv[rows, lanes]
                key = qkv[rows, two + h * HEAD : two + (h + 1) * HEAD]
                v = qkv[rows, 2 * two + h * HEAD : 2 * two + (h + 1) * HEAD]
                probs = jnp.where(mask, dot_rt(q, key) * decay[h], 0.0).astype(BF)
                old = state[h]
                old_bf = old.astype(BF)
                sin[b, h] = old_bf
                entry = cols[rows, 1 + h : 2 + h]
                tail = cols[rows, 3 + h : 4 + h]
                out = dot(probs, v) + entry * dot(q, old_bf)
                attn_s[b, :, lanes] = out.astype(BF)
                tailed = (key.astype(F32) * tail).astype(BF)
                state[h] = passing[pl.ds(2 * b + h, 1), :] * old + dot_lt(tailed, v)

            @pl.when(b != w)
            def _():
                spread_attn.copy(lax.rem(b - w + WIDE, WIDE), b).start()

            return carry

        lax.fori_loop(0, WIDE, attend, 0)
        stores.append(k.keep(sin, sin_in))
        own.append(k.keep(attn_s.at[w], attn_in.at[:, wide_cols(w)]))
        plane_out.finish_far()
        twin_out.send(3)
        for i in range(4):
            twin_out.wait(i)
        load_out = k.keep(wo_in, wout)
        line_fv.forward_far()
        spread_gate.finish()
        spread_attn.finish()
        for copy in own:
            copy.wait()
        loads = [k.keep(attn_in, attn), k.keep(gate_in, gate)]
        for copy in loads:
            copy.wait()

        def mix(rows):
            a = attn[rows, :].astype(F32)
            mixed[rows, :] = (a * row_scale(a) * gate[rows, :].astype(F32)).astype(BF)

        row_chunks(tok, mix)
        stores.append(k.keep(mixed, mixed_in))
        load_out.wait()

        def project_out(j, carry):
            lanes = at(j * 512, 512)
            part = dot(mixed[...], wout[:, :, :, lanes].reshape(-1, 512))
            x1[:, lanes] = x[:, lanes].astype(F32) + part
            return carry

        lax.fori_loop(0, width // 512, project_out, 0)
        stores.append(k.keep(x1, x1_in))

        def norm_mid(rows):
            v = x1[rows, :]
            x1n[rows, :] = (v * row_scale(v)).astype(BF)

        row_chunks(tok, norm_mid)
        k.keep(x1n, x1n_in.at[chip]).wait()
        plane_x1n.start()
        line_fg.forward()
        line_fo.start_away()
        plane_x1n.forward()
        plane_dy.start()
        line_fg.forward_far()
        for copy in stores:
            copy.wait()
        spread_gate.drain()
        spread_attn.drain()

    pl.run_scoped(
        before,
        pltpu.VMEM((tok, width), BF),
        pltpu.VMEM((WIDE, tok, width), BF),
        pltpu.VMEM(wqk_in.shape, BF),
        pltpu.VMEM(wvg_in.shape, BF),
        pltpu.VMEM(wo_in.shape, BF),
        pltpu.VMEM(slope_in.shape, BF),
        pltpu.VMEM(qkv_in.shape, BF),
        pltpu.VMEM((WIDE, tok, two), BF),
        pltpu.VMEM(sin_in.shape, BF),
        pltpu.VMEM((2, HEAD, HEAD), F32),
        pltpu.VMEM((WIDE, tok, two), BF),
        pltpu.VMEM((tok, width), BF),
        pltpu.VMEM((tok, width), BF),
        pltpu.VMEM((tok, width), BF),
        pltpu.VMEM((tok, width), F32),
        pltpu.VMEM((tok, width), BF),
        pltpu.VMEM(cols_in.shape, F32),
        pltpu.VMEM(decay_in.shape, F32),
    )

    def ffn(x1n, dy, fvw, fgw, fow, mix, val, gat, side):
        line_fv.finish(twin_fv.send)
        plane_x1n.finish_near()
        plane_x1n.finish_far()
        load_x1n = k.keep(x1n_in, x1n)
        for i in range(4):
            twin_fv.wait(i)
        load_fv = k.keep(fv_in, fvw)
        line_fo.forward()
        line_fg.finish(twin_fg.send)
        line_fo.start_home()
        for i in range(4):
            twin_fg.wait(i)
        load_fg = k.keep(fg_in, fgw)
        plane_dy.forward()
        for copy in (load_x1n, load_fv, load_fg):
            copy.wait()

        def up(j, carry):
            v = dot(x1n[j], fvw[...].reshape(width, ff))
            g = dot(x1n[j], fgw[...].reshape(width, ff))
            mix[j] = (v * g).astype(BF)
            val[j] = v.astype(BF)
            gat[j] = g.astype(BF)
            return carry

        lax.fori_loop(0, CHIPS // 2, up, 0)
        line_fo.forward_far()
        plane_dy.finish_near()
        plane_dy.finish_far()
        load_dy = k.keep(dy_in, dy)
        lax.fori_loop(CHIPS // 2, CHIPS, up, 0)
        load_dy.wait()

        def fo_grad(j, carry):
            chunk = lax.rem(j + 2 * other, chunks)
            rows = pl.ds(pl.multiple_of(jnp.minimum(chunk * 256, ff - 256), 128), 256)
            left = mix[:, :, rows].reshape(CHIPS * tok, 256)
            for h in range(2):
                lanes = slice(h * width // 2, (h + 1) * width // 2)
                right = dy[:, :, lanes].reshape(CHIPS * tok, -1)
                g_fo[rows, lanes] = dot_lt(left, right).astype(BF)
            return carry

        chunks = pl.cdiv(ff, 256)
        lax.fori_loop(0, 4, fo_grad, 0)
        for i in range(NARROW):
            twin(0, i, fo_part(other, i), twin_fo_land.at[i]).start()
        lax.fori_loop(4, chunks, fo_grad, 0)
        for i in range(NARROW):
            copy = twin(0, i, fo_part(other, i), twin_fo_land.at[i])
            copy.wait_recv()
            add_fo(fo_part(core, i), twin_fo_land.at[i])
            copy.wait_send()
        sum_fo.start()
        line_fo.finish(twin_fo.send)
        for i in range(4):
            twin_fo.wait(i)
        k.keep(fo_in, fow).wait()

        def down(q, carry):
            d_mix = dot_rt(dy[q], fow[...].reshape(ff, width))
            d_val = (d_mix * gat[q].astype(F32)).astype(BF)
            d_gat = (d_mix * val[q].astype(F32)).astype(BF)
            val[q] = d_val
            gat[q] = d_gat
            return carry

        lax.fori_loop(0, CHIPS, down, 0)

        def back(j, carry):
            q = nth(j)

            def back_lanes(i, carry):
                lanes = at(i * 512, 512)
                d_x = dot_rt(val[q], fvw[i].reshape(512, ff)) + dot_rt(
                    gat[q], fgw[i].reshape(512, ff)
                )
                stage[q, :, lanes] = d_x.astype(BF)

                @pl.when(j == 3)
                def _():
                    acc[:, lanes] = d_x

                return carry

            lax.fori_loop(0, width // 512, back_lanes, 0)
            for step, push in enumerate((plane_mid.send_far, plane_mid.send_x, plane_mid.send_y)):
                pl.when(j == step)(push)
            return carry

        for m, (d_ff, g_ff) in enumerate(((val, g_fv), (gat, g_fg))):

            def ff_grad(owner):
                left = x1n[:, :, at(owner * tok, tok)].reshape(CHIPS * tok, tok)
                g = dot_lt(left, d_ff[...].reshape(CHIPS * tok, ff)).astype(BF)
                return g.reshape(NARROW, -1, ff)

            def side_step(q, carry):
                slot = lax.rem(q, 2)

                @pl.when(q >= 2)
                def _():
                    twin(1 + m, q - 2, side.at[slot], twin_ff.at[m, q]).wait_send()

                side[slot] = ff_grad(2 * q + other)
                twin(1 + m, q, side.at[slot], twin_ff.at[m, q]).start()
                return carry

            def own_step(q, carry):
                g_ff[q] = ff_grad(2 * q + core)
                return carry

            lax.fori_loop(0, CHIPS, side_step, 0)
            lax.fori_loop(0, CHIPS, own_step, 0)
            for q in range(CHIPS):
                copy = twin(1 + m, q, side.at[q % 2], twin_ff.at[m, q])
                copy.wait_recv()
                add_ff(g_ff.at[q], twin_ff.at[m, q])
                if q >= 2:
                    copy.wait_send()
            sum_ff[m].start()
            if m == 0:
                lax.fori_loop(0, CHIPS, back, 0)
                plane_mid.combine(add_half)
                sum_fo.forward(add_fo)

        sum_fo.forward_near(add_fo)
        plane_mid.drain()

        def out_step(j, carry):
            q = nth(j)
            stage[q] = dot(mix[q], fow[...].reshape(ff, width)).astype(BF)
            return carry

        lax.fori_loop(0, CHIPS, out_step, 0)

    pl.run_scoped(
        ffn,
        pltpu.VMEM((CHIPS, tok, width), BF),
        pltpu.VMEM((CHIPS, tok, width), BF),
        pltpu.VMEM(fv_in.shape, BF),
        pltpu.VMEM(fg_in.shape, BF),
        pltpu.VMEM(fo_in.shape, BF),
        pltpu.VMEM((CHIPS, tok, ff), BF),
        pltpu.VMEM((CHIPS, tok, ff), BF),
        pltpu.VMEM((CHIPS, tok, ff), BF),
        pltpu.VMEM((2, *g_fv.shape[1:]), BF),
    )

    def rest(d_x1, d_branch, mixed, da_src, dg_src, side, stage_wo, own_res, g_wo, g_qk, g_vg):
        plane_out = plane_sum(2, stage_wo)
        own_res[...] = stage[chip]
        sum_wo = LineSum(k, lambda i: g_wo.at[i], lambda s: land_wo.at[s])
        sum_qk = [
            LineSum(k, lambda i, g=g: g.at[:, i], lambda s, m=m: land_qk.at[m, s])
            for m, g in enumerate((g_qk, g_vg))
        ]
        spread_a = Spread(
            k, lambda t: da_src.at[:, at(t * two, two)], lambda s: a_land.at[s]
        )
        spread_g = Spread(
            k, lambda t: dg_src.at[:, at(t * two, two)], lambda s: g_land.at[at(s * tok, tok)]
        )

        def middle(wo, x1, attn, gate, dy, d_mixed, pair):
            plane_mid.finish()
            loads = [k.keep(near.at[0], pair), k.keep(x1_in, x1), k.keep(dy_in.at[chip], dy)]
            late = [
                k.keep(wo_in, wo), k.keep(attn_in, attn), k.keep(gate_in, gate),
                k.keep(mixed_in, mixed),
            ]
            for copy in loads:
                copy.wait()

            def norm_back(rows):
                g = acc[rows, :] + pair[0, rows, :].astype(F32) + pair[1, rows, :].astype(F32)
                v = x1[rows, :]
                r = row_scale(v)
                u = v * r
                d = dy[rows, :].astype(F32) + r * (g - u * jnp.mean(g * u, axis=-1, keepdims=True))
                d_x1[rows, :] = d
                d_branch[rows, :] = d.astype(BF)

            row_chunks(tok, norm_back)
            for copy in late:
                copy.wait()

            def mixed_step(j, carry):
                d_mixed[:, at(j * 512, 512)] = dot_rt(
                    d_branch[...], wo[pl.ds(2 * j, 2)].reshape(512, width)
                )
                return carry

            lax.fori_loop(0, width // 512, mixed_step, 0)

            def attn_back(rows):
                a = attn[rows, :].astype(F32)
                s = row_scale(a)
                u = a * s
                d = d_mixed[rows, :]
                dg_src[rows, :] = (d * u).astype(BF)
                g = d * gate[rows, :].astype(F32)
                da_src[rows, :] = (
                    s * (g - u * jnp.mean(g * u, axis=-1, keepdims=True))
                ).astype(BF)

            row_chunks(tok, attn_back)
            spread_a.start()
            spread_g.start()
            plane_res.send_far()
            plane_res.send_x()
            plane_res.send_y()
            own = [
                k.keep(da_src.at[:, at(w * two, two)], a_land.at[w]),
                k.keep(dg_src.at[:, at(w * two, two)], g_land.at[at(w * tok, tok)]),
            ]

            for copy in own:
                copy.wait()

        pl.run_scoped(
            middle,
            pltpu.VMEM(wo_in.shape, BF),
            pltpu.VMEM((tok, width), F32),
            pltpu.VMEM((tok, width), BF),
            pltpu.VMEM((tok, width), BF),
            pltpu.VMEM((tok, width), BF),
            pltpu.VMEM((tok, width), F32),
            pltpu.VMEM((2, tok, width), BF),
        )
        def eight_way(plane, twin_index, landing, blocks, term):
            def side_step(j, carry):
                q = nth(j)
                side[q] = term(2 * q + other).astype(BF)
                twin(twin_index, j, side.at[q], landing.at[q]).start()
                return carry

            lax.fori_loop(0, CHIPS, side_step, 0)

            def own_step(j, carry):
                q = nth(j)
                v = term(2 * q + core)
                twin(twin_index, j, side.at[q], landing.at[q]).wait_recv()
                fetch(landing.at[q], tmp)
                v = v + tmp[...].astype(F32)

                @pl.when(j < 3)
                def _():
                    blocks[q] = v.astype(BF)

                for step, push in enumerate((plane.send_far, plane.send_x, plane.send_y)):
                    pl.when(j == step)(push)

                @pl.when(j == 3)
                def _():
                    acc[...] = v

                return carry

            lax.fori_loop(0, CHIPS, own_step, 0)
            for j in range(CHIPS):
                twin(twin_index, j, side.at[order[j]], landing.at[order[j]]).wait_send()

        eight_way(
            plane_out,
            3,
            twin_wo,
            stage_wo,
            lambda owner: dot_lt(mixed[:, at(owner * tok, tok)], d_branch[...]),
        )
        sum_ff[0].forward(add_ff)

        def attention(xn, d_qk, d_vg, state):
            state[...] = jnp.zeros_like(state)

            def heads(slope, qkv, sin, cols, decay, d_attn):
                loads = [
                    k.keep(qkv_in, qkv), k.keep(sin_in, sin), k.keep(slope_in, slope),
                    k.keep(cols_in, cols), k.keep(decay_in, decay),
                ]
                load_xn = k.keep(xn_in, xn)
                for copy in loads:
                    copy.wait()
                spread_a.finish()
                fetch(a_land, d_attn)

                def step(i, carry):
                    b = WIDE - 1 - i
                    rows = at(b * BLOCK, BLOCK)
                    mask = doc_mask(cols, rowdoc, decay, rows, b)
                    for h in range(2):
                        lanes = slice(h * HEAD, (h + 1) * HEAD)
                        key_lanes = slice(two + h * HEAD, two + (h + 1) * HEAD)
                        q = qkv[rows, lanes]
                        key = qkv[rows, key_lanes]
                        v = qkv[rows, 2 * two + h * HEAD : 2 * two + (h + 1) * HEAD]
                        d_o = d_attn[b, :, lanes]
                        factor = jnp.where(mask, decay[h], 0.0)
                        probs = (dot_rt(q, key) * factor).astype(BF)
                        d_probs = (dot_rt(d_o, v) * factor).astype(BF)
                        entry = cols[rows, 1 + h : 2 + h]
                        tail = cols[rows, 3 + h : 4 + h]
                        before = sin[b, h]
                        after = state[h]
                        after_bf = after.astype(BF)
                        tailed = (key.astype(F32) * tail).astype(BF)
                        entered = (q.astype(F32) * entry).astype(BF)
                        d_q = dot(d_probs, key) + entry * dot_rt(d_o, before)
                        d_k = dot_lt(d_probs, q) + tail * dot_rt(v, after_bf)
                        d_v = dot_lt(probs, d_o) + dot(tailed, after_bf)
                        d_qk[rows, lanes] = (d_q * slope[rows, lanes].astype(F32)).astype(BF)
                        d_qk[rows, key_lanes] = (d_k * slope[rows, key_lanes].astype(F32)).astype(BF)
                        d_vg[rows, lanes] = d_v.astype(BF)
                        state[h] = passing[pl.ds(2 * b + h, 1), :] * after + dot_lt(entered, d_o)
                    return carry

                lax.fori_loop(0, WIDE, step, 0)
                sum_ff[0].forward_near(add_ff)
                spread_g.finish()
                load_g = k.keep(g_land, d_vg.at[:, pl.ds(two, two)])
                load_g.wait()
                load_xn.wait()

            pl.run_scoped(
                heads,
                pltpu.VMEM(slope_in.shape, BF),
                pltpu.VMEM(qkv_in.shape, BF),
                pltpu.VMEM(sin_in.shape, BF),
                pltpu.VMEM(cols_in.shape, F32),
                pltpu.VMEM(decay_in.shape, F32),
                pltpu.VMEM((WIDE, tok, two), BF),
            )

            for m, (d_in, g_in) in enumerate(((d_qk, g_qk), (d_vg, g_vg))):

                def in_grad(s, carry):
                    left = xn[:, :, at(s * tok, tok)].reshape(WIDE * tok, tok)
                    g_in[s] = dot_lt(left, d_in[...]).astype(BF).reshape(NARROW, -1, 2 * two)
                    return carry

                lax.fori_loop(0, WIDE, in_grad, 0)
                sum_qk[m].start()

            plane_res.combine(add_half)
            plane_out.combine(add_half)
            sum_ff[1].forward(add_ff)
            plane_res.drain()
            g_wo[...] = acc[...].astype(BF).reshape(g_wo.shape)

            def spread_in(wqk, wvg):
                loads = [k.keep(wqk_in, wqk), k.keep(wvg_in, wvg)]
                for copy in loads:
                    copy.wait()

                def term(owner):
                    rows = at(owner * tok, tok)
                    return dot_rt(d_qk[rows, :], wqk[...].reshape(width, 2 * two)) + dot_rt(
                        d_vg[rows, :], wvg[...].reshape(width, 2 * two)
                    )

                eight_way(plane_in, 4, twin_xn_land, stage, term)

            pl.run_scoped(spread_in, pltpu.VMEM(wqk_in.shape, BF), pltpu.VMEM(wvg_in.shape, BF))

        pl.run_scoped(
            attention,
            pltpu.VMEM((WIDE, tok, width), BF),
            pltpu.VMEM((WIDE * tok, 2 * two), BF),
            pltpu.VMEM((WIDE * tok, 2 * two), BF),
            pltpu.VMEM((2, HEAD, HEAD), F32),
        )

        def last(
            x, x1, pair, three, three_ff, three_qk, ff_src, qk_src, ff_all, qk_all, ff_f32, w_f32, w_fo, tmp_qk
        ):
            add_qk = adder(tmp_qk)
            load_x, load_x1 = k.keep(x_in, x), k.keep(x1_in, x1)
            plane_in.combine(add_half)
            sum_ff[1].forward_near(add_ff)
            plane_out.finish()
            fetch(near.at[2], pair)
            for i in range(NARROW):
                rows = pl.ds(i * 64, 64)
                v = g_wo[i].astype(F32) + pair[0, rows, :].astype(F32) + pair[1, rows, :].astype(F32)
                g_wo[i] = v.astype(BF)
            sum_wo.start()

            def total(part, lands):
                return part.astype(F32) + lands[0].astype(F32) + lands[1].astype(F32)

            ff_turns = []
            for m, g_ff in enumerate((g_fv, g_fg)):
                sum_ff[m].finish(fetch, three_ff)
                for q in range(CHIPS):
                    ff_src[m, q] = total(g_ff[q, n], three_ff[:, q]).astype(BF)
                turn = Spread(
                    k,
                    lambda t, m=m: ff_src.at[m, lax.div(t, 2)],
                    lambda s, m=m: turn_ff.at[m, lax.div(s, 2)],
                    peers=CHIPS,
                )
                turn.start()
                ff_turns.append((turn, k.keep(ff_src.at[m, chip], turn_ff.at[m, chip])))
            sum_qk[0].forward(add_qk)
            sum_fo.finish(fetch, three.at[:, pl.ds(0, fo_rows)])
            own = fo_part(core, n)
            for r in range(0, fo_rows, 16):
                rows = pl.ds(r, 16)
                w_fo[rows, :] = total(own[rows, :], three[:, rows, :])
            stores = [k.keep(w_fo, gfo_o)]

            plane_res.finish()
            fetch(near.at[1], pair)
            load_x1.wait()

            def add_up(rows):
                v = x1[rows, :] + own_res[rows, :].astype(F32)
                v = v + pair[0, rows, :].astype(F32) + pair[1, rows, :].astype(F32)
                own_res[rows, :] = v.astype(BF)

            row_chunks(tok, add_up)
            stores.append(k.keep(own_res, result_o))
            sum_qk[1].forward(add_qk)
            sum_qk[0].forward_near(add_qk)
            load_x.wait()
            plane_in.finish()
            fetch(near.at[3], pair)

            def input_back(rows):
                g = acc[rows, :] + pair[0, rows, :].astype(F32) + pair[1, rows, :].astype(F32)
                v = x[rows, :].astype(F32)
                r = row_scale(v)
                u = v * r
                d_x1[rows, :] = d_x1[rows, :] + r * (
                    g - u * jnp.mean(g * u, axis=-1, keepdims=True)
                )

            row_chunks(tok, input_back)
            stores.append(k.keep(d_x1, dx_o))
            for m, (turn, copy) in enumerate(ff_turns):
                turn.finish()
                copy.wait()
                fetch(turn_ff.at[m], ff_all)
                for q in range(CHIPS):
                    ff_f32[m, :, q * ff : (q + 1) * ff] = ff_all[q].astype(F32)
                stores.append(k.keep(ff_f32.at[m], (gfv_o, gfg_o)[m]))
            sum_wo.forward(add_wo)
            sum_qk[1].forward_near(add_qk)
            qk_turns = []
            for m, g_in in enumerate((g_qk, g_vg)):
                sum_qk[m].finish(fetch, three_qk)
                for s in range(WIDE):
                    qk_src[m, s] = total(g_in[s, n], three_qk[:, s]).astype(BF)
                turn = Spread(
                    k,
                    lambda t, m=m: qk_src.at[m, t],
                    lambda s, m=m: turn_qk.at[m, s],
                )
                turn.start()
                qk_turns.append((turn, k.keep(qk_src.at[m, w], turn_qk.at[m, w])))
                if m == 0:
                    sum_wo.forward_near(add_wo)
            sum_wo.finish(fetch, three.at[:, pl.ds(0, 64)])
            w_f32[4] = total(g_wo[n], three[:, 0:64, :])
            stores.append(k.keep(w_f32.at[4], go_o))
            for m, (turn, copy) in enumerate(qk_turns):
                turn.finish()
                copy.wait()
                fetch(turn_qk.at[m], qk_all)
                for s in range(WIDE):
                    lanes = slice(s * two, (s + 1) * two)
                    w_f32[2 * m, :, lanes] = qk_all[s, :, 0:two].astype(F32)
                    w_f32[2 * m + 1, :, lanes] = qk_all[s, :, two:].astype(F32)
                outs = ((gq_o, gk_o), (gv_o, gg_o))[m]
                stores.append(k.keep(w_f32.at[2 * m], outs[0]))
                stores.append(k.keep(w_f32.at[2 * m + 1], outs[1]))
            for copy in stores:
                copy.wait()
            plane_in.drain()
            plane_out.drain()
            turns = [turn for turn, copy in ff_turns + qk_turns]
            for moved in (*lines, *planes, *twins, *spreads, *spread_ff):
                moved.drain()
            for sums in (sum_fo, sum_wo, *sum_ff, *sum_qk, spread_a, spread_g, *turns):
                sums.drain()

        pl.run_scoped(
            last,
            pltpu.VMEM((tok, width), BF),
            pltpu.VMEM((tok, width), F32),
            pltpu.VMEM((2, tok, width), BF),
            pltpu.VMEM((2, tok, width), BF),
            pltpu.VMEM((2, *land_ff.shape[2:]), BF),
            pltpu.VMEM((2, *land_qk.shape[2:]), BF),
            pltpu.VMEM((2, CHIPS, 64, ff), BF),
            pltpu.VMEM((2, WIDE, 64, 2 * two), BF),
            pltpu.VMEM((CHIPS, 64, ff), BF),
            pltpu.VMEM((WIDE, 64, 2 * two), BF),
            pltpu.VMEM((2, 64, CHIPS * ff), F32),
            pltpu.VMEM((5, 64, width), F32),
            pltpu.VMEM((fo_rows, width), F32),
            pltpu.VMEM((WIDE, 64, 2 * two), BF),
        )

    pl.run_scoped(
        rest,
        pltpu.VMEM((tok, width), F32),
        pltpu.VMEM((tok, width), BF),
        pltpu.VMEM((tok, width), BF),
        pltpu.VMEM((tok, width), BF),
        pltpu.VMEM((tok, width), BF),
        pltpu.VMEM((CHIPS, tok, width), BF),
        pltpu.VMEM((CHIPS, tok, width), BF),
        pltpu.VMEM((tok, width), BF),
        pltpu.VMEM((NARROW, 64, width), BF),
        pltpu.VMEM((WIDE, NARROW, 64, 2 * two), BF),
        pltpu.VMEM((WIDE, NARROW, 64, 2 * two), BF),
    )
    assert k.count <= send.shape[0] and k.kept <= here.shape[0], (k.count, k.kept)


def layer(tokens, weights, dy, cols, rowdoc, passing, decay):
    tok, width = tokens.shape
    shard = weights[0].shape[0]
    ff = weights[5].shape[1] // CHIPS
    fo_rows = weights[7].shape[0]
    full = WIDE * tok
    two = 2 * HEAD

    def arr(*shape, dtype=BF):
        return jax.ShapeDtypeStruct(shape, dtype)

    results = (
        arr(tok, width),
        arr(tok, width, dtype=F32),
        *[arr(shard, width, dtype=F32)] * 5,
        arr(shard, CHIPS * ff, dtype=F32),
        arr(shard, CHIPS * ff, dtype=F32),
        arr(fo_rows, width, dtype=F32),
    )
    held = (
        arr(WIDE, tok, width),
        arr(WIDE, NARROW, shard, 2 * two),
        arr(WIDE, NARROW, shard, 2 * two),
        arr(WIDE, NARROW, shard, width),
        arr(CHIPS, 2, NARROW, shard, ff),
        arr(CHIPS, 2, NARROW, shard, ff),
        arr(2, NARROW, fo_rows, width),
        arr(CHIPS, tok, width),
        arr(full, 2 * two),
        arr(full, 3 * two),
        arr(WIDE, 2, HEAD, HEAD),
        arr(tok, width),
        arr(tok, width),
        arr(tok, width),
        arr(tok, width, dtype=F32),
        arr(CHIPS, tok, width),
    )
    landings = (
        arr(4, 2, tok // 2, width),
        arr(4, 2, tok, width),
        arr(NARROW, fo_rows, width),
        arr(2, CHIPS, NARROW, shard, ff),
        arr(CHIPS, tok, width),
        arr(CHIPS, tok, width),
        arr(5, fo_rows, width),
        arr(2, 5, CHIPS, shard, ff),
        arr(5, shard, width),
        arr(2, 5, WIDE, shard, 2 * two),
        arr(2, CHIPS, shard, ff),
        arr(2, WIDE, shard, 2 * two),
        arr(WIDE, tok, two),
        arr(full, two),
    )
    out_shape = results + held + landings
    outs = pl.pallas_call(
        layer_kernel,
        out_shape=out_shape,
        in_specs=[ANY] * 12 + [VMEM] * 2,
        out_specs=(ANY,) * len(out_shape),
        scratch_shapes=[
            pltpu.VMEM((ff, width), BF),
            pltpu.VMEM((CHIPS, NARROW, shard, ff), BF),
            pltpu.VMEM((CHIPS, NARROW, shard, ff), BF),
            pltpu.VMEM((CHIPS, tok, width), BF),
            pltpu.VMEM((tok, width), F32),
            pltpu.VMEM((tok, width), BF),
            pltpu.VMEM((CHIPS, shard, ff), BF),
            pltpu.SemaphoreType.DMA((272,)),
            pltpu.SemaphoreType.DMA((272,)),
            pltpu.SemaphoreType.DMA((80,)),
        ],
        compiler_params=pltpu.CompilerParams(
            collective_id=0, has_side_effects=True, vmem_limit_bytes=63 * 2**20
        ),
        cost_estimate=pl.CostEstimate(flops=8 * 10**10, bytes_accessed=3 * 10**8, transcendentals=0),
    )(tokens, *weights, dy, cols, decay, rowdoc, passing)
    return outs[: len(results)]


def prepare(doc_starts, length):
    starts = lax.dynamic_slice_in_dim(doc_starts, lax.axis_index("narrow"), 1, 0)[0]
    blocks = length // BLOCK
    positions = jnp.arange(length, dtype=jnp.int32)
    doc_ids = jnp.sum((starts[None, :] <= positions[:, None]).astype(jnp.int32), axis=1)
    doc_ids = doc_ids.reshape(blocks, BLOCK).astype(F32)
    firsts = jnp.arange(blocks, dtype=jnp.int32) * BLOCK - 1
    prev_ids = jnp.sum((starts[None, :] <= firsts[:, None]).astype(jnp.int32), axis=1).astype(F32)
    slopes = lax.dynamic_slice_in_dim(head_slopes(), lax.axis_index("wide") * 2, 2, 0)
    offsets = jnp.arange(BLOCK, dtype=F32)
    lags = offsets[:, None] - offsets[None, :]
    decay = jnp.exp(-slopes[:, None, None] * jnp.maximum(lags, 0.0)[None])
    continues = (doc_ids == prev_ids[:, None]).astype(F32)
    entry = continues[..., None] * jnp.exp(-slopes[None, :] * (offsets[:, None] + 1.0))
    tail = (doc_ids == doc_ids[:, -1:]).astype(F32)[..., None] * jnp.exp(
        -slopes[None, :] * (BLOCK - 1.0 - offsets)[:, None]
    )
    passing = continues[:, -1:] * jnp.exp(-slopes * BLOCK)
    cols = jnp.concatenate([doc_ids[..., None], entry, tail], axis=-1).reshape(length, 5)
    cols = jnp.pad(cols, ((0, 0), (0, HEAD - 5)))
    passing = jnp.broadcast_to(passing.reshape(-1, 1), (2 * blocks, HEAD))
    return cols, doc_ids, passing, decay


def local_box(tokens, doc_starts, wq, wk, wv, wg, wo, fv, fg, fo, cotangent):
    tables = prepare(doc_starts, WIDE * tokens.shape[1])
    weights = (wq, wk, wv, wg, wo, fv, fg, fo)
    outs = layer(tokens[0], weights, cotangent[0], *tables)
    return (outs[0][None], outs[1][None]) + tuple(outs[2:])


def solution(mesh):
    box = (mesh.shape["wide"], mesh.shape["narrow"]) == (WIDE, NARROW)
    tok = P("narrow", "wide", None)
    row = P(BOTH, None)
    return jax.shard_map(
        local_box if box else local,
        mesh=mesh,
        in_specs=(tok, P()) + (row,) * 8 + (tok,),
        out_specs=(tok, tok) + (row,) * 8,
        check_vma=False,
    )
```

```python
import jax
import jax.numpy as jnp
from jax import lax
from jax.experimental import pallas as pl
from jax.experimental.pallas import tpu as pltpu
from jax.sharding import PartitionSpec as P

HEADS = 16
HEAD = 128
BLOCK = 256
LAYERS = 16
LAYER = 12

EPS = 1e-06
BOTH = ("wide", "narrow")
BF = jnp.bfloat16
F32 = jnp.float32


def normalize(values):
    scale = lax.rsqrt(jnp.mean(values * values, axis=-1, keepdims=True) + EPS)
    return (values * scale, scale)


def normalize_back(normed, scale, grad):
    return scale * (grad - normed * jnp.mean(grad * normed, axis=-1, keepdims=True))


def silu_slope(values):
    sigma = jax.nn.sigmoid(values)
    return sigma * (1.0 + values * (1.0 - sigma))


def matmul(left, right):
    return jnp.dot(left, right, preferred_element_type=F32)


def matmul_right_t(left, right):
    return lax.dot_general(left, right, (((1,), (1,)), ((), ())), preferred_element_type=F32)


def weight_grad(left, right):
    return lax.dot_general(left, right, (((0,), (0,)), ((), ())), preferred_element_type=F32)


def ein(spec, left, right):
    return jnp.einsum(spec, left, right, preferred_element_type=F32)


def head_slopes():
    order = jnp.arange(HEADS, dtype=F32)
    return jnp.exp2(-8.0 * (order + 1.0) / HEADS) * (1.0 - LAYER / (LAYERS - 1) + 1e-05)


def local(
    tokens,
    doc_starts,
    query_weight,
    key_weight,
    value_weight,
    gate_weight,
    out_weight,
    ffn_value_weight,
    ffn_gate_weight,
    ffn_out_weight,
    cotangent,
):
    wide, narrow = lax.axis_size("wide"), lax.axis_size("narrow")
    rows_here, width = tokens.shape[1:]
    length = rows_here * wide
    blocks = length // BLOCK
    heads_here = HEADS // wide
    shard = query_weight.shape[0]

    def reorder(values):
        return values.reshape(-1, wide, narrow, shard).swapaxes(1, 2).reshape(-1, width)

    def restore(values):
        return values.reshape(-1, narrow, wide, shard).swapaxes(1, 2).reshape(-1, width)

    def columns(weight):
        part = lax.all_to_all(weight, "wide", split_axis=1, concat_axis=0, tiled=True)
        return lax.all_gather(part, "narrow", axis=0, tiled=True)

    def gather_rows(values):
        return lax.all_gather(values, "wide", axis=0, tiled=True)

    def scatter_rows(values):
        return lax.psum_scatter(
            values.astype(BF), "wide", scatter_dimension=0, tiled=True
        ).astype(F32)

    def to_tokens(values):
        return lax.all_to_all(values, "wide", split_axis=0, concat_axis=1, tiled=True)

    def to_heads(values):
        return lax.all_to_all(values, "wide", split_axis=1, concat_axis=0, tiled=True)

    def column_sums(grad):
        part = lax.psum_scatter(grad.astype(BF), "narrow", scatter_dimension=0, tiled=True)
        return lax.all_to_all(part, "wide", split_axis=0, concat_axis=1, tiled=True).astype(F32)

    w_query, w_key, w_value, w_gate = map(
        columns, (query_weight, key_weight, value_weight, gate_weight)
    )
    w_out = lax.all_gather(out_weight, BOTH, axis=0, tiled=True)
    w_fval, w_fgate = map(columns, (ffn_value_weight, ffn_gate_weight))
    w_fout = lax.all_gather(ffn_out_weight, "narrow", axis=0, tiled=True)

    starts = lax.dynamic_slice_in_dim(doc_starts, lax.axis_index("narrow"), 1, 0)[0]
    positions = jnp.arange(length, dtype=jnp.int32)
    doc_ids = jnp.sum((starts[None, :] <= positions[:, None]).astype(jnp.int32), axis=1)
    doc_ids = doc_ids.reshape(blocks, BLOCK)
    firsts = jnp.arange(blocks, dtype=jnp.int32) * BLOCK - 1
    prev_ids = jnp.sum((starts[None, :] <= firsts[:, None]).astype(jnp.int32), axis=1)
    slopes = lax.dynamic_slice_in_dim(
        head_slopes(), lax.axis_index("wide") * heads_here, heads_here, 0
    )
    offsets = jnp.arange(BLOCK, dtype=F32)
    lags = offsets[:, None] - offsets[None, :]
    decays = jnp.exp(-slopes[:, None, None] * jnp.maximum(lags, 0.0)[None])
    within = (doc_ids[:, :, None] == doc_ids[:, None, :]) & (lags >= 0.0)
    block_mask = jnp.where(within[:, None], decays[None], 0.0)
    continues = (doc_ids == prev_ids[:, None]).astype(F32)
    entry_scale = continues[..., None] * jnp.exp(-slopes[None, :] * (offsets[:, None] + 1.0))
    tail_scale = (doc_ids == doc_ids[:, -1:]).astype(F32)[..., None] * jnp.exp(
        -slopes[None, :] * (BLOCK - 1.0 - offsets)[:, None]
    )
    passing = continues[:, -1:] * jnp.exp(-slopes * BLOCK)

    def split_heads(values):
        return values.reshape(blocks, BLOCK, heads_here, HEAD)

    inputs = tokens[0].astype(F32)
    normed, in_scale = normalize(inputs)
    normed_bf = gather_rows(reorder(normed.astype(BF)))
    query_pre = matmul(normed_bf, w_query)
    key_pre = matmul(normed_bf, w_key)
    queries = split_heads(jax.nn.silu(query_pre).astype(BF))
    keys = split_heads(jax.nn.silu(key_pre).astype(BF))
    values = split_heads(matmul(normed_bf, w_value).astype(BF))
    gate = matmul(normed_bf, w_gate)
    scores = ein("bihe,bjhe->bhij", queries, keys)
    probs = (scores * block_mask).astype(BF)
    inner = ein("bhij,bjhe->bihe", probs, values)
    tail_keys = (keys.astype(F32) * tail_scale[..., None]).astype(BF)
    fresh = ein("bjhe,bjhf->bhef", tail_keys, values)
    state = jnp.zeros((heads_here, HEAD, HEAD), F32)
    entering = []
    for b in range(blocks):
        entering.append(state)
        state = passing[b][:, None, None] * state + fresh[b]
    block_in = jnp.stack(entering).astype(BF)
    across = entry_scale[..., None] * ein("bihe,bhef->bihf", queries, block_in)
    attention = (inner + across).reshape(query_pre.shape)

    attn_tok = to_tokens(attention)
    gate_tok = to_tokens(gate)
    attn_n, attn_scale = normalize(attn_tok)
    mixed = (attn_n * gate_tok).astype(BF)
    middle = inputs + matmul(mixed, w_out)
    middle_n, middle_scale = normalize(middle)
    middle_bf = gather_rows(reorder(middle_n.astype(BF)))
    ffn_val = matmul(middle_bf, w_fval)
    ffn_gat = matmul(middle_bf, w_fgate)
    ffn_mix = (ffn_val * ffn_gat).astype(BF)
    result = middle + scatter_rows(matmul(ffn_mix, w_fout))

    upstream = cotangent[0]
    up_all = gather_rows(upstream)
    grad_fout = weight_grad(ffn_mix, up_all)
    d_mix = matmul_right_t(up_all, w_fout)
    d_val = (d_mix * ffn_gat).astype(BF)
    d_gat = (d_mix * ffn_val).astype(BF)
    grad_fval = weight_grad(middle_bf, d_val)
    grad_fgate = weight_grad(middle_bf, d_gat)
    d_middle_n = restore(
        scatter_rows(matmul_right_t(d_val, w_fval) + matmul_right_t(d_gat, w_fgate))
    )
    d_middle = upstream.astype(F32) + normalize_back(middle_n, middle_scale, d_middle_n)
    d_branch = d_middle.astype(BF)
    grad_out = weight_grad(mixed, d_branch)
    d_mixed = matmul_right_t(d_branch, w_out)
    d_gate = to_heads((d_mixed * attn_n).astype(BF))
    d_attn = to_heads(normalize_back(attn_n, attn_scale, d_mixed * gate_tok).astype(BF))

    d_heads = split_heads(d_attn)
    d_probs = ein("bihe,bjhe->bhij", d_heads, values)
    d_scores = (d_probs * block_mask).astype(BF)
    d_query = ein("bhij,bjhe->bihe", d_scores, keys)
    d_key = ein("bhij,bihe->bjhe", d_scores, queries)
    d_value = ein("bhij,bihe->bjhe", probs, d_heads)
    d_query = d_query + entry_scale[..., None] * ein("bihf,bhef->bihe", d_heads, block_in)
    entry_queries = (queries.astype(F32) * entry_scale[..., None]).astype(BF)
    grad_in = ein("bihe,bihf->bhef", entry_queries, d_heads)
    state = jnp.zeros((heads_here, HEAD, HEAD), F32)
    leaving = [None] * blocks
    for b in reversed(range(blocks)):
        leaving[b] = state
        state = passing[b][:, None, None] * state + grad_in[b]
    block_out = jnp.stack(leaving).astype(BF)
    d_key = d_key + tail_scale[..., None] * ein("bjhf,bhef->bjhe", values, block_out)
    d_value = d_value + ein("bjhe,bhef->bjhf", tail_keys, block_out)
    dq_pre = (d_query.reshape(query_pre.shape) * silu_slope(query_pre)).astype(BF)
    dk_pre = (d_key.reshape(key_pre.shape) * silu_slope(key_pre)).astype(BF)
    dv_pre = d_value.reshape(query_pre.shape).astype(BF)
    grad_query = weight_grad(normed_bf, dq_pre)
    grad_key = weight_grad(normed_bf, dk_pre)
    grad_value = weight_grad(normed_bf, dv_pre)
    grad_gate = weight_grad(normed_bf, d_gate)
    d_normed = restore(
        scatter_rows(
            matmul_right_t(dq_pre, w_query)
            + matmul_right_t(dk_pre, w_key)
            + matmul_right_t(dv_pre, w_value)
            + matmul_right_t(d_gate, w_gate)
        )
    )
    d_inputs = d_middle + normalize_back(normed, in_scale, d_normed)
    return (
        result.astype(BF)[None],
        d_inputs[None],
        column_sums(grad_query),
        column_sums(grad_key),
        column_sums(grad_value),
        column_sums(grad_gate),
        lax.psum_scatter(grad_out.astype(BF), BOTH, scatter_dimension=0, tiled=True).astype(F32),
        column_sums(grad_fval),
        column_sums(grad_fgate),
        lax.psum_scatter(grad_fout.astype(BF), "narrow", scatter_dimension=0, tiled=True).astype(
            F32
        ),
    )


MESH = pl.DeviceIdType.MESH
ANY = pl.BlockSpec(memory_space=pl.ANY)
VMEM = pl.BlockSpec(memory_space=pltpu.VMEM)
WIDE, NARROW = 8, 4
CHIPS = WIDE // 2


def dot(left, right):
    return jnp.dot(left, right, preferred_element_type=F32)


def dot_rt(left, right):
    return lax.dot_general(left, right, (((1,), (1,)), ((), ())), preferred_element_type=F32)


def dot_lt(left, right):
    return lax.dot_general(left, right, (((0,), (0,)), ((), ())), preferred_element_type=F32)


def at(start, size):
    return pl.ds(pl.multiple_of(start, size), size)


class Links:
    def __init__(self, send, recv, here):
        self.send, self.recv, self.here = send, recv, here
        self.count, self.kept = 0, 1
        w = lax.axis_index("wide")
        n = lax.axis_index("narrow")
        self.w, self.n = w, n
        self.core = lax.rem(w, 2)
        self.chip = lax.div(w, 2)
        x, y = lax.rem(self.chip, 2), lax.div(self.chip, 2)
        self.wx = w + 2 - 4 * x
        self.wy = w + 4 - 8 * y
        self.wd = w + 6 - 4 * x - 8 * y
        self.ws = w + 1 - 2 * self.core
        self.px = self.chip + 1 - 2 * x
        self.py = self.chip + 2 - 4 * y
        self.pd = 3 - self.chip
        self.mid = lax.rem(lax.div(n + 1, 2), 2)
        self.pair = n + 1 - 2 * lax.rem(n, 2)
        self.cross = 2 - lax.div(n, 2)
        self.far = 3 - 3 * lax.div(n, 2)
        self.end_to = 3 * lax.rem(n + 1, 2)
        self.end_part = lax.rem(2 * n, 3) + 3 * lax.div(n, 3)

    def greet(self):
        barrier = pltpu.get_barrier_semaphore()
        for d in range(1, WIDE):
            pl.semaphore_signal(
                barrier, inc=1, device_id=(lax.rem(self.w + d, WIDE), self.n), device_id_type=MESH
            )
        for d in range(1, NARROW):
            pl.semaphore_signal(
                barrier, inc=1, device_id=(self.w, lax.rem(self.n + d, NARROW)), device_id_type=MESH
            )

    def met(self):
        pl.semaphore_wait(pltpu.get_barrier_semaphore(), WIDE + NARROW - 2)

    def take(self, number):
        base = self.count
        self.count += number
        return base

    def remote(self, src, dst, send, recv, wide=None, narrow=None):
        return pltpu.make_async_remote_copy(
            src_ref=src,
            dst_ref=dst,
            send_sem=self.send.at[send],
            recv_sem=self.recv.at[recv],
            device_id=(self.w if wide is None else wide, self.n if narrow is None else narrow),
            device_id_type=MESH,
        )

    def arrived(self, ref, recv):
        self.remote(ref, ref, recv, recv, wide=self.ws).wait_recv()

    def keep(self, src, dst):
        copy = pltpu.make_async_copy(src, dst, self.here.at[self.kept])
        self.kept += 1
        copy.start()
        return copy


class Line:
    def __init__(self, links, part):
        self.links, self.part = links, part
        self.base = links.take(5)

    def copy(self, index):
        k, b = self.links, self.base
        which, to = (
            (k.n, k.pair),
            (k.n, k.cross),
            (k.pair, k.cross),
            (k.cross, k.pair),
            (k.far, k.pair),
        )[index]
        ref = self.part(which)
        return k.remote(ref, ref, b + index, b + which, narrow=to)

    def start(self):
        self.start_away()
        pl.when(self.links.mid == 1)(lambda: self.copy(0).start())

    def start_away(self):
        pl.when(self.links.mid == 1)(lambda: self.copy(1).start())
        pl.when(self.links.mid == 0)(lambda: self.copy(0).start())

    def start_home(self):
        pl.when(self.links.mid == 1)(lambda: self.copy(0).start())

    def wait(self, index):
        self.links.arrived(self.part(index), self.base + index)

    def forward(self):
        @pl.when(self.links.mid == 1)
        def _():
            self.wait(self.links.cross)
            self.copy(3).start()
            self.wait(self.links.pair)
            self.copy(2).start()

    def forward_far(self):
        @pl.when(self.links.mid == 1)
        def _():
            self.wait(self.links.far)
            self.copy(4).start()

    def finish(self, then=lambda place: None, late=lambda: None):
        k = self.links
        then(0)
        for place, index in enumerate((k.pair, k.cross, k.far)):
            if place == 2:
                late()
            pl.when(k.mid == 0)(lambda index=index: self.wait(index))
            then(place + 1)

    def drain(self):
        self.copy(0).wait_send()

        @pl.when(self.links.mid == 1)
        def _():
            for index in range(1, 5):
                self.copy(index).wait_send()


class Plane:
    def __init__(self, links, slot):
        self.links, self.slot = links, slot
        self.base = links.take(6)

    def copy(self, index):
        k, b = self.links, self.base
        owner, half, to = (
            (k.w, 0, k.wx),
            (k.w, 1, k.wy),
            (k.w, 1, k.wx),
            (k.w, 0, k.wy),
            (k.wx, 0, k.wy),
            (k.wy, 1, k.wx),
        )[index]
        ref = self.slot(owner, half)
        return k.remote(ref, ref, b + index, b + index, wide=to)

    def start(self):
        for index in range(4):
            self.copy(index).start()

    def forward(self):
        k, b, slot = self.links, self.base, self.slot
        k.arrived(slot(k.wx, 0), b)
        self.copy(4).start()
        k.arrived(slot(k.wy, 1), b + 1)
        self.copy(5).start()

    def finish_near(self):
        k, b, slot = self.links, self.base, self.slot
        k.arrived(slot(k.wx, 1), b + 2)
        k.arrived(slot(k.wy, 0), b + 3)

    def finish_far(self):
        k, b, slot = self.links, self.base, self.slot
        k.arrived(slot(k.wd, 0), b + 4)
        k.arrived(slot(k.wd, 1), b + 5)

    def drain(self):
        for index in range(6):
            self.copy(index).wait_send()


class Sibling:
    def __init__(self, links, block, twin, number):
        self.links, self.block, self.twin, self.number = links, block, twin, number
        self.base = links.take(number)

    def copy(self, index):
        k, b = self.links, self.base + index
        ref = self.block(index)
        return k.remote(ref, ref, b, b, wide=k.ws)

    def send(self, index):
        self.copy(index).start()

    def wait(self, index):
        self.links.arrived(self.twin(index), self.base + index)

    def drain(self):
        for index in range(self.number):
            self.copy(index).wait_send()


class Spread:
    def __init__(self, links, src, dst, peers=WIDE):
        self.links, self.src, self.dst = links, src, dst
        self.step = 1 if peers == WIDE else 2
        self.base = links.take(WIDE)

    def distances(self):
        return range(self.step, WIDE, self.step)

    def copy(self, d, to):
        k, b = self.links, self.base + d
        return k.remote(self.src(to), self.dst(k.w), b, b, wide=to)

    def start(self):
        for d in self.distances():
            self.copy(d, lax.rem(self.links.w + d, WIDE)).start()

    def finish(self):
        k = self.links
        for d in self.distances():
            k.arrived(self.dst(lax.rem(k.w + WIDE - d, WIDE)), self.base + d)

    def drain(self):
        for d in self.distances():
            self.copy(d, lax.rem(self.links.w + d, WIDE)).wait_send()


def row_scale(values):
    return lax.rsqrt(jnp.mean(values * values, axis=-1, keepdims=True) + EPS)


def row_chunks(rows, body, size=32):
    def step(r, carry):
        body(at(r * size, size))
        return carry

    lax.fori_loop(0, rows // size, step, 0)


def doc_mask(cols, rowdoc, decay, rows, block):
    tokens = decay.shape[-1]
    same = cols[rows, 0:1] == rowdoc[pl.ds(block, 1), :]
    i = lax.broadcasted_iota(jnp.int32, (tokens, tokens), 0)
    j = lax.broadcasted_iota(jnp.int32, (tokens, tokens), 1)
    return same & (i >= j)


class LineSum:
    def __init__(self, links, part, land):
        self.links, self.part, self.land = links, part, land
        self.base = links.take(5)
        self.onward = links.pair + links.mid * (links.cross - links.pair)

    def copy(self, index):
        k, b = self.links, self.base
        which, slot, to = (
            (k.far, 3 * k.mid, self.onward),
            (k.cross, 1 + 3 * k.mid, self.onward),
            (k.pair, 2 - 2 * k.mid, k.pair),
        )[index]
        return k.remote(self.part(which), self.land(slot), b + index, b + slot, narrow=to)

    def start(self):
        @pl.when(self.links.mid == 0)
        def _():
            for index in range(3):
                self.copy(index).start()

    def wait(self, slot):
        self.links.arrived(self.land(slot), self.base + slot)

    def pass_on(self, index, add):
        k = self.links
        which, slot = ((k.far, 0), (k.cross, 1), (k.pair, 3))[index]

        @pl.when(k.mid == 1)
        def _():
            self.wait(slot)
            add(self.part(which), self.land(slot))
            self.copy(index).start()

    def finish(self, fetch, spots):
        k = self.links
        pl.when(k.mid == 0)(lambda: self.wait(0))

        @pl.when(k.mid == 1)
        def _():
            self.wait(2)
            self.wait(4)
            fetch(self.land(4), spots.at[1])

        fetch(self.land(2 * k.mid), spots.at[0])

        @pl.when(k.mid == 0)
        def _():
            spots[1] = jnp.zeros(spots.shape[1:], spots.dtype)

    def drain(self):
        for index in range(3):
            self.copy(index).wait_send()


class PlaneSum:
    def __init__(self, links, block, corner, near, half, base=None):
        self.links, self.block, self.corner, self.near, self.half = links, block, corner, near, half
        self.base = links.take(6) if base is None else base

    def rows(self, h):
        return pl.ds(h * self.half, self.half)

    def copy(self, index):
        k = self.links
        chip, h, land, to = (
            (k.pd, 0, self.corner.at[0], k.wx),
            (k.pd, 1, self.corner.at[1], k.wy),
            (k.px, 0, self.near.at[0, self.rows(0)], k.wx),
            (k.py, 1, self.near.at[1, self.rows(1)], k.wy),
            (k.px, 1, self.near.at[0, self.rows(1)], k.wx),
            (k.py, 0, self.near.at[1, self.rows(0)], k.wy),
        )[index]
        sem = self.base + index
        return k.remote(self.block(chip).at[self.rows(h)], land, sem, sem, wide=to)

    def send_far(self):
        self.copy(0).start()
        self.copy(1).start()

    def send_x(self):
        self.copy(2).start()

    def send_y(self):
        self.copy(3).start()

    def combine(self, add):
        k = self.links
        self.copy(1).wait_recv()
        add(self.block(k.px).at[self.rows(1)], self.corner.at[1])
        self.copy(4).start()
        self.copy(0).wait_recv()
        add(self.block(k.py).at[self.rows(0)], self.corner.at[0])
        self.copy(5).start()

    def finish(self):
        for index in range(2, 6):
            self.copy(index).wait_recv()

    def drain(self):
        for index in range(6):
            self.copy(index).wait_send()


def layer_kernel(
    x_in, wq, wk, wv, wg, wo, fv, fg, fo, dy_arg, cols_in, decay_in, rowdoc, passing,
    result_o, dx_o, gq_o, gk_o, gv_o, gg_o, go_o, gfv_o, gfg_o, gfo_o,
    xn_in, wqk_in, wvg_in, wo_in, fv_in, fg_in, fo_in, dy_in, slope_in, qkv_in, sin_in, attn_in,
    gate_in, mixed_in, x1_in, x1n_in,
    corner, near, twin_fo_land, twin_ff, twin_wo, twin_xn_land, land_fo, land_ff, land_wo, land_qk,
    turn_ff, turn_qk, a_land, g_land,
    g_fo, g_fv, g_fg, stage, acc, tmp, own_res, tmp_ff,
    send, recv, here,
):
    k = Links(send, recv, here)
    w, n, core, chip = k.w, k.n, k.core, k.chip
    other = 1 - core
    tok, width = acc.shape
    ff = g_fv.shape[-1]
    fo_rows = land_fo.shape[1]
    half = tok // 2
    two = 2 * HEAD
    order = (k.pd, k.px, k.py, chip)

    def nth(j):
        flip_x, flip_y = 1 - lax.div(j, 2), 1 - lax.rem(j, 2)
        return (
            chip + flip_x * (1 - 2 * lax.rem(chip, 2)) + flip_y * (2 - 4 * lax.div(chip, 2))
        )

    def fetch(src, dst):
        copy = pltpu.make_async_copy(src, dst, here.at[0])
        copy.start()
        copy.wait()

    def adder(spot):
        def add(to, land):
            fetch(land, spot)
            to[...] = (to[...].astype(F32) + spot[...].astype(F32)).astype(BF)

        return add

    add_half = adder(tmp.at[pl.ds(0, half)])
    add_fo = adder(tmp.at[pl.ds(0, fo_rows)])
    add_wo = adder(tmp.at[pl.ds(0, 64)])
    add_ff = adder(tmp_ff)
    def fo_part(owner, i):
        return g_fo.at[pl.ds(pl.multiple_of((owner * NARROW + i) * fo_rows, 16), fo_rows)]

    sum_fo = LineSum(k, lambda i: fo_part(core, i), lambda s: land_fo.at[s])
    sum_ff = [
        LineSum(k, lambda i, g=g: g.at[:, i], lambda s, m=m: land_ff.at[m, s])
        for m, g in enumerate((g_fv, g_fg))
    ]
    def plane_sum(m, blocks, base=None):
        return PlaneSum(k, lambda q: blocks.at[q], corner.at[m], near.at[m], half, base)

    plane_mid, plane_in = (plane_sum(m, stage) for m in (0, 3))
    base_res = k.take(6)
    twin_base = k.take(4 * 5)

    def twin(m, j, src, dst):
        sem = twin_base + 4 * m + j
        return k.remote(src, dst, sem, sem, wide=k.ws)

    def wide_cols(index):
        return at(index * two, two)

    def chip_cols(index):
        return pl.ds(pl.multiple_of(index * ff, 128), ff)

    projections = ((wq, wqk_in), (wk, wqk_in), (wv, wvg_in), (wg, wvg_in))
    lines = line_out, line_qk, line_vg, line_fv, line_fg, line_fo = (
        Line(k, lambda i: wo_in.at[w, i]),
        Line(k, lambda i: wqk_in.at[:, i]),
        Line(k, lambda i: wvg_in.at[:, i]),
        Line(k, lambda i: fv_in.at[:, core, i]),
        Line(k, lambda i: fg_in.at[:, core, i]),
        Line(k, lambda i: fo_in.at[core, i]),
    )
    spreads = [
        Spread(
            k,
            lambda t, weight=weight: weight.at[:, wide_cols(t)],
            lambda s, m=m, to=to: to.at[s, n, :, pl.ds((m % 2) * two, two)],
        )
        for m, (weight, to) in enumerate(projections)
    ]
    spread_ff = [
        Spread(
            k,
            lambda t, weight=weight: weight.at[:, chip_cols(lax.div(t, 2))],
            lambda s, to=to: to.at[lax.div(s, 2), core, n],
            peers=CHIPS,
        )
        for weight, to in ((fv, fv_in), (fg, fg_in))
    ]
    planes = plane_xn, plane_out, plane_dy, plane_x1n = (
        Plane(k, lambda s, h: xn_in.at[s, pl.ds(h * half, half)]),
        Plane(k, lambda s, h: wo_in.at[s, pl.ds(h * 2, 2)]),
        Plane(k, lambda s, h: dy_in.at[lax.div(s, 2), pl.ds(h * half, half)]),
        Plane(k, lambda s, h: x1n_in.at[lax.div(s, 2), pl.ds(h * half, half)]),
    )
    here4 = (w, k.wx, k.wy, k.wd)
    there4 = tuple(s + 1 - 2 * core for s in here4)
    near4 = (n, k.pair, k.cross, k.far)
    twins = twin_xn, twin_out, twin_fv, twin_fg, twin_fo = (
        Sibling(k, lambda i: xn_in.at[here4[i]], lambda i: xn_in.at[there4[i]], 4),
        Sibling(k, lambda i: wo_in.at[here4[i]], lambda i: wo_in.at[there4[i]], 4),
        Sibling(k, lambda i: fv_in.at[:, core, near4[i]], lambda i: fv_in.at[:, other, near4[i]], 4),
        Sibling(k, lambda i: fg_in.at[:, core, near4[i]], lambda i: fg_in.at[:, other, near4[i]], 4),
        Sibling(k, lambda i: fo_in.at[core, near4[i]], lambda i: fo_in.at[other, near4[i]], 4),
    )

    k.greet()
    def before(
        x, xn, wqk, wvg, wout, slope, qkv, gates, sin, state, attn_s, attn, gate, mixed, x1, x1n,
        cols, decay,
    ):
        load_x = k.keep(x_in, x)
        held = [
            (k.keep(wo, mixed.at[pl.ds(0, 64)]), mixed.at[pl.ds(0, 64)], wo_in.at[w, n]),
            *[
                (
                    k.keep(weight.at[:, wide_cols(w)], spot.at[w, n, :, lanes]),
                    spot.at[w, n, :, lanes],
                    to.at[w, n, :, lanes],
                )
                for weight, spot, to, lanes in (
                    (wq, wqk, wqk_in, pl.ds(0, two)),
                    (wk, wqk, wqk_in, pl.ds(two, two)),
                    (wv, wvg, wvg_in, pl.ds(0, two)),
                    (wg, wvg, wvg_in, pl.ds(two, two)),
                )
            ],
            (k.keep(dy_arg, attn), attn, dy_in.at[chip]),
            *[
                (
                    k.keep(weight.at[:, chip_cols(chip)], tmp_ff.at[m]),
                    tmp_ff.at[m],
                    to.at[chip, core, n],
                )
                for m, (weight, to) in enumerate(((fv, fv_in), (fg, fg_in)))
            ],
            (k.keep(fo, gate.at[pl.ds(0, fo_rows)]), gate.at[pl.ds(0, fo_rows)], fo_in.at[core, n]),
        ]

        def place(index):
            load, spot, to = held[index]
            load.wait()
            return k.keep(spot, to)

        load_x.wait()

        def norm_in(rows):
            v = x[rows, :].astype(F32)
            x1n[rows, :] = (v * row_scale(v)).astype(BF)

        row_chunks(tok, norm_in)
        own_xn = k.keep(x1n, xn_in.at[w])
        own_in = [place(i) for i in range(5)]
        load_cols, load_decay = k.keep(cols_in, cols), k.keep(decay_in, decay)
        k.met()
        for spread in spreads:
            spread.start()
        own_in[0].wait()
        line_out.start()
        own_xn.wait()
        for copy in own_in[1:]:
            copy.wait()
        spreads[0].finish()
        spreads[1].finish()
        line_qk.start()
        plane_xn.start()
        twin_xn.send(0)
        spreads[2].finish()
        spreads[3].finish()
        line_vg.start()
        for spread in spread_ff:
            spread.start()
        own_ff = [place(i) for i in range(5, 9)]
        line_out.forward()
        plane_xn.forward()
        line_out.forward_far()
        line_qk.forward()
        plane_xn.finish_near()
        twin_xn.send(1)
        twin_xn.send(2)
        line_vg.forward()
        line_qk.forward_far()
        line_out.finish()
        plane_out.start()
        twin_out.send(0)
        plane_xn.finish_far()
        twin_xn.send(3)
        line_vg.forward_far()
        spread_ff[0].finish()
        spread_ff[1].finish()
        for copy in own_ff:
            copy.wait()
        line_fv.start()
        for i in range(4):
            twin_xn.wait(i)
        load_xn = k.keep(xn_in, xn)
        plane_out.forward()
        line_qk.finish()
        load_qk = k.keep(wqk_in, wqk)
        load_xn.wait()
        load_qk.wait()

        def project_qk(t, carry):
            v = dot(xn[t], wqk[...].reshape(width, 2 * two))
            rows = at(t * tok, tok)
            sigma = jax.nn.sigmoid(v)
            slope[rows, :] = (sigma * (1.0 + v * (1.0 - sigma))).astype(BF)
            qkv[rows, 0 : 2 * two] = (v * sigma).astype(BF)
            return carry

        lax.fori_loop(0, WIDE, project_qk, 0)
        stores = [k.keep(slope, slope_in)]
        plane_out.finish_near()
        twin_out.send(1)
        twin_out.send(2)
        line_vg.finish()
        k.keep(wvg_in, wvg).wait()

        def project_vg(t, carry):
            v = dot(xn[t], wvg[...].reshape(width, 2 * two)).astype(BF)
            qkv[at(t * tok, tok), 2 * two : 3 * two] = v[:, 0:two]
            gates[t] = v[:, two:]
            return carry

        lax.fori_loop(0, WIDE, project_vg, 0)
        line_fv.forward()
        line_fg.start()
        stores.append(k.keep(qkv, qkv_in))
        spread_gate = Spread(k, lambda t: gates.at[t], lambda s: gate_in.at[:, wide_cols(s)])
        spread_gate.start()
        own = [k.keep(gates.at[w], gate_in.at[:, wide_cols(w)])]
        load_cols.wait()
        load_decay.wait()
        state[...] = jnp.zeros_like(state)
        spread_attn = Spread(k, lambda t: attn_s.at[t], lambda s: attn_in.at[:, wide_cols(s)])

        def attend(b, carry):
            rows = at(b * BLOCK, BLOCK)
            mask = doc_mask(cols, rowdoc, decay, rows, b)
            for h in range(2):
                lanes = slice(h * HEAD, (h + 1) * HEAD)
                q = qkv[rows, lanes]
                key = qkv[rows, two + h * HEAD : two + (h + 1) * HEAD]
                v = qkv[rows, 2 * two + h * HEAD : 2 * two + (h + 1) * HEAD]
                probs = jnp.where(mask, dot_rt(q, key) * decay[h], 0.0).astype(BF)
                old = state[h]
                old_bf = old.astype(BF)
                sin[b, h] = old_bf
                entry = cols[rows, 1 + h : 2 + h]
                tail = cols[rows, 3 + h : 4 + h]
                out = dot(probs, v) + entry * dot(q, old_bf)
                attn_s[b, :, lanes] = out.astype(BF)
                tailed = (key.astype(F32) * tail).astype(BF)
                state[h] = passing[pl.ds(2 * b + h, 1), :] * old + dot_lt(tailed, v)

            @pl.when(b != w)
            def _():
                spread_attn.copy(lax.rem(b - w + WIDE, WIDE), b).start()

            return carry

        lax.fori_loop(0, WIDE, attend, 0)
        stores.append(k.keep(sin, sin_in))
        own.append(k.keep(attn_s.at[w], attn_in.at[:, wide_cols(w)]))
        plane_out.finish_far()
        twin_out.send(3)
        for i in range(4):
            twin_out.wait(i)
        load_out = k.keep(wo_in, wout)
        line_fv.forward_far()
        spread_gate.finish()
        spread_attn.finish()
        for copy in own:
            copy.wait()
        loads = [k.keep(attn_in, attn), k.keep(gate_in, gate)]
        for copy in loads:
            copy.wait()

        def mix(rows):
            a = attn[rows, :].astype(F32)
            mixed[rows, :] = (a * row_scale(a) * gate[rows, :].astype(F32)).astype(BF)

        row_chunks(tok, mix)
        stores.append(k.keep(mixed, mixed_in))
        load_out.wait()

        def project_out(j, carry):
            lanes = at(j * 512, 512)
            part = dot(mixed[...], wout[:, :, :, lanes].reshape(-1, 512))
            x1[:, lanes] = x[:, lanes].astype(F32) + part
            return carry

        lax.fori_loop(0, width // 512, project_out, 0)
        stores.append(k.keep(x1, x1_in))

        def norm_mid(rows):
            v = x1[rows, :]
            x1n[rows, :] = (v * row_scale(v)).astype(BF)

        row_chunks(tok, norm_mid)
        k.keep(x1n, x1n_in.at[chip]).wait()
        plane_x1n.start()
        line_fg.forward()
        line_fo.start_away()
        plane_x1n.forward()
        plane_dy.start()
        line_fg.forward_far()
        for copy in stores:
            copy.wait()
        spread_gate.drain()
        spread_attn.drain()

    pl.run_scoped(
        before,
        pltpu.VMEM((tok, width), BF),
        pltpu.VMEM((WIDE, tok, width), BF),
        pltpu.VMEM(wqk_in.shape, BF),
        pltpu.VMEM(wvg_in.shape, BF),
        pltpu.VMEM(wo_in.shape, BF),
        pltpu.VMEM(slope_in.shape, BF),
        pltpu.VMEM(qkv_in.shape, BF),
        pltpu.VMEM((WIDE, tok, two), BF),
        pltpu.VMEM(sin_in.shape, BF),
        pltpu.VMEM((2, HEAD, HEAD), F32),
        pltpu.VMEM((WIDE, tok, two), BF),
        pltpu.VMEM((tok, width), BF),
        pltpu.VMEM((tok, width), BF),
        pltpu.VMEM((tok, width), BF),
        pltpu.VMEM((tok, width), F32),
        pltpu.VMEM((tok, width), BF),
        pltpu.VMEM(cols_in.shape, F32),
        pltpu.VMEM(decay_in.shape, F32),
    )

    def ffn(x1n, dy, fvw, fgw, fow, mix, val, gat, side):
        def shares(moved, src, dst, places):
            copies = []
            for i in places:
                moved.wait(i)
                copies.append(k.keep(src.at[:, :, near4[i]], dst.at[:, :, near4[i]]))
            return copies

        def fo_shares(places):
            copies = []
            for i in places:
                twin_fo.wait(i)
                copies.append(k.keep(fo_in.at[:, near4[i]], fow.at[:, near4[i]]))
            return copies

        line_fv.finish(twin_fv.send)
        load_fv = shares(twin_fv, fv_in, fvw, range(4))
        plane_x1n.finish_near()
        plane_x1n.finish_far()
        load_x1n = k.keep(x1n_in, x1n)
        line_fo.forward()
        load_fg = []
        line_fg.finish(twin_fg.send, lambda: load_fg.extend(shares(twin_fg, fg_in, fgw, range(3))))
        line_fo.start_home()
        load_fg += shares(twin_fg, fg_in, fgw, range(3, 4))
        plane_dy.forward()
        for copy in (load_x1n, *load_fv, *load_fg):
            copy.wait()

        def up(j, carry):
            v = dot(x1n[j], fvw[...].reshape(width, ff))
            g = dot(x1n[j], fgw[...].reshape(width, ff))
            mix[j] = (v * g).astype(BF)
            val[j] = v.astype(BF)
            gat[j] = g.astype(BF)
            return carry

        lax.fori_loop(0, CHIPS // 2, up, 0)
        line_fo.forward_far()
        lax.fori_loop(CHIPS // 2, CHIPS, up, 0)
        plane_dy.finish_near()
        plane_dy.finish_far()
        k.keep(dy_in, dy).wait()

        def fo_grad(j, carry):
            chunk = lax.rem(j + 2 * other, chunks)
            rows = pl.ds(pl.multiple_of(jnp.minimum(chunk * 256, ff - 256), 128), 256)
            left = mix[:, :, rows].reshape(CHIPS * tok, 256)
            for h in range(2):
                lanes = slice(h * width // 2, (h + 1) * width // 2)
                right = dy[:, :, lanes].reshape(CHIPS * tok, -1)
                g_fo[rows, lanes] = dot_lt(left, right).astype(BF)
            return carry

        chunks = pl.cdiv(ff, 256)
        lax.fori_loop(0, 4, fo_grad, 0)
        for i in range(NARROW):
            twin(0, i, fo_part(other, i), twin_fo_land.at[i]).start()
        lax.fori_loop(4, chunks, fo_grad, 0)
        came = []
        for i in range(NARROW):
            copy = twin(0, i, fo_part(other, i), twin_fo_land.at[i])
            copy.wait_recv()
            spot = stage.at[i, pl.ds(0, fo_rows)]
            came.append((copy, k.keep(twin_fo_land.at[i], spot), spot))
        for i, (copy, load, spot) in enumerate(came):
            load.wait()
            own = fo_part(core, i)
            own[...] = (own[...].astype(F32) + spot[...].astype(F32)).astype(BF)
            copy.wait_send()
        sum_fo.start()
        load_fo = []
        line_fo.finish(twin_fo.send, lambda: load_fo.extend(fo_shares(range(3))))
        load_fo += fo_shares(range(3, 4))
        for copy in load_fo:
            copy.wait()

        def down(q, carry):
            d_mix = dot_rt(dy[q], fow[...].reshape(ff, width))
            d_val = (d_mix * gat[q].astype(F32)).astype(BF)
            d_gat = (d_mix * val[q].astype(F32)).astype(BF)
            val[q] = d_val
            gat[q] = d_gat
            return carry

        lax.fori_loop(0, CHIPS, down, 0)

        plane_res = plane_sum(1, dy, base_res)

        def out_step(j, carry):
            q = nth(j)
            dy[q] = dot(mix[q], fow[...].reshape(ff, width)).astype(BF)
            for step, push in enumerate((plane_res.send_far, plane_res.send_x, plane_res.send_y)):
                pl.when(j == step)(push)
            return carry

        lax.fori_loop(0, CHIPS, out_step, 0)

        def back(j, carry):
            q = nth(j)

            def back_lanes(i, carry):
                lanes = at(i * 512, 512)
                d_x = dot_rt(val[q], fvw[i].reshape(512, ff)) + dot_rt(
                    gat[q], fgw[i].reshape(512, ff)
                )
                stage[q, :, lanes] = d_x.astype(BF)

                @pl.when(j == 3)
                def _():
                    acc[:, lanes] = d_x

                return carry

            lax.fori_loop(0, width // 512, back_lanes, 0)
            for step, push in enumerate((plane_mid.send_far, plane_mid.send_x, plane_mid.send_y)):
                pl.when(j == step)(push)
            return carry

        for m, (d_ff, g_ff) in enumerate(((val, g_fv), (gat, g_fg))):

            def ff_grad(owner):
                left = x1n[:, :, at(owner * tok, tok)].reshape(CHIPS * tok, tok)
                g = dot_lt(left, d_ff[...].reshape(CHIPS * tok, ff)).astype(BF)
                return g.reshape(NARROW, -1, ff)

            def side_step(q, carry):
                slot = lax.rem(q, 2)

                @pl.when(q >= 2)
                def _():
                    twin(1 + m, q - 2, side.at[slot], twin_ff.at[m, q]).wait_send()

                side[slot] = ff_grad(2 * q + other)
                twin(1 + m, q, side.at[slot], twin_ff.at[m, q]).start()
                return carry

            def own_step(q, carry):
                g_ff[q] = ff_grad(2 * q + core)
                return carry

            lax.fori_loop(0, CHIPS, side_step, 0)
            lax.fori_loop(0, CHIPS, own_step, 0)
            for q in range(CHIPS):
                copy = twin(1 + m, q, side.at[q % 2], twin_ff.at[m, q])
                copy.wait_recv()
                add_ff(g_ff.at[q], twin_ff.at[m, q])
                if q >= 2:
                    copy.wait_send()
            sum_ff[m].start()
            if m == 0:
                lax.fori_loop(0, CHIPS, back, 0)
                plane_mid.combine(add_half)
                plane_res.combine(add_half)
                sum_fo.pass_on(0, add_fo)
                sum_fo.pass_on(1, add_fo)

        sum_fo.pass_on(2, add_fo)
        own_res[...] = dy[chip]
        plane_mid.drain()
        plane_res.drain()

    pl.run_scoped(
        ffn,
        pltpu.VMEM((CHIPS, tok, width), BF),
        pltpu.VMEM((CHIPS, tok, width), BF),
        pltpu.VMEM(fv_in.shape, BF),
        pltpu.VMEM(fg_in.shape, BF),
        pltpu.VMEM(fo_in.shape, BF),
        pltpu.VMEM((CHIPS, tok, ff), BF),
        pltpu.VMEM((CHIPS, tok, ff), BF),
        pltpu.VMEM((CHIPS, tok, ff), BF),
        pltpu.VMEM((2, *g_fv.shape[1:]), BF),
    )

    def rest(d_x1, d_branch, mixed, da_src, dg_src, side, stage_wo, g_wo, g_qk, g_vg):
        plane_out = plane_sum(2, stage_wo)
        sum_wo = LineSum(k, lambda i: g_wo.at[i], lambda s: land_wo.at[s])
        sum_qk = [
            LineSum(k, lambda i, g=g: g.at[:, i], lambda s, m=m: land_qk.at[m, s])
            for m, g in enumerate((g_qk, g_vg))
        ]
        spread_a = Spread(
            k, lambda t: da_src.at[:, at(t * two, two)], lambda s: a_land.at[s]
        )
        spread_g = Spread(
            k, lambda t: dg_src.at[:, at(t * two, two)], lambda s: g_land.at[at(s * tok, tok)]
        )

        def middle(wo, x1, attn, gate, dy, d_mixed, pair):
            plane_mid.finish()
            loads = [k.keep(near.at[0], pair), k.keep(x1_in, x1), k.keep(dy_in.at[chip], dy)]
            late = [
                k.keep(wo_in, wo), k.keep(attn_in, attn), k.keep(gate_in, gate),
                k.keep(mixed_in, mixed),
            ]
            for copy in loads:
                copy.wait()

            def norm_back(rows):
                g = acc[rows, :] + pair[0, rows, :].astype(F32) + pair[1, rows, :].astype(F32)
                v = x1[rows, :]
                r = row_scale(v)
                u = v * r
                d = dy[rows, :].astype(F32) + r * (g - u * jnp.mean(g * u, axis=-1, keepdims=True))
                d_x1[rows, :] = d
                d_branch[rows, :] = d.astype(BF)

            row_chunks(tok, norm_back)
            for copy in late:
                copy.wait()

            def mixed_step(j, carry):
                d_mixed[:, at(j * 512, 512)] = dot_rt(
                    d_branch[...], wo[pl.ds(2 * j, 2)].reshape(512, width)
                )
                return carry

            lax.fori_loop(0, width // 512, mixed_step, 0)

            def attn_back(rows):
                a = attn[rows, :].astype(F32)
                s = row_scale(a)
                u = a * s
                d = d_mixed[rows, :]
                dg_src[rows, :] = (d * u).astype(BF)
                g = d * gate[rows, :].astype(F32)
                da_src[rows, :] = (
                    s * (g - u * jnp.mean(g * u, axis=-1, keepdims=True))
                ).astype(BF)

            row_chunks(tok, attn_back)
            spread_a.start()
            spread_g.start()
            own = [
                k.keep(da_src.at[:, at(w * two, two)], a_land.at[w]),
                k.keep(dg_src.at[:, at(w * two, two)], g_land.at[at(w * tok, tok)]),
            ]

            for copy in own:
                copy.wait()

        pl.run_scoped(
            middle,
            pltpu.VMEM(wo_in.shape, BF),
            pltpu.VMEM((tok, width), F32),
            pltpu.VMEM((tok, width), BF),
            pltpu.VMEM((tok, width), BF),
            pltpu.VMEM((tok, width), BF),
            pltpu.VMEM((tok, width), F32),
            pltpu.VMEM((2, tok, width), BF),
        )
        def eight_way(plane, twin_index, landing, blocks, term):
            def side_step(j, carry):
                q = nth(j)
                side[q] = term(2 * q + other).astype(BF)
                twin(twin_index, j, side.at[q], landing.at[q]).start()
                return carry

            lax.fori_loop(0, CHIPS, side_step, 0)

            def own_step(j, carry):
                q = nth(j)
                v = term(2 * q + core)
                twin(twin_index, j, side.at[q], landing.at[q]).wait_recv()
                fetch(landing.at[q], tmp)
                v = v + tmp[...].astype(F32)

                @pl.when(j < 3)
                def _():
                    blocks[q] = v.astype(BF)

                for step, push in enumerate((plane.send_far, plane.send_x, plane.send_y)):
                    pl.when(j == step)(push)

                @pl.when(j == 3)
                def _():
                    acc[...] = v

                return carry

            lax.fori_loop(0, CHIPS, own_step, 0)
            for j in range(CHIPS):
                twin(twin_index, j, side.at[order[j]], landing.at[order[j]]).wait_send()

        eight_way(
            plane_out,
            3,
            twin_wo,
            stage_wo,
            lambda owner: dot_lt(mixed[:, at(owner * tok, tok)], d_branch[...]),
        )
        sum_ff[0].pass_on(0, add_ff)
        sum_ff[0].pass_on(1, add_ff)

        def attention(xn, d_qk, d_vg, state):
            state[...] = jnp.zeros_like(state)

            def heads(slope, qkv, sin, cols, decay, d_attn):
                loads = [
                    k.keep(qkv_in, qkv), k.keep(sin_in, sin), k.keep(slope_in, slope),
                    k.keep(cols_in, cols), k.keep(decay_in, decay),
                ]
                load_xn = k.keep(xn_in, xn)
                for copy in loads:
                    copy.wait()
                spread_a.finish()
                fetch(a_land, d_attn)

                def step(i, carry):
                    b = WIDE - 1 - i
                    rows = at(b * BLOCK, BLOCK)
                    mask = doc_mask(cols, rowdoc, decay, rows, b)
                    for h in range(2):
                        lanes = slice(h * HEAD, (h + 1) * HEAD)
                        key_lanes = slice(two + h * HEAD, two + (h + 1) * HEAD)
                        q = qkv[rows, lanes]
                        key = qkv[rows, key_lanes]
                        v = qkv[rows, 2 * two + h * HEAD : 2 * two + (h + 1) * HEAD]
                        d_o = d_attn[b, :, lanes]
                        factor = jnp.where(mask, decay[h], 0.0)
                        probs = (dot_rt(q, key) * factor).astype(BF)
                        d_probs = (dot_rt(d_o, v) * factor).astype(BF)
                        entry = cols[rows, 1 + h : 2 + h]
                        tail = cols[rows, 3 + h : 4 + h]
                        before = sin[b, h]
                        after = state[h]
                        after_bf = after.astype(BF)
                        tailed = (key.astype(F32) * tail).astype(BF)
                        entered = (q.astype(F32) * entry).astype(BF)
                        d_q = dot(d_probs, key) + entry * dot_rt(d_o, before)
                        d_k = dot_lt(d_probs, q) + tail * dot_rt(v, after_bf)
                        d_v = dot_lt(probs, d_o) + dot(tailed, after_bf)
                        d_qk[rows, lanes] = (d_q * slope[rows, lanes].astype(F32)).astype(BF)
                        d_qk[rows, key_lanes] = (d_k * slope[rows, key_lanes].astype(F32)).astype(BF)
                        d_vg[rows, lanes] = d_v.astype(BF)
                        state[h] = passing[pl.ds(2 * b + h, 1), :] * after + dot_lt(entered, d_o)
                    return carry

                lax.fori_loop(0, WIDE, step, 0)
                sum_ff[0].pass_on(2, add_ff)
                spread_g.finish()
                load_g = k.keep(g_land, d_vg.at[:, pl.ds(two, two)])
                load_g.wait()
                load_xn.wait()

            pl.run_scoped(
                heads,
                pltpu.VMEM(slope_in.shape, BF),
                pltpu.VMEM(qkv_in.shape, BF),
                pltpu.VMEM(sin_in.shape, BF),
                pltpu.VMEM(cols_in.shape, F32),
                pltpu.VMEM(decay_in.shape, F32),
                pltpu.VMEM((WIDE, tok, two), BF),
            )

            for m, (d_in, g_in) in enumerate(((d_qk, g_qk), (d_vg, g_vg))):

                def in_grad(s, carry):
                    left = xn[:, :, at(s * tok, tok)].reshape(WIDE * tok, tok)
                    g_in[s] = dot_lt(left, d_in[...]).astype(BF).reshape(NARROW, -1, 2 * two)
                    return carry

                lax.fori_loop(0, WIDE, in_grad, 0)
                sum_qk[m].start()

            plane_out.combine(add_half)
            sum_ff[1].pass_on(0, add_ff)
            sum_ff[1].pass_on(1, add_ff)
            g_wo[...] = acc[...].astype(BF).reshape(g_wo.shape)

            def spread_in(wqk, wvg):
                loads = [k.keep(wqk_in, wqk), k.keep(wvg_in, wvg)]
                for copy in loads:
                    copy.wait()

                def term(owner):
                    rows = at(owner * tok, tok)
                    return dot_rt(d_qk[rows, :], wqk[...].reshape(width, 2 * two)) + dot_rt(
                        d_vg[rows, :], wvg[...].reshape(width, 2 * two)
                    )

                eight_way(plane_in, 4, twin_xn_land, stage, term)

            pl.run_scoped(spread_in, pltpu.VMEM(wqk_in.shape, BF), pltpu.VMEM(wvg_in.shape, BF))

        pl.run_scoped(
            attention,
            pltpu.VMEM((WIDE, tok, width), BF),
            pltpu.VMEM((WIDE * tok, 2 * two), BF),
            pltpu.VMEM((WIDE * tok, 2 * two), BF),
            pltpu.VMEM((2, HEAD, HEAD), F32),
        )

        def last(
            x, x1, pair, three, three_ff, three_qk, ff_src, qk_src, ff_all, qk_all, ff_f32, w_f32, w_fo, tmp_qk
        ):
            add_qk = adder(tmp_qk)
            load_x, load_x1 = k.keep(x_in, x), k.keep(x1_in, x1)
            plane_in.combine(add_half)
            sum_ff[1].pass_on(2, add_ff)
            sum_qk[0].pass_on(0, add_qk)
            sum_qk[0].pass_on(1, add_qk)
            plane_out.finish()
            fetch(near.at[2], pair)
            for i in range(NARROW):
                rows = pl.ds(i * 64, 64)
                v = g_wo[i].astype(F32) + pair[0, rows, :].astype(F32) + pair[1, rows, :].astype(F32)
                g_wo[i] = v.astype(BF)
            sum_wo.start()

            def total(part, lands):
                return part.astype(F32) + lands[0].astype(F32) + lands[1].astype(F32)

            ff_turns = []
            for m, g_ff in enumerate((g_fv, g_fg)):
                sum_ff[m].finish(fetch, three_ff)
                for q in range(CHIPS):
                    ff_src[m, q] = total(g_ff[q, n], three_ff[:, q]).astype(BF)
                turn = Spread(
                    k,
                    lambda t, m=m: ff_src.at[m, lax.div(t, 2)],
                    lambda s, m=m: turn_ff.at[m, lax.div(s, 2)],
                    peers=CHIPS,
                )
                turn.start()
                ff_turns.append((turn, k.keep(ff_src.at[m, chip], turn_ff.at[m, chip])))
            sum_qk[0].pass_on(2, add_qk)
            sum_fo.finish(fetch, three.at[:, pl.ds(0, fo_rows)])
            own = fo_part(core, n)
            for r in range(0, fo_rows, 16):
                rows = pl.ds(r, 16)
                w_fo[rows, :] = total(own[rows, :], three[:, rows, :])
            stores = [k.keep(w_fo, gfo_o)]

            plane_sum(1, stage, base_res).finish()
            fetch(near.at[1], pair)
            load_x1.wait()

            def add_up(rows):
                v = x1[rows, :] + own_res[rows, :].astype(F32)
                v = v + pair[0, rows, :].astype(F32) + pair[1, rows, :].astype(F32)
                own_res[rows, :] = v.astype(BF)

            row_chunks(tok, add_up)
            stores.append(k.keep(own_res, result_o))
            sum_qk[1].pass_on(0, add_qk)
            sum_qk[1].pass_on(1, add_qk)
            load_x.wait()
            plane_in.finish()
            fetch(near.at[3], pair)

            def input_back(rows):
                g = acc[rows, :] + pair[0, rows, :].astype(F32) + pair[1, rows, :].astype(F32)
                v = x[rows, :].astype(F32)
                r = row_scale(v)
                u = v * r
                d_x1[rows, :] = d_x1[rows, :] + r * (
                    g - u * jnp.mean(g * u, axis=-1, keepdims=True)
                )

            row_chunks(tok, input_back)
            stores.append(k.keep(d_x1, dx_o))
            for m, (turn, copy) in enumerate(ff_turns):
                turn.finish()
                copy.wait()
                fetch(turn_ff.at[m], ff_all)
                for q in range(CHIPS):
                    ff_f32[m, :, q * ff : (q + 1) * ff] = ff_all[q].astype(F32)
                stores.append(k.keep(ff_f32.at[m], (gfv_o, gfg_o)[m]))
            qk_turns = []
            for m, g_in in enumerate((g_qk, g_vg)):
                if m == 1:
                    sum_qk[1].pass_on(2, add_qk)
                    sum_wo.pass_on(0, add_wo)
                    sum_wo.pass_on(1, add_wo)
                sum_qk[m].finish(fetch, three_qk)
                for s in range(WIDE):
                    qk_src[m, s] = total(g_in[s, n], three_qk[:, s]).astype(BF)
                turn = Spread(
                    k,
                    lambda t, m=m: qk_src.at[m, t],
                    lambda s, m=m: turn_qk.at[m, s],
                )
                turn.start()
                qk_turns.append((turn, k.keep(qk_src.at[m, w], turn_qk.at[m, w])))
            sum_wo.pass_on(2, add_wo)
            for m, (turn, copy) in enumerate(qk_turns):
                turn.finish()
                copy.wait()
                fetch(turn_qk.at[m], qk_all)
                for s in range(WIDE):
                    lanes = slice(s * two, (s + 1) * two)
                    w_f32[2 * m, :, lanes] = qk_all[s, :, 0:two].astype(F32)
                    w_f32[2 * m + 1, :, lanes] = qk_all[s, :, two:].astype(F32)
                outs = ((gq_o, gk_o), (gv_o, gg_o))[m]
                stores.append(k.keep(w_f32.at[2 * m], outs[0]))
                stores.append(k.keep(w_f32.at[2 * m + 1], outs[1]))
            sum_wo.finish(fetch, three.at[:, pl.ds(0, 64)])
            w_f32[4] = total(g_wo[n], three[:, 0:64, :])
            stores.append(k.keep(w_f32.at[4], go_o))
            for copy in stores:
                copy.wait()
            plane_in.drain()
            plane_out.drain()
            turns = [turn for turn, copy in ff_turns + qk_turns]
            for moved in (*lines, *planes, *twins, *spreads, *spread_ff):
                moved.drain()
            for sums in (sum_fo, sum_wo, *sum_ff, *sum_qk, spread_a, spread_g, *turns):
                sums.drain()

        pl.run_scoped(
            last,
            pltpu.VMEM((tok, width), BF),
            pltpu.VMEM((tok, width), F32),
            pltpu.VMEM((2, tok, width), BF),
            pltpu.VMEM((2, tok, width), BF),
            pltpu.VMEM((2, *land_ff.shape[2:]), BF),
            pltpu.VMEM((2, *land_qk.shape[2:]), BF),
            pltpu.VMEM((2, CHIPS, 64, ff), BF),
            pltpu.VMEM((2, WIDE, 64, 2 * two), BF),
            pltpu.VMEM((CHIPS, 64, ff), BF),
            pltpu.VMEM((WIDE, 64, 2 * two), BF),
            pltpu.VMEM((2, 64, CHIPS * ff), F32),
            pltpu.VMEM((5, 64, width), F32),
            pltpu.VMEM((fo_rows, width), F32),
            pltpu.VMEM((WIDE, 64, 2 * two), BF),
        )

    pl.run_scoped(
        rest,
        pltpu.VMEM((tok, width), F32),
        pltpu.VMEM((tok, width), BF),
        pltpu.VMEM((tok, width), BF),
        pltpu.VMEM((tok, width), BF),
        pltpu.VMEM((tok, width), BF),
        pltpu.VMEM((CHIPS, tok, width), BF),
        pltpu.VMEM((CHIPS, tok, width), BF),
        pltpu.VMEM((NARROW, 64, width), BF),
        pltpu.VMEM((WIDE, NARROW, 64, 2 * two), BF),
        pltpu.VMEM((WIDE, NARROW, 64, 2 * two), BF),
    )
    assert k.count <= send.shape[0] and k.kept <= here.shape[0], (k.count, k.kept)


def layer(tokens, weights, dy, cols, rowdoc, passing, decay):
    tok, width = tokens.shape
    shard = weights[0].shape[0]
    ff = weights[5].shape[1] // CHIPS
    fo_rows = weights[7].shape[0]
    full = WIDE * tok
    two = 2 * HEAD

    def arr(*shape, dtype=BF):
        return jax.ShapeDtypeStruct(shape, dtype)

    results = (
        arr(tok, width),
        arr(tok, width, dtype=F32),
        *[arr(shard, width, dtype=F32)] * 5,
        arr(shard, CHIPS * ff, dtype=F32),
        arr(shard, CHIPS * ff, dtype=F32),
        arr(fo_rows, width, dtype=F32),
    )
    held = (
        arr(WIDE, tok, width),
        arr(WIDE, NARROW, shard, 2 * two),
        arr(WIDE, NARROW, shard, 2 * two),
        arr(WIDE, NARROW, shard, width),
        arr(CHIPS, 2, NARROW, shard, ff),
        arr(CHIPS, 2, NARROW, shard, ff),
        arr(2, NARROW, fo_rows, width),
        arr(CHIPS, tok, width),
        arr(full, 2 * two),
        arr(full, 3 * two),
        arr(WIDE, 2, HEAD, HEAD),
        arr(tok, width),
        arr(tok, width),
        arr(tok, width),
        arr(tok, width, dtype=F32),
        arr(CHIPS, tok, width),
    )
    landings = (
        arr(4, 2, tok // 2, width),
        arr(4, 2, tok, width),
        arr(NARROW, fo_rows, width),
        arr(2, CHIPS, NARROW, shard, ff),
        arr(CHIPS, tok, width),
        arr(CHIPS, tok, width),
        arr(5, fo_rows, width),
        arr(2, 5, CHIPS, shard, ff),
        arr(5, shard, width),
        arr(2, 5, WIDE, shard, 2 * two),
        arr(2, CHIPS, shard, ff),
        arr(2, WIDE, shard, 2 * two),
        arr(WIDE, tok, two),
        arr(full, two),
    )
    out_shape = results + held + landings
    outs = pl.pallas_call(
        layer_kernel,
        out_shape=out_shape,
        in_specs=[ANY] * 12 + [VMEM] * 2,
        out_specs=(ANY,) * len(out_shape),
        scratch_shapes=[
            pltpu.VMEM((ff, width), BF),
            pltpu.VMEM((CHIPS, NARROW, shard, ff), BF),
            pltpu.VMEM((CHIPS, NARROW, shard, ff), BF),
            pltpu.VMEM((CHIPS, tok, width), BF),
            pltpu.VMEM((tok, width), F32),
            pltpu.VMEM((tok, width), BF),
            pltpu.VMEM((tok, width), BF),
            pltpu.VMEM((CHIPS, shard, ff), BF),
            pltpu.SemaphoreType.DMA((272,)),
            pltpu.SemaphoreType.DMA((272,)),
            pltpu.SemaphoreType.DMA((96,)),
        ],
        compiler_params=pltpu.CompilerParams(
            collective_id=0, has_side_effects=True, vmem_limit_bytes=63 * 2**20
        ),
        cost_estimate=pl.CostEstimate(flops=8 * 10**10, bytes_accessed=3 * 10**8, transcendentals=0),
    )(tokens, *weights, dy, cols, decay, rowdoc, passing)
    return outs[: len(results)]


def prepare(doc_starts, length):
    starts = lax.dynamic_slice_in_dim(doc_starts, lax.axis_index("narrow"), 1, 0)[0]
    blocks = length // BLOCK
    positions = jnp.arange(length, dtype=jnp.int32)
    doc_ids = jnp.sum((starts[None, :] <= positions[:, None]).astype(jnp.int32), axis=1)
    doc_ids = doc_ids.reshape(blocks, BLOCK).astype(F32)
    firsts = jnp.arange(blocks, dtype=jnp.int32) * BLOCK - 1
    prev_ids = jnp.sum((starts[None, :] <= firsts[:, None]).astype(jnp.int32), axis=1).astype(F32)
    slopes = lax.dynamic_slice_in_dim(head_slopes(), lax.axis_index("wide") * 2, 2, 0)
    offsets = jnp.arange(BLOCK, dtype=F32)
    lags = offsets[:, None] - offsets[None, :]
    decay = jnp.exp(-slopes[:, None, None] * jnp.maximum(lags, 0.0)[None])
    continues = (doc_ids == prev_ids[:, None]).astype(F32)
    entry = continues[..., None] * jnp.exp(-slopes[None, :] * (offsets[:, None] + 1.0))
    tail = (doc_ids == doc_ids[:, -1:]).astype(F32)[..., None] * jnp.exp(
        -slopes[None, :] * (BLOCK - 1.0 - offsets)[:, None]
    )
    passing = continues[:, -1:] * jnp.exp(-slopes * BLOCK)
    cols = jnp.concatenate([doc_ids[..., None], entry, tail], axis=-1).reshape(length, 5)
    cols = jnp.pad(cols, ((0, 0), (0, HEAD - 5)))
    passing = jnp.broadcast_to(passing.reshape(-1, 1), (2 * blocks, HEAD))
    return cols, doc_ids, passing, decay


def local_box(tokens, doc_starts, wq, wk, wv, wg, wo, fv, fg, fo, cotangent):
    tables = prepare(doc_starts, WIDE * tokens.shape[1])
    weights = (wq, wk, wv, wg, wo, fv, fg, fo)
    outs = layer(tokens[0], weights, cotangent[0], *tables)
    return (outs[0][None], outs[1][None]) + tuple(outs[2:])


def solution(mesh):
    box = (mesh.shape["wide"], mesh.shape["narrow"]) == (WIDE, NARROW)
    tok = P("narrow", "wide", None)
    row = P(BOTH, None)
    return jax.shard_map(
        local_box if box else local,
        mesh=mesh,
        in_specs=(tok, P()) + (row,) * 8 + (tok,),
        out_specs=(tok, tok) + (row,) * 8,
        check_vma=False,
    )
```

```python
import jax
import jax.numpy as jnp
from jax import lax
from jax.experimental import pallas as pl
from jax.experimental.pallas import tpu as pltpu
from jax.sharding import PartitionSpec as P

HEADS = 16
HEAD = 128
BLOCK = 256
LAYERS = 16
LAYER = 12

EPS = 1e-06
BOTH = ("wide", "narrow")
BF = jnp.bfloat16
F32 = jnp.float32


def normalize(values):
    scale = lax.rsqrt(jnp.mean(values * values, axis=-1, keepdims=True) + EPS)
    return (values * scale, scale)


def normalize_back(normed, scale, grad):
    return scale * (grad - normed * jnp.mean(grad * normed, axis=-1, keepdims=True))


def silu_slope(values):
    sigma = jax.nn.sigmoid(values)
    return sigma * (1.0 + values * (1.0 - sigma))


def matmul(left, right):
    return jnp.dot(left, right, preferred_element_type=F32)


def matmul_right_t(left, right):
    return lax.dot_general(left, right, (((1,), (1,)), ((), ())), preferred_element_type=F32)


def weight_grad(left, right):
    return lax.dot_general(left, right, (((0,), (0,)), ((), ())), preferred_element_type=F32)


def ein(spec, left, right):
    return jnp.einsum(spec, left, right, preferred_element_type=F32)


def head_slopes():
    order = jnp.arange(HEADS, dtype=F32)
    return jnp.exp2(-8.0 * (order + 1.0) / HEADS) * (1.0 - LAYER / (LAYERS - 1) + 1e-05)


def local(
    tokens,
    doc_starts,
    query_weight,
    key_weight,
    value_weight,
    gate_weight,
    out_weight,
    ffn_value_weight,
    ffn_gate_weight,
    ffn_out_weight,
    cotangent,
):
    wide, narrow = lax.axis_size("wide"), lax.axis_size("narrow")
    rows_here, width = tokens.shape[1:]
    length = rows_here * wide
    blocks = length // BLOCK
    heads_here = HEADS // wide
    shard = query_weight.shape[0]

    def reorder(values):
        return values.reshape(-1, wide, narrow, shard).swapaxes(1, 2).reshape(-1, width)

    def restore(values):
        return values.reshape(-1, narrow, wide, shard).swapaxes(1, 2).reshape(-1, width)

    def columns(weight):
        part = lax.all_to_all(weight, "wide", split_axis=1, concat_axis=0, tiled=True)
        return lax.all_gather(part, "narrow", axis=0, tiled=True)

    def gather_rows(values):
        return lax.all_gather(values, "wide", axis=0, tiled=True)

    def scatter_rows(values):
        return lax.psum_scatter(
            values.astype(BF), "wide", scatter_dimension=0, tiled=True
        ).astype(F32)

    def to_tokens(values):
        return lax.all_to_all(values, "wide", split_axis=0, concat_axis=1, tiled=True)

    def to_heads(values):
        return lax.all_to_all(values, "wide", split_axis=1, concat_axis=0, tiled=True)

    def column_sums(grad):
        part = lax.psum_scatter(grad.astype(BF), "narrow", scatter_dimension=0, tiled=True)
        return lax.all_to_all(part, "wide", split_axis=0, concat_axis=1, tiled=True).astype(F32)

    w_query, w_key, w_value, w_gate = map(
        columns, (query_weight, key_weight, value_weight, gate_weight)
    )
    w_out = lax.all_gather(out_weight, BOTH, axis=0, tiled=True)
    w_fval, w_fgate = map(columns, (ffn_value_weight, ffn_gate_weight))
    w_fout = lax.all_gather(ffn_out_weight, "narrow", axis=0, tiled=True)

    starts = lax.dynamic_slice_in_dim(doc_starts, lax.axis_index("narrow"), 1, 0)[0]
    positions = jnp.arange(length, dtype=jnp.int32)
    doc_ids = jnp.sum((starts[None, :] <= positions[:, None]).astype(jnp.int32), axis=1)
    doc_ids = doc_ids.reshape(blocks, BLOCK)
    firsts = jnp.arange(blocks, dtype=jnp.int32) * BLOCK - 1
    prev_ids = jnp.sum((starts[None, :] <= firsts[:, None]).astype(jnp.int32), axis=1)
    slopes = lax.dynamic_slice_in_dim(
        head_slopes(), lax.axis_index("wide") * heads_here, heads_here, 0
    )
    offsets = jnp.arange(BLOCK, dtype=F32)
    lags = offsets[:, None] - offsets[None, :]
    decays = jnp.exp(-slopes[:, None, None] * jnp.maximum(lags, 0.0)[None])
    within = (doc_ids[:, :, None] == doc_ids[:, None, :]) & (lags >= 0.0)
    block_mask = jnp.where(within[:, None], decays[None], 0.0)
    continues = (doc_ids == prev_ids[:, None]).astype(F32)
    entry_scale = continues[..., None] * jnp.exp(-slopes[None, :] * (offsets[:, None] + 1.0))
    tail_scale = (doc_ids == doc_ids[:, -1:]).astype(F32)[..., None] * jnp.exp(
        -slopes[None, :] * (BLOCK - 1.0 - offsets)[:, None]
    )
    passing = continues[:, -1:] * jnp.exp(-slopes * BLOCK)

    def split_heads(values):
        return values.reshape(blocks, BLOCK, heads_here, HEAD)

    inputs = tokens[0].astype(F32)
    normed, in_scale = normalize(inputs)
    normed_bf = gather_rows(reorder(normed.astype(BF)))
    query_pre = matmul(normed_bf, w_query)
    key_pre = matmul(normed_bf, w_key)
    queries = split_heads(jax.nn.silu(query_pre).astype(BF))
    keys = split_heads(jax.nn.silu(key_pre).astype(BF))
    values = split_heads(matmul(normed_bf, w_value).astype(BF))
    gate = matmul(normed_bf, w_gate)
    scores = ein("bihe,bjhe->bhij", queries, keys)
    probs = (scores * block_mask).astype(BF)
    inner = ein("bhij,bjhe->bihe", probs, values)
    tail_keys = (keys.astype(F32) * tail_scale[..., None]).astype(BF)
    fresh = ein("bjhe,bjhf->bhef", tail_keys, values)
    state = jnp.zeros((heads_here, HEAD, HEAD), F32)
    entering = []
    for b in range(blocks):
        entering.append(state)
        state = passing[b][:, None, None] * state + fresh[b]
    block_in = jnp.stack(entering).astype(BF)
    across = entry_scale[..., None] * ein("bihe,bhef->bihf", queries, block_in)
    attention = (inner + across).reshape(query_pre.shape)

    attn_tok = to_tokens(attention)
    gate_tok = to_tokens(gate)
    attn_n, attn_scale = normalize(attn_tok)
    mixed = (attn_n * gate_tok).astype(BF)
    middle = inputs + matmul(mixed, w_out)
    middle_n, middle_scale = normalize(middle)
    middle_bf = gather_rows(reorder(middle_n.astype(BF)))
    ffn_val = matmul(middle_bf, w_fval)
    ffn_gat = matmul(middle_bf, w_fgate)
    ffn_mix = (ffn_val * ffn_gat).astype(BF)
    result = middle + scatter_rows(matmul(ffn_mix, w_fout))

    upstream = cotangent[0]
    up_all = gather_rows(upstream)
    grad_fout = weight_grad(ffn_mix, up_all)
    d_mix = matmul_right_t(up_all, w_fout)
    d_val = (d_mix * ffn_gat).astype(BF)
    d_gat = (d_mix * ffn_val).astype(BF)
    grad_fval = weight_grad(middle_bf, d_val)
    grad_fgate = weight_grad(middle_bf, d_gat)
    d_middle_n = restore(
        scatter_rows(matmul_right_t(d_val, w_fval) + matmul_right_t(d_gat, w_fgate))
    )
    d_middle = upstream.astype(F32) + normalize_back(middle_n, middle_scale, d_middle_n)
    d_branch = d_middle.astype(BF)
    grad_out = weight_grad(mixed, d_branch)
    d_mixed = matmul_right_t(d_branch, w_out)
    d_gate = to_heads((d_mixed * attn_n).astype(BF))
    d_attn = to_heads(normalize_back(attn_n, attn_scale, d_mixed * gate_tok).astype(BF))

    d_heads = split_heads(d_attn)
    d_probs = ein("bihe,bjhe->bhij", d_heads, values)
    d_scores = (d_probs * block_mask).astype(BF)
    d_query = ein("bhij,bjhe->bihe", d_scores, keys)
    d_key = ein("bhij,bihe->bjhe", d_scores, queries)
    d_value = ein("bhij,bihe->bjhe", probs, d_heads)
    d_query = d_query + entry_scale[..., None] * ein("bihf,bhef->bihe", d_heads, block_in)
    entry_queries = (queries.astype(F32) * entry_scale[..., None]).astype(BF)
    grad_in = ein("bihe,bihf->bhef", entry_queries, d_heads)
    state = jnp.zeros((heads_here, HEAD, HEAD), F32)
    leaving = [None] * blocks
    for b in reversed(range(blocks)):
        leaving[b] = state
        state = passing[b][:, None, None] * state + grad_in[b]
    block_out = jnp.stack(leaving).astype(BF)
    d_key = d_key + tail_scale[..., None] * ein("bjhf,bhef->bjhe", values, block_out)
    d_value = d_value + ein("bjhe,bhef->bjhf", tail_keys, block_out)
    dq_pre = (d_query.reshape(query_pre.shape) * silu_slope(query_pre)).astype(BF)
    dk_pre = (d_key.reshape(key_pre.shape) * silu_slope(key_pre)).astype(BF)
    dv_pre = d_value.reshape(query_pre.shape).astype(BF)
    grad_query = weight_grad(normed_bf, dq_pre)
    grad_key = weight_grad(normed_bf, dk_pre)
    grad_value = weight_grad(normed_bf, dv_pre)
    grad_gate = weight_grad(normed_bf, d_gate)
    d_normed = restore(
        scatter_rows(
            matmul_right_t(dq_pre, w_query)
            + matmul_right_t(dk_pre, w_key)
            + matmul_right_t(dv_pre, w_value)
            + matmul_right_t(d_gate, w_gate)
        )
    )
    d_inputs = d_middle + normalize_back(normed, in_scale, d_normed)
    return (
        result.astype(BF)[None],
        d_inputs[None],
        column_sums(grad_query),
        column_sums(grad_key),
        column_sums(grad_value),
        column_sums(grad_gate),
        lax.psum_scatter(grad_out.astype(BF), BOTH, scatter_dimension=0, tiled=True).astype(F32),
        column_sums(grad_fval),
        column_sums(grad_fgate),
        lax.psum_scatter(grad_fout.astype(BF), "narrow", scatter_dimension=0, tiled=True).astype(
            F32
        ),
    )


MESH = pl.DeviceIdType.MESH
ANY = pl.BlockSpec(memory_space=pl.ANY)
VMEM = pl.BlockSpec(memory_space=pltpu.VMEM)
WIDE, NARROW = 8, 4
CHIPS = WIDE // 2


def dot(left, right):
    return jnp.dot(left, right, preferred_element_type=F32)


def dot_rt(left, right):
    return lax.dot_general(left, right, (((1,), (1,)), ((), ())), preferred_element_type=F32)


def dot_lt(left, right):
    return lax.dot_general(left, right, (((0,), (0,)), ((), ())), preferred_element_type=F32)


def at(start, size):
    return pl.ds(pl.multiple_of(start, size), size)


class Links:
    def __init__(self, send, recv, here):
        self.send, self.recv, self.here = send, recv, here
        self.count, self.kept = 0, 1
        w = lax.axis_index("wide")
        n = lax.axis_index("narrow")
        self.w, self.n = w, n
        self.core = lax.rem(w, 2)
        self.chip = lax.div(w, 2)
        x, y = lax.rem(self.chip, 2), lax.div(self.chip, 2)
        self.wx = w + 2 - 4 * x
        self.wy = w + 4 - 8 * y
        self.wd = w + 6 - 4 * x - 8 * y
        self.ws = w + 1 - 2 * self.core
        self.px = self.chip + 1 - 2 * x
        self.py = self.chip + 2 - 4 * y
        self.pd = 3 - self.chip
        self.mid = lax.rem(lax.div(n + 1, 2), 2)
        self.pair = n + 1 - 2 * lax.rem(n, 2)
        self.cross = 2 - lax.div(n, 2)
        self.far = 3 - 3 * lax.div(n, 2)
        self.end_to = 3 * lax.rem(n + 1, 2)
        self.end_part = lax.rem(2 * n, 3) + 3 * lax.div(n, 3)

    def greet(self):
        barrier = pltpu.get_barrier_semaphore()
        for d in range(1, WIDE):
            pl.semaphore_signal(
                barrier, inc=1, device_id=(lax.rem(self.w + d, WIDE), self.n), device_id_type=MESH
            )
        for d in range(1, NARROW):
            pl.semaphore_signal(
                barrier, inc=1, device_id=(self.w, lax.rem(self.n + d, NARROW)), device_id_type=MESH
            )

    def met(self):
        pl.semaphore_wait(pltpu.get_barrier_semaphore(), WIDE + NARROW - 2)

    def take(self, number):
        base = self.count
        self.count += number
        return base

    def remote(self, src, dst, send, recv, wide=None, narrow=None):
        return pltpu.make_async_remote_copy(
            src_ref=src,
            dst_ref=dst,
            send_sem=self.send.at[send],
            recv_sem=self.recv.at[recv],
            device_id=(self.w if wide is None else wide, self.n if narrow is None else narrow),
            device_id_type=MESH,
        )

    def arrived(self, ref, recv):
        self.remote(ref, ref, recv, recv, wide=self.ws).wait_recv()

    def keep(self, src, dst):
        copy = pltpu.make_async_copy(src, dst, self.here.at[self.kept])
        self.kept += 1
        copy.start()
        return copy


class Line:
    def __init__(self, links, part):
        self.links, self.part = links, part
        self.base = links.take(5)

    def copy(self, index):
        k, b = self.links, self.base
        which, to = (
            (k.n, k.pair),
            (k.n, k.cross),
            (k.pair, k.cross),
            (k.cross, k.pair),
            (k.far, k.pair),
        )[index]
        ref = self.part(which)
        return k.remote(ref, ref, b + index, b + which, narrow=to)

    def start(self):
        self.start_away()
        pl.when(self.links.mid == 1)(lambda: self.copy(0).start())

    def start_away(self):
        pl.when(self.links.mid == 1)(lambda: self.copy(1).start())
        pl.when(self.links.mid == 0)(lambda: self.copy(0).start())

    def start_home(self):
        pl.when(self.links.mid == 1)(lambda: self.copy(0).start())

    def wait(self, index):
        self.links.arrived(self.part(index), self.base + index)

    def forward(self):
        @pl.when(self.links.mid == 1)
        def _():
            self.wait(self.links.cross)
            self.copy(3).start()
            self.wait(self.links.pair)
            self.copy(2).start()

    def forward_far(self):
        @pl.when(self.links.mid == 1)
        def _():
            self.wait(self.links.far)
            self.copy(4).start()

    def finish(self, then=lambda place: None, late=lambda: None):
        k = self.links
        then(0)
        for place, index in enumerate((k.pair, k.cross, k.far)):
            if place == 2:
                late()
            pl.when(k.mid == 0)(lambda index=index: self.wait(index))
            then(place + 1)

    def drain(self):
        self.copy(0).wait_send()

        @pl.when(self.links.mid == 1)
        def _():
            for index in range(1, 5):
                self.copy(index).wait_send()


class Plane:
    def __init__(self, links, slot):
        self.links, self.slot = links, slot
        self.base = links.take(6)

    def copy(self, index):
        k, b = self.links, self.base
        owner, half, to = (
            (k.w, 0, k.wx),
            (k.w, 1, k.wy),
            (k.w, 1, k.wx),
            (k.w, 0, k.wy),
            (k.wx, 0, k.wy),
            (k.wy, 1, k.wx),
        )[index]
        ref = self.slot(owner, half)
        return k.remote(ref, ref, b + index, b + index, wide=to)

    def start(self):
        for index in range(4):
            self.copy(index).start()

    def forward(self):
        k, b, slot = self.links, self.base, self.slot
        k.arrived(slot(k.wx, 0), b)
        self.copy(4).start()
        k.arrived(slot(k.wy, 1), b + 1)
        self.copy(5).start()

    def finish_near(self):
        k, b, slot = self.links, self.base, self.slot
        k.arrived(slot(k.wx, 1), b + 2)
        k.arrived(slot(k.wy, 0), b + 3)

    def finish_far(self):
        k, b, slot = self.links, self.base, self.slot
        k.arrived(slot(k.wd, 0), b + 4)
        k.arrived(slot(k.wd, 1), b + 5)

    def drain(self):
        for index in range(6):
            self.copy(index).wait_send()


class Sibling:
    def __init__(self, links, block, twin, number):
        self.links, self.block, self.twin, self.number = links, block, twin, number
        self.base = links.take(number)

    def copy(self, index):
        k, b = self.links, self.base + index
        ref = self.block(index)
        return k.remote(ref, ref, b, b, wide=k.ws)

    def send(self, index):
        self.copy(index).start()

    def wait(self, index):
        self.links.arrived(self.twin(index), self.base + index)

    def drain(self):
        for index in range(self.number):
            self.copy(index).wait_send()


class Spread:
    def __init__(self, links, src, dst, peers=WIDE):
        self.links, self.src, self.dst = links, src, dst
        self.step = 1 if peers == WIDE else 2
        self.base = links.take(WIDE)

    def distances(self):
        return range(self.step, WIDE, self.step)

    def copy(self, d, to):
        k, b = self.links, self.base + d
        return k.remote(self.src(to), self.dst(k.w), b, b, wide=to)

    def start(self):
        for d in self.distances():
            self.copy(d, lax.rem(self.links.w + d, WIDE)).start()

    def finish(self):
        k = self.links
        for d in self.distances():
            k.arrived(self.dst(lax.rem(k.w + WIDE - d, WIDE)), self.base + d)

    def drain(self):
        for d in self.distances():
            self.copy(d, lax.rem(self.links.w + d, WIDE)).wait_send()


def row_scale(values):
    return lax.rsqrt(jnp.mean(values * values, axis=-1, keepdims=True) + EPS)


def row_chunks(rows, body, size=32):
    def step(r, carry):
        body(at(r * size, size))
        return carry

    lax.fori_loop(0, rows // size, step, 0)


class LineSum:
    def __init__(self, links, part, land):
        self.links, self.part, self.land = links, part, land
        self.base = links.take(5)
        self.onward = links.pair + links.mid * (links.cross - links.pair)

    def copy(self, index):
        k, b = self.links, self.base
        which, slot, to = (
            (k.far, 3 * k.mid, self.onward),
            (k.cross, 1 + 3 * k.mid, self.onward),
            (k.pair, 2 - 2 * k.mid, k.pair),
        )[index]
        return k.remote(self.part(which), self.land(slot), b + index, b + slot, narrow=to)

    def begin(self, index):
        pl.when(self.links.mid == 0)(lambda: self.copy(index).start())

    def start(self):
        for index in range(3):
            self.begin(index)

    def wait(self, slot):
        self.links.arrived(self.land(slot), self.base + slot)

    def pass_on(self, index, add):
        k = self.links
        which, slot = ((k.far, 0), (k.cross, 1), (k.pair, 3))[index]

        @pl.when(k.mid == 1)
        def _():
            self.wait(slot)
            add(self.part(which), self.land(slot))
            self.copy(index).start()

    def finish(self, fetch, spots):
        k = self.links
        pl.when(k.mid == 0)(lambda: self.wait(0))

        @pl.when(k.mid == 1)
        def _():
            self.wait(2)
            self.wait(4)
            fetch(self.land(4), spots.at[1])

        fetch(self.land(2 * k.mid), spots.at[0])

        @pl.when(k.mid == 0)
        def _():
            spots[1] = jnp.zeros(spots.shape[1:], spots.dtype)

    def drain(self):
        for index in range(3):
            self.copy(index).wait_send()


class PlaneSum:
    def __init__(self, links, block, corner, near, half, base=None, late=None):
        self.late = late
        self.links, self.block, self.corner, self.near, self.half = links, block, corner, near, half
        self.base = links.take(6) if base is None else base

    def rows(self, h):
        return pl.ds(h * self.half, self.half)

    def copy(self, index):
        k = self.links
        chip, h, land, to = (
            (k.pd, 0, self.corner.at[0], k.wx),
            (k.pd, 1, self.corner.at[1], k.wy),
            (k.px, 0, self.near.at[0, self.rows(0)], k.wx),
            (k.py, 1, self.near.at[1, self.rows(1)], k.wy),
            (k.px, 1, self.near.at[0, self.rows(1)], k.wx),
            (k.py, 0, self.near.at[1, self.rows(0)], k.wy),
        )[index]
        sem = self.base + index
        src = self.block(chip).at[self.rows(h)]
        if self.late is not None and index >= 4:
            src = self.late.at[self.rows(index - 4)]
        return k.remote(src, land, sem, sem, wide=to)

    def send_far(self):
        self.copy(0).start()
        self.copy(1).start()

    def send_x(self):
        self.copy(2).start()

    def send_y(self):
        self.copy(3).start()

    def combine(self, add):
        k = self.links
        for index, corner, chip, h in ((4, 1, k.px, 1), (5, 0, k.py, 0)):
            self.copy(corner).wait_recv()
            own = self.block(chip).at[self.rows(h)]
            to = own if self.late is None else self.late.at[self.rows(index - 4)]
            add(to, self.corner.at[corner], own)
            self.copy(index).start()

    def finish(self):
        for index in range(2, 6):
            self.copy(index).wait_recv()

    def drain(self, first=0, last=6):
        for index in range(first, last):
            self.copy(index).wait_send()


def layer_kernel(
    x_in, wq, wk, wv, wg, wo, fv, fg, fo, dy_arg, starts,
    result_o, dx_o, go_o, gfo_o, turn_ff, turn_qk,
    xn_in, wqk_in, wvg_in, wo_in, fv_in, fg_in, fo_in, dy_in, slope_in, qkv_in, sin_in, attn_in,
    gate_in, mixed_in, x1_in, x1n_in,
    corner, near, twin_fo_land, twin_ff, twin_wo, twin_xn_land, land_fo, land_ff, land_wo, land_qk,
    a_land, g_land,
    g_fo, g_fv, g_fg, stage, acc, tmp, tmp_ff,
    send, recv, here,
):
    k = Links(send, recv, here)
    w, n, core, chip = k.w, k.n, k.core, k.chip
    other = 1 - core
    tok, width = acc.shape
    ff = g_fv.shape[-1]
    fo_rows = land_fo.shape[1]
    half = tok // 2
    two = 2 * HEAD
    order = (k.pd, k.px, k.py, chip)
    begins = [starts[n, j] for j in range(starts.shape[1])]

    def docs(positions):
        return sum((positions >= begin).astype(jnp.int32) for begin in begins)

    def slope(h):
        head = (2 * w + h + 1).astype(F32)
        rate = 1.0 - LAYER / (LAYERS - 1) + 1e-05
        return jnp.exp2(jnp.full((1, HEAD), -8.0 / HEADS, F32) * head)[:, 0:1] * rate

    def fill_decay(decay):
        i = lax.broadcasted_iota(jnp.int32, (BLOCK, BLOCK), 0)
        j = lax.broadcasted_iota(jnp.int32, (BLOCK, BLOCK), 1)
        lags = jnp.maximum(i - j, 0).astype(F32)
        for h in range(2):
            decay[h] = jnp.exp(-slope(h) * lags)

    def block_tables(b):
        first = b * BLOCK
        i = lax.broadcasted_iota(jnp.int32, (BLOCK, 1), 0)
        j = lax.broadcasted_iota(jnp.int32, (1, BLOCK), 1)
        ids = docs(first + i)
        mask = (ids == docs(first + j)) & (i >= j)
        before, at_end = docs(first - 1), docs(first + BLOCK - 1)
        steps = i.astype(F32)
        factors = []
        for h in range(2):
            rate = slope(h)
            entry = jnp.where(ids == before, jnp.exp(-rate * (steps + 1.0)), 0.0)
            tail = jnp.where(ids == at_end, jnp.exp(-rate * (BLOCK - 1.0 - steps)), 0.0)
            through = jnp.where(before == at_end, jnp.exp(-rate * BLOCK), 0.0)
            factors.append((entry, tail, through))
        return mask, factors

    def nth(j):
        flip_x, flip_y = 1 - lax.div(j, 2), 1 - lax.rem(j, 2)
        return (
            chip + flip_x * (1 - 2 * lax.rem(chip, 2)) + flip_y * (2 - 4 * lax.div(chip, 2))
        )

    def fetch(src, dst):
        copy = pltpu.make_async_copy(src, dst, here.at[0])
        copy.start()
        copy.wait()

    def adder(spot):
        def add(to, land, own=None):
            fetch(land, spot)
            own = to if own is None else own
            to[...] = (own[...].astype(F32) + spot[...].astype(F32)).astype(BF)

        return add

    add_half = adder(tmp.at[pl.ds(0, half)])
    add_fo = adder(tmp.at[pl.ds(0, fo_rows)])
    add_wo = adder(tmp.at[pl.ds(0, 64)])
    add_ff = adder(tmp_ff)
    def fo_part(owner, i):
        return g_fo.at[pl.ds(pl.multiple_of((owner * NARROW + i) * fo_rows, 16), fo_rows)]

    sum_fo = LineSum(k, lambda i: fo_part(core, i), lambda s: land_fo.at[s])
    sum_ff = [
        LineSum(k, lambda i, g=g: g.at[:, i], lambda s, m=m: land_ff.at[m, s])
        for m, g in enumerate((g_fv, g_fg))
    ]
    def plane_sum(m, blocks, base=None, late=None):
        return PlaneSum(k, lambda q: blocks.at[q], corner.at[m], near.at[m], half, base, late)

    plane_mid, plane_in = (plane_sum(m, stage) for m in (0, 3))
    base_res = k.take(6)
    twin_base = k.take(4 * 5)

    def twin(m, j, src, dst):
        sem = twin_base + 4 * m + j
        return k.remote(src, dst, sem, sem, wide=k.ws)

    def wide_cols(index):
        return at(index * two, two)

    def chip_cols(index):
        return pl.ds(pl.multiple_of(index * ff, 128), ff)

    projections = ((wq, wqk_in), (wk, wqk_in), (wv, wvg_in), (wg, wvg_in))
    lines = line_out, line_qk, line_vg, line_fv, line_fg, line_fo = (
        Line(k, lambda i: wo_in.at[w, i]),
        Line(k, lambda i: wqk_in.at[:, i]),
        Line(k, lambda i: wvg_in.at[:, i]),
        Line(k, lambda i: fv_in.at[:, core, i]),
        Line(k, lambda i: fg_in.at[:, core, i]),
        Line(k, lambda i: fo_in.at[core, i]),
    )
    spreads = [
        Spread(
            k,
            lambda t, weight=weight: weight.at[:, wide_cols(t)],
            lambda s, m=m, to=to: to.at[s, n, :, pl.ds((m % 2) * two, two)],
        )
        for m, (weight, to) in enumerate(projections)
    ]
    spread_ff = [
        Spread(
            k,
            lambda t, weight=weight: weight.at[:, chip_cols(lax.div(t, 2))],
            lambda s, to=to: to.at[lax.div(s, 2), core, n],
            peers=CHIPS,
        )
        for weight, to in ((fv, fv_in), (fg, fg_in))
    ]
    planes = plane_xn, plane_out, plane_dy, plane_x1n = (
        Plane(k, lambda s, h: xn_in.at[s, pl.ds(h * half, half)]),
        Plane(k, lambda s, h: wo_in.at[s, pl.ds(h * 2, 2)]),
        Plane(k, lambda s, h: dy_in.at[lax.div(s, 2), pl.ds(h * half, half)]),
        Plane(k, lambda s, h: x1n_in.at[lax.div(s, 2), pl.ds(h * half, half)]),
    )
    here4 = (w, k.wx, k.wy, k.wd)
    there4 = tuple(s + 1 - 2 * core for s in here4)
    near4 = (n, k.pair, k.cross, k.far)
    twins = twin_xn, twin_out, twin_fv, twin_fg, twin_fo = (
        Sibling(k, lambda i: xn_in.at[here4[i]], lambda i: xn_in.at[there4[i]], 4),
        Sibling(k, lambda i: wo_in.at[here4[i]], lambda i: wo_in.at[there4[i]], 4),
        Sibling(k, lambda i: fv_in.at[:, core, near4[i]], lambda i: fv_in.at[:, other, near4[i]], 4),
        Sibling(k, lambda i: fg_in.at[:, core, near4[i]], lambda i: fg_in.at[:, other, near4[i]], 4),
        Sibling(k, lambda i: fo_in.at[core, near4[i]], lambda i: fo_in.at[other, near4[i]], 4),
    )

    k.greet()
    def before(
        x, xn, wqk, wvg, wout, slopes, qkv, gates, sin, state, attn_s, attn, gate, mixed, x1, x1n,
        decay,
    ):
        load_x = k.keep(x_in, x)
        held = [
            (k.keep(wo, mixed.at[pl.ds(0, 64)]), mixed.at[pl.ds(0, 64)], wo_in.at[w, n]),
            *[
                (
                    k.keep(weight.at[:, wide_cols(w)], spot.at[w, n, :, lanes]),
                    spot.at[w, n, :, lanes],
                    to.at[w, n, :, lanes],
                )
                for weight, spot, to, lanes in (
                    (wq, wqk, wqk_in, pl.ds(0, two)),
                    (wk, wqk, wqk_in, pl.ds(two, two)),
                    (wv, wvg, wvg_in, pl.ds(0, two)),
                    (wg, wvg, wvg_in, pl.ds(two, two)),
                )
            ],
            (k.keep(dy_arg, attn), attn, dy_in.at[chip]),
            *[
                (
                    k.keep(weight.at[:, chip_cols(chip)], tmp_ff.at[m]),
                    tmp_ff.at[m],
                    to.at[chip, core, n],
                )
                for m, (weight, to) in enumerate(((fv, fv_in), (fg, fg_in)))
            ],
            (k.keep(fo, gate.at[pl.ds(0, fo_rows)]), gate.at[pl.ds(0, fo_rows)], fo_in.at[core, n]),
        ]

        def place(index):
            load, spot, to = held[index]
            load.wait()
            return k.keep(spot, to)

        load_x.wait()

        def norm_in(rows):
            v = x[rows, :].astype(F32)
            x1n[rows, :] = (v * row_scale(v)).astype(BF)

        row_chunks(tok, norm_in)
        own_xn = k.keep(x1n, xn_in.at[w])
        own_in = [place(i) for i in range(5)]
        k.met()
        for spread in spreads:
            spread.start()
        own_in[0].wait()
        line_out.start()
        own_xn.wait()
        for copy in own_in[1:]:
            copy.wait()
        spreads[0].finish()
        spreads[1].finish()
        line_qk.start()
        plane_xn.start()
        twin_xn.send(0)
        spreads[2].finish()
        spreads[3].finish()
        line_vg.start()
        for spread in spread_ff:
            spread.start()
        own_ff = [place(i) for i in range(5, 9)]
        line_out.forward()
        plane_xn.forward()
        line_out.forward_far()
        line_qk.forward()
        plane_xn.finish_near()
        twin_xn.send(1)
        twin_xn.send(2)
        line_vg.forward()
        line_qk.forward_far()
        line_out.finish()
        plane_out.start()
        twin_out.send(0)
        plane_xn.finish_far()
        twin_xn.send(3)
        line_vg.forward_far()
        spread_ff[0].finish()
        spread_ff[1].finish()
        for copy in own_ff:
            copy.wait()
        line_fv.start()
        for i in range(4):
            twin_xn.wait(i)
        load_xn = k.keep(xn_in, xn)
        plane_out.forward()
        line_qk.finish()
        load_qk = k.keep(wqk_in, wqk)
        load_xn.wait()
        load_qk.wait()

        def project_qk(t, carry):
            v = dot(xn[t], wqk[...].reshape(width, 2 * two))
            rows = at(t * tok, tok)
            sigma = jax.nn.sigmoid(v)
            slopes[rows, :] = (sigma * (1.0 + v * (1.0 - sigma))).astype(BF)
            qkv[rows, 0 : 2 * two] = (v * sigma).astype(BF)
            return carry

        lax.fori_loop(0, WIDE, project_qk, 0)
        stores = [k.keep(slopes, slope_in)]
        plane_out.finish_near()
        twin_out.send(1)
        twin_out.send(2)
        line_vg.finish()
        k.keep(wvg_in, wvg).wait()

        def project_vg(t, carry):
            v = dot(xn[t], wvg[...].reshape(width, 2 * two)).astype(BF)
            qkv[at(t * tok, tok), 2 * two : 3 * two] = v[:, 0:two]
            gates[t] = v[:, two:]
            return carry

        lax.fori_loop(0, WIDE, project_vg, 0)
        line_fv.forward()
        line_fg.start()
        stores.append(k.keep(qkv, qkv_in))
        spread_gate = Spread(k, lambda t: gates.at[t], lambda s: gate_in.at[:, wide_cols(s)])
        spread_gate.start()
        own = [k.keep(gates.at[w], gate_in.at[:, wide_cols(w)])]
        fill_decay(decay)
        state[...] = jnp.zeros_like(state)
        spread_attn = Spread(k, lambda t: attn_s.at[t], lambda s: attn_in.at[:, wide_cols(s)])

        def attend(b, carry):
            rows = at(b * BLOCK, BLOCK)
            mask, factors = block_tables(b)
            for h in range(2):
                lanes = slice(h * HEAD, (h + 1) * HEAD)
                entry, tail, through = factors[h]
                q = qkv[rows, lanes]
                key = qkv[rows, two + h * HEAD : two + (h + 1) * HEAD]
                v = qkv[rows, 2 * two + h * HEAD : 2 * two + (h + 1) * HEAD]
                probs = jnp.where(mask, dot_rt(q, key) * decay[h], 0.0).astype(BF)
                old = state[h]
                old_bf = old.astype(BF)
                sin[b, h] = old_bf
                out = dot(probs, v) + entry * dot(q, old_bf)
                attn_s[b, :, lanes] = out.astype(BF)
                tailed = (key.astype(F32) * tail).astype(BF)
                state[h] = through * old + dot_lt(tailed, v)

            @pl.when(b != w)
            def _():
                spread_attn.copy(lax.rem(b - w + WIDE, WIDE), b).start()

            return carry

        lax.fori_loop(0, WIDE, attend, 0)
        stores.append(k.keep(sin, sin_in))
        own.append(k.keep(attn_s.at[w], attn_in.at[:, wide_cols(w)]))
        plane_out.finish_far()
        twin_out.send(3)
        for i in range(4):
            twin_out.wait(i)
        load_out = k.keep(wo_in, wout)
        line_fv.forward_far()
        spread_gate.finish()
        spread_attn.finish()
        for copy in own:
            copy.wait()
        loads = [k.keep(attn_in, attn), k.keep(gate_in, gate)]
        for copy in loads:
            copy.wait()

        def mix(rows):
            a = attn[rows, :].astype(F32)
            mixed[rows, :] = (a * row_scale(a) * gate[rows, :].astype(F32)).astype(BF)

        row_chunks(tok, mix)
        stores.append(k.keep(mixed, mixed_in))
        load_out.wait()

        def project_out(j, carry):
            lanes = at(j * 512, 512)
            part = dot(mixed[...], wout[:, :, :, lanes].reshape(-1, 512))
            x1[:, lanes] = x[:, lanes].astype(F32) + part
            return carry

        lax.fori_loop(0, width // 512, project_out, 0)
        stores.append(k.keep(x1, x1_in))

        def norm_mid(rows):
            v = x1[rows, :]
            x1n[rows, :] = (v * row_scale(v)).astype(BF)

        row_chunks(tok, norm_mid)
        k.keep(x1n, x1n_in.at[chip]).wait()
        plane_x1n.start()
        line_fg.forward()
        line_fo.start_away()
        plane_x1n.forward()
        plane_dy.start()
        line_fg.forward_far()
        for copy in stores:
            copy.wait()
        spread_gate.drain()
        spread_attn.drain()

    pl.run_scoped(
        before,
        pltpu.VMEM((tok, width), BF),
        pltpu.VMEM((WIDE, tok, width), BF),
        pltpu.VMEM(wqk_in.shape, BF),
        pltpu.VMEM(wvg_in.shape, BF),
        pltpu.VMEM(wo_in.shape, BF),
        pltpu.VMEM(slope_in.shape, BF),
        pltpu.VMEM(qkv_in.shape, BF),
        pltpu.VMEM((WIDE, tok, two), BF),
        pltpu.VMEM(sin_in.shape, BF),
        pltpu.VMEM((2, HEAD, HEAD), F32),
        pltpu.VMEM((WIDE, tok, two), BF),
        pltpu.VMEM((tok, width), BF),
        pltpu.VMEM((tok, width), BF),
        pltpu.VMEM((tok, width), BF),
        pltpu.VMEM((tok, width), F32),
        pltpu.VMEM((tok, width), BF),
        pltpu.VMEM((2, BLOCK, BLOCK), F32),
    )

    def ffn(x1n, dy, fvw, fgw, fow, mix, val, gat, side, tmp_twin):
        def shares(moved, src, dst, places):
            copies = []
            for i in places:
                moved.wait(i)
                copies.append(k.keep(src.at[:, :, near4[i]], dst.at[:, :, near4[i]]))
            return copies

        def fo_shares(places):
            copies = []
            for i in places:
                twin_fo.wait(i)
                copies.append(k.keep(fo_in.at[:, near4[i]], fow.at[:, near4[i]]))
            return copies

        line_fv.finish(twin_fv.send)
        load_fv = shares(twin_fv, fv_in, fvw, range(4))
        plane_x1n.finish_near()
        plane_x1n.finish_far()
        load_x1n = k.keep(x1n_in, x1n)
        for copy in (load_x1n, *load_fv):
            copy.wait()

        def up_val(j, carry):
            val[j] = dot(x1n[j], fvw[...].reshape(width, ff)).astype(BF)
            return carry

        def up_gat(j, carry):
            g = dot(x1n[j], fgw[...].reshape(width, ff))
            gat[j] = g.astype(BF)
            mix[j] = (val[j].astype(F32) * g).astype(BF)
            return carry

        lax.fori_loop(0, CHIPS, up_val, 0)
        line_fo.forward()
        plane_dy.forward()
        load_fg = []
        line_fg.finish(twin_fg.send, lambda: load_fg.extend(shares(twin_fg, fg_in, fgw, range(3))))
        line_fo.start_home()
        load_fg += shares(twin_fg, fg_in, fgw, range(3, 4))
        for copy in load_fg:
            copy.wait()
        line_fo.forward_far()
        lax.fori_loop(0, CHIPS // 2, up_gat, 0)
        plane_dy.finish_near()
        plane_dy.finish_far()
        load_dy = k.keep(dy_in, dy)
        lax.fori_loop(CHIPS // 2, CHIPS, up_gat, 0)
        load_dy.wait()

        def fo_grad(j, carry):
            chunk = lax.rem(j + 2 * other, chunks)
            rows = pl.ds(pl.multiple_of(jnp.minimum(chunk * 256, ff - 256), 128), 256)
            left = mix[:, :, rows].reshape(CHIPS * tok, 256)
            for h in range(2):
                lanes = slice(h * width // 2, (h + 1) * width // 2)
                right = dy[:, :, lanes].reshape(CHIPS * tok, -1)
                g_fo[rows, lanes] = dot_lt(left, right).astype(BF)
            return carry

        chunks = pl.cdiv(ff, 256)
        lax.fori_loop(0, 4, fo_grad, 0)
        for i in range(NARROW):
            there = near4[NARROW - 1 - i]
            twin(0, there, fo_part(other, there), twin_fo_land.at[there]).start()
        lax.fori_loop(4, chunks, fo_grad, 0)
        came = []
        for i in reversed(range(NARROW)):
            copy = twin(0, near4[i], fo_part(other, near4[i]), twin_fo_land.at[near4[i]])
            copy.wait_recv()
            spot = stage.at[i, pl.ds(0, fo_rows)]
            came.append((i, copy, k.keep(twin_fo_land.at[near4[i]], spot), spot))
        for i, copy, load, spot in came:
            load.wait()
            own = fo_part(core, near4[i])
            own[...] = (own[...].astype(F32) + spot[...].astype(F32)).astype(BF)
            copy.wait_send()
            if i > 0:
                sum_fo.begin(3 - i)
        load_fo = []
        line_fo.finish(twin_fo.send, lambda: load_fo.extend(fo_shares(range(3))))
        load_fo += fo_shares(range(3, 4))
        for copy in load_fo:
            copy.wait()

        def down(q, carry):
            d_mix = dot_rt(dy[q], fow[...].reshape(ff, width))
            d_val = (d_mix * gat[q].astype(F32)).astype(BF)
            d_gat = (d_mix * val[q].astype(F32)).astype(BF)
            val[q] = d_val
            gat[q] = d_gat
            return carry

        lax.fori_loop(0, CHIPS, down, 0)

        plane_res = plane_sum(1, dy, base_res, stage.at[chip])

        def out_step(j, carry):
            q = nth(j)
            dy[q] = dot(mix[q], fow[...].reshape(ff, width)).astype(BF)
            for step, push in enumerate((plane_res.send_far, plane_res.send_x, plane_res.send_y)):
                pl.when(j == step)(push)
            return carry

        lax.fori_loop(0, CHIPS, out_step, 0)

        def back(j, carry):
            q = nth(j)

            def back_lanes(i, carry):
                lanes = at(i * 512, 512)
                d_x = dot_rt(val[q], fvw[i].reshape(512, ff)) + dot_rt(
                    gat[q], fgw[i].reshape(512, ff)
                )

                @pl.when(j < 3)
                def _():
                    stage[q, :, lanes] = d_x.astype(BF)

                @pl.when(j == 3)
                def _():
                    acc[:, lanes] = d_x

                return carry

            lax.fori_loop(0, width // 512, back_lanes, 0)
            for step, push in enumerate((plane_mid.send_far, plane_mid.send_x, plane_mid.send_y)):
                pl.when(j == step)(push)
            return carry

        for m, (d_ff, g_ff) in enumerate(((val, g_fv), (gat, g_fg))):

            def ff_grad(owner):
                left = x1n[:, :, at(owner * tok, tok)].reshape(CHIPS * tok, tok)
                g = dot_lt(left, d_ff[...].reshape(CHIPS * tok, ff)).astype(BF)
                return g.reshape(NARROW, -1, ff)

            def side_step(q, carry):
                slot = lax.rem(q, 2)

                @pl.when(q >= 2)
                def _():
                    twin(1 + m, q - 2, side.at[slot], twin_ff.at[m, q]).wait_send()

                side[slot] = ff_grad(2 * q + other)
                twin(1 + m, q, side.at[slot], twin_ff.at[m, q]).start()
                return carry

            def own_step(q, carry):
                g_ff[q] = ff_grad(2 * q + core)
                return carry

            lax.fori_loop(0, CHIPS, side_step, 0)
            lax.fori_loop(0, CHIPS, own_step, 0)
            loads = []
            for q in range(CHIPS + 1):
                if q < CHIPS:
                    twin(1 + m, q, side.at[q % 2], twin_ff.at[m, q]).wait_recv()
                    loads.append(k.keep(twin_ff.at[m, q], (tmp_ff, tmp_twin)[q % 2]))
                if q > 0:
                    loads[q - 1].wait()
                    own = g_ff.at[q - 1]
                    own[...] = (
                        own[...].astype(F32) + (tmp_ff, tmp_twin)[(q - 1) % 2][...].astype(F32)
                    ).astype(BF)
            for q in range(2, CHIPS):
                twin(1 + m, q, side.at[q % 2], twin_ff.at[m, q]).wait_send()
            sum_ff[m].start()
            if m == 0:
                lax.fori_loop(0, CHIPS, back, 0)
                plane_mid.combine(add_half)
                plane_res.combine(add_half)
                sum_fo.pass_on(0, add_fo)
                sum_fo.pass_on(1, add_fo)

        sum_fo.pass_on(2, add_fo)
        store = k.keep(dy.at[chip], result_o)
        plane_mid.drain()
        plane_res.drain(0, 4)
        store.wait()

    pl.run_scoped(
        ffn,
        pltpu.VMEM((CHIPS, tok, width), BF),
        pltpu.VMEM((CHIPS, tok, width), BF),
        pltpu.VMEM(fv_in.shape, BF),
        pltpu.VMEM(fg_in.shape, BF),
        pltpu.VMEM(fo_in.shape, BF),
        pltpu.VMEM((CHIPS, tok, ff), BF),
        pltpu.VMEM((CHIPS, tok, ff), BF),
        pltpu.VMEM((CHIPS, tok, ff), BF),
        pltpu.VMEM((2, *g_fv.shape[1:]), BF),
        pltpu.VMEM(g_fv.shape[1:], BF),
    )

    def rest(d_x1, d_branch, mixed, da_src, dg_src, side, stage_wo, g_wo, g_qk, g_vg):
        plane_out = plane_sum(2, stage_wo)
        sum_wo = LineSum(k, lambda i: g_wo.at[i], lambda s: land_wo.at[s])
        sum_qk = [
            LineSum(k, lambda i, g=g: g.at[:, i], lambda s, m=m: land_qk.at[m, s])
            for m, g in enumerate((g_qk, g_vg))
        ]
        spread_a = Spread(
            k, lambda t: da_src.at[:, at(t * two, two)], lambda s: a_land.at[s]
        )
        spread_g = Spread(
            k, lambda t: dg_src.at[:, at(t * two, two)], lambda s: g_land.at[at(s * tok, tok)]
        )

        def middle(wo, x1, attn, gate, dy, d_mixed, pair):
            plane_mid.finish()
            loads = [k.keep(near.at[0], pair), k.keep(x1_in, x1), k.keep(dy_in.at[chip], dy)]
            late = [
                k.keep(wo_in, wo), k.keep(attn_in, attn), k.keep(gate_in, gate),
                k.keep(mixed_in, mixed),
            ]
            for copy in loads:
                copy.wait()

            def norm_back(rows):
                g = acc[rows, :] + pair[0, rows, :].astype(F32) + pair[1, rows, :].astype(F32)
                v = x1[rows, :]
                r = row_scale(v)
                u = v * r
                d = dy[rows, :].astype(F32) + r * (g - u * jnp.mean(g * u, axis=-1, keepdims=True))
                d_x1[rows, :] = d
                d_branch[rows, :] = d.astype(BF)

            row_chunks(tok, norm_back)
            for copy in late:
                copy.wait()

            def mixed_step(j, carry):
                d_mixed[:, at(j * 512, 512)] = dot_rt(
                    d_branch[...], wo[pl.ds(2 * j, 2)].reshape(512, width)
                )
                return carry

            lax.fori_loop(0, width // 512, mixed_step, 0)

            def attn_back(rows):
                a = attn[rows, :].astype(F32)
                s = row_scale(a)
                u = a * s
                d = d_mixed[rows, :]
                dg_src[rows, :] = (d * u).astype(BF)
                g = d * gate[rows, :].astype(F32)
                da_src[rows, :] = (
                    s * (g - u * jnp.mean(g * u, axis=-1, keepdims=True))
                ).astype(BF)

            row_chunks(tok, attn_back)
            spread_a.start()
            spread_g.start()
            own = [
                k.keep(da_src.at[:, at(w * two, two)], a_land.at[w]),
                k.keep(dg_src.at[:, at(w * two, two)], g_land.at[at(w * tok, tok)]),
            ]

            for copy in own:
                copy.wait()

        pl.run_scoped(
            middle,
            pltpu.VMEM(wo_in.shape, BF),
            pltpu.VMEM((tok, width), F32),
            pltpu.VMEM((tok, width), BF),
            pltpu.VMEM((tok, width), BF),
            pltpu.VMEM((tok, width), BF),
            pltpu.VMEM((tok, width), F32),
            pltpu.VMEM((2, tok, width), BF),
        )
        def eight_way(plane, twin_index, landing, blocks, spots, term):
            def side_step(j, carry):
                q = nth(j)
                side[q] = term(2 * q + other).astype(BF)
                twin(twin_index, j, side.at[q], landing.at[q]).start()
                return carry

            lax.fori_loop(0, CHIPS, side_step, 0)

            def load(j):
                q = order[j]
                twin(twin_index, j, side.at[q], landing.at[q]).wait_recv()
                return k.keep(landing.at[q], spots[j % 2])

            pushes = (plane.send_far, plane.send_x, plane.send_y)
            loads = [load(0)]
            for j in range(CHIPS):
                if j + 1 < CHIPS and spots[0] is not spots[1]:
                    loads.append(load(j + 1))
                v = term(2 * order[j] + core)
                loads[j].wait()
                v = v + spots[j % 2][...].astype(F32)
                if j < 3:
                    blocks[order[j]] = v.astype(BF)
                    pushes[j]()
                else:
                    acc[...] = v
                if j + 1 < CHIPS and spots[0] is spots[1]:
                    loads.append(load(j + 1))
            for j in range(CHIPS):
                twin(twin_index, j, side.at[order[j]], landing.at[order[j]]).wait_send()

        eight_way(
            plane_out,
            3,
            twin_wo,
            stage_wo,
            (tmp, tmp),
            lambda owner: dot_lt(mixed[:, at(owner * tok, tok)], d_branch[...]),
        )
        sum_ff[0].pass_on(0, add_ff)
        sum_ff[0].pass_on(1, add_ff)

        def attention(xn, d_qk, d_vg, state):
            state[...] = jnp.zeros_like(state)

            def heads(slopes, qkv, sin, decay, d_attn):
                loads = [
                    k.keep(qkv_in, qkv), k.keep(sin_in, sin), k.keep(slope_in, slopes),
                ]
                fill_decay(decay)
                for copy in loads:
                    copy.wait()
                spread_a.finish()
                fetch(a_land, d_attn)
                load_xn = k.keep(xn_in, xn)

                def step(i, carry):
                    b = WIDE - 1 - i
                    rows = at(b * BLOCK, BLOCK)
                    mask, factors = block_tables(b)
                    for h in range(2):
                        entry, tail, through = factors[h]
                        lanes = slice(h * HEAD, (h + 1) * HEAD)
                        key_lanes = slice(two + h * HEAD, two + (h + 1) * HEAD)
                        q = qkv[rows, lanes]
                        key = qkv[rows, key_lanes]
                        v = qkv[rows, 2 * two + h * HEAD : 2 * two + (h + 1) * HEAD]
                        d_o = d_attn[b, :, lanes]
                        factor = jnp.where(mask, decay[h], 0.0)
                        probs = (dot_rt(q, key) * factor).astype(BF)
                        d_probs = (dot_rt(d_o, v) * factor).astype(BF)
                        before = sin[b, h]
                        after = state[h]
                        after_bf = after.astype(BF)
                        tailed = (key.astype(F32) * tail).astype(BF)
                        entered = (q.astype(F32) * entry).astype(BF)
                        d_q = dot(d_probs, key) + entry * dot_rt(d_o, before)
                        d_k = dot_lt(d_probs, q) + tail * dot_rt(v, after_bf)
                        d_v = dot_lt(probs, d_o) + dot(tailed, after_bf)
                        d_qk[rows, lanes] = (d_q * slopes[rows, lanes].astype(F32)).astype(BF)
                        d_qk[rows, key_lanes] = (d_k * slopes[rows, key_lanes].astype(F32)).astype(BF)
                        d_vg[rows, lanes] = d_v.astype(BF)
                        state[h] = through * after + dot_lt(entered, d_o)
                    return carry

                lax.fori_loop(0, WIDE, step, 0)
                sum_ff[0].pass_on(2, add_ff)
                spread_g.finish()
                load_g = k.keep(g_land, d_vg.at[:, pl.ds(two, two)])
                load_g.wait()
                load_xn.wait()

            pl.run_scoped(
                heads,
                pltpu.VMEM(slope_in.shape, BF),
                pltpu.VMEM(qkv_in.shape, BF),
                pltpu.VMEM(sin_in.shape, BF),
                pltpu.VMEM((2, BLOCK, BLOCK), F32),
                pltpu.VMEM((WIDE, tok, two), BF),
            )

            for m, (d_in, g_in) in enumerate(((d_qk, g_qk), (d_vg, g_vg))):

                def in_grad(s, carry):
                    left = xn[:, :, at(s * tok, tok)].reshape(WIDE * tok, tok)
                    g_in[s] = dot_lt(left, d_in[...]).astype(BF).reshape(NARROW, -1, 2 * two)
                    return carry

                lax.fori_loop(0, WIDE, in_grad, 0)
                sum_qk[m].start()

            plane_out.combine(add_half)
            sum_ff[1].pass_on(0, add_ff)
            sum_ff[1].pass_on(1, add_ff)
            g_wo[...] = acc[...].astype(BF).reshape(g_wo.shape)

            def spread_in(wqk, wvg):
                loads = [k.keep(wqk_in, wqk), k.keep(wvg_in, wvg)]
                for copy in loads:
                    copy.wait()

                def term(owner):
                    rows = at(owner * tok, tok)
                    return dot_rt(d_qk[rows, :], wqk[...].reshape(width, 2 * two)) + dot_rt(
                        d_vg[rows, :], wvg[...].reshape(width, 2 * two)
                    )

                spread_a.drain()
                eight_way(plane_in, 4, twin_xn_land, stage, (tmp, da_src), term)

            pl.run_scoped(spread_in, pltpu.VMEM(wqk_in.shape, BF), pltpu.VMEM(wvg_in.shape, BF))

        pl.run_scoped(
            attention,
            pltpu.VMEM((WIDE, tok, width), BF),
            pltpu.VMEM((WIDE * tok, 2 * two), BF),
            pltpu.VMEM((WIDE * tok, 2 * two), BF),
            pltpu.VMEM((2, HEAD, HEAD), F32),
        )

        def last(
            x, x1, own_res, pair, three, three_ff, three_qk, ff_src, qk_src, w_f32, w_fo, tmp_qk
        ):
            add_qk = adder(tmp_qk)
            load_x, load_x1 = k.keep(x_in, x), k.keep(x1_in, x1)
            load_res = k.keep(result_o, own_res)
            plane_in.combine(add_half)
            sum_ff[1].pass_on(2, add_ff)
            sum_qk[0].pass_on(0, add_qk)
            sum_qk[0].pass_on(1, add_qk)
            plane_out.finish()
            fetch(near.at[2], pair)
            for i in range(NARROW):
                rows = pl.ds(i * 64, 64)
                v = g_wo[i].astype(F32) + pair[0, rows, :].astype(F32) + pair[1, rows, :].astype(F32)
                g_wo[i] = v.astype(BF)
            sum_wo.start()

            def total(part, lands):
                return part.astype(F32) + lands[0].astype(F32) + lands[1].astype(F32)

            ff_turns = []
            for m, g_ff in enumerate((g_fv, g_fg)):
                sum_ff[m].finish(fetch, three_ff)
                for q in range(CHIPS):
                    ff_src[m, q] = total(g_ff[q, n], three_ff[:, q]).astype(BF)
                turn = Spread(
                    k,
                    lambda t, m=m: ff_src.at[m, lax.div(t, 2)],
                    lambda s, m=m: turn_ff.at[m, lax.div(s, 2)],
                    peers=CHIPS,
                )
                turn.start()
                ff_turns.append((turn, k.keep(ff_src.at[m, chip], turn_ff.at[m, chip])))
            sum_qk[0].pass_on(2, add_qk)
            sum_fo.finish(fetch, three.at[:, pl.ds(0, fo_rows)])
            own = fo_part(core, n)
            for r in range(0, fo_rows, 16):
                rows = pl.ds(r, 16)
                w_fo[rows, :] = total(own[rows, :], three[:, rows, :])
            stores = [k.keep(w_fo, gfo_o)]

            plane_sum(1, stage, base_res).finish()
            fetch(near.at[1], pair)
            load_x1.wait()
            load_res.wait()

            def add_up(rows):
                v = x1[rows, :] + own_res[rows, :].astype(F32)
                v = v + pair[0, rows, :].astype(F32) + pair[1, rows, :].astype(F32)
                own_res[rows, :] = v.astype(BF)

            row_chunks(tok, add_up)
            stores.append(k.keep(own_res, result_o))
            sum_qk[1].pass_on(0, add_qk)
            sum_qk[1].pass_on(1, add_qk)
            load_x.wait()
            plane_in.finish()
            fetch(near.at[3], pair)

            def input_back(rows):
                g = acc[rows, :] + pair[0, rows, :].astype(F32) + pair[1, rows, :].astype(F32)
                v = x[rows, :].astype(F32)
                r = row_scale(v)
                u = v * r
                d_x1[rows, :] = d_x1[rows, :] + r * (
                    g - u * jnp.mean(g * u, axis=-1, keepdims=True)
                )

            row_chunks(tok, input_back)
            stores.append(k.keep(d_x1, dx_o))
            for m, (turn, copy) in enumerate(ff_turns):
                turn.finish()
                copy.wait()
            qk_turns = []
            for m, g_in in enumerate((g_qk, g_vg)):
                if m == 1:
                    sum_qk[1].pass_on(2, add_qk)
                    sum_wo.pass_on(0, add_wo)
                    sum_wo.pass_on(1, add_wo)
                sum_qk[m].finish(fetch, three_qk)
                for s in range(WIDE):
                    qk_src[m, s] = total(g_in[s, n], three_qk[:, s]).astype(BF)
                turn = Spread(
                    k,
                    lambda t, m=m: qk_src.at[m, t],
                    lambda s, m=m: turn_qk.at[m, s],
                )
                turn.start()
                qk_turns.append((turn, k.keep(qk_src.at[m, w], turn_qk.at[m, w])))
            sum_wo.pass_on(2, add_wo)
            for m, (turn, copy) in enumerate(qk_turns):
                turn.finish()
                copy.wait()
            sum_wo.finish(fetch, three.at[:, pl.ds(0, 64)])
            w_f32[...] = total(g_wo[n], three[:, 0:64, :])
            stores.append(k.keep(w_f32, go_o))
            for copy in stores:
                copy.wait()
            plane_in.drain()
            plane_out.drain()
            plane_sum(1, stage, base_res, stage.at[chip]).drain(4, 6)
            turns = [turn for turn, copy in ff_turns + qk_turns]
            for moved in (*lines, *planes, *twins, *spreads, *spread_ff):
                moved.drain()
            for sums in (sum_fo, sum_wo, *sum_ff, *sum_qk, spread_g, *turns):
                sums.drain()

        pl.run_scoped(
            last,
            pltpu.VMEM((tok, width), BF),
            pltpu.VMEM((tok, width), F32),
            pltpu.VMEM((tok, width), BF),
            pltpu.VMEM((2, tok, width), BF),
            pltpu.VMEM((2, tok, width), BF),
            pltpu.VMEM((2, *land_ff.shape[2:]), BF),
            pltpu.VMEM((2, *land_qk.shape[2:]), BF),
            pltpu.VMEM((2, CHIPS, 64, ff), BF),
            pltpu.VMEM((2, WIDE, 64, 2 * two), BF),
            pltpu.VMEM((64, width), F32),
            pltpu.VMEM((fo_rows, width), F32),
            pltpu.VMEM((WIDE, 64, 2 * two), BF),
        )

    pl.run_scoped(
        rest,
        pltpu.VMEM((tok, width), F32),
        pltpu.VMEM((tok, width), BF),
        pltpu.VMEM((tok, width), BF),
        pltpu.VMEM((tok, width), BF),
        pltpu.VMEM((tok, width), BF),
        pltpu.VMEM((CHIPS, tok, width), BF),
        pltpu.VMEM((CHIPS, tok, width), BF),
        pltpu.VMEM((NARROW, 64, width), BF),
        pltpu.VMEM((WIDE, NARROW, 64, 2 * two), BF),
        pltpu.VMEM((WIDE, NARROW, 64, 2 * two), BF),
    )
    assert k.count <= send.shape[0] and k.kept <= here.shape[0], (k.count, k.kept)


def finish_kernel(
    result, d_x, g_out, g_fout, turn_ff, turn_qk,
    result_o, d_x_o, gq_o, gk_o, gv_o, gg_o, go_o, gfv_o, gfg_o, gfo_o,
    result_v, d_x_v, g_out_v, g_fout_v, ff_v, qk_v, ff_f32, qk_f32, sems,
):
    copies = []

    def copy(src, dst):
        made = pltpu.make_async_copy(src, dst, sems.at[len(copies)])
        made.start()
        copies.append(made)
        return made

    ff, two = ff_v.shape[-1], qk_v.shape[-1] // 2
    load_ff, load_qk = copy(turn_ff, ff_v), copy(turn_qk, qk_v)
    through = (
        (d_x, d_x_v, d_x_o),
        (g_fout, g_fout_v, gfo_o),
        (result, result_v, result_o),
        (g_out, g_out_v, go_o),
    )
    loads = [copy(src, held) for src, held, _ in through]
    stores = []
    load_ff.wait()
    for m, out in enumerate((gfv_o, gfg_o)):
        for q in range(CHIPS):
            ff_f32[m, :, q * ff : (q + 1) * ff] = ff_v[m, q].astype(F32)
        stores.append(copy(ff_f32.at[m], out))
    load_qk.wait()
    for m, outs in enumerate(((gq_o, gk_o), (gv_o, gg_o))):
        for s in range(WIDE):
            lanes = slice(s * two, (s + 1) * two)
            qk_f32[2 * m, :, lanes] = qk_v[m, s, :, 0:two].astype(F32)
            qk_f32[2 * m + 1, :, lanes] = qk_v[m, s, :, two:].astype(F32)
        stores += [copy(qk_f32.at[2 * m + i], out) for i, out in enumerate(outs)]
    for load, (_, held, out) in zip(loads, through):
        load.wait()
        stores.append(copy(held, out))
    for store in stores:
        store.wait()


def finish(results, moved):
    out_shape = moved
    return pl.pallas_call(
        finish_kernel,
        out_shape=out_shape,
        in_specs=[ANY] * 6,
        out_specs=(ANY,) * len(out_shape),
        scratch_shapes=[
            *[pltpu.VMEM(r.shape, r.dtype) for r in results],
            pltpu.VMEM((2, *out_shape[7].shape), F32),
            pltpu.VMEM((4, *out_shape[2].shape), F32),
            pltpu.SemaphoreType.DMA((20,)),
        ],
        compiler_params=pltpu.CompilerParams(vmem_limit_bytes=63 * 2**20),
    )(*results)


def layer(tokens, weights, dy, starts):
    tok, width = tokens.shape
    shard = weights[0].shape[0]
    ff = weights[5].shape[1] // CHIPS
    fo_rows = weights[7].shape[0]
    full = WIDE * tok
    two = 2 * HEAD

    def arr(*shape, dtype=BF):
        return jax.ShapeDtypeStruct(shape, dtype)

    finals = (
        arr(tok, width),
        arr(tok, width, dtype=F32),
        *[arr(shard, width, dtype=F32)] * 5,
        arr(shard, CHIPS * ff, dtype=F32),
        arr(shard, CHIPS * ff, dtype=F32),
        arr(fo_rows, width, dtype=F32),
    )
    results = (
        arr(tok, width),
        arr(tok, width, dtype=F32),
        arr(shard, width, dtype=F32),
        arr(fo_rows, width, dtype=F32),
        arr(2, CHIPS, shard, ff),
        arr(2, WIDE, shard, 2 * two),
    )
    held = (
        arr(WIDE, tok, width),
        arr(WIDE, NARROW, shard, 2 * two),
        arr(WIDE, NARROW, shard, 2 * two),
        arr(WIDE, NARROW, shard, width),
        arr(CHIPS, 2, NARROW, shard, ff),
        arr(CHIPS, 2, NARROW, shard, ff),
        arr(2, NARROW, fo_rows, width),
        arr(CHIPS, tok, width),
        arr(full, 2 * two),
        arr(full, 3 * two),
        arr(WIDE, 2, HEAD, HEAD),
        arr(tok, width),
        arr(tok, width),
        arr(tok, width),
        arr(tok, width, dtype=F32),
        arr(CHIPS, tok, width),
    )
    landings = (
        arr(4, 2, tok // 2, width),
        arr(4, 2, tok, width),
        arr(NARROW, fo_rows, width),
        arr(2, CHIPS, NARROW, shard, ff),
        arr(CHIPS, tok, width),
        arr(CHIPS, tok, width),
        arr(5, fo_rows, width),
        arr(2, 5, CHIPS, shard, ff),
        arr(5, shard, width),
        arr(2, 5, WIDE, shard, 2 * two),
        arr(WIDE, tok, two),
        arr(full, two),
    )
    out_shape = results + held + landings
    outs = pl.pallas_call(
        layer_kernel,
        out_shape=out_shape,
        in_specs=[ANY] * 10 + [pl.BlockSpec(memory_space=pltpu.SMEM)],
        out_specs=(ANY,) * len(out_shape),
        scratch_shapes=[
            pltpu.VMEM((ff, width), BF),
            pltpu.VMEM((CHIPS, NARROW, shard, ff), BF),
            pltpu.VMEM((CHIPS, NARROW, shard, ff), BF),
            pltpu.VMEM((CHIPS, tok, width), BF),
            pltpu.VMEM((tok, width), F32),
            pltpu.VMEM((tok, width), BF),
            pltpu.VMEM((CHIPS, shard, ff), BF),
            pltpu.SemaphoreType.DMA((272,)),
            pltpu.SemaphoreType.DMA((272,)),
            pltpu.SemaphoreType.DMA((120,)),
        ],
        compiler_params=pltpu.CompilerParams(
            collective_id=0, has_side_effects=True, vmem_limit_bytes=63 * 2**20
        ),
        cost_estimate=pl.CostEstimate(flops=8 * 10**10, bytes_accessed=3 * 10**8, transcendentals=0),
    )(tokens, *weights, dy, starts)
    return finish(outs[: len(results)], finals)


def local_box(tokens, doc_starts, wq, wk, wv, wg, wo, fv, fg, fo, cotangent):
    weights = (wq, wk, wv, wg, wo, fv, fg, fo)
    outs = layer(tokens[0], weights, cotangent[0], doc_starts)
    return (outs[0][None], outs[1][None]) + tuple(outs[2:])


def solution(mesh):
    box = (mesh.shape["wide"], mesh.shape["narrow"]) == (WIDE, NARROW)
    tok = P("narrow", "wide", None)
    row = P(BOTH, None)
    return jax.shard_map(
        local_box if box else local,
        mesh=mesh,
        in_specs=(tok, P()) + (row,) * 8 + (tok,),
        out_specs=(tok, tok) + (row,) * 8,
        check_vma=False,
    )
```

```python
import jax
import jax.numpy as jnp
from jax import lax
from jax.experimental import pallas as pl
from jax.experimental.pallas import tpu as pltpu
from jax.sharding import PartitionSpec as P

HEADS = 16
HEAD = 128
BLOCK = 256
LAYERS = 16
LAYER = 12

EPS = 1e-06
BOTH = ("wide", "narrow")
BF = jnp.bfloat16
F32 = jnp.float32


def normalize(values):
    scale = lax.rsqrt(jnp.mean(values * values, axis=-1, keepdims=True) + EPS)
    return (values * scale, scale)


def normalize_back(normed, scale, grad):
    return scale * (grad - normed * jnp.mean(grad * normed, axis=-1, keepdims=True))


def silu_slope(values):
    sigma = jax.nn.sigmoid(values)
    return sigma * (1.0 + values * (1.0 - sigma))


def matmul(left, right):
    return jnp.dot(left, right, preferred_element_type=F32)


def matmul_right_t(left, right):
    return lax.dot_general(left, right, (((1,), (1,)), ((), ())), preferred_element_type=F32)


def weight_grad(left, right):
    return lax.dot_general(left, right, (((0,), (0,)), ((), ())), preferred_element_type=F32)


def ein(spec, left, right):
    return jnp.einsum(spec, left, right, preferred_element_type=F32)


def head_slopes():
    order = jnp.arange(HEADS, dtype=F32)
    return jnp.exp2(-8.0 * (order + 1.0) / HEADS) * (1.0 - LAYER / (LAYERS - 1) + 1e-05)


def local(
    tokens,
    doc_starts,
    query_weight,
    key_weight,
    value_weight,
    gate_weight,
    out_weight,
    ffn_value_weight,
    ffn_gate_weight,
    ffn_out_weight,
    cotangent,
):
    wide, narrow = lax.axis_size("wide"), lax.axis_size("narrow")
    rows_here, width = tokens.shape[1:]
    length = rows_here * wide
    blocks = length // BLOCK
    heads_here = HEADS // wide
    shard = query_weight.shape[0]

    def reorder(values):
        return values.reshape(-1, wide, narrow, shard).swapaxes(1, 2).reshape(-1, width)

    def restore(values):
        return values.reshape(-1, narrow, wide, shard).swapaxes(1, 2).reshape(-1, width)

    def columns(weight):
        part = lax.all_to_all(weight, "wide", split_axis=1, concat_axis=0, tiled=True)
        return lax.all_gather(part, "narrow", axis=0, tiled=True)

    def gather_rows(values):
        return lax.all_gather(values, "wide", axis=0, tiled=True)

    def scatter_rows(values):
        return lax.psum_scatter(
            values.astype(BF), "wide", scatter_dimension=0, tiled=True
        ).astype(F32)

    def to_tokens(values):
        return lax.all_to_all(values, "wide", split_axis=0, concat_axis=1, tiled=True)

    def to_heads(values):
        return lax.all_to_all(values, "wide", split_axis=1, concat_axis=0, tiled=True)

    def column_sums(grad):
        part = lax.psum_scatter(grad.astype(BF), "narrow", scatter_dimension=0, tiled=True)
        return lax.all_to_all(part, "wide", split_axis=0, concat_axis=1, tiled=True).astype(F32)

    w_query, w_key, w_value, w_gate = map(
        columns, (query_weight, key_weight, value_weight, gate_weight)
    )
    w_out = lax.all_gather(out_weight, BOTH, axis=0, tiled=True)
    w_fval, w_fgate = map(columns, (ffn_value_weight, ffn_gate_weight))
    w_fout = lax.all_gather(ffn_out_weight, "narrow", axis=0, tiled=True)

    starts = lax.dynamic_slice_in_dim(doc_starts, lax.axis_index("narrow"), 1, 0)[0]
    positions = jnp.arange(length, dtype=jnp.int32)
    doc_ids = jnp.sum((starts[None, :] <= positions[:, None]).astype(jnp.int32), axis=1)
    doc_ids = doc_ids.reshape(blocks, BLOCK)
    firsts = jnp.arange(blocks, dtype=jnp.int32) * BLOCK - 1
    prev_ids = jnp.sum((starts[None, :] <= firsts[:, None]).astype(jnp.int32), axis=1)
    slopes = lax.dynamic_slice_in_dim(
        head_slopes(), lax.axis_index("wide") * heads_here, heads_here, 0
    )
    offsets = jnp.arange(BLOCK, dtype=F32)
    lags = offsets[:, None] - offsets[None, :]
    decays = jnp.exp(-slopes[:, None, None] * jnp.maximum(lags, 0.0)[None])
    within = (doc_ids[:, :, None] == doc_ids[:, None, :]) & (lags >= 0.0)
    block_mask = jnp.where(within[:, None], decays[None], 0.0)
    continues = (doc_ids == prev_ids[:, None]).astype(F32)
    entry_scale = continues[..., None] * jnp.exp(-slopes[None, :] * (offsets[:, None] + 1.0))
    tail_scale = (doc_ids == doc_ids[:, -1:]).astype(F32)[..., None] * jnp.exp(
        -slopes[None, :] * (BLOCK - 1.0 - offsets)[:, None]
    )
    passing = continues[:, -1:] * jnp.exp(-slopes * BLOCK)

    def split_heads(values):
        return values.reshape(blocks, BLOCK, heads_here, HEAD)

    inputs = tokens[0].astype(F32)
    normed, in_scale = normalize(inputs)
    normed_bf = gather_rows(reorder(normed.astype(BF)))
    query_pre = matmul(normed_bf, w_query)
    key_pre = matmul(normed_bf, w_key)
    queries = split_heads(jax.nn.silu(query_pre).astype(BF))
    keys = split_heads(jax.nn.silu(key_pre).astype(BF))
    values = split_heads(matmul(normed_bf, w_value).astype(BF))
    gate = matmul(normed_bf, w_gate)
    scores = ein("bihe,bjhe->bhij", queries, keys)
    probs = (scores * block_mask).astype(BF)
    inner = ein("bhij,bjhe->bihe", probs, values)
    tail_keys = (keys.astype(F32) * tail_scale[..., None]).astype(BF)
    fresh = ein("bjhe,bjhf->bhef", tail_keys, values)
    state = jnp.zeros((heads_here, HEAD, HEAD), F32)
    entering = []
    for b in range(blocks):
        entering.append(state)
        state = passing[b][:, None, None] * state + fresh[b]
    block_in = jnp.stack(entering).astype(BF)
    across = entry_scale[..., None] * ein("bihe,bhef->bihf", queries, block_in)
    attention = (inner + across).reshape(query_pre.shape)

    attn_tok = to_tokens(attention)
    gate_tok = to_tokens(gate)
    attn_n, attn_scale = normalize(attn_tok)
    mixed = (attn_n * gate_tok).astype(BF)
    middle = inputs + matmul(mixed, w_out)
    middle_n, middle_scale = normalize(middle)
    middle_bf = gather_rows(reorder(middle_n.astype(BF)))
    ffn_val = matmul(middle_bf, w_fval)
    ffn_gat = matmul(middle_bf, w_fgate)
    ffn_mix = (ffn_val * ffn_gat).astype(BF)
    result = middle + scatter_rows(matmul(ffn_mix, w_fout))

    upstream = cotangent[0]
    up_all = gather_rows(upstream)
    grad_fout = weight_grad(ffn_mix, up_all)
    d_mix = matmul_right_t(up_all, w_fout)
    d_val = (d_mix * ffn_gat).astype(BF)
    d_gat = (d_mix * ffn_val).astype(BF)
    grad_fval = weight_grad(middle_bf, d_val)
    grad_fgate = weight_grad(middle_bf, d_gat)
    d_middle_n = restore(
        scatter_rows(matmul_right_t(d_val, w_fval) + matmul_right_t(d_gat, w_fgate))
    )
    d_middle = upstream.astype(F32) + normalize_back(middle_n, middle_scale, d_middle_n)
    d_branch = d_middle.astype(BF)
    grad_out = weight_grad(mixed, d_branch)
    d_mixed = matmul_right_t(d_branch, w_out)
    d_gate = to_heads((d_mixed * attn_n).astype(BF))
    d_attn = to_heads(normalize_back(attn_n, attn_scale, d_mixed * gate_tok).astype(BF))

    d_heads = split_heads(d_attn)
    d_probs = ein("bihe,bjhe->bhij", d_heads, values)
    d_scores = (d_probs * block_mask).astype(BF)
    d_query = ein("bhij,bjhe->bihe", d_scores, keys)
    d_key = ein("bhij,bihe->bjhe", d_scores, queries)
    d_value = ein("bhij,bihe->bjhe", probs, d_heads)
    d_query = d_query + entry_scale[..., None] * ein("bihf,bhef->bihe", d_heads, block_in)
    entry_queries = (queries.astype(F32) * entry_scale[..., None]).astype(BF)
    grad_in = ein("bihe,bihf->bhef", entry_queries, d_heads)
    state = jnp.zeros((heads_here, HEAD, HEAD), F32)
    leaving = [None] * blocks
    for b in reversed(range(blocks)):
        leaving[b] = state
        state = passing[b][:, None, None] * state + grad_in[b]
    block_out = jnp.stack(leaving).astype(BF)
    d_key = d_key + tail_scale[..., None] * ein("bjhf,bhef->bjhe", values, block_out)
    d_value = d_value + ein("bjhe,bhef->bjhf", tail_keys, block_out)
    dq_pre = (d_query.reshape(query_pre.shape) * silu_slope(query_pre)).astype(BF)
    dk_pre = (d_key.reshape(key_pre.shape) * silu_slope(key_pre)).astype(BF)
    dv_pre = d_value.reshape(query_pre.shape).astype(BF)
    grad_query = weight_grad(normed_bf, dq_pre)
    grad_key = weight_grad(normed_bf, dk_pre)
    grad_value = weight_grad(normed_bf, dv_pre)
    grad_gate = weight_grad(normed_bf, d_gate)
    d_normed = restore(
        scatter_rows(
            matmul_right_t(dq_pre, w_query)
            + matmul_right_t(dk_pre, w_key)
            + matmul_right_t(dv_pre, w_value)
            + matmul_right_t(d_gate, w_gate)
        )
    )
    d_inputs = d_middle + normalize_back(normed, in_scale, d_normed)
    return (
        result.astype(BF)[None],
        d_inputs[None],
        column_sums(grad_query),
        column_sums(grad_key),
        column_sums(grad_value),
        column_sums(grad_gate),
        lax.psum_scatter(grad_out.astype(BF), BOTH, scatter_dimension=0, tiled=True).astype(F32),
        column_sums(grad_fval),
        column_sums(grad_fgate),
        lax.psum_scatter(grad_fout.astype(BF), "narrow", scatter_dimension=0, tiled=True).astype(
            F32
        ),
    )


MESH = pl.DeviceIdType.MESH
ANY = pl.BlockSpec(memory_space=pl.ANY)
VMEM = pl.BlockSpec(memory_space=pltpu.VMEM)
WIDE, NARROW = 8, 4
CHIPS = WIDE // 2


def dot(left, right):
    return jnp.dot(left, right, preferred_element_type=F32)


def dot_rt(left, right):
    return lax.dot_general(left, right, (((1,), (1,)), ((), ())), preferred_element_type=F32)


def dot_lt(left, right):
    return lax.dot_general(left, right, (((0,), (0,)), ((), ())), preferred_element_type=F32)


def at(start, size):
    return pl.ds(pl.multiple_of(start, size), size)


class Links:
    def __init__(self, send, recv, here):
        self.send, self.recv, self.here = send, recv, here
        self.count = 0
        self.free = list(range(1, here.shape[0]))
        w = lax.axis_index("wide")
        n = lax.axis_index("narrow")
        self.w, self.n = w, n
        self.core = lax.rem(w, 2)
        self.chip = lax.div(w, 2)
        x, y = lax.rem(self.chip, 2), lax.div(self.chip, 2)
        self.wx = w + 2 - 4 * x
        self.wy = w + 4 - 8 * y
        self.wd = w + 6 - 4 * x - 8 * y
        self.ws = w + 1 - 2 * self.core
        self.px = self.chip + 1 - 2 * x
        self.py = self.chip + 2 - 4 * y
        self.pd = 3 - self.chip
        self.mid = lax.rem(lax.div(n + 1, 2), 2)
        self.pair = n + 1 - 2 * lax.rem(n, 2)
        self.cross = 2 - lax.div(n, 2)
        self.far = 3 - 3 * lax.div(n, 2)
        self.end_to = 3 * lax.rem(n + 1, 2)
        self.end_part = lax.rem(2 * n, 3) + 3 * lax.div(n, 3)

    def greet(self):
        barrier = pltpu.get_barrier_semaphore()
        for d in range(1, WIDE):
            pl.semaphore_signal(
                barrier, inc=1, device_id=(lax.rem(self.w + d, WIDE), self.n), device_id_type=MESH
            )
        for d in range(1, NARROW):
            pl.semaphore_signal(
                barrier, inc=1, device_id=(self.w, lax.rem(self.n + d, NARROW)), device_id_type=MESH
            )

    def met(self):
        pl.semaphore_wait(pltpu.get_barrier_semaphore(), WIDE + NARROW - 2)

    def take(self, number):
        base = self.count
        self.count += number
        return base

    def remote(self, src, dst, send, recv, wide=None, narrow=None):
        return pltpu.make_async_remote_copy(
            src_ref=src,
            dst_ref=dst,
            send_sem=self.send.at[send],
            recv_sem=self.recv.at[recv],
            device_id=(self.w if wide is None else wide, self.n if narrow is None else narrow),
            device_id_type=MESH,
        )

    def arrived(self, ref, recv):
        self.remote(ref, ref, recv, recv, wide=self.ws).wait_recv()

    def keep(self, src, dst):
        return Kept(self, src, dst)


class Kept:
    def __init__(self, links, src, dst):
        self.links, self.index = links, links.free.pop(0)
        self.copy = pltpu.make_async_copy(src, dst, links.here.at[self.index])
        self.copy.start()

    def wait(self):
        self.copy.wait()
        self.links.free.append(self.index)


class Line:
    def __init__(self, links, part):
        self.links, self.part = links, part
        self.base = links.take(5)

    def copy(self, index):
        k, b = self.links, self.base
        which, to = (
            (k.n, k.pair),
            (k.n, k.cross),
            (k.pair, k.cross),
            (k.cross, k.pair),
            (k.far, k.pair),
        )[index]
        ref = self.part(which)
        return k.remote(ref, ref, b + index, b + which, narrow=to)

    def start(self):
        self.start_away()
        pl.when(self.links.mid == 1)(lambda: self.copy(0).start())

    def start_away(self):
        pl.when(self.links.mid == 1)(lambda: self.copy(1).start())
        pl.when(self.links.mid == 0)(lambda: self.copy(0).start())

    def start_home(self):
        pl.when(self.links.mid == 1)(lambda: self.copy(0).start())

    def wait(self, index):
        self.links.arrived(self.part(index), self.base + index)

    def forward(self):
        @pl.when(self.links.mid == 1)
        def _():
            self.wait(self.links.cross)
            self.copy(3).start()
            self.wait(self.links.pair)
            self.copy(2).start()

    def forward_far(self):
        @pl.when(self.links.mid == 1)
        def _():
            self.wait(self.links.far)
            self.copy(4).start()

    def finish(self, then=lambda place: None, late=lambda: None):
        k = self.links
        then(0)
        for place, index in enumerate((k.pair, k.cross, k.far)):
            if place == 2:
                late()
            pl.when(k.mid == 0)(lambda index=index: self.wait(index))
            then(place + 1)

    def drain(self):
        self.copy(0).wait_send()

        @pl.when(self.links.mid == 1)
        def _():
            for index in range(1, 5):
                self.copy(index).wait_send()


class Plane:
    def __init__(self, links, slot):
        self.links, self.slot = links, slot
        self.base = links.take(6)

    def copy(self, index):
        k, b = self.links, self.base
        owner, half, to = (
            (k.w, 0, k.wx),
            (k.w, 1, k.wy),
            (k.w, 1, k.wx),
            (k.w, 0, k.wy),
            (k.wx, 0, k.wy),
            (k.wy, 1, k.wx),
        )[index]
        ref = self.slot(owner, half)
        return k.remote(ref, ref, b + index, b + index, wide=to)

    def start(self):
        for index in range(4):
            self.copy(index).start()

    def forward(self):
        k, b, slot = self.links, self.base, self.slot
        k.arrived(slot(k.wx, 0), b)
        self.copy(4).start()
        k.arrived(slot(k.wy, 1), b + 1)
        self.copy(5).start()

    def finish_near(self):
        k, b, slot = self.links, self.base, self.slot
        k.arrived(slot(k.wx, 1), b + 2)
        k.arrived(slot(k.wy, 0), b + 3)

    def finish_far(self):
        k, b, slot = self.links, self.base, self.slot
        k.arrived(slot(k.wd, 0), b + 4)
        k.arrived(slot(k.wd, 1), b + 5)

    def drain(self):
        for index in range(6):
            self.copy(index).wait_send()


class Sibling:
    def __init__(self, links, block, twin, number):
        self.links, self.block, self.twin, self.number = links, block, twin, number
        self.base = links.take(number)

    def copy(self, index):
        k, b = self.links, self.base + index
        ref = self.block(index)
        return k.remote(ref, ref, b, b, wide=k.ws)

    def send(self, index):
        self.copy(index).start()

    def wait(self, index):
        self.links.arrived(self.twin(index), self.base + index)

    def drain(self):
        for index in range(self.number):
            self.copy(index).wait_send()


class Spread:
    def __init__(self, links, src, dst, bulk, peers=WIDE):
        self.links, self.src, self.dst, self.bulk = links, src, dst, bulk
        self.step = 1 if peers == WIDE else 2
        self.base = links.take(1)

    def distances(self):
        return range(self.step, WIDE, self.step)

    def copy(self, to):
        k = self.links
        return k.remote(self.src(to), self.dst(k.w), self.base, self.base, wide=to)

    def start(self):
        for d in self.distances():
            self.copy(lax.rem(self.links.w + d, WIDE)).start()

    def finish(self):
        self.links.arrived(self.bulk, self.base)

    def drain(self):
        k = self.links
        k.remote(self.bulk, self.bulk, self.base, self.base, wide=k.ws).wait_send()


def row_scale(values):
    return lax.rsqrt(jnp.mean(values * values, axis=-1, keepdims=True) + EPS)


def row_chunks(rows, body, size=32):
    def step(r, carry):
        body(at(r * size, size))
        return carry

    lax.fori_loop(0, rows // size, step, 0)


class LineSum:
    def __init__(self, links, part, land):
        self.links, self.part, self.land = links, part, land
        self.base = links.take(5)
        self.onward = links.pair + links.mid * (links.cross - links.pair)

    def copy(self, index):
        k, b = self.links, self.base
        which, slot, to = (
            (k.far, 3 * k.mid, self.onward),
            (k.cross, 1 + 3 * k.mid, self.onward),
            (k.pair, 2 - 2 * k.mid, k.pair),
        )[index]
        return k.remote(self.part(which), self.land(slot), b + index, b + slot, narrow=to)

    def begin(self, index):
        pl.when(self.links.mid == 0)(lambda: self.copy(index).start())

    def start(self):
        for index in range(3):
            self.begin(index)

    def wait(self, slot):
        self.links.arrived(self.land(slot), self.base + slot)

    def pass_on(self, index, add):
        k = self.links
        which, slot = ((k.far, 0), (k.cross, 1), (k.pair, 3))[index]

        @pl.when(k.mid == 1)
        def _():
            self.wait(slot)
            add(self.part(which), self.land(slot))
            self.copy(index).start()

    def finish(self, fetch, spots):
        k = self.links
        pl.when(k.mid == 0)(lambda: self.wait(0))

        @pl.when(k.mid == 1)
        def _():
            self.wait(2)
            self.wait(4)
            fetch(self.land(4), spots.at[1])

        fetch(self.land(2 * k.mid), spots.at[0])

        @pl.when(k.mid == 0)
        def _():
            spots[1] = jnp.zeros(spots.shape[1:], spots.dtype)

    def drain(self):
        for index in range(3):
            self.copy(index).wait_send()


class PlaneSum:
    def __init__(self, links, block, corner, near, half, base=None, late=None):
        self.late = late
        self.links, self.block, self.corner, self.near, self.half = links, block, corner, near, half
        self.base = links.take(6) if base is None else base

    def rows(self, h):
        return pl.ds(h * self.half, self.half)

    def copy(self, index):
        k = self.links
        chip, h, land, to = (
            (k.pd, 0, self.corner.at[0], k.wx),
            (k.pd, 1, self.corner.at[1], k.wy),
            (k.px, 0, self.near.at[0, self.rows(0)], k.wx),
            (k.py, 1, self.near.at[1, self.rows(1)], k.wy),
            (k.px, 1, self.near.at[0, self.rows(1)], k.wx),
            (k.py, 0, self.near.at[1, self.rows(0)], k.wy),
        )[index]
        sem = self.base + index
        src = self.block(chip).at[self.rows(h)]
        if self.late is not None and index >= 4:
            src = self.late.at[self.rows(index - 4)]
        return k.remote(src, land, sem, sem, wide=to)

    def send_far(self):
        self.copy(0).start()
        self.copy(1).start()

    def send_x(self):
        self.copy(2).start()

    def send_y(self):
        self.copy(3).start()

    def combine(self, add):
        k = self.links
        for index, corner, chip, h in ((4, 1, k.px, 1), (5, 0, k.py, 0)):
            self.copy(corner).wait_recv()
            own = self.block(chip).at[self.rows(h)]
            to = own if self.late is None else self.late.at[self.rows(index - 4)]
            add(to, self.corner.at[corner], own)
            self.copy(index).start()

    def finish(self):
        for index in range(2, 6):
            self.copy(index).wait_recv()

    def drain(self, first=0, last=6):
        for index in range(first, last):
            self.copy(index).wait_send()


def layer_kernel(
    x_in, wq, wk, wv, wg, wo, fv, fg, fo, dy_arg, starts,
    result_o, dx_o, go_o, gfo_o, turn_ff, turn_qk,
    xn_in, wqk_in, wvg_in, wo_in, fv_in, fg_in, fo_in, dy_in, slope_in, qkv_in, sin_in, attn_in,
    gate_in, gated_in, mixed_in, x1_in, x1n_in,
    corner, near, twin_fo_land, twin_ff, twin_wo, twin_xn_land, land_fo, land_ff, land_wo, land_qk,
    a_land, s_land, sq_land, res_in,
    g_fo, g_fv, g_fg, stage, acc, tmp, scales, tmp_ff,
    send, recv, here,
):
    k = Links(send, recv, here)
    w, n, core, chip = k.w, k.n, k.core, k.chip
    other = 1 - core
    tok, width = acc.shape
    ff = g_fv.shape[-1]
    fo_rows = land_fo.shape[1]
    half = tok // 2
    two = 2 * HEAD
    order = (k.pd, k.px, k.py, chip)
    begins = [starts[n, j] for j in range(starts.shape[1])]

    def docs(positions):
        return sum((positions >= begin).astype(jnp.int32) for begin in begins)

    def slope(h):
        head = (2 * w + h + 1).astype(F32)
        rate = 1.0 - LAYER / (LAYERS - 1) + 1e-05
        return jnp.exp2(jnp.full((1, HEAD), -8.0 / HEADS, F32) * head)[:, 0:1] * rate

    def fill_decay(decay):
        i = lax.broadcasted_iota(jnp.int32, (BLOCK, BLOCK), 0)
        j = lax.broadcasted_iota(jnp.int32, (BLOCK, BLOCK), 1)
        lags = jnp.maximum(i - j, 0).astype(F32)
        for h in range(2):
            decay[h] = jnp.exp(-slope(h) * lags)

    def block_tables(b):
        first = b * BLOCK
        i = lax.broadcasted_iota(jnp.int32, (BLOCK, 1), 0)
        j = lax.broadcasted_iota(jnp.int32, (1, BLOCK), 1)
        ids = docs(first + i)
        mask = (ids == docs(first + j)) & (i >= j)
        before, at_end = docs(first - 1), docs(first + BLOCK - 1)
        steps = i.astype(F32)
        factors = []
        for h in range(2):
            rate = slope(h)
            entry = jnp.where(ids == before, jnp.exp(-rate * (steps + 1.0)), 0.0)
            tail = jnp.where(ids == at_end, jnp.exp(-rate * (BLOCK - 1.0 - steps)), 0.0)
            through = jnp.where(before == at_end, jnp.exp(-rate * BLOCK), 0.0)
            factors.append((entry, tail, through))
        return mask, factors

    def nth(j):
        flip_x, flip_y = 1 - lax.div(j, 2), 1 - lax.rem(j, 2)
        return (
            chip + flip_x * (1 - 2 * lax.rem(chip, 2)) + flip_y * (2 - 4 * lax.div(chip, 2))
        )

    def fetch(src, dst):
        copy = pltpu.make_async_copy(src, dst, here.at[0])
        copy.start()
        copy.wait()

    def adder(spot):
        def add(to, land, own=None):
            fetch(land, spot)
            own = to if own is None else own
            to[...] = (own[...].astype(F32) + spot[...].astype(F32)).astype(BF)

        return add

    add_half = adder(tmp.at[pl.ds(0, half)])
    add_fo = adder(tmp.at[pl.ds(0, fo_rows)])
    add_wo = adder(tmp.at[pl.ds(0, 64)])
    add_ff = adder(tmp_ff)

    def add_res(to, land, own):
        fetch(own, to)
        add_half(to, land)

    def fo_part(owner, i):
        return g_fo.at[pl.ds(pl.multiple_of((owner * NARROW + i) * fo_rows, 16), fo_rows)]

    sum_fo = LineSum(k, lambda i: fo_part(core, i), lambda s: land_fo.at[s])
    sum_ff = [
        LineSum(k, lambda i, g=g: g.at[:, i], lambda s, m=m: land_ff.at[m, s])
        for m, g in enumerate((g_fv, g_fg))
    ]
    def plane_sum(m, blocks, base=None, late=None):
        return PlaneSum(k, lambda q: blocks.at[q], corner.at[m], near.at[m], half, base, late)

    plane_mid, plane_in = (plane_sum(m, stage) for m in (0, 3))
    plane_res = plane_sum(1, res_in, late=stage.at[chip])
    twin_base = k.take(4 * 5)

    def twin(m, j, src, dst):
        sem = twin_base + 4 * m + j
        return k.remote(src, dst, sem, sem, wide=k.ws)

    def wide_cols(index):
        return at(index * two, two)

    def chip_cols(index):
        return pl.ds(pl.multiple_of(index * ff, 128), ff)

    projections = ((wq, wqk_in), (wk, wqk_in), (wv, wvg_in), (wg, wvg_in))
    lines = line_out, line_qk, line_vg, line_fv, line_fg, line_fo = (
        Line(k, lambda i: wo_in.at[w, i]),
        Line(k, lambda i: wqk_in.at[:, i]),
        Line(k, lambda i: wvg_in.at[:, i]),
        Line(k, lambda i: fv_in.at[:, core, i]),
        Line(k, lambda i: fg_in.at[:, core, i]),
        Line(k, lambda i: fo_in.at[core, i]),
    )
    spreads = [
        Spread(
            k,
            lambda t, weight=weight: weight.at[:, wide_cols(t)],
            lambda s, m=m, to=to: to.at[s, n, :, pl.ds((m % 2) * two, two)],
            to.at[pl.ds(0, WIDE - 1), n, :, pl.ds((m % 2) * two, two)],
        )
        for m, (weight, to) in enumerate(projections)
    ]
    spread_ff = [
        Spread(
            k,
            lambda t, weight=weight: weight.at[:, chip_cols(lax.div(t, 2))],
            lambda s, to=to: to.at[lax.div(s, 2), core, n],
            to.at[pl.ds(0, CHIPS - 1), core, n],
            peers=CHIPS,
        )
        for weight, to in ((fv, fv_in), (fg, fg_in))
    ]
    planes = plane_xn, plane_out, plane_dy, plane_x1n = (
        Plane(k, lambda s, h: xn_in.at[s, pl.ds(h * half, half)]),
        Plane(k, lambda s, h: wo_in.at[s, pl.ds(h * 2, 2)]),
        Plane(k, lambda s, h: dy_in.at[lax.div(s, 2), pl.ds(h * half, half)]),
        Plane(k, lambda s, h: x1n_in.at[lax.div(s, 2), pl.ds(h * half, half)]),
    )
    here4 = (w, k.wx, k.wy, k.wd)
    there4 = tuple(s + 1 - 2 * core for s in here4)
    near4 = (n, k.pair, k.cross, k.far)
    twins = twin_xn, twin_out, twin_fv, twin_fg, twin_fo = (
        Sibling(k, lambda i: xn_in.at[here4[i]], lambda i: xn_in.at[there4[i]], 4),
        Sibling(k, lambda i: wo_in.at[here4[i]], lambda i: wo_in.at[there4[i]], 4),
        Sibling(k, lambda i: fv_in.at[:, core, near4[i]], lambda i: fv_in.at[:, other, near4[i]], 4),
        Sibling(k, lambda i: fg_in.at[:, core, near4[i]], lambda i: fg_in.at[:, other, near4[i]], 4),
        Sibling(k, lambda i: fo_in.at[core, near4[i]], lambda i: fo_in.at[other, near4[i]], 4),
    )

    k.greet()
    def before(
        x, xn, wqk, wvg, wout, slopes, qkv, gates, sin, state, attn_s, gated_s,
        squares, sums, gated, mixed, x1, x1n, decay,
    ):
        load_x = k.keep(x_in, x)
        held = [
            (k.keep(wo, mixed.at[pl.ds(0, 64)]), mixed.at[pl.ds(0, 64)], wo_in.at[w, n]),
            *[
                (
                    k.keep(weight.at[:, wide_cols(w)], spot.at[w, n, :, lanes]),
                    spot.at[w, n, :, lanes],
                    to.at[w, n, :, lanes],
                )
                for weight, spot, to, lanes in (
                    (wq, wqk, wqk_in, pl.ds(0, two)),
                    (wk, wqk, wqk_in, pl.ds(two, two)),
                    (wv, wvg, wvg_in, pl.ds(0, two)),
                    (wg, wvg, wvg_in, pl.ds(two, two)),
                )
            ],
            (k.keep(dy_arg, gated), gated, dy_in.at[chip]),
            *[
                (
                    k.keep(weight.at[:, chip_cols(chip)], tmp_ff.at[m]),
                    tmp_ff.at[m],
                    to.at[chip, core, n],
                )
                for m, (weight, to) in enumerate(((fv, fv_in), (fg, fg_in)))
            ],
            (k.keep(fo, tmp.at[pl.ds(0, fo_rows)]), tmp.at[pl.ds(0, fo_rows)], fo_in.at[core, n]),
        ]

        def place(index):
            load, spot, to = held[index]
            load.wait()
            return k.keep(spot, to)

        load_x.wait()

        def norm_in(rows):
            v = x[rows, :].astype(F32)
            x1n[rows, :] = (v * row_scale(v)).astype(BF)

        row_chunks(tok, norm_in)
        own_xn = k.keep(x1n, xn_in.at[w])
        own_in = [place(i) for i in range(5)]
        k.met()
        for spread in spreads:
            spread.start()
        own_in[0].wait()
        line_out.start()
        own_xn.wait()
        for copy in own_in[1:]:
            copy.wait()
        spreads[0].finish()
        spreads[1].finish()
        line_qk.start()
        plane_xn.start()
        twin_xn.send(0)
        spreads[2].finish()
        spreads[3].finish()
        line_vg.start()
        for spread in spread_ff:
            spread.start()
        own_ff = [place(i) for i in range(5, 9)]
        line_out.forward()
        plane_xn.forward()
        line_out.forward_far()
        line_qk.forward()
        plane_xn.finish_near()
        twin_xn.send(1)
        twin_xn.send(2)
        line_vg.forward()
        line_qk.forward_far()
        line_out.finish()
        plane_out.start()
        twin_out.send(0)
        plane_xn.finish_far()
        twin_xn.send(3)
        line_vg.forward_far()
        spread_ff[0].finish()
        spread_ff[1].finish()
        for copy in own_ff:
            copy.wait()
        line_fv.start()
        for i in range(4):
            twin_xn.wait(i)
        load_xn = k.keep(xn_in, xn)
        plane_out.forward()
        line_qk.finish()
        load_qk = k.keep(wqk_in, wqk)
        load_xn.wait()
        load_qk.wait()

        def project_qk(t, carry):
            v = dot(xn[t], wqk[...].reshape(width, 2 * two))
            rows = at(t * tok, tok)
            sigma = jax.nn.sigmoid(v)
            slopes[rows, :] = (sigma * (1.0 + v * (1.0 - sigma))).astype(BF)
            qkv[rows, 0 : 2 * two] = (v * sigma).astype(BF)
            return carry

        lax.fori_loop(0, WIDE, project_qk, 0)
        stores = [k.keep(slopes, slope_in)]
        plane_out.finish_near()
        twin_out.send(1)
        twin_out.send(2)
        line_vg.finish()
        k.keep(wvg_in, wvg).wait()

        def project_vg(t, carry):
            v = dot(xn[t], wvg[...].reshape(width, 2 * two)).astype(BF)
            qkv[at(t * tok, tok), 2 * two : 3 * two] = v[:, 0:two]
            gates[t] = v[:, two:]
            return carry

        lax.fori_loop(0, WIDE, project_vg, 0)
        line_fv.forward()
        line_fg.start()
        stores.append(k.keep(qkv, qkv_in))
        stores.append(k.keep(gates, gate_in))
        fill_decay(decay)
        state[...] = jnp.zeros_like(state)
        spread_gated = Spread(
            k,
            lambda t: gated_s.at[t],
            lambda s: gated_in.at[:, wide_cols(s)],
            gated_in.at[:, pl.ds(0, (WIDE - 1) * two)],
        )
        spread_sq = Spread(
            k, lambda t: squares.at[t], lambda s: sq_land.at[s], sq_land.at[pl.ds(0, WIDE - 1)]
        )

        def attend(b, carry):
            rows = at(b * BLOCK, BLOCK)
            mask, factors = block_tables(b)
            for h in range(2):
                lanes = slice(h * HEAD, (h + 1) * HEAD)
                entry, tail, through = factors[h]
                q = qkv[rows, lanes]
                key = qkv[rows, two + h * HEAD : two + (h + 1) * HEAD]
                v = qkv[rows, 2 * two + h * HEAD : 2 * two + (h + 1) * HEAD]
                probs = jnp.where(mask, dot_rt(q, key) * decay[h], 0.0).astype(BF)
                old = state[h]
                old_bf = old.astype(BF)
                sin[b, h] = old_bf
                out = dot(probs, v) + entry * dot(q, old_bf)
                attn_s[b, :, lanes] = out.astype(BF)
                gated_s[b, :, lanes] = (out * gates[b, :, lanes].astype(F32)).astype(BF)
                tailed = (key.astype(F32) * tail).astype(BF)
                state[h] = through * old + dot_lt(tailed, v)

            a = attn_s[b].astype(F32)
            squares[b] = dot_rt(jnp.ones((8, two), BF), (a * a).astype(BF))

            @pl.when(b != w)
            def _():
                spread_sq.copy(b).start()
                spread_gated.copy(b).start()

            return carry

        lax.fori_loop(0, WIDE, attend, 0)
        stores.append(k.keep(sin, sin_in))
        stores.append(k.keep(attn_s, attn_in))
        own = [
            k.keep(gated_s.at[w], gated_in.at[:, wide_cols(w)]),
            k.keep(squares.at[w], sq_land.at[w]),
        ]
        plane_out.finish_far()
        twin_out.send(3)
        for i in range(4):
            twin_out.wait(i)
        load_out = k.keep(wo_in, wout)
        line_fv.forward_far()
        spread_sq.finish()
        spread_gated.finish()
        for copy in own:
            copy.wait()
        loads = [k.keep(gated_in, gated), k.keep(sq_land, sums)]
        for copy in loads:
            copy.wait()
        total_sq = sum(sums[s, 0:1, :] for s in range(WIDE))
        scales[...] = jnp.transpose(
            jnp.broadcast_to(lax.rsqrt(total_sq * (1.0 / width) + EPS), (HEAD, tok))
        )

        def mix(rows):
            mixed[rows, :] = (gated[rows, :].astype(F32) * scales[rows, 0:1]).astype(BF)

        row_chunks(tok, mix)
        stores.append(k.keep(mixed, mixed_in))
        load_out.wait()

        def project_out(j, carry):
            lanes = at(j * 512, 512)
            part = dot(mixed[...], wout[:, :, :, lanes].reshape(-1, 512))
            x1[:, lanes] = x[:, lanes].astype(F32) + part
            return carry

        lax.fori_loop(0, width // 512, project_out, 0)
        stores.append(k.keep(x1, x1_in))

        def norm_mid(rows):
            v = x1[rows, :]
            x1n[rows, :] = (v * row_scale(v)).astype(BF)

        row_chunks(tok, norm_mid)
        k.keep(x1n, x1n_in.at[chip]).wait()
        plane_x1n.start()
        line_fg.forward()
        line_fo.start_away()
        plane_x1n.forward()
        plane_dy.start()
        line_fg.forward_far()
        for copy in stores:
            copy.wait()
        spread_sq.drain()
        spread_gated.drain()

    pl.run_scoped(
        before,
        pltpu.VMEM((tok, width), BF),
        pltpu.VMEM((WIDE, tok, width), BF),
        pltpu.VMEM(wqk_in.shape, BF),
        pltpu.VMEM(wvg_in.shape, BF),
        pltpu.VMEM(wo_in.shape, BF),
        pltpu.VMEM(slope_in.shape, BF),
        pltpu.VMEM(qkv_in.shape, BF),
        pltpu.VMEM((WIDE, tok, two), BF),
        pltpu.VMEM(sin_in.shape, BF),
        pltpu.VMEM((2, HEAD, HEAD), F32),
        pltpu.VMEM((WIDE, tok, two), BF),
        pltpu.VMEM((WIDE, tok, two), BF),
        pltpu.VMEM((WIDE, 8, tok), F32),
        pltpu.VMEM((WIDE, 8, tok), F32),
        pltpu.VMEM((tok, width), BF),
        pltpu.VMEM((tok, width), BF),
        pltpu.VMEM((tok, width), F32),
        pltpu.VMEM((tok, width), BF),
        pltpu.VMEM((2, BLOCK, BLOCK), F32),
    )

    def ffn(x1n, dy, fvw, fgw, fow, mix, val, gat, side, tmp_twin):
        def shares(moved, src, dst, places):
            copies = []
            for i in places:
                moved.wait(i)
                copies.append(k.keep(src.at[:, :, near4[i]], dst.at[:, :, near4[i]]))
            return copies

        def fo_shares(places):
            copies = []
            for i in places:
                twin_fo.wait(i)
                copies.append(k.keep(fo_in.at[:, near4[i]], fow.at[:, near4[i]]))
            return copies

        line_fv.finish(twin_fv.send)
        load_fv = shares(twin_fv, fv_in, fvw, range(4))
        plane_x1n.finish_near()
        plane_x1n.finish_far()
        load_x1n = k.keep(x1n_in, x1n)
        for copy in (load_x1n, *load_fv):
            copy.wait()

        def up_val(j, carry):
            val[j] = dot(x1n[j], fvw[...].reshape(width, ff)).astype(BF)
            return carry

        def up_gat(j, carry):
            g = dot(x1n[j], fgw[...].reshape(width, ff))
            gat[j] = g.astype(BF)
            mix[j] = (val[j].astype(F32) * g).astype(BF)
            return carry

        lax.fori_loop(0, CHIPS, up_val, 0)
        line_fo.forward()
        plane_dy.forward()
        load_fg = []
        line_fg.finish(twin_fg.send, lambda: load_fg.extend(shares(twin_fg, fg_in, fgw, range(3))))
        line_fo.start_home()
        load_fg += shares(twin_fg, fg_in, fgw, range(3, 4))
        for copy in load_fg:
            copy.wait()
        line_fo.forward_far()
        lax.fori_loop(0, CHIPS // 2, up_gat, 0)
        plane_dy.finish_near()
        plane_dy.finish_far()
        load_dy = k.keep(dy_in, dy)
        lax.fori_loop(CHIPS // 2, CHIPS, up_gat, 0)
        load_dy.wait()

        def fo_grad(j, carry):
            chunk = lax.rem(j + 2 * other, chunks)
            rows = pl.ds(pl.multiple_of(jnp.minimum(chunk * 256, ff - 256), 128), 256)
            left = mix[:, :, rows].reshape(CHIPS * tok, 256)
            for h in range(2):
                lanes = slice(h * width // 2, (h + 1) * width // 2)
                right = dy[:, :, lanes].reshape(CHIPS * tok, -1)
                g_fo[rows, lanes] = dot_lt(left, right).astype(BF)
            return carry

        chunks = pl.cdiv(ff, 256)
        lax.fori_loop(0, 4, fo_grad, 0)
        for i in range(NARROW):
            there = near4[NARROW - 1 - i]
            twin(0, there, fo_part(other, there), twin_fo_land.at[there]).start()
        lax.fori_loop(4, chunks, fo_grad, 0)
        came = []
        for i in reversed(range(NARROW)):
            copy = twin(0, near4[i], fo_part(other, near4[i]), twin_fo_land.at[near4[i]])
            copy.wait_recv()
            spot = stage.at[i, pl.ds(0, fo_rows)]
            came.append((i, copy, k.keep(twin_fo_land.at[near4[i]], spot), spot))
        for i, copy, load, spot in came:
            load.wait()
            own = fo_part(core, near4[i])
            own[...] = (own[...].astype(F32) + spot[...].astype(F32)).astype(BF)
            copy.wait_send()
            if i > 0:
                sum_fo.begin(3 - i)
        load_fo = []
        line_fo.finish(twin_fo.send, lambda: load_fo.extend(fo_shares(range(3))))
        load_fo += fo_shares(range(3, 4))
        for copy in load_fo:
            copy.wait()

        def down(q, carry):
            d_mix = dot_rt(dy[q], fow[...].reshape(ff, width))
            d_val = (d_mix * gat[q].astype(F32)).astype(BF)
            d_gat = (d_mix * val[q].astype(F32)).astype(BF)
            val[q] = d_val
            gat[q] = d_gat
            return carry

        lax.fori_loop(0, CHIPS, down, 0)

        def out_step(q, carry):
            dy[q] = dot(mix[q], fow[...].reshape(ff, width)).astype(BF)
            return carry

        def back(j, carry):
            q = nth(j)

            def back_lanes(i, carry):
                lanes = at(i * 512, 512)
                d_x = dot_rt(val[q], fvw[i].reshape(512, ff)) + dot_rt(
                    gat[q], fgw[i].reshape(512, ff)
                )

                @pl.when(j < 3)
                def _():
                    stage[q, :, lanes] = d_x.astype(BF)

                @pl.when(j == 3)
                def _():
                    acc[:, lanes] = d_x

                return carry

            lax.fori_loop(0, width // 512, back_lanes, 0)
            for step, push in enumerate((plane_mid.send_far, plane_mid.send_x, plane_mid.send_y)):
                pl.when(j == step)(push)
            return carry

        for m, (d_ff, g_ff) in enumerate(((val, g_fv), (gat, g_fg))):

            def ff_grad(owner):
                left = x1n[:, :, at(owner * tok, tok)].reshape(CHIPS * tok, tok)
                g = dot_lt(left, d_ff[...].reshape(CHIPS * tok, ff)).astype(BF)
                return g.reshape(NARROW, -1, ff)

            def side_step(q, carry):
                slot = lax.rem(q, 2)

                @pl.when(q >= 2)
                def _():
                    twin(1 + m, q - 2, side.at[slot], twin_ff.at[m, q]).wait_send()

                side[slot] = ff_grad(2 * q + other)
                twin(1 + m, q, side.at[slot], twin_ff.at[m, q]).start()
                return carry

            def own_step(q, carry):
                g_ff[q] = ff_grad(2 * q + core)
                return carry

            lax.fori_loop(0, CHIPS, side_step, 0)
            lax.fori_loop(0, CHIPS, own_step, 0)
            loads = []
            for q in range(CHIPS + 1):
                if q < CHIPS:
                    twin(1 + m, q, side.at[q % 2], twin_ff.at[m, q]).wait_recv()
                    loads.append(k.keep(twin_ff.at[m, q], (tmp_ff, tmp_twin)[q % 2]))
                if q > 0:
                    loads[q - 1].wait()
                    own = g_ff.at[q - 1]
                    own[...] = (
                        own[...].astype(F32) + (tmp_ff, tmp_twin)[(q - 1) % 2][...].astype(F32)
                    ).astype(BF)
            for q in range(2, CHIPS):
                twin(1 + m, q, side.at[q % 2], twin_ff.at[m, q]).wait_send()
            sum_ff[m].start()
            if m == 0:
                lax.fori_loop(0, CHIPS, back, 0)
                lax.fori_loop(0, CHIPS, out_step, 0)
                store = k.keep(dy, res_in)
                plane_mid.combine(add_half)
                store.wait()
                plane_res.send_far()
                plane_res.send_x()
                plane_res.send_y()
                sum_fo.pass_on(0, add_fo)
                sum_fo.pass_on(1, add_fo)

        sum_fo.pass_on(2, add_fo)
        plane_mid.drain()

    pl.run_scoped(
        ffn,
        pltpu.VMEM((CHIPS, tok, width), BF),
        pltpu.VMEM((CHIPS, tok, width), BF),
        pltpu.VMEM(fv_in.shape, BF),
        pltpu.VMEM(fg_in.shape, BF),
        pltpu.VMEM(fo_in.shape, BF),
        pltpu.VMEM((CHIPS, tok, ff), BF),
        pltpu.VMEM((CHIPS, tok, ff), BF),
        pltpu.VMEM((CHIPS, tok, ff), BF),
        pltpu.VMEM((2, *g_fv.shape[1:]), BF),
        pltpu.VMEM(g_fv.shape[1:], BF),
    )

    def rest(d_x1, d_branch, mixed, da_src, factors_src, side, stage_wo, g_wo, g_qk, g_vg):
        plane_out = plane_sum(2, stage_wo)
        sum_wo = LineSum(k, lambda i: g_wo.at[i], lambda s: land_wo.at[s])
        sum_qk = [
            LineSum(k, lambda i, g=g: g.at[:, i], lambda s, m=m: land_qk.at[m, s])
            for m, g in enumerate((g_qk, g_vg))
        ]
        spread_a = Spread(
            k,
            lambda t: da_src.at[:, at(t * two, two)],
            lambda s: a_land.at[s],
            a_land.at[pl.ds(0, WIDE - 1)],
        )
        spread_s = Spread(
            k, lambda t: factors_src, lambda s: s_land.at[s], s_land.at[pl.ds(0, WIDE - 1)]
        )

        def middle(wo, x1, gated, means, dy, d_mixed, pair):
            plane_mid.finish()
            loads = [k.keep(near.at[0], pair), k.keep(x1_in, x1), k.keep(dy_in.at[chip], dy)]
            late = [
                k.keep(wo_in, wo), k.keep(gated_in, gated), k.keep(mixed_in, mixed),
            ]
            for copy in loads:
                copy.wait()

            def norm_back(rows):
                g = acc[rows, :] + pair[0, rows, :].astype(F32) + pair[1, rows, :].astype(F32)
                v = x1[rows, :]
                r = row_scale(v)
                u = v * r
                d = dy[rows, :].astype(F32) + r * (g - u * jnp.mean(g * u, axis=-1, keepdims=True))
                d_x1[rows, :] = d
                d_branch[rows, :] = d.astype(BF)

            row_chunks(tok, norm_back)
            for copy in late:
                copy.wait()

            def mixed_step(j, carry):
                d_mixed[:, at(j * 512, 512)] = dot_rt(
                    d_branch[...], wo[pl.ds(2 * j, 2)].reshape(512, width)
                )
                return carry

            lax.fori_loop(0, width // 512, mixed_step, 0)

            def mixed_back(rows):
                d = d_mixed[rows, :]
                da_src[rows, :] = d.astype(BF)
                mean = jnp.mean(d * gated[rows, :].astype(F32), axis=-1, keepdims=True)
                means[rows, :] = jnp.broadcast_to(mean * scales[rows, 0:1], (mean.shape[0], HEAD))

            row_chunks(tok, mixed_back)
            factors_src[0] = jnp.transpose(scales[...])[0:8]
            factors_src[1] = jnp.transpose(means[...])[0:8]
            spread_s.start()
            spread_a.start()
            own = [
                k.keep(da_src.at[:, at(w * two, two)], a_land.at[w]),
                k.keep(factors_src, s_land.at[w]),
            ]

            for copy in own:
                copy.wait()

        pl.run_scoped(
            middle,
            pltpu.VMEM(wo_in.shape, BF),
            pltpu.VMEM((tok, width), F32),
            pltpu.VMEM((tok, width), BF),
            pltpu.VMEM((tok, HEAD), F32),
            pltpu.VMEM((tok, width), BF),
            pltpu.VMEM((tok, width), F32),
            pltpu.VMEM((2, tok, width), BF),
        )
        def eight_way(plane, twin_index, landing, blocks, spots, term):
            def side_step(j, carry):
                q = nth(j)
                side[q] = term(2 * q + other).astype(BF)
                twin(twin_index, j, side.at[q], landing.at[q]).start()
                return carry

            lax.fori_loop(0, CHIPS, side_step, 0)

            def load(j):
                q = order[j]
                twin(twin_index, j, side.at[q], landing.at[q]).wait_recv()
                return k.keep(landing.at[q], spots[j % 2])

            pushes = (plane.send_far, plane.send_x, plane.send_y)
            loads = [load(0)]
            for j in range(CHIPS):
                if j + 1 < CHIPS and spots[0] is not spots[1]:
                    loads.append(load(j + 1))
                v = term(2 * order[j] + core)
                loads[j].wait()
                v = v + spots[j % 2][...].astype(F32)
                if j < 3:
                    blocks[order[j]] = v.astype(BF)
                    pushes[j]()
                else:
                    acc[...] = v
                if j + 1 < CHIPS and spots[0] is spots[1]:
                    loads.append(load(j + 1))
            for j in range(CHIPS):
                twin(twin_index, j, side.at[order[j]], landing.at[order[j]]).wait_send()

        eight_way(
            plane_out,
            3,
            twin_wo,
            stage_wo,
            (tmp, tmp),
            lambda owner: dot_lt(mixed[:, at(owner * tok, tok)], d_branch[...]),
        )
        sum_ff[0].pass_on(0, add_ff)
        sum_ff[0].pass_on(1, add_ff)

        def attention(xn, d_qk, d_vg, state):
            state[...] = jnp.zeros_like(state)

            def heads(slopes, qkv, sin, decay, attn, gate, d_mixed, factors_in):
                loads = [
                    k.keep(qkv_in, qkv), k.keep(sin_in, sin), k.keep(slope_in, slopes),
                    k.keep(attn_in, attn), k.keep(gate_in, gate),
                ]
                fill_decay(decay)
                for copy in loads:
                    copy.wait()
                spread_s.finish()
                spread_a.finish()
                loads = [k.keep(a_land, d_mixed), k.keep(s_land, factors_in)]
                for copy in loads:
                    copy.wait()
                load_xn = k.keep(xn_in, xn)

                def step(i, carry):
                    b = WIDE - 1 - i
                    rows = at(b * BLOCK, BLOCK)
                    mask, factors = block_tables(b)
                    scale, mean = (
                        jnp.transpose(jnp.broadcast_to(factors_in[b, i, 0:1], (HEAD, tok)))[:, 0:1]
                        for i in range(2)
                    )
                    normed = attn[b].astype(F32) * scale
                    d_m = d_mixed[b].astype(F32)
                    d_vg[rows, two:] = (d_m * normed).astype(BF)
                    d_attn = (scale * (d_m * gate[b].astype(F32) - normed * mean)).astype(BF)
                    for h in range(2):
                        entry, tail, through = factors[h]
                        lanes = slice(h * HEAD, (h + 1) * HEAD)
                        key_lanes = slice(two + h * HEAD, two + (h + 1) * HEAD)
                        q = qkv[rows, lanes]
                        key = qkv[rows, key_lanes]
                        v = qkv[rows, 2 * two + h * HEAD : 2 * two + (h + 1) * HEAD]
                        d_o = d_attn[:, lanes]
                        factor = jnp.where(mask, decay[h], 0.0)
                        probs = (dot_rt(q, key) * factor).astype(BF)
                        d_probs = (dot_rt(d_o, v) * factor).astype(BF)
                        before = sin[b, h]
                        after = state[h]
                        after_bf = after.astype(BF)
                        tailed = (key.astype(F32) * tail).astype(BF)
                        entered = (q.astype(F32) * entry).astype(BF)
                        d_q = dot(d_probs, key) + entry * dot_rt(d_o, before)
                        d_k = dot_lt(d_probs, q) + tail * dot_rt(v, after_bf)
                        d_v = dot_lt(probs, d_o) + dot(tailed, after_bf)
                        d_qk[rows, lanes] = (d_q * slopes[rows, lanes].astype(F32)).astype(BF)
                        d_qk[rows, key_lanes] = (d_k * slopes[rows, key_lanes].astype(F32)).astype(BF)
                        d_vg[rows, lanes] = d_v.astype(BF)
                        state[h] = through * after + dot_lt(entered, d_o)
                    return carry

                lax.fori_loop(0, WIDE, step, 0)
                sum_ff[0].pass_on(2, add_ff)
                load_xn.wait()

            pl.run_scoped(
                heads,
                pltpu.VMEM(slope_in.shape, BF),
                pltpu.VMEM(qkv_in.shape, BF),
                pltpu.VMEM(sin_in.shape, BF),
                pltpu.VMEM((2, BLOCK, BLOCK), F32),
                pltpu.VMEM((WIDE, tok, two), BF),
                pltpu.VMEM((WIDE, tok, two), BF),
                pltpu.VMEM((WIDE, tok, two), BF),
                pltpu.VMEM(s_land.shape, F32),
            )

            for m, (d_in, g_in) in enumerate(((d_qk, g_qk), (d_vg, g_vg))):

                def in_grad(s, carry):
                    left = xn[:, :, at(s * tok, tok)].reshape(WIDE * tok, tok)
                    g_in[s] = dot_lt(left, d_in[...]).astype(BF).reshape(NARROW, -1, 2 * two)
                    return carry

                lax.fori_loop(0, WIDE, in_grad, 0)
                sum_qk[m].start()

            plane_out.combine(add_half)
            plane_res.combine(add_res)
            sum_ff[1].pass_on(0, add_ff)
            sum_ff[1].pass_on(1, add_ff)
            g_wo[...] = acc[...].astype(BF).reshape(g_wo.shape)

            def spread_in(wqk, wvg):
                loads = [k.keep(wqk_in, wqk), k.keep(wvg_in, wvg)]
                for copy in loads:
                    copy.wait()

                def term(owner):
                    rows = at(owner * tok, tok)
                    return dot_rt(d_qk[rows, :], wqk[...].reshape(width, 2 * two)) + dot_rt(
                        d_vg[rows, :], wvg[...].reshape(width, 2 * two)
                    )

                spread_a.drain()
                eight_way(plane_in, 4, twin_xn_land, stage, (tmp, da_src), term)

            pl.run_scoped(spread_in, pltpu.VMEM(wqk_in.shape, BF), pltpu.VMEM(wvg_in.shape, BF))

        pl.run_scoped(
            attention,
            pltpu.VMEM((WIDE, tok, width), BF),
            pltpu.VMEM((WIDE * tok, 2 * two), BF),
            pltpu.VMEM((WIDE * tok, 2 * two), BF),
            pltpu.VMEM((2, HEAD, HEAD), F32),
        )

        def last(
            x, x1, own_res, pair, three, three_ff, three_qk, ff_src, qk_src, w_f32, w_fo, tmp_qk
        ):
            add_qk = adder(tmp_qk)
            load_x, load_x1 = k.keep(x_in, x), k.keep(x1_in, x1)
            load_res = k.keep(res_in.at[chip], own_res)
            plane_in.combine(add_half)
            sum_ff[1].pass_on(2, add_ff)
            sum_qk[0].pass_on(0, add_qk)
            sum_qk[0].pass_on(1, add_qk)
            plane_out.finish()
            fetch(near.at[2], pair)
            for i in range(NARROW):
                rows = pl.ds(i * 64, 64)
                v = g_wo[i].astype(F32) + pair[0, rows, :].astype(F32) + pair[1, rows, :].astype(F32)
                g_wo[i] = v.astype(BF)
            sum_wo.start()

            def total(part, lands):
                return part.astype(F32) + lands[0].astype(F32) + lands[1].astype(F32)

            ff_turns = []
            for m, g_ff in enumerate((g_fv, g_fg)):
                sum_ff[m].finish(fetch, three_ff)
                for q in range(CHIPS):
                    ff_src[m, q] = total(g_ff[q, n], three_ff[:, q]).astype(BF)
                turn = Spread(
                    k,
                    lambda t, m=m: ff_src.at[m, lax.div(t, 2)],
                    lambda s, m=m: turn_ff.at[m, lax.div(s, 2)],
                    turn_ff.at[m, pl.ds(0, CHIPS - 1)],
                    peers=CHIPS,
                )
                turn.start()
                ff_turns.append((turn, k.keep(ff_src.at[m, chip], turn_ff.at[m, chip])))
            sum_qk[0].pass_on(2, add_qk)
            sum_fo.finish(fetch, three.at[:, pl.ds(0, fo_rows)])
            own = fo_part(core, n)
            for r in range(0, fo_rows, 16):
                rows = pl.ds(r, 16)
                w_fo[rows, :] = total(own[rows, :], three[:, rows, :])
            stores = [k.keep(w_fo, gfo_o)]

            plane_res.finish()
            fetch(near.at[1], pair)
            load_x1.wait()
            load_res.wait()

            def add_up(rows):
                v = x1[rows, :] + own_res[rows, :].astype(F32)
                v = v + pair[0, rows, :].astype(F32) + pair[1, rows, :].astype(F32)
                own_res[rows, :] = v.astype(BF)

            row_chunks(tok, add_up)
            stores.append(k.keep(own_res, result_o))
            sum_qk[1].pass_on(0, add_qk)
            sum_qk[1].pass_on(1, add_qk)
            load_x.wait()
            plane_in.finish()
            fetch(near.at[3], pair)

            def input_back(rows):
                g = acc[rows, :] + pair[0, rows, :].astype(F32) + pair[1, rows, :].astype(F32)
                v = x[rows, :].astype(F32)
                r = row_scale(v)
                u = v * r
                d_x1[rows, :] = d_x1[rows, :] + r * (
                    g - u * jnp.mean(g * u, axis=-1, keepdims=True)
                )

            row_chunks(tok, input_back)
            stores.append(k.keep(d_x1, dx_o))
            qk_turns = []
            for m, g_in in enumerate((g_qk, g_vg)):
                if m == 1:
                    sum_qk[1].pass_on(2, add_qk)
                    sum_wo.pass_on(0, add_wo)
                    sum_wo.pass_on(1, add_wo)
                sum_qk[m].finish(fetch, three_qk)
                for s in range(WIDE):
                    qk_src[m, s] = total(g_in[s, n], three_qk[:, s]).astype(BF)
                turn = Spread(
                    k,
                    lambda t, m=m: qk_src.at[m, t],
                    lambda s, m=m: turn_qk.at[m, s],
                    turn_qk.at[m, pl.ds(0, WIDE - 1)],
                )
                turn.start()
                qk_turns.append((turn, k.keep(qk_src.at[m, w], turn_qk.at[m, w])))
            sum_wo.pass_on(2, add_wo)
            for turn, copy in ff_turns + qk_turns:
                turn.finish()
                copy.wait()
            sum_wo.finish(fetch, three.at[:, pl.ds(0, 64)])
            w_f32[...] = total(g_wo[n], three[:, 0:64, :])
            stores.append(k.keep(w_f32, go_o))
            for copy in stores:
                copy.wait()
            plane_in.drain()
            plane_out.drain()
            plane_res.drain()
            turns = [turn for turn, copy in ff_turns + qk_turns]
            for moved in (*lines, *planes, *twins, *spreads, *spread_ff):
                moved.drain()
            for sums in (sum_fo, sum_wo, *sum_ff, *sum_qk, spread_s, *turns):
                sums.drain()

        pl.run_scoped(
            last,
            pltpu.VMEM((tok, width), BF),
            pltpu.VMEM((tok, width), F32),
            pltpu.VMEM((tok, width), BF),
            pltpu.VMEM((2, tok, width), BF),
            pltpu.VMEM((2, tok, width), BF),
            pltpu.VMEM((2, *land_ff.shape[2:]), BF),
            pltpu.VMEM((2, *land_qk.shape[2:]), BF),
            pltpu.VMEM((2, CHIPS, 64, ff), BF),
            pltpu.VMEM((2, WIDE, 64, 2 * two), BF),
            pltpu.VMEM((64, width), F32),
            pltpu.VMEM((fo_rows, width), F32),
            pltpu.VMEM((WIDE, 64, 2 * two), BF),
        )

    pl.run_scoped(
        rest,
        pltpu.VMEM((tok, width), F32),
        pltpu.VMEM((tok, width), BF),
        pltpu.VMEM((tok, width), BF),
        pltpu.VMEM((tok, width), BF),
        pltpu.VMEM((2, 8, tok), F32),
        pltpu.VMEM((CHIPS, tok, width), BF),
        pltpu.VMEM((CHIPS, tok, width), BF),
        pltpu.VMEM((NARROW, 64, width), BF),
        pltpu.VMEM((WIDE, NARROW, 64, 2 * two), BF),
        pltpu.VMEM((WIDE, NARROW, 64, 2 * two), BF),
    )
    assert k.count <= send.shape[0], k.count


def finish_kernel(
    result, d_x, g_out, g_fout, turn_ff, turn_qk,
    result_o, d_x_o, gq_o, gk_o, gv_o, gg_o, go_o, gfv_o, gfg_o, gfo_o,
    result_v, d_x_v, g_out_v, g_fout_v, ff_v, qk_v, ff_f32, qk_f32, sems,
):
    copies = []

    def copy(src, dst):
        made = pltpu.make_async_copy(src, dst, sems.at[len(copies)])
        made.start()
        copies.append(made)
        return made

    ff, two = ff_v.shape[-1], qk_v.shape[-1] // 2
    load_ff, load_qk = copy(turn_ff, ff_v), copy(turn_qk, qk_v)
    through = (
        (d_x, d_x_v, d_x_o),
        (g_fout, g_fout_v, gfo_o),
        (result, result_v, result_o),
        (g_out, g_out_v, go_o),
    )
    loads = [copy(src, held) for src, held, _ in through]
    stores = []
    load_ff.wait()
    for m, out in enumerate((gfv_o, gfg_o)):
        for q in range(CHIPS):
            ff_f32[m, :, q * ff : (q + 1) * ff] = ff_v[m, q].astype(F32)
        stores.append(copy(ff_f32.at[m], out))
    load_qk.wait()
    for m, outs in enumerate(((gq_o, gk_o), (gv_o, gg_o))):
        for s in range(WIDE):
            lanes = slice(s * two, (s + 1) * two)
            qk_f32[2 * m, :, lanes] = qk_v[m, s, :, 0:two].astype(F32)
            qk_f32[2 * m + 1, :, lanes] = qk_v[m, s, :, two:].astype(F32)
        stores += [copy(qk_f32.at[2 * m + i], out) for i, out in enumerate(outs)]
    for load, (_, held, out) in zip(loads, through):
        load.wait()
        stores.append(copy(held, out))
    for store in stores:
        store.wait()


def finish(results, moved):
    out_shape = moved
    return pl.pallas_call(
        finish_kernel,
        out_shape=out_shape,
        in_specs=[ANY] * 6,
        out_specs=(ANY,) * len(out_shape),
        scratch_shapes=[
            *[pltpu.VMEM(r.shape, r.dtype) for r in results],
            pltpu.VMEM((2, *out_shape[7].shape), F32),
            pltpu.VMEM((4, *out_shape[2].shape), F32),
            pltpu.SemaphoreType.DMA((20,)),
        ],
        compiler_params=pltpu.CompilerParams(vmem_limit_bytes=63 * 2**20),
    )(*results)


def layer(tokens, weights, dy, starts):
    tok, width = tokens.shape
    shard = weights[0].shape[0]
    ff = weights[5].shape[1] // CHIPS
    fo_rows = weights[7].shape[0]
    full = WIDE * tok
    two = 2 * HEAD

    def arr(*shape, dtype=BF):
        return jax.ShapeDtypeStruct(shape, dtype)

    finals = (
        arr(tok, width),
        arr(tok, width, dtype=F32),
        *[arr(shard, width, dtype=F32)] * 5,
        arr(shard, CHIPS * ff, dtype=F32),
        arr(shard, CHIPS * ff, dtype=F32),
        arr(fo_rows, width, dtype=F32),
    )
    results = (
        arr(tok, width),
        arr(tok, width, dtype=F32),
        arr(shard, width, dtype=F32),
        arr(fo_rows, width, dtype=F32),
        arr(2, CHIPS, shard, ff),
        arr(2, WIDE, shard, 2 * two),
    )
    held = (
        arr(WIDE, tok, width),
        arr(WIDE, NARROW, shard, 2 * two),
        arr(WIDE, NARROW, shard, 2 * two),
        arr(WIDE, NARROW, shard, width),
        arr(CHIPS, 2, NARROW, shard, ff),
        arr(CHIPS, 2, NARROW, shard, ff),
        arr(2, NARROW, fo_rows, width),
        arr(CHIPS, tok, width),
        arr(full, 2 * two),
        arr(full, 3 * two),
        arr(WIDE, 2, HEAD, HEAD),
        arr(WIDE, tok, two),
        arr(WIDE, tok, two),
        arr(tok, width),
        arr(tok, width),
        arr(tok, width, dtype=F32),
        arr(CHIPS, tok, width),
    )
    landings = (
        arr(4, 2, tok // 2, width),
        arr(4, 2, tok, width),
        arr(NARROW, fo_rows, width),
        arr(2, CHIPS, NARROW, shard, ff),
        arr(CHIPS, tok, width),
        arr(CHIPS, tok, width),
        arr(5, fo_rows, width),
        arr(2, 5, CHIPS, shard, ff),
        arr(5, shard, width),
        arr(2, 5, WIDE, shard, 2 * two),
        arr(WIDE, tok, two),
        arr(WIDE, 2, 8, tok, dtype=F32),
        arr(WIDE, 8, tok, dtype=F32),
        arr(CHIPS, tok, width),
    )
    out_shape = results + held + landings
    outs = pl.pallas_call(
        layer_kernel,
        out_shape=out_shape,
        in_specs=[ANY] * 10 + [pl.BlockSpec(memory_space=pltpu.SMEM)],
        out_specs=(ANY,) * len(out_shape),
        scratch_shapes=[
            pltpu.VMEM((ff, width), BF),
            pltpu.VMEM((CHIPS, NARROW, shard, ff), BF),
            pltpu.VMEM((CHIPS, NARROW, shard, ff), BF),
            pltpu.VMEM((CHIPS, tok, width), BF),
            pltpu.VMEM((tok, width), F32),
            pltpu.VMEM((tok, width), BF),
            pltpu.VMEM((tok, HEAD), F32),
            pltpu.VMEM((CHIPS, shard, ff), BF),
            pltpu.SemaphoreType.DMA((162,)),
            pltpu.SemaphoreType.DMA((162,)),
            pltpu.SemaphoreType.DMA((40,)),
        ],
        compiler_params=pltpu.CompilerParams(
            collective_id=0, has_side_effects=True, vmem_limit_bytes=65300 * 2**10
        ),
        cost_estimate=pl.CostEstimate(flops=8 * 10**10, bytes_accessed=3 * 10**8, transcendentals=0),
    )(tokens, *weights, dy, starts)
    return finish(outs[: len(results)], finals)


def local_box(tokens, doc_starts, wq, wk, wv, wg, wo, fv, fg, fo, cotangent):
    weights = (wq, wk, wv, wg, wo, fv, fg, fo)
    outs = layer(tokens[0], weights, cotangent[0], doc_starts)
    return (outs[0][None], outs[1][None]) + tuple(outs[2:])


def solution(mesh):
    box = (mesh.shape["wide"], mesh.shape["narrow"]) == (WIDE, NARROW)
    tok = P("narrow", "wide", None)
    row = P(BOTH, None)
    return jax.shard_map(
        local_box if box else local,
        mesh=mesh,
        in_specs=(tok, P()) + (row,) * 8 + (tok,),
        out_specs=(tok, tok) + (row,) * 8,
        check_vma=False,
    )
```

```python
import jax
import jax.numpy as jnp
from jax import lax
from jax.experimental import pallas as pl
from jax.experimental.pallas import tpu as pltpu
from jax.sharding import PartitionSpec as P

HEADS = 16
HEAD = 128
BLOCK = 256
LAYERS = 16
LAYER = 12

EPS = 1e-06
BOTH = ("wide", "narrow")
BF = jnp.bfloat16
F32 = jnp.float32


def normalize(values):
    scale = lax.rsqrt(jnp.mean(values * values, axis=-1, keepdims=True) + EPS)
    return (values * scale, scale)


def normalize_back(normed, scale, grad):
    return scale * (grad - normed * jnp.mean(grad * normed, axis=-1, keepdims=True))


def silu_slope(values):
    sigma = jax.nn.sigmoid(values)
    return sigma * (1.0 + values * (1.0 - sigma))


def matmul(left, right):
    return jnp.dot(left, right, preferred_element_type=F32)


def matmul_right_t(left, right):
    return lax.dot_general(left, right, (((1,), (1,)), ((), ())), preferred_element_type=F32)


def weight_grad(left, right):
    return lax.dot_general(left, right, (((0,), (0,)), ((), ())), preferred_element_type=F32)


def ein(spec, left, right):
    return jnp.einsum(spec, left, right, preferred_element_type=F32)


def head_slopes():
    order = jnp.arange(HEADS, dtype=F32)
    return jnp.exp2(-8.0 * (order + 1.0) / HEADS) * (1.0 - LAYER / (LAYERS - 1) + 1e-05)


def local(
    tokens,
    doc_starts,
    query_weight,
    key_weight,
    value_weight,
    gate_weight,
    out_weight,
    ffn_value_weight,
    ffn_gate_weight,
    ffn_out_weight,
    cotangent,
):
    wide, narrow = lax.axis_size("wide"), lax.axis_size("narrow")
    rows_here, width = tokens.shape[1:]
    length = rows_here * wide
    blocks = length // BLOCK
    heads_here = HEADS // wide
    shard = query_weight.shape[0]

    def reorder(values):
        return values.reshape(-1, wide, narrow, shard).swapaxes(1, 2).reshape(-1, width)

    def restore(values):
        return values.reshape(-1, narrow, wide, shard).swapaxes(1, 2).reshape(-1, width)

    def columns(weight):
        part = lax.all_to_all(weight, "wide", split_axis=1, concat_axis=0, tiled=True)
        return lax.all_gather(part, "narrow", axis=0, tiled=True)

    def gather_rows(values):
        return lax.all_gather(values, "wide", axis=0, tiled=True)

    def scatter_rows(values):
        return lax.psum_scatter(
            values.astype(BF), "wide", scatter_dimension=0, tiled=True
        ).astype(F32)

    def to_tokens(values):
        return lax.all_to_all(values, "wide", split_axis=0, concat_axis=1, tiled=True)

    def to_heads(values):
        return lax.all_to_all(values, "wide", split_axis=1, concat_axis=0, tiled=True)

    def column_sums(grad):
        part = lax.psum_scatter(grad.astype(BF), "narrow", scatter_dimension=0, tiled=True)
        return lax.all_to_all(part, "wide", split_axis=0, concat_axis=1, tiled=True).astype(F32)

    w_query, w_key, w_value, w_gate = map(
        columns, (query_weight, key_weight, value_weight, gate_weight)
    )
    w_out = lax.all_gather(out_weight, BOTH, axis=0, tiled=True)
    w_fval, w_fgate = map(columns, (ffn_value_weight, ffn_gate_weight))
    w_fout = lax.all_gather(ffn_out_weight, "narrow", axis=0, tiled=True)

    starts = lax.dynamic_slice_in_dim(doc_starts, lax.axis_index("narrow"), 1, 0)[0]
    positions = jnp.arange(length, dtype=jnp.int32)
    doc_ids = jnp.sum((starts[None, :] <= positions[:, None]).astype(jnp.int32), axis=1)
    doc_ids = doc_ids.reshape(blocks, BLOCK)
    firsts = jnp.arange(blocks, dtype=jnp.int32) * BLOCK - 1
    prev_ids = jnp.sum((starts[None, :] <= firsts[:, None]).astype(jnp.int32), axis=1)
    slopes = lax.dynamic_slice_in_dim(
        head_slopes(), lax.axis_index("wide") * heads_here, heads_here, 0
    )
    offsets = jnp.arange(BLOCK, dtype=F32)
    lags = offsets[:, None] - offsets[None, :]
    decays = jnp.exp(-slopes[:, None, None] * jnp.maximum(lags, 0.0)[None])
    within = (doc_ids[:, :, None] == doc_ids[:, None, :]) & (lags >= 0.0)
    block_mask = jnp.where(within[:, None], decays[None], 0.0)
    continues = (doc_ids == prev_ids[:, None]).astype(F32)
    entry_scale = continues[..., None] * jnp.exp(-slopes[None, :] * (offsets[:, None] + 1.0))
    tail_scale = (doc_ids == doc_ids[:, -1:]).astype(F32)[..., None] * jnp.exp(
        -slopes[None, :] * (BLOCK - 1.0 - offsets)[:, None]
    )
    passing = continues[:, -1:] * jnp.exp(-slopes * BLOCK)

    def split_heads(values):
        return values.reshape(blocks, BLOCK, heads_here, HEAD)

    inputs = tokens[0].astype(F32)
    normed, in_scale = normalize(inputs)
    normed_bf = gather_rows(reorder(normed.astype(BF)))
    query_pre = matmul(normed_bf, w_query)
    key_pre = matmul(normed_bf, w_key)
    queries = split_heads(jax.nn.silu(query_pre).astype(BF))
    keys = split_heads(jax.nn.silu(key_pre).astype(BF))
    values = split_heads(matmul(normed_bf, w_value).astype(BF))
    gate = matmul(normed_bf, w_gate)
    scores = ein("bihe,bjhe->bhij", queries, keys)
    probs = (scores * block_mask).astype(BF)
    inner = ein("bhij,bjhe->bihe", probs, values)
    tail_keys = (keys.astype(F32) * tail_scale[..., None]).astype(BF)
    fresh = ein("bjhe,bjhf->bhef", tail_keys, values)
    state = jnp.zeros((heads_here, HEAD, HEAD), F32)
    entering = []
    for b in range(blocks):
        entering.append(state)
        state = passing[b][:, None, None] * state + fresh[b]
    block_in = jnp.stack(entering).astype(BF)
    across = entry_scale[..., None] * ein("bihe,bhef->bihf", queries, block_in)
    attention = (inner + across).reshape(query_pre.shape)

    attn_tok = to_tokens(attention)
    gate_tok = to_tokens(gate)
    attn_n, attn_scale = normalize(attn_tok)
    mixed = (attn_n * gate_tok).astype(BF)
    middle = inputs + matmul(mixed, w_out)
    middle_n, middle_scale = normalize(middle)
    middle_bf = gather_rows(reorder(middle_n.astype(BF)))
    ffn_val = matmul(middle_bf, w_fval)
    ffn_gat = matmul(middle_bf, w_fgate)
    ffn_mix = (ffn_val * ffn_gat).astype(BF)
    result = middle + scatter_rows(matmul(ffn_mix, w_fout))

    upstream = cotangent[0]
    up_all = gather_rows(upstream)
    grad_fout = weight_grad(ffn_mix, up_all)
    d_mix = matmul_right_t(up_all, w_fout)
    d_val = (d_mix * ffn_gat).astype(BF)
    d_gat = (d_mix * ffn_val).astype(BF)
    grad_fval = weight_grad(middle_bf, d_val)
    grad_fgate = weight_grad(middle_bf, d_gat)
    d_middle_n = restore(
        scatter_rows(matmul_right_t(d_val, w_fval) + matmul_right_t(d_gat, w_fgate))
    )
    d_middle = upstream.astype(F32) + normalize_back(middle_n, middle_scale, d_middle_n)
    d_branch = d_middle.astype(BF)
    grad_out = weight_grad(mixed, d_branch)
    d_mixed = matmul_right_t(d_branch, w_out)
    d_gate = to_heads((d_mixed * attn_n).astype(BF))
    d_attn = to_heads(normalize_back(attn_n, attn_scale, d_mixed * gate_tok).astype(BF))

    d_heads = split_heads(d_attn)
    d_probs = ein("bihe,bjhe->bhij", d_heads, values)
    d_scores = (d_probs * block_mask).astype(BF)
    d_query = ein("bhij,bjhe->bihe", d_scores, keys)
    d_key = ein("bhij,bihe->bjhe", d_scores, queries)
    d_value = ein("bhij,bihe->bjhe", probs, d_heads)
    d_query = d_query + entry_scale[..., None] * ein("bihf,bhef->bihe", d_heads, block_in)
    entry_queries = (queries.astype(F32) * entry_scale[..., None]).astype(BF)
    grad_in = ein("bihe,bihf->bhef", entry_queries, d_heads)
    state = jnp.zeros((heads_here, HEAD, HEAD), F32)
    leaving = [None] * blocks
    for b in reversed(range(blocks)):
        leaving[b] = state
        state = passing[b][:, None, None] * state + grad_in[b]
    block_out = jnp.stack(leaving).astype(BF)
    d_key = d_key + tail_scale[..., None] * ein("bjhf,bhef->bjhe", values, block_out)
    d_value = d_value + ein("bjhe,bhef->bjhf", tail_keys, block_out)
    dq_pre = (d_query.reshape(query_pre.shape) * silu_slope(query_pre)).astype(BF)
    dk_pre = (d_key.reshape(key_pre.shape) * silu_slope(key_pre)).astype(BF)
    dv_pre = d_value.reshape(query_pre.shape).astype(BF)
    grad_query = weight_grad(normed_bf, dq_pre)
    grad_key = weight_grad(normed_bf, dk_pre)
    grad_value = weight_grad(normed_bf, dv_pre)
    grad_gate = weight_grad(normed_bf, d_gate)
    d_normed = restore(
        scatter_rows(
            matmul_right_t(dq_pre, w_query)
            + matmul_right_t(dk_pre, w_key)
            + matmul_right_t(dv_pre, w_value)
            + matmul_right_t(d_gate, w_gate)
        )
    )
    d_inputs = d_middle + normalize_back(normed, in_scale, d_normed)
    return (
        result.astype(BF)[None],
        d_inputs[None],
        column_sums(grad_query),
        column_sums(grad_key),
        column_sums(grad_value),
        column_sums(grad_gate),
        lax.psum_scatter(grad_out.astype(BF), BOTH, scatter_dimension=0, tiled=True).astype(F32),
        column_sums(grad_fval),
        column_sums(grad_fgate),
        lax.psum_scatter(grad_fout.astype(BF), "narrow", scatter_dimension=0, tiled=True).astype(
            F32
        ),
    )


MESH = pl.DeviceIdType.MESH
ANY = pl.BlockSpec(memory_space=pl.ANY)
VMEM = pl.BlockSpec(memory_space=pltpu.VMEM)
WIDE, NARROW = 8, 4
CHIPS = WIDE // 2


def dot(left, right):
    return jnp.dot(left, right, preferred_element_type=F32)


def dot_rt(left, right):
    return lax.dot_general(left, right, (((1,), (1,)), ((), ())), preferred_element_type=F32)


def dot_lt(left, right):
    return lax.dot_general(left, right, (((0,), (0,)), ((), ())), preferred_element_type=F32)


def at(start, size):
    return pl.ds(pl.multiple_of(start, size), size)


class Links:
    def __init__(self, send, recv, here):
        self.send, self.recv, self.here = send, recv, here
        self.count = 0
        self.free = list(range(1, here.shape[0]))
        w = lax.axis_index("wide")
        n = lax.axis_index("narrow")
        self.w, self.n = w, n
        self.core = lax.rem(w, 2)
        self.chip = lax.div(w, 2)
        x, y = lax.rem(self.chip, 2), lax.div(self.chip, 2)
        self.wx = w + 2 - 4 * x
        self.wy = w + 4 - 8 * y
        self.wd = w + 6 - 4 * x - 8 * y
        self.ws = w + 1 - 2 * self.core
        self.px = self.chip + 1 - 2 * x
        self.py = self.chip + 2 - 4 * y
        self.pd = 3 - self.chip
        self.mid = lax.rem(lax.div(n + 1, 2), 2)
        self.pair = n + 1 - 2 * lax.rem(n, 2)
        self.cross = 2 - lax.div(n, 2)
        self.far = 3 - 3 * lax.div(n, 2)
        self.end_to = 3 * lax.rem(n + 1, 2)
        self.end_part = lax.rem(2 * n, 3) + 3 * lax.div(n, 3)

    def greet(self):
        barrier = pltpu.get_barrier_semaphore()
        for d in range(1, WIDE):
            pl.semaphore_signal(
                barrier, inc=1, device_id=(lax.rem(self.w + d, WIDE), self.n), device_id_type=MESH
            )
        for d in range(1, NARROW):
            pl.semaphore_signal(
                barrier, inc=1, device_id=(self.w, lax.rem(self.n + d, NARROW)), device_id_type=MESH
            )

    def met(self):
        pl.semaphore_wait(pltpu.get_barrier_semaphore(), WIDE + NARROW - 2)

    def take(self, number):
        base = self.count
        self.count += number
        return base

    def remote(self, src, dst, send, recv, wide=None, narrow=None):
        return pltpu.make_async_remote_copy(
            src_ref=src,
            dst_ref=dst,
            send_sem=self.send.at[send],
            recv_sem=self.recv.at[recv],
            device_id=(self.w if wide is None else wide, self.n if narrow is None else narrow),
            device_id_type=MESH,
        )

    def arrived(self, ref, recv):
        self.remote(ref, ref, recv, recv, wide=self.ws).wait_recv()

    def keep(self, src, dst):
        return Kept(self, src, dst)


class Kept:
    def __init__(self, links, src, dst):
        self.links, self.index = links, links.free.pop(0)
        self.copy = pltpu.make_async_copy(src, dst, links.here.at[self.index])
        self.copy.start()

    def wait(self):
        self.copy.wait()
        self.links.free.append(self.index)


class Line:
    def __init__(self, links, part):
        self.links, self.part = links, part
        self.base = links.take(5)

    def copy(self, index):
        k, b = self.links, self.base
        which, to = (
            (k.n, k.pair),
            (k.n, k.cross),
            (k.pair, k.cross),
            (k.cross, k.pair),
            (k.far, k.pair),
        )[index]
        ref = self.part(which)
        return k.remote(ref, ref, b + index, b + which, narrow=to)

    def start(self):
        self.start_away()
        pl.when(self.links.mid == 1)(lambda: self.copy(0).start())

    def start_away(self):
        pl.when(self.links.mid == 1)(lambda: self.copy(1).start())
        pl.when(self.links.mid == 0)(lambda: self.copy(0).start())

    def start_home(self):
        pl.when(self.links.mid == 1)(lambda: self.copy(0).start())

    def wait(self, index):
        self.links.arrived(self.part(index), self.base + index)

    def forward(self):
        @pl.when(self.links.mid == 1)
        def _():
            self.wait(self.links.cross)
            self.copy(3).start()
            self.wait(self.links.pair)
            self.copy(2).start()

    def forward_far(self):
        @pl.when(self.links.mid == 1)
        def _():
            self.wait(self.links.far)
            self.copy(4).start()

    def finish(self, then=lambda place: None, late=lambda: None):
        k = self.links
        then(0)
        for place, index in enumerate((k.pair, k.cross, k.far)):
            if place == 2:
                late()
            pl.when(k.mid == 0)(lambda index=index: self.wait(index))
            then(place + 1)

    def drain(self):
        self.copy(0).wait_send()

        @pl.when(self.links.mid == 1)
        def _():
            for index in range(1, 5):
                self.copy(index).wait_send()


class Plane:
    def __init__(self, links, slot):
        self.links, self.slot = links, slot
        self.base = links.take(6)

    def copy(self, index):
        k, b = self.links, self.base
        owner, half, to = (
            (k.w, 0, k.wx),
            (k.w, 1, k.wy),
            (k.w, 1, k.wx),
            (k.w, 0, k.wy),
            (k.wx, 0, k.wy),
            (k.wy, 1, k.wx),
        )[index]
        ref = self.slot(owner, half)
        return k.remote(ref, ref, b + index, b + index, wide=to)

    def start(self):
        for index in range(4):
            self.copy(index).start()

    def forward(self):
        k, b, slot = self.links, self.base, self.slot
        k.arrived(slot(k.wx, 0), b)
        self.copy(4).start()
        k.arrived(slot(k.wy, 1), b + 1)
        self.copy(5).start()

    def finish_near(self):
        k, b, slot = self.links, self.base, self.slot
        k.arrived(slot(k.wx, 1), b + 2)
        k.arrived(slot(k.wy, 0), b + 3)

    def finish_far(self):
        k, b, slot = self.links, self.base, self.slot
        k.arrived(slot(k.wd, 0), b + 4)
        k.arrived(slot(k.wd, 1), b + 5)

    def drain(self):
        for index in range(6):
            self.copy(index).wait_send()


class Sibling:
    def __init__(self, links, block, twin, number):
        self.links, self.block, self.twin, self.number = links, block, twin, number
        self.base = links.take(number)

    def copy(self, index):
        k, b = self.links, self.base + index
        ref = self.block(index)
        return k.remote(ref, ref, b, b, wide=k.ws)

    def send(self, index):
        self.copy(index).start()

    def wait(self, index):
        self.links.arrived(self.twin(index), self.base + index)

    def drain(self):
        for index in range(self.number):
            self.copy(index).wait_send()


class Spread:
    def __init__(self, links, src, dst, bulk, peers=WIDE):
        self.links, self.src, self.dst, self.bulk = links, src, dst, bulk
        self.step = 1 if peers == WIDE else 2
        self.base = links.take(1)

    def distances(self):
        return range(self.step, WIDE, self.step)

    def copy(self, to):
        k = self.links
        return k.remote(self.src(to), self.dst(k.w), self.base, self.base, wide=to)

    def start(self):
        for d in self.distances():
            self.copy(lax.rem(self.links.w + d, WIDE)).start()

    def finish(self):
        self.links.arrived(self.bulk, self.base)

    def drain(self):
        k = self.links
        k.remote(self.bulk, self.bulk, self.base, self.base, wide=k.ws).wait_send()


def row_scale(values):
    return lax.rsqrt(jnp.mean(values * values, axis=-1, keepdims=True) + EPS)


def row_chunks(rows, body, size=32):
    def step(r, carry):
        body(at(r * size, size))
        return carry

    lax.fori_loop(0, rows // size, step, 0)


class LineSum:
    def __init__(self, links, part, land, half=None):
        self.links, self.part, self.land, self.half = links, part, land, half
        self.base = links.take(5 if half is None else 6)
        self.onward = links.pair + links.mid * (links.cross - links.pair)

    def copy(self, index):
        k, b = self.links, self.base
        which, slot, to = (
            (k.far, 3 * k.mid, self.onward),
            (k.cross, 1 + 3 * k.mid, self.onward),
            (k.pair, 2 - 2 * k.mid, k.pair),
        )[index]
        return k.remote(self.part(which), self.land(slot), b + index, b + slot, narrow=to)

    def half_copy(self, h):
        k, sem = self.links, self.base + 5 * h
        src, dst = self.half(self.part(k.far), h), self.half(self.land(0), h)
        return k.remote(src, dst, sem, sem, narrow=k.pair)

    def begin_half(self, h):
        pl.when(self.links.mid == 0)(lambda: self.half_copy(h).start())

    def begin(self, index):
        pl.when(self.links.mid == 0)(lambda: self.copy(index).start())

    def start(self):
        for index in range(3):
            self.begin(index)

    def wait(self, slot):
        self.links.arrived(self.land(slot), self.base + slot)

    def pass_on(self, index, add):
        k = self.links
        which, slot = ((k.far, 0), (k.cross, 1), (k.pair, 3))[index]

        @pl.when(k.mid == 1)
        def _():
            if self.half is not None and index == 0:
                for h in range(2):
                    k.arrived(self.half(self.land(0), h), self.base + 5 * h)
            else:
                self.wait(slot)
            add(self.part(which), self.land(slot))
            self.copy(index).start()

    def finish(self, fetch, spots):
        k = self.links
        pl.when(k.mid == 0)(lambda: self.wait(0))

        @pl.when(k.mid == 1)
        def _():
            self.wait(2)
            self.wait(4)
            fetch(self.land(4), spots.at[1])

        fetch(self.land(2 * k.mid), spots.at[0])

        @pl.when(k.mid == 0)
        def _():
            spots[1] = jnp.zeros(spots.shape[1:], spots.dtype)

    def drain(self):
        if self.half is None:
            self.copy(0).wait_send()
        else:

            @pl.when(self.links.mid == 0)
            def _():
                for h in range(2):
                    self.half_copy(h).wait_send()

            pl.when(self.links.mid == 1)(lambda: self.copy(0).wait_send())
        for index in range(1, 3):
            self.copy(index).wait_send()


class PlaneSum:
    def __init__(self, links, block, corner, near, half, base=None, late=None):
        self.late = late
        self.links, self.block, self.corner, self.near, self.half = links, block, corner, near, half
        self.base = links.take(6) if base is None else base

    def rows(self, h):
        return pl.ds(h * self.half, self.half)

    def copy(self, index):
        k = self.links
        chip, h, land, to = (
            (k.pd, 0, self.corner.at[0], k.wx),
            (k.pd, 1, self.corner.at[1], k.wy),
            (k.px, 0, self.near.at[0, self.rows(0)], k.wx),
            (k.py, 1, self.near.at[1, self.rows(1)], k.wy),
            (k.px, 1, self.near.at[0, self.rows(1)], k.wx),
            (k.py, 0, self.near.at[1, self.rows(0)], k.wy),
        )[index]
        sem = self.base + index
        src = self.block(chip).at[self.rows(h)]
        if self.late is not None and index >= 4:
            src = self.late.at[self.rows(index - 4)]
        return k.remote(src, land, sem, sem, wide=to)

    def send_far(self):
        self.copy(0).start()
        self.copy(1).start()

    def send_x(self):
        self.copy(2).start()

    def send_y(self):
        self.copy(3).start()

    def combine(self, add):
        k = self.links
        for index, corner, chip, h in ((4, 1, k.px, 1), (5, 0, k.py, 0)):
            self.copy(corner).wait_recv()
            own = self.block(chip).at[self.rows(h)]
            to = own if self.late is None else self.late.at[self.rows(index - 4)]
            add(to, self.corner.at[corner], own)
            self.copy(index).start()

    def finish(self):
        for index in range(2, 6):
            self.copy(index).wait_recv()

    def drain(self, first=0, last=6):
        for index in range(first, last):
            self.copy(index).wait_send()


def layer_kernel(
    x_in, wq, wk, wv, wg, wo, fv, fg, fo, dy_arg, starts,
    result_o, dx_o, go_o, gfo_o, turn_ff, turn_qk,
    xn_in, wqk_in, wvg_in, wo_in, fv_in, fg_in, fo_in, dy_in, slope_in, qkv_in, sin_in, attn_in,
    gate_in, gated_in, mixed_in, x1_in, x1n_in,
    corner, near, twin_fo_land, twin_ff, twin_wo, twin_xn_land, land_fo, land_ff, land_wo, land_qk,
    a_land, s_land, sq_land, res_in,
    g_fo, g_fv, g_fg, stage, acc, tmp, scales, tmp_ff,
    send, recv, here,
):
    k = Links(send, recv, here)
    w, n, core, chip = k.w, k.n, k.core, k.chip
    other = 1 - core
    tok, width = acc.shape
    ff = g_fv.shape[-1]
    fo_rows = land_fo.shape[1]
    half = tok // 2
    two = 2 * HEAD
    order = (k.pd, k.px, k.py, chip)
    begins = [starts[n, j] for j in range(starts.shape[1])]

    def docs(positions):
        return sum((positions >= begin).astype(jnp.int32) for begin in begins)

    def slope(h):
        head = (2 * w + h + 1).astype(F32)
        rate = 1.0 - LAYER / (LAYERS - 1) + 1e-05
        return jnp.exp2(jnp.full((1, HEAD), -8.0 / HEADS, F32) * head)[:, 0:1] * rate

    def fill_decay(decay):
        i = lax.broadcasted_iota(jnp.int32, (BLOCK, BLOCK), 0)
        j = lax.broadcasted_iota(jnp.int32, (BLOCK, BLOCK), 1)
        lags = jnp.maximum(i - j, 0).astype(F32)
        for h in range(2):
            decay[h] = jnp.exp(-slope(h) * lags)

    def block_tables(b):
        first = b * BLOCK
        i = lax.broadcasted_iota(jnp.int32, (BLOCK, 1), 0)
        j = lax.broadcasted_iota(jnp.int32, (1, BLOCK), 1)
        ids = docs(first + i)
        mask = (ids == docs(first + j)) & (i >= j)
        before, at_end = docs(first - 1), docs(first + BLOCK - 1)
        steps = i.astype(F32)
        factors = []
        for h in range(2):
            rate = slope(h)
            entry = jnp.where(ids == before, jnp.exp(-rate * (steps + 1.0)), 0.0)
            tail = jnp.where(ids == at_end, jnp.exp(-rate * (BLOCK - 1.0 - steps)), 0.0)
            through = jnp.where(before == at_end, jnp.exp(-rate * BLOCK), 0.0)
            factors.append((entry, tail, through))
        return mask, factors

    def nth(j):
        flip_x, flip_y = 1 - lax.div(j, 2), 1 - lax.rem(j, 2)
        return (
            chip + flip_x * (1 - 2 * lax.rem(chip, 2)) + flip_y * (2 - 4 * lax.div(chip, 2))
        )

    def fetch(src, dst):
        copy = pltpu.make_async_copy(src, dst, here.at[0])
        copy.start()
        copy.wait()

    def adder(spot):
        def add(to, land, own=None):
            fetch(land, spot)
            own = to if own is None else own
            to[...] = (own[...].astype(F32) + spot[...].astype(F32)).astype(BF)

        return add

    add_half = adder(tmp.at[pl.ds(0, half)])
    add_fo = adder(tmp.at[pl.ds(0, fo_rows)])
    add_wo = adder(tmp.at[pl.ds(0, 64)])
    add_ff = adder(tmp_ff)

    def add_res(to, land, own):
        fetch(own, to)
        add_half(to, land)

    def fo_part(owner, i):
        return g_fo.at[pl.ds(pl.multiple_of((owner * NARROW + i) * fo_rows, 16), fo_rows)]

    sum_fo = LineSum(k, lambda i: fo_part(core, i), lambda s: land_fo.at[s])
    sum_ff = [
        LineSum(k, lambda i, g=g: g.at[:, i], lambda s, m=m: land_ff.at[m, s], half)
        for m, (g, half) in enumerate(
            ((g_fv, lambda ref, h: ref.at[pl.ds(2 * h, 2)]), (g_fg, None))
        )
    ]
    def plane_sum(m, blocks, base=None, late=None):
        return PlaneSum(k, lambda q: blocks.at[q], corner.at[m], near.at[m], half, base, late)

    plane_mid, plane_in = (plane_sum(m, stage) for m in (0, 3))
    plane_res = plane_sum(1, res_in, late=stage.at[chip])
    twin_base = k.take(4 * 5)

    def twin(m, j, src, dst):
        sem = twin_base + 4 * m + j
        return k.remote(src, dst, sem, sem, wide=k.ws)

    def wide_cols(index):
        return at(index * two, two)

    def chip_cols(index):
        return pl.ds(pl.multiple_of(index * ff, 128), ff)

    projections = ((wq, wqk_in), (wk, wqk_in), (wv, wvg_in), (wg, wvg_in))
    lines = line_out, line_qk, line_vg, line_fv, line_fg, line_fo = (
        Line(k, lambda i: wo_in.at[w, i]),
        Line(k, lambda i: wqk_in.at[:, i]),
        Line(k, lambda i: wvg_in.at[:, i]),
        Line(k, lambda i: fv_in.at[:, core, i]),
        Line(k, lambda i: fg_in.at[:, core, i]),
        Line(k, lambda i: fo_in.at[core, i]),
    )
    spreads = [
        Spread(
            k,
            lambda t, weight=weight: weight.at[:, wide_cols(t)],
            lambda s, m=m, to=to: to.at[s, n, :, pl.ds((m % 2) * two, two)],
            to.at[pl.ds(0, WIDE - 1), n, :, pl.ds((m % 2) * two, two)],
        )
        for m, (weight, to) in enumerate(projections)
    ]
    spread_ff = [
        Spread(
            k,
            lambda t, weight=weight: weight.at[:, chip_cols(lax.div(t, 2))],
            lambda s, to=to: to.at[lax.div(s, 2), core, n],
            to.at[pl.ds(0, CHIPS - 1), core, n],
            peers=CHIPS,
        )
        for weight, to in ((fv, fv_in), (fg, fg_in))
    ]
    planes = plane_xn, plane_out, plane_dy, plane_x1n = (
        Plane(k, lambda s, h: xn_in.at[s, pl.ds(h * half, half)]),
        Plane(k, lambda s, h: wo_in.at[s, pl.ds(h * 2, 2)]),
        Plane(k, lambda s, h: dy_in.at[lax.div(s, 2), pl.ds(h * half, half)]),
        Plane(k, lambda s, h: x1n_in.at[lax.div(s, 2), pl.ds(h * half, half)]),
    )
    here4 = (w, k.wx, k.wy, k.wd)
    there4 = tuple(s + 1 - 2 * core for s in here4)
    near4 = (n, k.pair, k.cross, k.far)
    twins = twin_xn, twin_out, twin_fv, twin_fg, twin_fo = (
        Sibling(k, lambda i: xn_in.at[here4[i]], lambda i: xn_in.at[there4[i]], 4),
        Sibling(k, lambda i: wo_in.at[here4[i]], lambda i: wo_in.at[there4[i]], 4),
        Sibling(k, lambda i: fv_in.at[:, core, near4[i]], lambda i: fv_in.at[:, other, near4[i]], 4),
        Sibling(k, lambda i: fg_in.at[:, core, near4[i]], lambda i: fg_in.at[:, other, near4[i]], 4),
        Sibling(k, lambda i: fo_in.at[core, near4[i]], lambda i: fo_in.at[other, near4[i]], 4),
    )

    k.greet()
    def before(
        x, xn, wqk, wvg, wout, slopes, qkv, gates, sin, state, attn_s, gated_s,
        squares, sums, gated, mixed, x1, x1n, decay,
    ):
        load_x = k.keep(x_in, x)
        held = [
            (k.keep(wo, mixed.at[pl.ds(0, 64)]), mixed.at[pl.ds(0, 64)], wo_in.at[w, n]),
            *[
                (
                    k.keep(weight.at[:, wide_cols(w)], spot.at[w, n, :, lanes]),
                    spot.at[w, n, :, lanes],
                    to.at[w, n, :, lanes],
                )
                for weight, spot, to, lanes in (
                    (wq, wqk, wqk_in, pl.ds(0, two)),
                    (wk, wqk, wqk_in, pl.ds(two, two)),
                    (wv, wvg, wvg_in, pl.ds(0, two)),
                    (wg, wvg, wvg_in, pl.ds(two, two)),
                )
            ],
            (k.keep(dy_arg, gated), gated, dy_in.at[chip]),
            *[
                (
                    k.keep(weight.at[:, chip_cols(chip)], tmp_ff.at[m]),
                    tmp_ff.at[m],
                    to.at[chip, core, n],
                )
                for m, (weight, to) in enumerate(((fv, fv_in), (fg, fg_in)))
            ],
            (k.keep(fo, tmp.at[pl.ds(0, fo_rows)]), tmp.at[pl.ds(0, fo_rows)], fo_in.at[core, n]),
        ]

        def place(index):
            load, spot, to = held[index]
            load.wait()
            return k.keep(spot, to)

        load_x.wait()

        def norm_in(rows):
            v = x[rows, :].astype(F32)
            x1n[rows, :] = (v * row_scale(v)).astype(BF)

        row_chunks(tok, norm_in)
        own_xn = k.keep(x1n, xn_in.at[w])
        own_in = [place(i) for i in range(5)]
        k.met()
        for spread in spreads:
            spread.start()
        own_in[0].wait()
        line_out.start()
        own_xn.wait()
        for copy in own_in[1:]:
            copy.wait()
        spreads[0].finish()
        spreads[1].finish()
        line_qk.start()
        plane_xn.start()
        twin_xn.send(0)
        spreads[2].finish()
        spreads[3].finish()
        line_vg.start()
        for spread in spread_ff:
            spread.start()
        own_ff = [place(i) for i in range(5, 9)]
        line_out.forward()
        plane_xn.forward()
        line_out.forward_far()
        line_qk.forward()
        plane_xn.finish_near()
        twin_xn.send(1)
        twin_xn.send(2)
        line_vg.forward()
        line_qk.forward_far()
        line_out.finish()
        plane_out.start()
        twin_out.send(0)
        plane_xn.finish_far()
        twin_xn.send(3)
        line_vg.forward_far()
        spread_ff[0].finish()
        spread_ff[1].finish()
        for copy in own_ff:
            copy.wait()
        line_fv.start()
        for i in range(4):
            twin_xn.wait(i)
        load_xn = k.keep(xn_in, xn)
        plane_out.forward()
        line_qk.finish()
        load_qk = k.keep(wqk_in, wqk)
        load_xn.wait()
        load_qk.wait()

        def project_qk(t, carry):
            v = dot(xn[t], wqk[...].reshape(width, 2 * two))
            rows = at(t * tok, tok)
            sigma = jax.nn.sigmoid(v)
            slopes[rows, :] = (sigma * (1.0 + v * (1.0 - sigma))).astype(BF)
            qkv[rows, 0 : 2 * two] = (v * sigma).astype(BF)
            return carry

        lax.fori_loop(0, WIDE, project_qk, 0)
        stores = [k.keep(slopes, slope_in)]
        plane_out.finish_near()
        twin_out.send(1)
        twin_out.send(2)
        line_vg.finish()
        k.keep(wvg_in, wvg).wait()

        def project_vg(t, carry):
            v = dot(xn[t], wvg[...].reshape(width, 2 * two)).astype(BF)
            qkv[at(t * tok, tok), 2 * two : 3 * two] = v[:, 0:two]
            gates[t] = v[:, two:]
            return carry

        lax.fori_loop(0, WIDE, project_vg, 0)
        line_fv.forward()
        line_fg.start()
        stores.append(k.keep(qkv, qkv_in))
        stores.append(k.keep(gates, gate_in))
        fill_decay(decay)
        state[...] = jnp.zeros_like(state)
        spread_gated = Spread(
            k,
            lambda t: gated_s.at[t],
            lambda s: gated_in.at[:, wide_cols(s)],
            gated_in.at[:, pl.ds(0, (WIDE - 1) * two)],
        )
        spread_sq = Spread(
            k, lambda t: squares.at[t], lambda s: sq_land.at[s], sq_land.at[pl.ds(0, WIDE - 1)]
        )

        def attend(b, carry):
            rows = at(b * BLOCK, BLOCK)
            mask, factors = block_tables(b)
            for h in range(2):
                lanes = slice(h * HEAD, (h + 1) * HEAD)
                entry, tail, through = factors[h]
                q = qkv[rows, lanes]
                key = qkv[rows, two + h * HEAD : two + (h + 1) * HEAD]
                v = qkv[rows, 2 * two + h * HEAD : 2 * two + (h + 1) * HEAD]
                probs = jnp.where(mask, dot_rt(q, key) * decay[h], 0.0).astype(BF)
                old = state[h]
                old_bf = old.astype(BF)
                sin[b, h] = old_bf
                out = dot(probs, v) + entry * dot(q, old_bf)
                attn_s[b, :, lanes] = out.astype(BF)
                gated_s[b, :, lanes] = (out * gates[b, :, lanes].astype(F32)).astype(BF)
                tailed = (key.astype(F32) * tail).astype(BF)
                state[h] = through * old + dot_lt(tailed, v)

            a = attn_s[b].astype(F32)
            squares[b] = dot_rt(jnp.ones((8, two), BF), (a * a).astype(BF))

            @pl.when(b != w)
            def _():
                spread_sq.copy(b).start()
                spread_gated.copy(b).start()

            return carry

        lax.fori_loop(0, WIDE, attend, 0)
        stores.append(k.keep(sin, sin_in))
        stores.append(k.keep(attn_s, attn_in))
        own = [
            k.keep(gated_s.at[w], gated_in.at[:, wide_cols(w)]),
            k.keep(squares.at[w], sq_land.at[w]),
        ]
        plane_out.finish_far()
        twin_out.send(3)
        for i in range(4):
            twin_out.wait(i)
        load_out = k.keep(wo_in, wout)
        line_fv.forward_far()
        spread_sq.finish()
        spread_gated.finish()
        for copy in own:
            copy.wait()
        loads = [k.keep(gated_in, gated), k.keep(sq_land, sums)]
        for copy in loads:
            copy.wait()
        total_sq = sum(sums[s, 0:1, :] for s in range(WIDE))
        scales[...] = jnp.transpose(
            jnp.broadcast_to(lax.rsqrt(total_sq * (1.0 / width) + EPS), (HEAD, tok))
        )

        def mix(rows):
            mixed[rows, :] = (gated[rows, :].astype(F32) * scales[rows, 0:1]).astype(BF)

        row_chunks(tok, mix)
        stores.append(k.keep(mixed, mixed_in))
        load_out.wait()

        def project_out(j, carry):
            lanes = at(j * 512, 512)
            part = dot(mixed[...], wout[:, :, :, lanes].reshape(-1, 512))
            x1[:, lanes] = x[:, lanes].astype(F32) + part
            return carry

        lax.fori_loop(0, width // 512, project_out, 0)
        stores.append(k.keep(x1, x1_in))

        def norm_mid(rows):
            v = x1[rows, :]
            x1n[rows, :] = (v * row_scale(v)).astype(BF)

        row_chunks(tok, norm_mid)
        k.keep(x1n, x1n_in.at[chip]).wait()
        plane_x1n.start()
        line_fg.forward()
        line_fo.start_away()
        plane_x1n.forward()
        plane_dy.start()
        line_fg.forward_far()
        for copy in stores:
            copy.wait()
        spread_sq.drain()
        spread_gated.drain()

    pl.run_scoped(
        before,
        pltpu.VMEM((tok, width), BF),
        pltpu.VMEM((WIDE, tok, width), BF),
        pltpu.VMEM(wqk_in.shape, BF),
        pltpu.VMEM(wvg_in.shape, BF),
        pltpu.VMEM(wo_in.shape, BF),
        pltpu.VMEM(slope_in.shape, BF),
        pltpu.VMEM(qkv_in.shape, BF),
        pltpu.VMEM((WIDE, tok, two), BF),
        pltpu.VMEM(sin_in.shape, BF),
        pltpu.VMEM((2, HEAD, HEAD), F32),
        pltpu.VMEM((WIDE, tok, two), BF),
        pltpu.VMEM((WIDE, tok, two), BF),
        pltpu.VMEM((WIDE, 8, tok), F32),
        pltpu.VMEM((WIDE, 8, tok), F32),
        pltpu.VMEM((tok, width), BF),
        pltpu.VMEM((tok, width), BF),
        pltpu.VMEM((tok, width), F32),
        pltpu.VMEM((tok, width), BF),
        pltpu.VMEM((2, BLOCK, BLOCK), F32),
    )

    def ffn(x1n, dy, fvw, fgw, fow, mix, val, gat, side, tmp_twin):
        def shares(moved, src, dst, places):
            copies = []
            for i in places:
                moved.wait(i)
                copies.append(k.keep(src.at[:, :, near4[i]], dst.at[:, :, near4[i]]))
            return copies

        def fo_shares(places):
            copies = []
            for i in places:
                twin_fo.wait(i)
                for c in range(2):
                    row = pl.multiple_of((c * NARROW + near4[i]) * fo_rows, 16)
                    copies.append(k.keep(fo_in.at[c, near4[i]], fow.at[pl.ds(row, fo_rows)]))
            return copies

        line_fv.finish(twin_fv.send)
        load_fv = shares(twin_fv, fv_in, fvw, range(4))
        plane_x1n.finish_near()
        plane_x1n.finish_far()
        load_x1n = k.keep(x1n_in, x1n)
        for copy in (load_x1n, *load_fv):
            copy.wait()

        def up_val(j, carry):
            val[j] = dot(x1n[j], fvw[...].reshape(width, ff)).astype(BF)
            return carry

        def up_gat(j, carry):
            g = dot(x1n[j], fgw[...].reshape(width, ff))
            gat[j] = g.astype(BF)
            mix[j] = (val[j].astype(F32) * g).astype(BF)
            return carry

        lax.fori_loop(0, CHIPS, up_val, 0)
        line_fo.forward()
        plane_dy.forward()
        load_fg = []
        line_fg.finish(twin_fg.send, lambda: load_fg.extend(shares(twin_fg, fg_in, fgw, range(3))))
        line_fo.start_home()
        load_fg += shares(twin_fg, fg_in, fgw, range(3, 4))
        for copy in load_fg:
            copy.wait()
        line_fo.forward_far()
        lax.fori_loop(0, CHIPS // 2, up_gat, 0)
        plane_dy.finish_near()
        plane_dy.finish_far()
        load_dy = k.keep(dy_in, dy)
        lax.fori_loop(CHIPS // 2, CHIPS, up_gat, 0)
        load_dy.wait()

        def digits(*chunks):
            return sum(chunk * 8**place for place, chunk in enumerate(chunks))

        high = lax.div(k.far, 3)
        chunk_order = (
            (1 - core) * ((1 - high) * digits(2, 3, 0, 4, 5, 1) + high * digits(5, 2, 3, 4, 0, 1))
            + core * ((1 - high) * digits(0, 2, 3, 1, 4, 5) + high * digits(2, 5, 0, 1, 3, 4))
        )

        def fo_grad(j, left_over):
            chunk = lax.rem(left_over, 8)
            rows = pl.ds(pl.multiple_of(chunk * 256 - lax.div(chunk, 4) * 128, 128), 256)
            left = mix[:, :, rows].reshape(CHIPS * tok, 256)
            for h in range(2):
                lanes = slice(h * width // 2, (h + 1) * width // 2)
                right = dy[:, :, lanes].reshape(CHIPS * tok, -1)
                g_fo[rows, lanes] = dot_lt(left, right).astype(BF)
            return lax.div(left_over, 8)

        def fo_twin(i):
            return twin(0, near4[i], fo_part(other, near4[i]), twin_fo_land.at[near4[i]])

        def fo_load(i):
            fo_twin(i).wait_recv()
            return k.keep(twin_fo_land.at[near4[i]], stage.at[i, pl.ds(0, fo_rows)])

        def fo_add(i, load):
            load.wait()
            own = fo_part(core, near4[i])
            own[...] = (own[...].astype(F32) + stage[i, 0:fo_rows].astype(F32)).astype(BF)
            fo_twin(i).wait_send()
            if i > 0:
                sum_fo.begin(3 - i)

        chunk_order = lax.fori_loop(0, 2, fo_grad, chunk_order)
        fo_twin(3).start()
        chunk_order = lax.fori_loop(2, 3, fo_grad, chunk_order)
        fo_add(3, fo_load(3))
        chunk_order = lax.fori_loop(3, 5, fo_grad, chunk_order)
        for i in reversed(range(3)):
            fo_twin(i).start()
        lax.fori_loop(5, 6, fo_grad, chunk_order)
        loads = [fo_load(i) for i in reversed(range(3))]
        for i, load in zip(reversed(range(3)), loads):
            fo_add(i, load)
        load_fo = []
        line_fo.finish(twin_fo.send, lambda: load_fo.extend(fo_shares(range(3))))
        load_fo += fo_shares(range(3, 4))
        for copy in load_fo:
            copy.wait()

        def down(q, carry):
            d_mix = dot_rt(dy[q], fow[...])
            d_val = (d_mix * gat[q].astype(F32)).astype(BF)
            d_gat = (d_mix * val[q].astype(F32)).astype(BF)
            val[q] = d_val
            gat[q] = d_gat
            return carry

        lax.fori_loop(0, CHIPS, down, 0)

        def out_step(q, carry):
            dy[q] = dot(mix[q], fow[...]).astype(BF)
            return carry

        def back(j, carry):
            q = nth(j)

            def back_lanes(i, carry):
                lanes = at(i * 512, 512)
                d_x = dot_rt(val[q], fvw[i].reshape(512, ff)) + dot_rt(
                    gat[q], fgw[i].reshape(512, ff)
                )

                @pl.when(j < 3)
                def _():
                    stage[q, :, lanes] = d_x.astype(BF)

                @pl.when(j == 3)
                def _():
                    acc[:, lanes] = d_x

                return carry

            lax.fori_loop(0, width // 512, back_lanes, 0)
            for step, push in enumerate((plane_mid.send_far, plane_mid.send_x, plane_mid.send_y)):
                pl.when(j == step)(push)
            return carry

        for m, (d_ff, g_ff) in enumerate(((val, g_fv), (gat, g_fg))):

            def ff_grad(owner):
                left = x1n[:, :, at(owner * tok, tok)].reshape(CHIPS * tok, tok)
                g = dot_lt(left, d_ff[...].reshape(CHIPS * tok, ff)).astype(BF)
                return g.reshape(NARROW, -1, ff)

            def side_step(q, carry):
                slot = lax.rem(q, 2)

                @pl.when(q >= 2)
                def _():
                    twin(1 + m, q - 2, side.at[slot], twin_ff.at[m, q]).wait_send()

                side[slot] = ff_grad(2 * q + other)
                twin(1 + m, q, side.at[slot], twin_ff.at[m, q]).start()
                return carry

            def own_step(q, carry):
                g_ff[q] = ff_grad(2 * q + core)
                return carry

            for h in range(2):
                lax.fori_loop(2 * h, 2 * h + 2, side_step, 0)
                lax.fori_loop(2 * h, 2 * h + 2, own_step, 0)
                loads = []
                for q in (2 * h, 2 * h + 1):
                    twin(1 + m, q, side.at[q % 2], twin_ff.at[m, q]).wait_recv()
                    loads.append(k.keep(twin_ff.at[m, q], (tmp_ff, tmp_twin)[q % 2]))
                for q, load in zip((2 * h, 2 * h + 1), loads):
                    load.wait()
                    own = g_ff.at[q]
                    own[...] = (
                        own[...].astype(F32) + (tmp_ff, tmp_twin)[q % 2][...].astype(F32)
                    ).astype(BF)
                if m == 0:
                    sum_ff[m].begin_half(h)
            for q in range(2, CHIPS):
                twin(1 + m, q, side.at[q % 2], twin_ff.at[m, q]).wait_send()
            if m == 1:
                sum_ff[m].begin(0)
            sum_ff[m].begin(1)
            sum_ff[m].begin(2)
            if m == 0:
                lax.fori_loop(0, CHIPS, back, 0)
                lax.fori_loop(0, CHIPS, out_step, 0)
                store = k.keep(dy, res_in)
                plane_mid.combine(add_half)
                store.wait()
                plane_res.send_far()
                plane_res.send_x()
                plane_res.send_y()
                sum_fo.pass_on(0, add_fo)
                sum_fo.pass_on(1, add_fo)

        sum_fo.pass_on(2, add_fo)
        plane_mid.drain()

    pl.run_scoped(
        ffn,
        pltpu.VMEM((CHIPS, tok, width), BF),
        pltpu.VMEM((CHIPS, tok, width), BF),
        pltpu.VMEM(fv_in.shape, BF),
        pltpu.VMEM(fg_in.shape, BF),
        pltpu.VMEM((ff, width), BF),
        pltpu.VMEM((CHIPS, tok, ff), BF),
        pltpu.VMEM((CHIPS, tok, ff), BF),
        pltpu.VMEM((CHIPS, tok, ff), BF),
        pltpu.VMEM((2, *g_fv.shape[1:]), BF),
        pltpu.VMEM(g_fv.shape[1:], BF),
    )

    def rest(d_x1, d_branch, mixed, da_src, factors_src, side, stage_wo, g_wo, g_qk, g_vg):
        plane_out = plane_sum(2, stage_wo)
        sum_wo = LineSum(k, lambda i: g_wo.at[i], lambda s: land_wo.at[s])
        sum_qk = [
            LineSum(k, lambda i, g=g: g.at[:, i], lambda s, m=m: land_qk.at[m, s])
            for m, g in enumerate((g_qk, g_vg))
        ]
        spread_a = Spread(
            k,
            lambda t: da_src.at[:, at(t * two, two)],
            lambda s: a_land.at[s],
            a_land.at[pl.ds(0, WIDE - 1)],
        )
        spread_s = Spread(
            k, lambda t: factors_src, lambda s: s_land.at[s], s_land.at[pl.ds(0, WIDE - 1)]
        )

        def middle(wo, x1, gated, means, dy, d_mixed, pair):
            plane_mid.finish()
            loads = [k.keep(near.at[0], pair), k.keep(x1_in, x1), k.keep(dy_in.at[chip], dy)]
            late = [
                k.keep(wo_in, wo), k.keep(gated_in, gated), k.keep(mixed_in, mixed),
            ]
            for copy in loads:
                copy.wait()

            def norm_back(rows):
                g = acc[rows, :] + pair[0, rows, :].astype(F32) + pair[1, rows, :].astype(F32)
                v = x1[rows, :]
                r = row_scale(v)
                u = v * r
                d = dy[rows, :].astype(F32) + r * (g - u * jnp.mean(g * u, axis=-1, keepdims=True))
                d_x1[rows, :] = d
                d_branch[rows, :] = d.astype(BF)

            row_chunks(tok, norm_back)
            for copy in late:
                copy.wait()

            def mixed_step(j, carry):
                d_mixed[:, at(j * 512, 512)] = dot_rt(
                    d_branch[...], wo[pl.ds(2 * j, 2)].reshape(512, width)
                )
                return carry

            lax.fori_loop(0, width // 512, mixed_step, 0)

            def mixed_back(rows):
                d = d_mixed[rows, :]
                da_src[rows, :] = d.astype(BF)
                mean = jnp.mean(d * gated[rows, :].astype(F32), axis=-1, keepdims=True)
                means[rows, :] = jnp.broadcast_to(mean * scales[rows, 0:1], (mean.shape[0], HEAD))

            row_chunks(tok, mixed_back)
            factors_src[0] = jnp.transpose(scales[...])[0:8]
            factors_src[1] = jnp.transpose(means[...])[0:8]
            spread_s.start()
            spread_a.start()
            own = [
                k.keep(da_src.at[:, at(w * two, two)], a_land.at[w]),
                k.keep(factors_src, s_land.at[w]),
            ]

            for copy in own:
                copy.wait()

        pl.run_scoped(
            middle,
            pltpu.VMEM(wo_in.shape, BF),
            pltpu.VMEM((tok, width), F32),
            pltpu.VMEM((tok, width), BF),
            pltpu.VMEM((tok, HEAD), F32),
            pltpu.VMEM((tok, width), BF),
            pltpu.VMEM((tok, width), F32),
            pltpu.VMEM((2, tok, width), BF),
        )
        def eight_way(plane, twin_index, landing, blocks, spots, term):
            def side_step(j, carry):
                q = nth(j)
                side[q] = term(2 * q + other).astype(BF)
                twin(twin_index, j, side.at[q], landing.at[q]).start()
                return carry

            lax.fori_loop(0, CHIPS, side_step, 0)

            def load(j):
                q = order[j]
                twin(twin_index, j, side.at[q], landing.at[q]).wait_recv()
                return k.keep(landing.at[q], spots[j % 2])

            pushes = (plane.send_far, plane.send_x, plane.send_y)
            loads = [load(0)]
            for j in range(CHIPS):
                if j + 1 < CHIPS and spots[0] is not spots[1]:
                    loads.append(load(j + 1))
                v = term(2 * order[j] + core)
                loads[j].wait()
                v = v + spots[j % 2][...].astype(F32)
                if j < 3:
                    blocks[order[j]] = v.astype(BF)
                    pushes[j]()
                else:
                    acc[...] = v
                if j + 1 < CHIPS and spots[0] is spots[1]:
                    loads.append(load(j + 1))
            for j in range(CHIPS):
                twin(twin_index, j, side.at[order[j]], landing.at[order[j]]).wait_send()

        eight_way(
            plane_out,
            3,
            twin_wo,
            stage_wo,
            (tmp, tmp),
            lambda owner: dot_lt(mixed[:, at(owner * tok, tok)], d_branch[...]),
        )
        sum_ff[0].pass_on(0, add_ff)
        sum_ff[0].pass_on(1, add_ff)

        def attention(xn, d_qk, d_vg, state):
            state[...] = jnp.zeros_like(state)

            def heads(slopes, qkv, sin, decay, attn, gate, d_mixed, factors_in):
                loads = [
                    k.keep(qkv_in, qkv), k.keep(sin_in, sin), k.keep(slope_in, slopes),
                    k.keep(attn_in, attn), k.keep(gate_in, gate),
                ]
                fill_decay(decay)
                for copy in loads:
                    copy.wait()
                spread_s.finish()
                spread_a.finish()
                loads = [k.keep(a_land, d_mixed), k.keep(s_land, factors_in)]
                for copy in loads:
                    copy.wait()
                load_xn = k.keep(xn_in, xn)

                def step(i, carry):
                    b = WIDE - 1 - i
                    rows = at(b * BLOCK, BLOCK)
                    mask, factors = block_tables(b)
                    scale, mean = (
                        jnp.transpose(jnp.broadcast_to(factors_in[b, i, 0:1], (HEAD, tok)))[:, 0:1]
                        for i in range(2)
                    )
                    normed = attn[b].astype(F32) * scale
                    d_m = d_mixed[b].astype(F32)
                    d_vg[rows, two:] = (d_m * normed).astype(BF)
                    d_attn = (scale * (d_m * gate[b].astype(F32) - normed * mean)).astype(BF)
                    for h in range(2):
                        entry, tail, through = factors[h]
                        lanes = slice(h * HEAD, (h + 1) * HEAD)
                        key_lanes = slice(two + h * HEAD, two + (h + 1) * HEAD)
                        q = qkv[rows, lanes]
                        key = qkv[rows, key_lanes]
                        v = qkv[rows, 2 * two + h * HEAD : 2 * two + (h + 1) * HEAD]
                        d_o = d_attn[:, lanes]
                        factor = jnp.where(mask, decay[h], 0.0)
                        probs = (dot_rt(q, key) * factor).astype(BF)
                        d_probs = (dot_rt(d_o, v) * factor).astype(BF)
                        before = sin[b, h]
                        after = state[h]
                        after_bf = after.astype(BF)
                        tailed = (key.astype(F32) * tail).astype(BF)
                        entered = (q.astype(F32) * entry).astype(BF)
                        d_q = dot(d_probs, key) + entry * dot_rt(d_o, before)
                        d_k = dot_lt(d_probs, q) + tail * dot_rt(v, after_bf)
                        d_v = dot_lt(probs, d_o) + dot(tailed, after_bf)
                        d_qk[rows, lanes] = (d_q * slopes[rows, lanes].astype(F32)).astype(BF)
                        d_qk[rows, key_lanes] = (d_k * slopes[rows, key_lanes].astype(F32)).astype(BF)
                        d_vg[rows, lanes] = d_v.astype(BF)
                        state[h] = through * after + dot_lt(entered, d_o)
                    return carry

                lax.fori_loop(0, WIDE, step, 0)
                sum_ff[0].pass_on(2, add_ff)
                load_xn.wait()

            pl.run_scoped(
                heads,
                pltpu.VMEM(slope_in.shape, BF),
                pltpu.VMEM(qkv_in.shape, BF),
                pltpu.VMEM(sin_in.shape, BF),
                pltpu.VMEM((2, BLOCK, BLOCK), F32),
                pltpu.VMEM((WIDE, tok, two), BF),
                pltpu.VMEM((WIDE, tok, two), BF),
                pltpu.VMEM((WIDE, tok, two), BF),
                pltpu.VMEM(s_land.shape, F32),
            )

            for m, (d_in, g_in) in enumerate(((d_qk, g_qk), (d_vg, g_vg))):

                def in_grad(s, carry):
                    left = xn[:, :, at(s * tok, tok)].reshape(WIDE * tok, tok)
                    g_in[s] = dot_lt(left, d_in[...]).astype(BF).reshape(NARROW, -1, 2 * two)
                    return carry

                lax.fori_loop(0, WIDE, in_grad, 0)
                sum_qk[m].begin(0)
                sum_qk[m].begin(1)
                if m == 0:
                    sum_qk[m].begin(2)
                    plane_out.combine(add_half)
                    plane_res.combine(add_res)

            sum_ff[1].pass_on(0, add_ff)
            sum_ff[1].pass_on(1, add_ff)
            g_wo[...] = acc[...].astype(BF).reshape(g_wo.shape)

            def spread_in(wqk, wvg):
                loads = [k.keep(wqk_in, wqk), k.keep(wvg_in, wvg)]
                for copy in loads:
                    copy.wait()

                def term(owner):
                    rows = at(owner * tok, tok)
                    return dot_rt(d_qk[rows, :], wqk[...].reshape(width, 2 * two)) + dot_rt(
                        d_vg[rows, :], wvg[...].reshape(width, 2 * two)
                    )

                spread_a.drain()
                eight_way(plane_in, 4, twin_xn_land, stage, (tmp, da_src), term)

            pl.run_scoped(spread_in, pltpu.VMEM(wqk_in.shape, BF), pltpu.VMEM(wvg_in.shape, BF))

        pl.run_scoped(
            attention,
            pltpu.VMEM((WIDE, tok, width), BF),
            pltpu.VMEM((WIDE * tok, 2 * two), BF),
            pltpu.VMEM((WIDE * tok, 2 * two), BF),
            pltpu.VMEM((2, HEAD, HEAD), F32),
        )

        def last(
            x, x1, own_res, pair, three, three_ff, three_qk, ff_src, qk_src, w_f32, w_fo, tmp_qk
        ):
            add_qk = adder(tmp_qk)
            load_x, load_x1 = k.keep(x_in, x), k.keep(x1_in, x1)
            load_res = k.keep(res_in.at[chip], own_res)
            plane_out.finish()
            fetch(near.at[2], pair)
            for i in range(NARROW):
                rows = pl.ds(i * 64, 64)
                v = g_wo[i].astype(F32) + pair[0, rows, :].astype(F32) + pair[1, rows, :].astype(F32)
                g_wo[i] = v.astype(BF)
            sum_wo.begin(0)
            sum_wo.begin(1)
            sum_qk[1].begin(2)
            sum_wo.begin(2)
            sum_qk[0].pass_on(0, add_qk)
            sum_qk[0].pass_on(1, add_qk)
            plane_in.combine(add_half)
            sum_ff[1].pass_on(2, add_ff)

            def total(part, lands):
                return part.astype(F32) + lands[0].astype(F32) + lands[1].astype(F32)

            ff_turns = []
            for m, g_ff in enumerate((g_fv, g_fg)):
                sum_ff[m].finish(fetch, three_ff)
                for q in range(CHIPS):
                    ff_src[m, q] = total(g_ff[q, n], three_ff[:, q]).astype(BF)
                turn = Spread(
                    k,
                    lambda t, m=m: ff_src.at[m, lax.div(t, 2)],
                    lambda s, m=m: turn_ff.at[m, lax.div(s, 2)],
                    turn_ff.at[m, pl.ds(0, CHIPS - 1)],
                    peers=CHIPS,
                )
                turn.start()
                ff_turns.append((turn, k.keep(ff_src.at[m, chip], turn_ff.at[m, chip])))
            sum_qk[0].pass_on(2, add_qk)
            sum_fo.finish(fetch, three.at[:, pl.ds(0, fo_rows)])
            own = fo_part(core, n)
            for r in range(0, fo_rows, 16):
                rows = pl.ds(r, 16)
                w_fo[rows, :] = total(own[rows, :], three[:, rows, :])
            stores = [k.keep(w_fo, gfo_o)]

            plane_res.finish()
            fetch(near.at[1], pair)
            load_x1.wait()
            load_res.wait()

            def add_up(rows):
                v = x1[rows, :] + own_res[rows, :].astype(F32)
                v = v + pair[0, rows, :].astype(F32) + pair[1, rows, :].astype(F32)
                own_res[rows, :] = v.astype(BF)

            row_chunks(tok, add_up)
            stores.append(k.keep(own_res, result_o))
            sum_qk[1].pass_on(0, add_qk)
            sum_qk[1].pass_on(1, add_qk)
            sum_qk[1].pass_on(2, add_qk)

            def move_qk(m, g_in):
                sum_qk[m].finish(fetch, three_qk)
                for s in range(WIDE):
                    qk_src[m, s] = total(g_in[s, n], three_qk[:, s]).astype(BF)
                turn = Spread(
                    k,
                    lambda t: qk_src.at[m, t],
                    lambda s: turn_qk.at[m, s],
                    turn_qk.at[m, pl.ds(0, WIDE - 1)],
                )
                turn.start()
                return turn, k.keep(qk_src.at[m, w], turn_qk.at[m, w])

            qk_turns = [move_qk(0, g_qk)]
            sum_wo.pass_on(0, add_wo)
            sum_wo.pass_on(1, add_wo)
            load_x.wait()
            plane_in.finish()
            fetch(near.at[3], pair)

            def input_back(rows):
                g = acc[rows, :] + pair[0, rows, :].astype(F32) + pair[1, rows, :].astype(F32)
                v = x[rows, :].astype(F32)
                r = row_scale(v)
                u = v * r
                d_x1[rows, :] = d_x1[rows, :] + r * (
                    g - u * jnp.mean(g * u, axis=-1, keepdims=True)
                )

            row_chunks(tok, input_back)
            stores.append(k.keep(d_x1, dx_o))
            sum_wo.pass_on(2, add_wo)
            qk_turns.append(move_qk(1, g_vg))
            for turn, copy in ff_turns + qk_turns:
                turn.finish()
                copy.wait()
            sum_wo.finish(fetch, three.at[:, pl.ds(0, 64)])
            w_f32[...] = total(g_wo[n], three[:, 0:64, :])
            stores.append(k.keep(w_f32, go_o))
            for copy in stores:
                copy.wait()
            plane_in.drain()
            plane_out.drain()
            plane_res.drain()
            turns = [turn for turn, copy in ff_turns + qk_turns]
            for moved in (*lines, *planes, *twins, *spreads, *spread_ff):
                moved.drain()
            for sums in (sum_fo, sum_wo, *sum_ff, *sum_qk, spread_s, *turns):
                sums.drain()

        pl.run_scoped(
            last,
            pltpu.VMEM((tok, width), BF),
            pltpu.VMEM((tok, width), F32),
            pltpu.VMEM((tok, width), BF),
            pltpu.VMEM((2, tok, width), BF),
            pltpu.VMEM((2, tok, width), BF),
            pltpu.VMEM((2, *land_ff.shape[2:]), BF),
            pltpu.VMEM((2, *land_qk.shape[2:]), BF),
            pltpu.VMEM((2, CHIPS, 64, ff), BF),
            pltpu.VMEM((2, WIDE, 64, 2 * two), BF),
            pltpu.VMEM((64, width), F32),
            pltpu.VMEM((fo_rows, width), F32),
            pltpu.VMEM((WIDE, 64, 2 * two), BF),
        )

    pl.run_scoped(
        rest,
        pltpu.VMEM((tok, width), F32),
        pltpu.VMEM((tok, width), BF),
        pltpu.VMEM((tok, width), BF),
        pltpu.VMEM((tok, width), BF),
        pltpu.VMEM((2, 8, tok), F32),
        pltpu.VMEM((CHIPS, tok, width), BF),
        pltpu.VMEM((CHIPS, tok, width), BF),
        pltpu.VMEM((NARROW, 64, width), BF),
        pltpu.VMEM((WIDE, NARROW, 64, 2 * two), BF),
        pltpu.VMEM((WIDE, NARROW, 64, 2 * two), BF),
    )
    assert k.count <= send.shape[0], k.count


def finish_kernel(
    result, d_x, g_out, g_fout, turn_ff, turn_qk,
    result_o, d_x_o, gq_o, gk_o, gv_o, gg_o, go_o, gfv_o, gfg_o, gfo_o,
    result_v, d_x_v, g_out_v, g_fout_v, ff_v, qk_v, ff_f32, qk_f32, sems,
):
    copies = []

    def copy(src, dst):
        made = pltpu.make_async_copy(src, dst, sems.at[len(copies)])
        made.start()
        copies.append(made)
        return made

    ff, two = ff_v.shape[-1], qk_v.shape[-1] // 2
    load_ff, load_qk = copy(turn_ff, ff_v), copy(turn_qk, qk_v)
    through = (
        (d_x, d_x_v, d_x_o),
        (g_fout, g_fout_v, gfo_o),
        (result, result_v, result_o),
        (g_out, g_out_v, go_o),
    )
    loads = [copy(src, held) for src, held, _ in through]
    stores = []
    load_ff.wait()
    for m, out in enumerate((gfv_o, gfg_o)):
        for q in range(CHIPS):
            ff_f32[m, :, q * ff : (q + 1) * ff] = ff_v[m, q].astype(F32)
        stores.append(copy(ff_f32.at[m], out))
    load_qk.wait()
    for m, outs in enumerate(((gq_o, gk_o), (gv_o, gg_o))):
        for s in range(WIDE):
            lanes = slice(s * two, (s + 1) * two)
            qk_f32[2 * m, :, lanes] = qk_v[m, s, :, 0:two].astype(F32)
            qk_f32[2 * m + 1, :, lanes] = qk_v[m, s, :, two:].astype(F32)
        stores += [copy(qk_f32.at[2 * m + i], out) for i, out in enumerate(outs)]
    for load, (_, held, out) in zip(loads, through):
        load.wait()
        stores.append(copy(held, out))
    for store in stores:
        store.wait()


def finish(results, moved):
    out_shape = moved
    return pl.pallas_call(
        finish_kernel,
        out_shape=out_shape,
        in_specs=[ANY] * 6,
        out_specs=(ANY,) * len(out_shape),
        scratch_shapes=[
            *[pltpu.VMEM(r.shape, r.dtype) for r in results],
            pltpu.VMEM((2, *out_shape[7].shape), F32),
            pltpu.VMEM((4, *out_shape[2].shape), F32),
            pltpu.SemaphoreType.DMA((20,)),
        ],
        compiler_params=pltpu.CompilerParams(vmem_limit_bytes=63 * 2**20),
    )(*results)


def layer(tokens, weights, dy, starts):
    tok, width = tokens.shape
    shard = weights[0].shape[0]
    ff = weights[5].shape[1] // CHIPS
    fo_rows = weights[7].shape[0]
    full = WIDE * tok
    two = 2 * HEAD

    def arr(*shape, dtype=BF):
        return jax.ShapeDtypeStruct(shape, dtype)

    finals = (
        arr(tok, width),
        arr(tok, width, dtype=F32),
        *[arr(shard, width, dtype=F32)] * 5,
        arr(shard, CHIPS * ff, dtype=F32),
        arr(shard, CHIPS * ff, dtype=F32),
        arr(fo_rows, width, dtype=F32),
    )
    results = (
        arr(tok, width),
        arr(tok, width, dtype=F32),
        arr(shard, width, dtype=F32),
        arr(fo_rows, width, dtype=F32),
        arr(2, CHIPS, shard, ff),
        arr(2, WIDE, shard, 2 * two),
    )
    held = (
        arr(WIDE, tok, width),
        arr(WIDE, NARROW, shard, 2 * two),
        arr(WIDE, NARROW, shard, 2 * two),
        arr(WIDE, NARROW, shard, width),
        arr(CHIPS, 2, NARROW, shard, ff),
        arr(CHIPS, 2, NARROW, shard, ff),
        arr(2, NARROW, fo_rows, width),
        arr(CHIPS, tok, width),
        arr(full, 2 * two),
        arr(full, 3 * two),
        arr(WIDE, 2, HEAD, HEAD),
        arr(WIDE, tok, two),
        arr(WIDE, tok, two),
        arr(tok, width),
        arr(tok, width),
        arr(tok, width, dtype=F32),
        arr(CHIPS, tok, width),
    )
    landings = (
        arr(4, 2, tok // 2, width),
        arr(4, 2, tok, width),
        arr(NARROW, fo_rows, width),
        arr(2, CHIPS, NARROW, shard, ff),
        arr(CHIPS, tok, width),
        arr(CHIPS, tok, width),
        arr(5, fo_rows, width),
        arr(2, 5, CHIPS, shard, ff),
        arr(5, shard, width),
        arr(2, 5, WIDE, shard, 2 * two),
        arr(WIDE, tok, two),
        arr(WIDE, 2, 8, tok, dtype=F32),
        arr(WIDE, 8, tok, dtype=F32),
        arr(CHIPS, tok, width),
    )
    out_shape = results + held + landings
    outs = pl.pallas_call(
        layer_kernel,
        out_shape=out_shape,
        in_specs=[ANY] * 10 + [pl.BlockSpec(memory_space=pltpu.SMEM)],
        out_specs=(ANY,) * len(out_shape),
        scratch_shapes=[
            pltpu.VMEM((ff, width), BF),
            pltpu.VMEM((CHIPS, NARROW, shard, ff), BF),
            pltpu.VMEM((CHIPS, NARROW, shard, ff), BF),
            pltpu.VMEM((CHIPS, tok, width), BF),
            pltpu.VMEM((tok, width), F32),
            pltpu.VMEM((tok, width), BF),
            pltpu.VMEM((tok, HEAD), F32),
            pltpu.VMEM((CHIPS, shard, ff), BF),
            pltpu.SemaphoreType.DMA((163,)),
            pltpu.SemaphoreType.DMA((163,)),
            pltpu.SemaphoreType.DMA((40,)),
        ],
        compiler_params=pltpu.CompilerParams(
            collective_id=0, has_side_effects=True, vmem_limit_bytes=65300 * 2**10
        ),
        cost_estimate=pl.CostEstimate(flops=8 * 10**10, bytes_accessed=3 * 10**8, transcendentals=0),
    )(tokens, *weights, dy, starts)
    return finish(outs[: len(results)], finals)


def local_box(tokens, doc_starts, wq, wk, wv, wg, wo, fv, fg, fo, cotangent):
    weights = (wq, wk, wv, wg, wo, fv, fg, fo)
    outs = layer(tokens[0], weights, cotangent[0], doc_starts)
    return (outs[0][None], outs[1][None]) + tuple(outs[2:])


def solution(mesh):
    box = (mesh.shape["wide"], mesh.shape["narrow"]) == (WIDE, NARROW)
    tok = P("narrow", "wide", None)
    row = P(BOTH, None)
    return jax.shard_map(
        local_box if box else local,
        mesh=mesh,
        in_specs=(tok, P()) + (row,) * 8 + (tok,),
        out_specs=(tok, tok) + (row,) * 8,
        check_vma=False,
    )
```

```python
import jax
import jax.numpy as jnp
from jax import lax
from jax.experimental import pallas as pl
from jax.experimental.pallas import tpu as pltpu
from jax.sharding import PartitionSpec as P

HEADS = 16
HEAD = 128
BLOCK = 256
LAYERS = 16
LAYER = 12

EPS = 1e-06
BOTH = ("wide", "narrow")
BF = jnp.bfloat16
F32 = jnp.float32


def normalize(values):
    scale = lax.rsqrt(jnp.mean(values * values, axis=-1, keepdims=True) + EPS)
    return (values * scale, scale)


def normalize_back(normed, scale, grad):
    return scale * (grad - normed * jnp.mean(grad * normed, axis=-1, keepdims=True))


def silu_slope(values):
    sigma = jax.nn.sigmoid(values)
    return sigma * (1.0 + values * (1.0 - sigma))


def matmul(left, right):
    return jnp.dot(left, right, preferred_element_type=F32)


def matmul_right_t(left, right):
    return lax.dot_general(left, right, (((1,), (1,)), ((), ())), preferred_element_type=F32)


def weight_grad(left, right):
    return lax.dot_general(left, right, (((0,), (0,)), ((), ())), preferred_element_type=F32)


def ein(spec, left, right):
    return jnp.einsum(spec, left, right, preferred_element_type=F32)


def head_slopes():
    order = jnp.arange(HEADS, dtype=F32)
    return jnp.exp2(-8.0 * (order + 1.0) / HEADS) * (1.0 - LAYER / (LAYERS - 1) + 1e-05)


def local(
    tokens,
    doc_starts,
    query_weight,
    key_weight,
    value_weight,
    gate_weight,
    out_weight,
    ffn_value_weight,
    ffn_gate_weight,
    ffn_out_weight,
    cotangent,
):
    wide, narrow = lax.axis_size("wide"), lax.axis_size("narrow")
    rows_here, width = tokens.shape[1:]
    length = rows_here * wide
    blocks = length // BLOCK
    heads_here = HEADS // wide
    shard = query_weight.shape[0]

    def reorder(values):
        return values.reshape(-1, wide, narrow, shard).swapaxes(1, 2).reshape(-1, width)

    def restore(values):
        return values.reshape(-1, narrow, wide, shard).swapaxes(1, 2).reshape(-1, width)

    def columns(weight):
        part = lax.all_to_all(weight, "wide", split_axis=1, concat_axis=0, tiled=True)
        return lax.all_gather(part, "narrow", axis=0, tiled=True)

    def gather_rows(values):
        return lax.all_gather(values, "wide", axis=0, tiled=True)

    def scatter_rows(values):
        return lax.psum_scatter(
            values.astype(BF), "wide", scatter_dimension=0, tiled=True
        ).astype(F32)

    def to_tokens(values):
        return lax.all_to_all(values, "wide", split_axis=0, concat_axis=1, tiled=True)

    def to_heads(values):
        return lax.all_to_all(values, "wide", split_axis=1, concat_axis=0, tiled=True)

    def column_sums(grad):
        part = lax.psum_scatter(grad.astype(BF), "narrow", scatter_dimension=0, tiled=True)
        return lax.all_to_all(part, "wide", split_axis=0, concat_axis=1, tiled=True).astype(F32)

    w_query, w_key, w_value, w_gate = map(
        columns, (query_weight, key_weight, value_weight, gate_weight)
    )
    w_out = lax.all_gather(out_weight, BOTH, axis=0, tiled=True)
    w_fval, w_fgate = map(columns, (ffn_value_weight, ffn_gate_weight))
    w_fout = lax.all_gather(ffn_out_weight, "narrow", axis=0, tiled=True)

    starts = lax.dynamic_slice_in_dim(doc_starts, lax.axis_index("narrow"), 1, 0)[0]
    positions = jnp.arange(length, dtype=jnp.int32)
    doc_ids = jnp.sum((starts[None, :] <= positions[:, None]).astype(jnp.int32), axis=1)
    doc_ids = doc_ids.reshape(blocks, BLOCK)
    firsts = jnp.arange(blocks, dtype=jnp.int32) * BLOCK - 1
    prev_ids = jnp.sum((starts[None, :] <= firsts[:, None]).astype(jnp.int32), axis=1)
    slopes = lax.dynamic_slice_in_dim(
        head_slopes(), lax.axis_index("wide") * heads_here, heads_here, 0
    )
    offsets = jnp.arange(BLOCK, dtype=F32)
    lags = offsets[:, None] - offsets[None, :]
    decays = jnp.exp(-slopes[:, None, None] * jnp.maximum(lags, 0.0)[None])
    within = (doc_ids[:, :, None] == doc_ids[:, None, :]) & (lags >= 0.0)
    block_mask = jnp.where(within[:, None], decays[None], 0.0)
    continues = (doc_ids == prev_ids[:, None]).astype(F32)
    entry_scale = continues[..., None] * jnp.exp(-slopes[None, :] * (offsets[:, None] + 1.0))
    tail_scale = (doc_ids == doc_ids[:, -1:]).astype(F32)[..., None] * jnp.exp(
        -slopes[None, :] * (BLOCK - 1.0 - offsets)[:, None]
    )
    passing = continues[:, -1:] * jnp.exp(-slopes * BLOCK)

    def split_heads(values):
        return values.reshape(blocks, BLOCK, heads_here, HEAD)

    inputs = tokens[0].astype(F32)
    normed, in_scale = normalize(inputs)
    normed_bf = gather_rows(reorder(normed.astype(BF)))
    query_pre = matmul(normed_bf, w_query)
    key_pre = matmul(normed_bf, w_key)
    queries = split_heads(jax.nn.silu(query_pre).astype(BF))
    keys = split_heads(jax.nn.silu(key_pre).astype(BF))
    values = split_heads(matmul(normed_bf, w_value).astype(BF))
    gate = matmul(normed_bf, w_gate)
    scores = ein("bihe,bjhe->bhij", queries, keys)
    probs = (scores * block_mask).astype(BF)
    inner = ein("bhij,bjhe->bihe", probs, values)
    tail_keys = (keys.astype(F32) * tail_scale[..., None]).astype(BF)
    fresh = ein("bjhe,bjhf->bhef", tail_keys, values)
    state = jnp.zeros((heads_here, HEAD, HEAD), F32)
    entering = []
    for b in range(blocks):
        entering.append(state)
        state = passing[b][:, None, None] * state + fresh[b]
    block_in = jnp.stack(entering).astype(BF)
    across = entry_scale[..., None] * ein("bihe,bhef->bihf", queries, block_in)
    attention = (inner + across).reshape(query_pre.shape)

    attn_tok = to_tokens(attention)
    gate_tok = to_tokens(gate)
    attn_n, attn_scale = normalize(attn_tok)
    mixed = (attn_n * gate_tok).astype(BF)
    middle = inputs + matmul(mixed, w_out)
    middle_n, middle_scale = normalize(middle)
    middle_bf = gather_rows(reorder(middle_n.astype(BF)))
    ffn_val = matmul(middle_bf, w_fval)
    ffn_gat = matmul(middle_bf, w_fgate)
    ffn_mix = (ffn_val * ffn_gat).astype(BF)
    result = middle + scatter_rows(matmul(ffn_mix, w_fout))

    upstream = cotangent[0]
    up_all = gather_rows(upstream)
    grad_fout = weight_grad(ffn_mix, up_all)
    d_mix = matmul_right_t(up_all, w_fout)
    d_val = (d_mix * ffn_gat).astype(BF)
    d_gat = (d_mix * ffn_val).astype(BF)
    grad_fval = weight_grad(middle_bf, d_val)
    grad_fgate = weight_grad(middle_bf, d_gat)
    d_middle_n = restore(
        scatter_rows(matmul_right_t(d_val, w_fval) + matmul_right_t(d_gat, w_fgate))
    )
    d_middle = upstream.astype(F32) + normalize_back(middle_n, middle_scale, d_middle_n)
    d_branch = d_middle.astype(BF)
    grad_out = weight_grad(mixed, d_branch)
    d_mixed = matmul_right_t(d_branch, w_out)
    d_gate = to_heads((d_mixed * attn_n).astype(BF))
    d_attn = to_heads(normalize_back(attn_n, attn_scale, d_mixed * gate_tok).astype(BF))

    d_heads = split_heads(d_attn)
    d_probs = ein("bihe,bjhe->bhij", d_heads, values)
    d_scores = (d_probs * block_mask).astype(BF)
    d_query = ein("bhij,bjhe->bihe", d_scores, keys)
    d_key = ein("bhij,bihe->bjhe", d_scores, queries)
    d_value = ein("bhij,bihe->bjhe", probs, d_heads)
    d_query = d_query + entry_scale[..., None] * ein("bihf,bhef->bihe", d_heads, block_in)
    entry_queries = (queries.astype(F32) * entry_scale[..., None]).astype(BF)
    grad_in = ein("bihe,bihf->bhef", entry_queries, d_heads)
    state = jnp.zeros((heads_here, HEAD, HEAD), F32)
    leaving = [None] * blocks
    for b in reversed(range(blocks)):
        leaving[b] = state
        state = passing[b][:, None, None] * state + grad_in[b]
    block_out = jnp.stack(leaving).astype(BF)
    d_key = d_key + tail_scale[..., None] * ein("bjhf,bhef->bjhe", values, block_out)
    d_value = d_value + ein("bjhe,bhef->bjhf", tail_keys, block_out)
    dq_pre = (d_query.reshape(query_pre.shape) * silu_slope(query_pre)).astype(BF)
    dk_pre = (d_key.reshape(key_pre.shape) * silu_slope(key_pre)).astype(BF)
    dv_pre = d_value.reshape(query_pre.shape).astype(BF)
    grad_query = weight_grad(normed_bf, dq_pre)
    grad_key = weight_grad(normed_bf, dk_pre)
    grad_value = weight_grad(normed_bf, dv_pre)
    grad_gate = weight_grad(normed_bf, d_gate)
    d_normed = restore(
        scatter_rows(
            matmul_right_t(dq_pre, w_query)
            + matmul_right_t(dk_pre, w_key)
            + matmul_right_t(dv_pre, w_value)
            + matmul_right_t(d_gate, w_gate)
        )
    )
    d_inputs = d_middle + normalize_back(normed, in_scale, d_normed)
    return (
        result.astype(BF)[None],
        d_inputs[None],
        column_sums(grad_query),
        column_sums(grad_key),
        column_sums(grad_value),
        column_sums(grad_gate),
        lax.psum_scatter(grad_out.astype(BF), BOTH, scatter_dimension=0, tiled=True).astype(F32),
        column_sums(grad_fval),
        column_sums(grad_fgate),
        lax.psum_scatter(grad_fout.astype(BF), "narrow", scatter_dimension=0, tiled=True).astype(
            F32
        ),
    )


MESH = pl.DeviceIdType.MESH
ANY = pl.BlockSpec(memory_space=pl.ANY)
VMEM = pl.BlockSpec(memory_space=pltpu.VMEM)
WIDE, NARROW = 8, 4
CHIPS = WIDE // 2


def dot(left, right):
    return jnp.dot(left, right, preferred_element_type=F32)


def dot_rt(left, right):
    return lax.dot_general(left, right, (((1,), (1,)), ((), ())), preferred_element_type=F32)


def dot_lt(left, right):
    return lax.dot_general(left, right, (((0,), (0,)), ((), ())), preferred_element_type=F32)


def at(start, size):
    return pl.ds(pl.multiple_of(start, size), size)


class Links:
    def __init__(self, send, recv, here):
        self.send, self.recv, self.here = send, recv, here
        self.count = 0
        self.free = list(range(1, here.shape[0]))
        w = lax.axis_index("wide")
        n = lax.axis_index("narrow")
        self.w, self.n = w, n
        self.core = lax.rem(w, 2)
        self.chip = lax.div(w, 2)
        x, y = lax.rem(self.chip, 2), lax.div(self.chip, 2)
        self.wx = w + 2 - 4 * x
        self.wy = w + 4 - 8 * y
        self.wd = w + 6 - 4 * x - 8 * y
        self.ws = w + 1 - 2 * self.core
        self.px = self.chip + 1 - 2 * x
        self.py = self.chip + 2 - 4 * y
        self.pd = 3 - self.chip
        self.mid = lax.rem(lax.div(n + 1, 2), 2)
        self.pair = n + 1 - 2 * lax.rem(n, 2)
        self.cross = 2 - lax.div(n, 2)
        self.far = 3 - 3 * lax.div(n, 2)
        self.end_to = 3 * lax.rem(n + 1, 2)
        self.end_part = lax.rem(2 * n, 3) + 3 * lax.div(n, 3)

    def greet(self):
        barrier = pltpu.get_barrier_semaphore()
        for d in range(1, WIDE):
            pl.semaphore_signal(
                barrier, inc=1, device_id=(lax.rem(self.w + d, WIDE), self.n), device_id_type=MESH
            )
        for d in range(1, NARROW):
            pl.semaphore_signal(
                barrier, inc=1, device_id=(self.w, lax.rem(self.n + d, NARROW)), device_id_type=MESH
            )

    def met(self):
        pl.semaphore_wait(pltpu.get_barrier_semaphore(), WIDE + NARROW - 2)

    def take(self, number):
        base = self.count
        self.count += number
        return base

    def remote(self, src, dst, send, recv, wide=None, narrow=None):
        return pltpu.make_async_remote_copy(
            src_ref=src,
            dst_ref=dst,
            send_sem=self.send.at[send],
            recv_sem=self.recv.at[recv],
            device_id=(self.w if wide is None else wide, self.n if narrow is None else narrow),
            device_id_type=MESH,
        )

    def arrived(self, ref, recv):
        self.remote(ref, ref, recv, recv, wide=self.ws).wait_recv()

    def keep(self, src, dst):
        return Kept(self, src, dst)


class Kept:
    def __init__(self, links, src, dst):
        self.links, self.index = links, links.free.pop(0)
        self.copy = pltpu.make_async_copy(src, dst, links.here.at[self.index])
        self.copy.start()

    def wait(self):
        self.copy.wait()
        self.links.free.append(self.index)


class Line:
    def __init__(self, links, part):
        self.links, self.part = links, part
        self.base = links.take(5)

    def copy(self, index):
        k, b = self.links, self.base
        which, to = (
            (k.n, k.pair),
            (k.n, k.cross),
            (k.pair, k.cross),
            (k.cross, k.pair),
            (k.far, k.pair),
        )[index]
        ref = self.part(which)
        return k.remote(ref, ref, b + index, b + which, narrow=to)

    def start(self):
        self.start_away()
        pl.when(self.links.mid == 1)(lambda: self.copy(0).start())

    def start_away(self):
        pl.when(self.links.mid == 1)(lambda: self.copy(1).start())
        pl.when(self.links.mid == 0)(lambda: self.copy(0).start())

    def start_home(self):
        pl.when(self.links.mid == 1)(lambda: self.copy(0).start())

    def wait(self, index):
        self.links.arrived(self.part(index), self.base + index)

    def forward(self):
        @pl.when(self.links.mid == 1)
        def _():
            self.wait(self.links.cross)
            self.copy(3).start()
            self.wait(self.links.pair)
            self.copy(2).start()

    def forward_far(self):
        @pl.when(self.links.mid == 1)
        def _():
            self.wait(self.links.far)
            self.copy(4).start()

    def finish(self, then=lambda place: None, late=lambda: None):
        k = self.links
        then(0)
        for place, index in enumerate((k.pair, k.cross, k.far)):
            if place == 2:
                late()
            pl.when(k.mid == 0)(lambda index=index: self.wait(index))
            then(place + 1)

    def drain(self):
        self.copy(0).wait_send()

        @pl.when(self.links.mid == 1)
        def _():
            for index in range(1, 5):
                self.copy(index).wait_send()


class Plane:
    def __init__(self, links, slot):
        self.links, self.slot = links, slot
        self.base = links.take(6)

    def copy(self, index):
        k, b = self.links, self.base
        owner, half, to = (
            (k.w, 0, k.wx),
            (k.w, 1, k.wy),
            (k.w, 1, k.wx),
            (k.w, 0, k.wy),
            (k.wx, 0, k.wy),
            (k.wy, 1, k.wx),
        )[index]
        ref = self.slot(owner, half)
        return k.remote(ref, ref, b + index, b + index, wide=to)

    def start(self):
        for index in range(4):
            self.copy(index).start()

    def forward(self):
        k, b, slot = self.links, self.base, self.slot
        k.arrived(slot(k.wx, 0), b)
        self.copy(4).start()
        k.arrived(slot(k.wy, 1), b + 1)
        self.copy(5).start()

    def finish_near(self):
        k, b, slot = self.links, self.base, self.slot
        k.arrived(slot(k.wx, 1), b + 2)
        k.arrived(slot(k.wy, 0), b + 3)

    def finish_far(self):
        k, b, slot = self.links, self.base, self.slot
        k.arrived(slot(k.wd, 0), b + 4)
        k.arrived(slot(k.wd, 1), b + 5)

    def drain(self):
        for index in range(6):
            self.copy(index).wait_send()


class Sibling:
    def __init__(self, links, block, twin, number):
        self.links, self.block, self.twin, self.number = links, block, twin, number
        self.base = links.take(number)

    def copy(self, index):
        k, b = self.links, self.base + index
        ref = self.block(index)
        return k.remote(ref, ref, b, b, wide=k.ws)

    def send(self, index):
        self.copy(index).start()

    def wait(self, index):
        self.links.arrived(self.twin(index), self.base + index)

    def drain(self):
        for index in range(self.number):
            self.copy(index).wait_send()


class Spread:
    def __init__(self, links, src, dst, bulk, peers=WIDE):
        self.links, self.src, self.dst, self.bulk = links, src, dst, bulk
        self.step = 1 if peers == WIDE else 2
        self.base = links.take(1)

    def distances(self):
        return range(self.step, WIDE, self.step)

    def copy(self, to):
        k = self.links
        return k.remote(self.src(to), self.dst(k.w), self.base, self.base, wide=to)

    def start(self):
        for d in self.distances():
            self.copy(lax.rem(self.links.w + d, WIDE)).start()

    def finish(self):
        self.links.arrived(self.bulk, self.base)

    def drain(self):
        k = self.links
        k.remote(self.bulk, self.bulk, self.base, self.base, wide=k.ws).wait_send()


def row_scale(values):
    return lax.rsqrt(jnp.mean(values * values, axis=-1, keepdims=True) + EPS)


def row_chunks(rows, body, size=32):
    def step(r, carry):
        body(at(r * size, size))
        return carry

    lax.fori_loop(0, rows // size, step, 0)


class LineSum:
    def __init__(self, links, part, land, half=None):
        self.links, self.part, self.land, self.half = links, part, land, half
        self.base = links.take(5 if half is None else 6)
        self.onward = links.pair + links.mid * (links.cross - links.pair)

    def copy(self, index):
        k, b = self.links, self.base
        which, slot, to = (
            (k.far, 3 * k.mid, self.onward),
            (k.cross, 1 + 3 * k.mid, self.onward),
            (k.pair, 2 - 2 * k.mid, k.pair),
        )[index]
        return k.remote(self.part(which), self.land(slot), b + index, b + slot, narrow=to)

    def half_copy(self, h):
        k, sem = self.links, self.base + 5 * h
        src, dst = self.half(self.part(k.far), h), self.half(self.land(0), h)
        return k.remote(src, dst, sem, sem, narrow=k.pair)

    def begin_half(self, h):
        pl.when(self.links.mid == 0)(lambda: self.half_copy(h).start())

    def begin(self, index):
        pl.when(self.links.mid == 0)(lambda: self.copy(index).start())

    def start(self):
        for index in range(3):
            self.begin(index)

    def wait(self, slot):
        self.links.arrived(self.land(slot), self.base + slot)

    def pass_on(self, index, add):
        k = self.links
        which, slot = ((k.far, 0), (k.cross, 1), (k.pair, 3))[index]

        @pl.when(k.mid == 1)
        def _():
            if self.half is not None and index == 0:
                for h in range(2):
                    k.arrived(self.half(self.land(0), h), self.base + 5 * h)
            else:
                self.wait(slot)
            add(self.part(which), self.land(slot))
            self.copy(index).start()

    def finish(self, fetch, spots):
        k = self.links
        pl.when(k.mid == 0)(lambda: self.wait(0))

        @pl.when(k.mid == 1)
        def _():
            self.wait(2)
            self.wait(4)
            fetch(self.land(4), spots.at[1])

        fetch(self.land(2 * k.mid), spots.at[0])

        @pl.when(k.mid == 0)
        def _():
            spots[1] = jnp.zeros(spots.shape[1:], spots.dtype)

    def drain(self):
        if self.half is None:
            self.copy(0).wait_send()
        else:

            @pl.when(self.links.mid == 0)
            def _():
                for h in range(2):
                    self.half_copy(h).wait_send()

            pl.when(self.links.mid == 1)(lambda: self.copy(0).wait_send())
        for index in range(1, 3):
            self.copy(index).wait_send()


class PlaneSum:
    def __init__(self, links, block, corner, near, half, base=None, late=None):
        self.late = late
        self.links, self.block, self.corner, self.near, self.half = links, block, corner, near, half
        self.base = links.take(6) if base is None else base

    def rows(self, h):
        return pl.ds(h * self.half, self.half)

    def copy(self, index):
        k = self.links
        chip, h, land, to = (
            (k.pd, 0, self.corner.at[0], k.wx),
            (k.pd, 1, self.corner.at[1], k.wy),
            (k.px, 0, self.near.at[0, self.rows(0)], k.wx),
            (k.py, 1, self.near.at[1, self.rows(1)], k.wy),
            (k.px, 1, self.near.at[0, self.rows(1)], k.wx),
            (k.py, 0, self.near.at[1, self.rows(0)], k.wy),
        )[index]
        sem = self.base + index
        src = self.block(chip).at[self.rows(h)]
        if self.late is not None and index >= 4:
            src = self.late.at[self.rows(index - 4)]
        return k.remote(src, land, sem, sem, wide=to)

    def send_far(self):
        self.copy(0).start()
        self.copy(1).start()

    def send_x(self):
        self.copy(2).start()

    def send_y(self):
        self.copy(3).start()

    def combine(self, add):
        k = self.links
        for index, corner, chip, h in ((4, 1, k.px, 1), (5, 0, k.py, 0)):
            self.copy(corner).wait_recv()
            own = self.block(chip).at[self.rows(h)]
            to = own if self.late is None else self.late.at[self.rows(index - 4)]
            add(to, self.corner.at[corner], own)
            self.copy(index).start()

    def finish(self):
        for index in range(2, 6):
            self.copy(index).wait_recv()

    def drain(self, first=0, last=6):
        for index in range(first, last):
            self.copy(index).wait_send()


def layer_kernel(
    x_in, wq, wk, wv, wg, wo, fv, fg, fo, dy_arg, starts,
    result_o, dx_o, go_o, gfo_o, turn_ff, turn_qk,
    xn_in, wqk_in, wvg_in, wo_in, fv_in, fg_in, fo_in, dy_in, slope_in, qkv_in, sin_in, attn_in,
    gate_in, gated_in, mixed_in, x1_in, x1n_in,
    corner, near, twin_fo_land, twin_ff, twin_wo, twin_xn_land, land_fo, land_ff, land_wo, land_qk,
    a_land, s_land, sq_land, res_in,
    g_fo, g_fv, g_fg, stage, acc, tmp, scales, tmp_ff,
    send, recv, here,
):
    k = Links(send, recv, here)
    w, n, core, chip = k.w, k.n, k.core, k.chip
    other = 1 - core
    tok, width = acc.shape
    ff = g_fv.shape[-1]
    fo_rows = land_fo.shape[1]
    half = tok // 2
    two = 2 * HEAD
    order = (k.pd, k.px, k.py, chip)
    begins = [starts[n, j] for j in range(starts.shape[1])]

    def docs(positions):
        return sum((positions >= begin).astype(jnp.int32) for begin in begins)

    def slope(h):
        head = (2 * w + h + 1).astype(F32)
        rate = 1.0 - LAYER / (LAYERS - 1) + 1e-05
        return jnp.exp2(jnp.full((1, HEAD), -8.0 / HEADS, F32) * head)[:, 0:1] * rate

    def fill_decay(decay):
        i = lax.broadcasted_iota(jnp.int32, (BLOCK, BLOCK), 0)
        j = lax.broadcasted_iota(jnp.int32, (BLOCK, BLOCK), 1)
        lags = jnp.maximum(i - j, 0).astype(F32)
        for h in range(2):
            decay[h] = jnp.exp(-slope(h) * lags)

    def block_tables(b):
        first = b * BLOCK
        i = lax.broadcasted_iota(jnp.int32, (BLOCK, 1), 0)
        j = lax.broadcasted_iota(jnp.int32, (1, BLOCK), 1)
        ids = docs(first + i)
        mask = (ids == docs(first + j)) & (i >= j)
        before, at_end = docs(first - 1), docs(first + BLOCK - 1)
        steps = i.astype(F32)
        factors = []
        for h in range(2):
            rate = slope(h)
            entry = jnp.where(ids == before, jnp.exp(-rate * (steps + 1.0)), 0.0)
            tail = jnp.where(ids == at_end, jnp.exp(-rate * (BLOCK - 1.0 - steps)), 0.0)
            through = jnp.where(before == at_end, jnp.exp(-rate * BLOCK), 0.0)
            factors.append((entry, tail, through))
        return mask, factors

    def nth(j):
        flip_x, flip_y = 1 - lax.div(j, 2), 1 - lax.rem(j, 2)
        return (
            chip + flip_x * (1 - 2 * lax.rem(chip, 2)) + flip_y * (2 - 4 * lax.div(chip, 2))
        )

    def fetch(src, dst):
        copy = pltpu.make_async_copy(src, dst, here.at[0])
        copy.start()
        copy.wait()

    def adder(spot):
        def add(to, land, own=None):
            fetch(land, spot)
            own = to if own is None else own
            to[...] = (own[...].astype(F32) + spot[...].astype(F32)).astype(BF)

        return add

    add_half = adder(tmp.at[pl.ds(0, half)])
    add_fo = adder(tmp.at[pl.ds(0, fo_rows)])
    add_wo = adder(tmp.at[pl.ds(0, 64)])
    add_ff = adder(tmp_ff)

    def add_res(to, land, own):
        fetch(own, to)
        add_half(to, land)

    def fo_part(owner, i):
        return g_fo.at[pl.ds(pl.multiple_of((owner * NARROW + i) * fo_rows, 16), fo_rows)]

    sum_fo = LineSum(k, lambda i: fo_part(core, i), lambda s: land_fo.at[s])
    sum_ff = [
        LineSum(k, lambda i, g=g: g.at[:, i], lambda s, m=m: land_ff.at[m, s], half)
        for m, (g, half) in enumerate(
            ((g_fv, lambda ref, h: ref.at[pl.ds(2 * h, 2)]), (g_fg, None))
        )
    ]
    def plane_sum(m, blocks, base=None, late=None):
        return PlaneSum(k, lambda q: blocks.at[q], corner.at[m], near.at[m], half, base, late)

    plane_mid, plane_in = (plane_sum(m, stage) for m in (0, 3))
    plane_res = plane_sum(1, res_in, late=stage.at[chip])
    twin_base = k.take(4 * 5)

    def twin(m, j, src, dst):
        sem = twin_base + 4 * m + j
        return k.remote(src, dst, sem, sem, wide=k.ws)

    def wide_cols(index):
        return at(index * two, two)

    def chip_cols(index):
        return pl.ds(pl.multiple_of(index * ff, 128), ff)

    projections = ((wq, wqk_in), (wk, wqk_in), (wv, wvg_in), (wg, wvg_in))
    lines = line_out, line_qk, line_vg, line_fv, line_fg, line_fo = (
        Line(k, lambda i: wo_in.at[w, i]),
        Line(k, lambda i: wqk_in.at[:, i]),
        Line(k, lambda i: wvg_in.at[:, i]),
        Line(k, lambda i: fv_in.at[:, core, i]),
        Line(k, lambda i: fg_in.at[:, core, i]),
        Line(k, lambda i: fo_in.at[core, i]),
    )
    spreads = [
        Spread(
            k,
            lambda t, weight=weight: weight.at[:, wide_cols(t)],
            lambda s, m=m, to=to: to.at[s, n, :, pl.ds((m % 2) * two, two)],
            to.at[pl.ds(0, WIDE - 1), n, :, pl.ds((m % 2) * two, two)],
        )
        for m, (weight, to) in enumerate(projections)
    ]
    spread_ff = [
        Spread(
            k,
            lambda t, weight=weight: weight.at[:, chip_cols(lax.div(t, 2))],
            lambda s, to=to: to.at[lax.div(s, 2), core, n],
            to.at[pl.ds(0, CHIPS - 1), core, n],
            peers=CHIPS,
        )
        for weight, to in ((fv, fv_in), (fg, fg_in))
    ]
    planes = plane_xn, plane_out, plane_dy, plane_x1n = (
        Plane(k, lambda s, h: xn_in.at[s, pl.ds(h * half, half)]),
        Plane(k, lambda s, h: wo_in.at[s, pl.ds(h * 2, 2)]),
        Plane(k, lambda s, h: dy_in.at[lax.div(s, 2), pl.ds(h * half, half)]),
        Plane(k, lambda s, h: x1n_in.at[lax.div(s, 2), pl.ds(h * half, half)]),
    )
    here4 = (w, k.wx, k.wy, k.wd)
    there4 = tuple(s + 1 - 2 * core for s in here4)
    near4 = (n, k.pair, k.cross, k.far)
    twins = twin_xn, twin_out, twin_fv, twin_fg, twin_fo = (
        Sibling(k, lambda i: xn_in.at[here4[i]], lambda i: xn_in.at[there4[i]], 4),
        Sibling(k, lambda i: wo_in.at[here4[i]], lambda i: wo_in.at[there4[i]], 4),
        Sibling(k, lambda i: fv_in.at[:, core, near4[i]], lambda i: fv_in.at[:, other, near4[i]], 4),
        Sibling(k, lambda i: fg_in.at[:, core, near4[i]], lambda i: fg_in.at[:, other, near4[i]], 4),
        Sibling(k, lambda i: fo_in.at[core, near4[i]], lambda i: fo_in.at[other, near4[i]], 4),
    )

    k.greet()
    def before(
        x, xn, wqk, wvg, wout, slopes, qkv, gates, sin, state, attn_s, gated_s,
        squares, sums, gated, mixed, x1, x1n, decay,
    ):
        load_x = k.keep(x_in, x)
        held = [
            (k.keep(wo, mixed.at[pl.ds(0, 64)]), mixed.at[pl.ds(0, 64)], wo_in.at[w, n]),
            *[
                (
                    k.keep(weight.at[:, wide_cols(w)], spot.at[w, n, :, lanes]),
                    spot.at[w, n, :, lanes],
                    to.at[w, n, :, lanes],
                )
                for weight, spot, to, lanes in (
                    (wq, wqk, wqk_in, pl.ds(0, two)),
                    (wk, wqk, wqk_in, pl.ds(two, two)),
                    (wv, wvg, wvg_in, pl.ds(0, two)),
                    (wg, wvg, wvg_in, pl.ds(two, two)),
                )
            ],
            (k.keep(dy_arg, gated), gated, dy_in.at[chip]),
            *[
                (
                    k.keep(weight.at[:, chip_cols(chip)], tmp_ff.at[m]),
                    tmp_ff.at[m],
                    to.at[chip, core, n],
                )
                for m, (weight, to) in enumerate(((fv, fv_in), (fg, fg_in)))
            ],
            (k.keep(fo, tmp.at[pl.ds(0, fo_rows)]), tmp.at[pl.ds(0, fo_rows)], fo_in.at[core, n]),
        ]

        def place(index):
            load, spot, to = held[index]
            load.wait()
            return k.keep(spot, to)

        load_x.wait()

        def norm_in(rows):
            v = x[rows, :].astype(F32)
            x1n[rows, :] = (v * row_scale(v)).astype(BF)

        row_chunks(tok, norm_in)
        own_xn = k.keep(x1n, xn_in.at[w])
        own_in = [place(i) for i in range(5)]
        k.met()
        for spread in spreads:
            spread.start()
        own_in[0].wait()
        line_out.start()
        own_xn.wait()
        for copy in own_in[1:]:
            copy.wait()
        spreads[0].finish()
        line_out.forward()
        spreads[1].finish()
        line_qk.start()
        plane_xn.start()
        twin_xn.send(0)
        spreads[2].finish()
        spreads[3].finish()
        line_vg.start()
        for spread in spread_ff:
            spread.start()
        own_ff = [place(i) for i in range(5, 9)]
        line_out.forward_far()
        line_qk.forward()
        plane_xn.forward()
        line_vg.forward()
        plane_xn.finish_near()
        twin_xn.send(1)
        twin_xn.send(2)
        line_qk.forward_far()
        line_out.finish()
        plane_out.start()
        twin_out.send(0)
        plane_xn.finish_far()
        twin_xn.send(3)
        line_vg.forward_far()
        spread_ff[0].finish()
        spread_ff[1].finish()
        for copy in own_ff:
            copy.wait()
        line_fv.start()
        for i in range(4):
            twin_xn.wait(i)
        load_xn = k.keep(xn_in, xn)
        plane_out.forward()
        line_qk.finish()
        load_qk = k.keep(wqk_in, wqk)
        load_xn.wait()
        load_qk.wait()

        def project_qk(t, carry):
            v = dot(xn[t], wqk[...].reshape(width, 2 * two))
            rows = at(t * tok, tok)
            sigma = jax.nn.sigmoid(v)
            slopes[rows, :] = (sigma * (1.0 + v * (1.0 - sigma))).astype(BF)
            qkv[rows, 0 : 2 * two] = (v * sigma).astype(BF)
            return carry

        lax.fori_loop(0, WIDE, project_qk, 0)
        stores = [k.keep(slopes, slope_in)]
        plane_out.finish_near()
        twin_out.send(1)
        twin_out.send(2)
        line_vg.finish()
        k.keep(wvg_in, wvg).wait()

        def project_vg(t, carry):
            v = dot(xn[t], wvg[...].reshape(width, 2 * two)).astype(BF)
            qkv[at(t * tok, tok), 2 * two : 3 * two] = v[:, 0:two]
            gates[t] = v[:, two:]
            return carry

        lax.fori_loop(0, WIDE, project_vg, 0)
        line_fv.forward()
        line_fg.start()
        stores.append(k.keep(qkv, qkv_in))
        stores.append(k.keep(gates, gate_in))
        fill_decay(decay)
        state[...] = jnp.zeros_like(state)
        spread_gated = Spread(
            k,
            lambda t: gated_s.at[t],
            lambda s: gated_in.at[:, wide_cols(s)],
            gated_in.at[:, pl.ds(0, (WIDE - 1) * two)],
        )
        spread_sq = Spread(
            k, lambda t: squares.at[t], lambda s: sq_land.at[s], sq_land.at[pl.ds(0, WIDE - 1)]
        )

        def attend(b, carry):
            rows = at(b * BLOCK, BLOCK)
            mask, factors = block_tables(b)
            for h in range(2):
                lanes = slice(h * HEAD, (h + 1) * HEAD)
                entry, tail, through = factors[h]
                q = qkv[rows, lanes]
                key = qkv[rows, two + h * HEAD : two + (h + 1) * HEAD]
                v = qkv[rows, 2 * two + h * HEAD : 2 * two + (h + 1) * HEAD]
                probs = jnp.where(mask, dot_rt(q, key) * decay[h], 0.0).astype(BF)
                old = state[h]
                old_bf = old.astype(BF)
                sin[b, h] = old_bf
                out = dot(probs, v) + entry * dot(q, old_bf)
                attn_s[b, :, lanes] = out.astype(BF)
                gated_s[b, :, lanes] = (out * gates[b, :, lanes].astype(F32)).astype(BF)
                tailed = (key.astype(F32) * tail).astype(BF)
                state[h] = through * old + dot_lt(tailed, v)

            a = attn_s[b].astype(F32)
            squares[b] = dot_rt(jnp.ones((8, two), BF), (a * a).astype(BF))

            @pl.when(b != w)
            def _():
                spread_sq.copy(b).start()
                spread_gated.copy(b).start()

            return carry

        lax.fori_loop(0, WIDE, attend, 0)
        stores.append(k.keep(sin, sin_in))
        stores.append(k.keep(attn_s, attn_in))
        own = [
            k.keep(gated_s.at[w], gated_in.at[:, wide_cols(w)]),
            k.keep(squares.at[w], sq_land.at[w]),
        ]
        plane_out.finish_far()
        twin_out.send(3)
        for i in range(4):
            twin_out.wait(i)
        load_out = k.keep(wo_in, wout)
        line_fv.forward_far()
        spread_sq.finish()
        spread_gated.finish()
        for copy in own:
            copy.wait()
        loads = [k.keep(gated_in, gated), k.keep(sq_land, sums)]
        for copy in loads:
            copy.wait()
        total_sq = sum(sums[s, 0:1, :] for s in range(WIDE))
        scales[...] = jnp.transpose(
            jnp.broadcast_to(lax.rsqrt(total_sq * (1.0 / width) + EPS), (HEAD, tok))
        )

        def mix(rows):
            mixed[rows, :] = (gated[rows, :].astype(F32) * scales[rows, 0:1]).astype(BF)

        row_chunks(tok, mix)
        stores.append(k.keep(mixed, mixed_in))
        load_out.wait()

        def project_out(j, carry):
            lanes = at(j * 512, 512)
            part = dot(mixed[...], wout[:, :, :, lanes].reshape(-1, 512))
            x1[:, lanes] = x[:, lanes].astype(F32) + part
            return carry

        lax.fori_loop(0, width // 512, project_out, 0)
        stores.append(k.keep(x1, x1_in))

        def norm_mid(rows):
            v = x1[rows, :]
            x1n[rows, :] = (v * row_scale(v)).astype(BF)

        row_chunks(tok, norm_mid)
        k.keep(x1n, x1n_in.at[chip]).wait()
        plane_x1n.start()
        line_fg.forward()
        line_fo.start_away()
        plane_x1n.forward()
        plane_dy.start()
        line_fg.forward_far()
        for copy in stores:
            copy.wait()
        spread_sq.drain()
        spread_gated.drain()

    pl.run_scoped(
        before,
        pltpu.VMEM((tok, width), BF),
        pltpu.VMEM((WIDE, tok, width), BF),
        pltpu.VMEM(wqk_in.shape, BF),
        pltpu.VMEM(wvg_in.shape, BF),
        pltpu.VMEM(wo_in.shape, BF),
        pltpu.VMEM(slope_in.shape, BF),
        pltpu.VMEM(qkv_in.shape, BF),
        pltpu.VMEM((WIDE, tok, two), BF),
        pltpu.VMEM(sin_in.shape, BF),
        pltpu.VMEM((2, HEAD, HEAD), F32),
        pltpu.VMEM((WIDE, tok, two), BF),
        pltpu.VMEM((WIDE, tok, two), BF),
        pltpu.VMEM((WIDE, 8, tok), F32),
        pltpu.VMEM((WIDE, 8, tok), F32),
        pltpu.VMEM((tok, width), BF),
        pltpu.VMEM((tok, width), BF),
        pltpu.VMEM((tok, width), F32),
        pltpu.VMEM((tok, width), BF),
        pltpu.VMEM((2, BLOCK, BLOCK), F32),
    )

    def ffn(x1n, dy, fvw, fgw, fow, mix, val, gat, side, tmp_twin):
        def shares(moved, src, dst, places):
            copies = []
            for i in places:
                moved.wait(i)
                copies.append(k.keep(src.at[:, :, near4[i]], dst.at[:, :, near4[i]]))
            return copies

        def fo_shares(places):
            copies = []
            for i in places:
                twin_fo.wait(i)
                for c in range(2):
                    row = pl.multiple_of((c * NARROW + near4[i]) * fo_rows, 16)
                    copies.append(k.keep(fo_in.at[c, near4[i]], fow.at[pl.ds(row, fo_rows)]))
            return copies

        line_fv.finish(twin_fv.send)
        load_fv = shares(twin_fv, fv_in, fvw, range(4))
        plane_x1n.finish_near()
        plane_x1n.finish_far()
        load_x1n = k.keep(x1n_in, x1n)
        for copy in (load_x1n, *load_fv):
            copy.wait()

        def up_val(j, carry):
            val[j] = dot(x1n[j], fvw[...].reshape(width, ff)).astype(BF)
            return carry

        def up_gat(j, carry):
            g = dot(x1n[j], fgw[...].reshape(width, ff))
            gat[j] = g.astype(BF)
            mix[j] = (val[j].astype(F32) * g).astype(BF)
            return carry

        lax.fori_loop(0, CHIPS, up_val, 0)
        line_fo.forward()
        plane_dy.forward()
        load_fg = []
        line_fg.finish(twin_fg.send, lambda: load_fg.extend(shares(twin_fg, fg_in, fgw, range(3))))
        line_fo.start_home()
        load_fg += shares(twin_fg, fg_in, fgw, range(3, 4))
        for copy in load_fg:
            copy.wait()
        line_fo.forward_far()
        lax.fori_loop(0, CHIPS // 2, up_gat, 0)
        plane_dy.finish_near()
        plane_dy.finish_far()
        load_dy = k.keep(dy_in, dy)
        lax.fori_loop(CHIPS // 2, CHIPS, up_gat, 0)
        load_dy.wait()

        def digits(*chunks):
            return sum(chunk * 8**place for place, chunk in enumerate(chunks))

        high = lax.div(k.far, 3)
        chunk_order = (
            (1 - core) * ((1 - high) * digits(2, 3, 0, 4, 5, 1) + high * digits(5, 2, 3, 4, 0, 1))
            + core * ((1 - high) * digits(0, 2, 3, 1, 4, 5) + high * digits(2, 5, 0, 1, 3, 4))
        )

        def fo_grad(j, left_over):
            chunk = lax.rem(left_over, 8)
            rows = pl.ds(pl.multiple_of(chunk * 256 - lax.div(chunk, 4) * 128, 128), 256)
            left = mix[:, :, rows].reshape(CHIPS * tok, 256)
            for h in range(2):
                lanes = slice(h * width // 2, (h + 1) * width // 2)
                right = dy[:, :, lanes].reshape(CHIPS * tok, -1)
                g_fo[rows, lanes] = dot_lt(left, right).astype(BF)
            return lax.div(left_over, 8)

        def fo_twin(i):
            return twin(0, near4[i], fo_part(other, near4[i]), twin_fo_land.at[near4[i]])

        def fo_load(i):
            fo_twin(i).wait_recv()
            return k.keep(twin_fo_land.at[near4[i]], stage.at[i, pl.ds(0, fo_rows)])

        def fo_add(i, load):
            load.wait()
            own = fo_part(core, near4[i])
            own[...] = (own[...].astype(F32) + stage[i, 0:fo_rows].astype(F32)).astype(BF)
            fo_twin(i).wait_send()
            if i > 0:
                sum_fo.begin(3 - i)

        chunk_order = lax.fori_loop(0, 2, fo_grad, chunk_order)
        fo_twin(3).start()
        chunk_order = lax.fori_loop(2, 3, fo_grad, chunk_order)
        fo_add(3, fo_load(3))
        chunk_order = lax.fori_loop(3, 5, fo_grad, chunk_order)
        for i in reversed(range(3)):
            fo_twin(i).start()
        lax.fori_loop(5, 6, fo_grad, chunk_order)
        loads = [fo_load(i) for i in reversed(range(3))]
        for i, load in zip(reversed(range(3)), loads):
            fo_add(i, load)
        load_fo = []
        line_fo.finish(twin_fo.send, lambda: load_fo.extend(fo_shares(range(3))))
        load_fo += fo_shares(range(3, 4))
        for copy in load_fo:
            copy.wait()

        def down(q, carry):
            d_mix = dot_rt(dy[q], fow[...])
            d_val = (d_mix * gat[q].astype(F32)).astype(BF)
            d_gat = (d_mix * val[q].astype(F32)).astype(BF)
            val[q] = d_val
            gat[q] = d_gat
            return carry

        lax.fori_loop(0, CHIPS, down, 0)

        def out_step(q, carry):
            dy[q] = dot(mix[q], fow[...]).astype(BF)
            return carry

        def back(j, carry):
            q = nth(j)

            def back_lanes(i, carry):
                lanes = at(i * 512, 512)
                d_x = dot_rt(val[q], fvw[i].reshape(512, ff)) + dot_rt(
                    gat[q], fgw[i].reshape(512, ff)
                )

                @pl.when(j < 3)
                def _():
                    stage[q, :, lanes] = d_x.astype(BF)

                @pl.when(j == 3)
                def _():
                    acc[:, lanes] = d_x

                return carry

            lax.fori_loop(0, width // 512, back_lanes, 0)
            for step, push in enumerate((plane_mid.send_far, plane_mid.send_x, plane_mid.send_y)):
                pl.when(j == step)(push)
            return carry

        for m, (d_ff, g_ff) in enumerate(((val, g_fv), (gat, g_fg))):

            def ff_grad(owner):
                left = x1n[:, :, at(owner * tok, tok)].reshape(CHIPS * tok, tok)
                g = dot_lt(left, d_ff[...].reshape(CHIPS * tok, ff)).astype(BF)
                return g.reshape(NARROW, -1, ff)

            def side_step(q, carry):
                slot = lax.rem(q, 2)

                @pl.when(q >= 2)
                def _():
                    twin(1 + m, q - 2, side.at[slot], twin_ff.at[m, q]).wait_send()

                side[slot] = ff_grad(2 * q + other)
                twin(1 + m, q, side.at[slot], twin_ff.at[m, q]).start()
                return carry

            def own_step(q, carry):
                g_ff[q] = ff_grad(2 * q + core)
                return carry

            for h in range(2):
                lax.fori_loop(2 * h, 2 * h + 2, side_step, 0)
                lax.fori_loop(2 * h, 2 * h + 2, own_step, 0)
                loads = []
                for q in (2 * h, 2 * h + 1):
                    twin(1 + m, q, side.at[q % 2], twin_ff.at[m, q]).wait_recv()
                    loads.append(k.keep(twin_ff.at[m, q], (tmp_ff, tmp_twin)[q % 2]))
                for q, load in zip((2 * h, 2 * h + 1), loads):
                    load.wait()
                    own = g_ff.at[q]
                    own[...] = (
                        own[...].astype(F32) + (tmp_ff, tmp_twin)[q % 2][...].astype(F32)
                    ).astype(BF)
                if m == 0:
                    sum_ff[m].begin_half(h)
            for q in range(2, CHIPS):
                twin(1 + m, q, side.at[q % 2], twin_ff.at[m, q]).wait_send()
            if m == 1:
                sum_ff[m].begin(0)
            sum_ff[m].begin(1)
            sum_ff[m].begin(2)
            if m == 0:
                lax.fori_loop(0, CHIPS, back, 0)
                lax.fori_loop(0, CHIPS, out_step, 0)
                store = k.keep(dy, res_in)
                plane_mid.combine(add_half)
                store.wait()
                plane_res.send_far()
                plane_res.send_x()
                plane_res.send_y()
                sum_fo.pass_on(0, add_fo)
                sum_fo.pass_on(1, add_fo)

        sum_fo.pass_on(2, add_fo)
        plane_mid.drain()

    pl.run_scoped(
        ffn,
        pltpu.VMEM((CHIPS, tok, width), BF),
        pltpu.VMEM((CHIPS, tok, width), BF),
        pltpu.VMEM(fv_in.shape, BF),
        pltpu.VMEM(fg_in.shape, BF),
        pltpu.VMEM((ff, width), BF),
        pltpu.VMEM((CHIPS, tok, ff), BF),
        pltpu.VMEM((CHIPS, tok, ff), BF),
        pltpu.VMEM((CHIPS, tok, ff), BF),
        pltpu.VMEM((2, *g_fv.shape[1:]), BF),
        pltpu.VMEM(g_fv.shape[1:], BF),
    )

    def rest(d_x1, d_branch, mixed, da_src, factors_src, side, stage_wo, g_wo, g_qk, g_vg):
        plane_out = plane_sum(2, stage_wo)
        sum_wo = LineSum(k, lambda i: g_wo.at[i], lambda s: land_wo.at[s])
        sum_qk = [
            LineSum(k, lambda i, g=g: g.at[:, i], lambda s, m=m: land_qk.at[m, s])
            for m, g in enumerate((g_qk, g_vg))
        ]
        spread_a = Spread(
            k,
            lambda t: da_src.at[:, at(t * two, two)],
            lambda s: a_land.at[s],
            a_land.at[pl.ds(0, WIDE - 1)],
        )
        spread_s = Spread(
            k, lambda t: factors_src, lambda s: s_land.at[s], s_land.at[pl.ds(0, WIDE - 1)]
        )

        def middle(wo, x1, gated, means, dy, d_mixed, pair):
            plane_mid.finish()
            loads = [k.keep(near.at[0], pair), k.keep(x1_in, x1), k.keep(dy_in.at[chip], dy)]
            late = [
                k.keep(wo_in, wo), k.keep(gated_in, gated), k.keep(mixed_in, mixed),
            ]
            for copy in loads:
                copy.wait()

            def norm_back(rows):
                g = acc[rows, :] + pair[0, rows, :].astype(F32) + pair[1, rows, :].astype(F32)
                v = x1[rows, :]
                r = row_scale(v)
                u = v * r
                d = dy[rows, :].astype(F32) + r * (g - u * jnp.mean(g * u, axis=-1, keepdims=True))
                d_x1[rows, :] = d
                d_branch[rows, :] = d.astype(BF)

            row_chunks(tok, norm_back)
            for copy in late:
                copy.wait()

            def mixed_step(j, carry):
                d_mixed[:, at(j * 512, 512)] = dot_rt(
                    d_branch[...], wo[pl.ds(2 * j, 2)].reshape(512, width)
                )
                return carry

            lax.fori_loop(0, width // 512, mixed_step, 0)

            def mixed_back(rows):
                d = d_mixed[rows, :]
                da_src[rows, :] = d.astype(BF)
                mean = jnp.mean(d * gated[rows, :].astype(F32), axis=-1, keepdims=True)
                means[rows, :] = jnp.broadcast_to(mean * scales[rows, 0:1], (mean.shape[0], HEAD))

            row_chunks(tok, mixed_back)
            factors_src[0] = jnp.transpose(scales[...])[0:8]
            factors_src[1] = jnp.transpose(means[...])[0:8]
            spread_s.start()
            spread_a.start()
            own = [
                k.keep(da_src.at[:, at(w * two, two)], a_land.at[w]),
                k.keep(factors_src, s_land.at[w]),
            ]

            for copy in own:
                copy.wait()

        pl.run_scoped(
            middle,
            pltpu.VMEM(wo_in.shape, BF),
            pltpu.VMEM((tok, width), F32),
            pltpu.VMEM((tok, width), BF),
            pltpu.VMEM((tok, HEAD), F32),
            pltpu.VMEM((tok, width), BF),
            pltpu.VMEM((tok, width), F32),
            pltpu.VMEM((2, tok, width), BF),
        )
        ff_turns = [
            Spread(
                k,
                lambda t, g=g: g.at[lax.div(t, 2), n],
                lambda s, m=m: turn_ff.at[m, lax.div(s, 2)],
                turn_ff.at[m, pl.ds(0, CHIPS - 1)],
                peers=CHIPS,
            )
            for m, g in enumerate((g_fv, g_fg))
        ]

        def total(part, lands):
            return part.astype(F32) + lands[0].astype(F32) + lands[1].astype(F32)

        def move_ff(m, g_ff, three_ff):
            sum_ff[m].finish(fetch, three_ff)
            for q in range(CHIPS):
                g_ff[q, n] = total(g_ff[q, n], three_ff[:, q]).astype(BF)
            ff_turns[m].start()
            k.keep(g_ff.at[chip, n], turn_ff.at[m, chip]).wait()

        def eight_way(plane, twin_index, landing, blocks, spots, term):
            def side_step(j, carry):
                q = nth(j)
                side[q] = term(2 * q + other).astype(BF)
                twin(twin_index, j, side.at[q], landing.at[q]).start()
                return carry

            lax.fori_loop(0, CHIPS, side_step, 0)

            def load(j):
                q = order[j]
                twin(twin_index, j, side.at[q], landing.at[q]).wait_recv()
                return k.keep(landing.at[q], spots[j % 2])

            pushes = (plane.send_far, plane.send_x, plane.send_y)
            loads = [load(0)]
            for j in range(CHIPS):
                if j + 1 < CHIPS and spots[0] is not spots[1]:
                    loads.append(load(j + 1))
                v = term(2 * order[j] + core)
                loads[j].wait()
                v = v + spots[j % 2][...].astype(F32)
                if j < 3:
                    blocks[order[j]] = v.astype(BF)
                    pushes[j]()
                else:
                    acc[...] = v
                if j + 1 < CHIPS and spots[0] is spots[1]:
                    loads.append(load(j + 1))
            for j in range(CHIPS):
                twin(twin_index, j, side.at[order[j]], landing.at[order[j]]).wait_send()

        eight_way(
            plane_out,
            3,
            twin_wo,
            stage_wo,
            (tmp, tmp),
            lambda owner: dot_lt(mixed[:, at(owner * tok, tok)], d_branch[...]),
        )
        sum_ff[0].pass_on(0, add_ff)
        sum_ff[0].pass_on(1, add_ff)

        def attention(xn, d_qk, d_vg, state):
            state[...] = jnp.zeros_like(state)

            def heads(slopes, qkv, sin, decay, attn, gate, d_mixed, factors_in):
                loads = [
                    k.keep(qkv_in, qkv), k.keep(sin_in, sin), k.keep(slope_in, slopes),
                    k.keep(attn_in, attn), k.keep(gate_in, gate),
                ]
                fill_decay(decay)
                for copy in loads:
                    copy.wait()
                plane_res.combine(add_res)
                spread_s.finish()
                spread_a.finish()
                loads = [k.keep(a_land, d_mixed), k.keep(s_land, factors_in)]
                for copy in loads:
                    copy.wait()
                load_xn = k.keep(xn_in, xn)

                def step(i, carry):
                    b = WIDE - 1 - i
                    rows = at(b * BLOCK, BLOCK)
                    mask, factors = block_tables(b)
                    scale, mean = (
                        jnp.transpose(jnp.broadcast_to(factors_in[b, i, 0:1], (HEAD, tok)))[:, 0:1]
                        for i in range(2)
                    )
                    normed = attn[b].astype(F32) * scale
                    d_m = d_mixed[b].astype(F32)
                    d_vg[rows, two:] = (d_m * normed).astype(BF)
                    d_attn = (scale * (d_m * gate[b].astype(F32) - normed * mean)).astype(BF)
                    for h in range(2):
                        entry, tail, through = factors[h]
                        lanes = slice(h * HEAD, (h + 1) * HEAD)
                        key_lanes = slice(two + h * HEAD, two + (h + 1) * HEAD)
                        q = qkv[rows, lanes]
                        key = qkv[rows, key_lanes]
                        v = qkv[rows, 2 * two + h * HEAD : 2 * two + (h + 1) * HEAD]
                        d_o = d_attn[:, lanes]
                        factor = jnp.where(mask, decay[h], 0.0)
                        probs = (dot_rt(q, key) * factor).astype(BF)
                        d_probs = (dot_rt(d_o, v) * factor).astype(BF)
                        before = sin[b, h]
                        after = state[h]
                        after_bf = after.astype(BF)
                        tailed = (key.astype(F32) * tail).astype(BF)
                        entered = (q.astype(F32) * entry).astype(BF)
                        d_q = dot(d_probs, key) + entry * dot_rt(d_o, before)
                        d_k = dot_lt(d_probs, q) + tail * dot_rt(v, after_bf)
                        d_v = dot_lt(probs, d_o) + dot(tailed, after_bf)
                        d_qk[rows, lanes] = (d_q * slopes[rows, lanes].astype(F32)).astype(BF)
                        d_qk[rows, key_lanes] = (d_k * slopes[rows, key_lanes].astype(F32)).astype(BF)
                        d_vg[rows, lanes] = d_v.astype(BF)
                        state[h] = through * after + dot_lt(entered, d_o)
                    return carry

                lax.fori_loop(0, WIDE, step, 0)
                sum_ff[0].pass_on(2, add_ff)
                load_xn.wait()

            pl.run_scoped(
                heads,
                pltpu.VMEM(slope_in.shape, BF),
                pltpu.VMEM(qkv_in.shape, BF),
                pltpu.VMEM(sin_in.shape, BF),
                pltpu.VMEM((2, BLOCK, BLOCK), F32),
                pltpu.VMEM((WIDE, tok, two), BF),
                pltpu.VMEM((WIDE, tok, two), BF),
                pltpu.VMEM((WIDE, tok, two), BF),
                pltpu.VMEM(s_land.shape, F32),
            )

            for m, (d_in, g_in) in enumerate(((d_qk, g_qk), (d_vg, g_vg))):

                def in_grad(s, carry):
                    left = xn[:, :, at(s * tok, tok)].reshape(WIDE * tok, tok)
                    g_in[s] = dot_lt(left, d_in[...]).astype(BF).reshape(NARROW, -1, 2 * two)
                    return carry

                lax.fori_loop(0, WIDE, in_grad, 0)
                sum_qk[m].begin(0)
                sum_qk[m].begin(1)
                if m == 0:
                    sum_qk[m].begin(2)
                    plane_out.combine(add_half)
                    pl.run_scoped(
                        lambda three_ff: pl.when(k.mid == 0)(lambda: move_ff(0, g_fv, three_ff)),
                        pltpu.VMEM((2, *land_ff.shape[2:]), BF),
                    )

            sum_ff[1].pass_on(0, add_ff)
            sum_ff[1].pass_on(1, add_ff)
            g_wo[...] = acc[...].astype(BF).reshape(g_wo.shape)

            def spread_in(wqk, wvg):
                loads = [k.keep(wqk_in, wqk), k.keep(wvg_in, wvg)]
                for copy in loads:
                    copy.wait()

                def term(owner):
                    rows = at(owner * tok, tok)
                    return dot_rt(d_qk[rows, :], wqk[...].reshape(width, 2 * two)) + dot_rt(
                        d_vg[rows, :], wvg[...].reshape(width, 2 * two)
                    )

                spread_a.drain()
                eight_way(plane_in, 4, twin_xn_land, stage, (tmp, da_src), term)

            pl.run_scoped(spread_in, pltpu.VMEM(wqk_in.shape, BF), pltpu.VMEM(wvg_in.shape, BF))

        pl.run_scoped(
            attention,
            pltpu.VMEM((WIDE, tok, width), BF),
            pltpu.VMEM((WIDE * tok, 2 * two), BF),
            pltpu.VMEM((WIDE * tok, 2 * two), BF),
            pltpu.VMEM((2, HEAD, HEAD), F32),
        )

        def last(
            x, x1, own_res, pair, three, three_ff, three_qk, qk_src, w_f32, w_fo, tmp_qk
        ):
            add_qk = adder(tmp_qk)
            load_x, load_x1 = k.keep(x_in, x), k.keep(x1_in, x1)
            load_res = k.keep(res_in.at[chip], own_res)
            plane_out.finish()
            fetch(near.at[2], pair)
            for i in range(NARROW):
                rows = pl.ds(i * 64, 64)
                v = g_wo[i].astype(F32) + pair[0, rows, :].astype(F32) + pair[1, rows, :].astype(F32)
                g_wo[i] = v.astype(BF)
            sum_wo.begin(0)
            sum_wo.begin(1)
            sum_qk[1].begin(2)
            sum_wo.begin(2)
            sum_qk[0].pass_on(0, add_qk)
            sum_qk[0].pass_on(1, add_qk)
            sum_ff[1].pass_on(2, add_ff)

            pl.when(k.mid == 0)(lambda: move_ff(1, g_fg, three_ff))
            plane_in.combine(add_half)
            sum_qk[0].pass_on(2, add_qk)
            sum_fo.finish(fetch, three.at[:, pl.ds(0, fo_rows)])
            own = fo_part(core, n)
            for r in range(0, fo_rows, 16):
                rows = pl.ds(r, 16)
                w_fo[rows, :] = total(own[rows, :], three[:, rows, :])
            stores = [k.keep(w_fo, gfo_o)]

            plane_res.finish()
            fetch(near.at[1], pair)
            load_x1.wait()
            load_res.wait()

            def add_up(rows):
                v = x1[rows, :] + own_res[rows, :].astype(F32)
                v = v + pair[0, rows, :].astype(F32) + pair[1, rows, :].astype(F32)
                own_res[rows, :] = v.astype(BF)

            row_chunks(tok, add_up)
            stores.append(k.keep(own_res, result_o))
            sum_qk[1].pass_on(0, add_qk)
            pl.when(k.mid == 1)(lambda: move_ff(0, g_fv, three_ff))
            sum_qk[1].pass_on(1, add_qk)
            sum_qk[1].pass_on(2, add_qk)

            def move_qk(m, g_in):
                sum_qk[m].finish(fetch, three_qk)
                for s in range(WIDE):
                    qk_src[m, s] = total(g_in[s, n], three_qk[:, s]).astype(BF)
                turn = Spread(
                    k,
                    lambda t: qk_src.at[m, t],
                    lambda s: turn_qk.at[m, s],
                    turn_qk.at[m, pl.ds(0, WIDE - 1)],
                )
                turn.start()
                return turn, k.keep(qk_src.at[m, w], turn_qk.at[m, w])

            qk_turns = [move_qk(0, g_qk)]
            sum_wo.pass_on(0, add_wo)
            pl.when(k.mid == 1)(lambda: move_ff(1, g_fg, three_ff))
            sum_wo.pass_on(1, add_wo)
            sum_wo.pass_on(2, add_wo)
            qk_turns.append(move_qk(1, g_vg))
            load_x.wait()
            plane_in.finish()
            fetch(near.at[3], pair)

            def input_back(rows):
                g = acc[rows, :] + pair[0, rows, :].astype(F32) + pair[1, rows, :].astype(F32)
                v = x[rows, :].astype(F32)
                r = row_scale(v)
                u = v * r
                d_x1[rows, :] = d_x1[rows, :] + r * (
                    g - u * jnp.mean(g * u, axis=-1, keepdims=True)
                )

            row_chunks(tok, input_back)
            stores.append(k.keep(d_x1, dx_o))
            for turn in ff_turns:
                turn.finish()
            for turn, copy in qk_turns:
                turn.finish()
                copy.wait()
            sum_wo.finish(fetch, three.at[:, pl.ds(0, 64)])
            w_f32[...] = total(g_wo[n], three[:, 0:64, :])
            stores.append(k.keep(w_f32, go_o))
            for copy in stores:
                copy.wait()
            plane_in.drain()
            plane_out.drain()
            plane_res.drain()
            turns = ff_turns + [turn for turn, copy in qk_turns]
            for moved in (*lines, *planes, *twins, *spreads, *spread_ff):
                moved.drain()
            for sums in (sum_fo, sum_wo, *sum_ff, *sum_qk, spread_s, *turns):
                sums.drain()

        pl.run_scoped(
            last,
            pltpu.VMEM((tok, width), BF),
            pltpu.VMEM((tok, width), F32),
            pltpu.VMEM((tok, width), BF),
            pltpu.VMEM((2, tok, width), BF),
            pltpu.VMEM((2, tok, width), BF),
            pltpu.VMEM((2, *land_ff.shape[2:]), BF),
            pltpu.VMEM((2, *land_qk.shape[2:]), BF),
            pltpu.VMEM((2, WIDE, 64, 2 * two), BF),
            pltpu.VMEM((64, width), F32),
            pltpu.VMEM((fo_rows, width), F32),
            pltpu.VMEM((WIDE, 64, 2 * two), BF),
        )

    pl.run_scoped(
        rest,
        pltpu.VMEM((tok, width), F32),
        pltpu.VMEM((tok, width), BF),
        pltpu.VMEM((tok, width), BF),
        pltpu.VMEM((tok, width), BF),
        pltpu.VMEM((2, 8, tok), F32),
        pltpu.VMEM((CHIPS, tok, width), BF),
        pltpu.VMEM((CHIPS, tok, width), BF),
        pltpu.VMEM((NARROW, 64, width), BF),
        pltpu.VMEM((WIDE, NARROW, 64, 2 * two), BF),
        pltpu.VMEM((WIDE, NARROW, 64, 2 * two), BF),
    )
    assert k.count <= send.shape[0], k.count


def finish_kernel(
    result, d_x, g_out, g_fout, turn_ff, turn_qk,
    result_o, d_x_o, gq_o, gk_o, gv_o, gg_o, go_o, gfv_o, gfg_o, gfo_o,
    result_v, d_x_v, g_out_v, g_fout_v, ff_v, qk_v, ff_f32, qk_f32, sems,
):
    copies = []

    def copy(src, dst):
        made = pltpu.make_async_copy(src, dst, sems.at[len(copies)])
        made.start()
        copies.append(made)
        return made

    ff, two = ff_v.shape[-1], qk_v.shape[-1] // 2
    load_ff, load_qk = copy(turn_ff, ff_v), copy(turn_qk, qk_v)
    through = (
        (d_x, d_x_v, d_x_o),
        (g_fout, g_fout_v, gfo_o),
        (result, result_v, result_o),
        (g_out, g_out_v, go_o),
    )
    loads = [copy(src, held) for src, held, _ in through]
    stores = []
    load_ff.wait()
    for m, out in enumerate((gfv_o, gfg_o)):
        for q in range(CHIPS):
            ff_f32[m, :, q * ff : (q + 1) * ff] = ff_v[m, q].astype(F32)
        stores.append(copy(ff_f32.at[m], out))
    load_qk.wait()
    for m, outs in enumerate(((gq_o, gk_o), (gv_o, gg_o))):
        for s in range(WIDE):
            lanes = slice(s * two, (s + 1) * two)
            qk_f32[2 * m, :, lanes] = qk_v[m, s, :, 0:two].astype(F32)
            qk_f32[2 * m + 1, :, lanes] = qk_v[m, s, :, two:].astype(F32)
        stores += [copy(qk_f32.at[2 * m + i], out) for i, out in enumerate(outs)]
    for load, (_, held, out) in zip(loads, through):
        load.wait()
        stores.append(copy(held, out))
    for store in stores:
        store.wait()


def finish(results, moved):
    out_shape = moved
    return pl.pallas_call(
        finish_kernel,
        out_shape=out_shape,
        in_specs=[ANY] * 6,
        out_specs=(ANY,) * len(out_shape),
        scratch_shapes=[
            *[pltpu.VMEM(r.shape, r.dtype) for r in results],
            pltpu.VMEM((2, *out_shape[7].shape), F32),
            pltpu.VMEM((4, *out_shape[2].shape), F32),
            pltpu.SemaphoreType.DMA((20,)),
        ],
        compiler_params=pltpu.CompilerParams(vmem_limit_bytes=63 * 2**20),
    )(*results)


def layer(tokens, weights, dy, starts):
    tok, width = tokens.shape
    shard = weights[0].shape[0]
    ff = weights[5].shape[1] // CHIPS
    fo_rows = weights[7].shape[0]
    full = WIDE * tok
    two = 2 * HEAD

    def arr(*shape, dtype=BF):
        return jax.ShapeDtypeStruct(shape, dtype)

    finals = (
        arr(tok, width),
        arr(tok, width, dtype=F32),
        *[arr(shard, width, dtype=F32)] * 5,
        arr(shard, CHIPS * ff, dtype=F32),
        arr(shard, CHIPS * ff, dtype=F32),
        arr(fo_rows, width, dtype=F32),
    )
    results = (
        arr(tok, width),
        arr(tok, width, dtype=F32),
        arr(shard, width, dtype=F32),
        arr(fo_rows, width, dtype=F32),
        arr(2, CHIPS, shard, ff),
        arr(2, WIDE, shard, 2 * two),
    )
    held = (
        arr(WIDE, tok, width),
        arr(WIDE, NARROW, shard, 2 * two),
        arr(WIDE, NARROW, shard, 2 * two),
        arr(WIDE, NARROW, shard, width),
        arr(CHIPS, 2, NARROW, shard, ff),
        arr(CHIPS, 2, NARROW, shard, ff),
        arr(2, NARROW, fo_rows, width),
        arr(CHIPS, tok, width),
        arr(full, 2 * two),
        arr(full, 3 * two),
        arr(WIDE, 2, HEAD, HEAD),
        arr(WIDE, tok, two),
        arr(WIDE, tok, two),
        arr(tok, width),
        arr(tok, width),
        arr(tok, width, dtype=F32),
        arr(CHIPS, tok, width),
    )
    landings = (
        arr(4, 2, tok // 2, width),
        arr(4, 2, tok, width),
        arr(NARROW, fo_rows, width),
        arr(2, CHIPS, NARROW, shard, ff),
        arr(CHIPS, tok, width),
        arr(CHIPS, tok, width),
        arr(5, fo_rows, width),
        arr(2, 5, CHIPS, shard, ff),
        arr(5, shard, width),
        arr(2, 5, WIDE, shard, 2 * two),
        arr(WIDE, tok, two),
        arr(WIDE, 2, 8, tok, dtype=F32),
        arr(WIDE, 8, tok, dtype=F32),
        arr(CHIPS, tok, width),
    )
    out_shape = results + held + landings
    outs = pl.pallas_call(
        layer_kernel,
        out_shape=out_shape,
        in_specs=[ANY] * 10 + [pl.BlockSpec(memory_space=pltpu.SMEM)],
        out_specs=(ANY,) * len(out_shape),
        scratch_shapes=[
            pltpu.VMEM((ff, width), BF),
            pltpu.VMEM((CHIPS, NARROW, shard, ff), BF),
            pltpu.VMEM((CHIPS, NARROW, shard, ff), BF),
            pltpu.VMEM((CHIPS, tok, width), BF),
            pltpu.VMEM((tok, width), F32),
            pltpu.VMEM((tok, width), BF),
            pltpu.VMEM((tok, HEAD), F32),
            pltpu.VMEM((CHIPS, shard, ff), BF),
            pltpu.SemaphoreType.DMA((163,)),
            pltpu.SemaphoreType.DMA((163,)),
            pltpu.SemaphoreType.DMA((40,)),
        ],
        compiler_params=pltpu.CompilerParams(
            collective_id=0, has_side_effects=True, vmem_limit_bytes=65300 * 2**10
        ),
        cost_estimate=pl.CostEstimate(flops=8 * 10**10, bytes_accessed=3 * 10**8, transcendentals=0),
    )(tokens, *weights, dy, starts)
    return finish(outs[: len(results)], finals)


def local_box(tokens, doc_starts, wq, wk, wv, wg, wo, fv, fg, fo, cotangent):
    weights = (wq, wk, wv, wg, wo, fv, fg, fo)
    outs = layer(tokens[0], weights, cotangent[0], doc_starts)
    return (outs[0][None], outs[1][None]) + tuple(outs[2:])


def solution(mesh):
    box = (mesh.shape["wide"], mesh.shape["narrow"]) == (WIDE, NARROW)
    tok = P("narrow", "wide", None)
    row = P(BOTH, None)
    return jax.shard_map(
        local_box if box else local,
        mesh=mesh,
        in_specs=(tok, P()) + (row,) * 8 + (tok,),
        out_specs=(tok, tok) + (row,) * 8,
        check_vma=False,
    )
```
